32 devices in a mesh: wide: 8 (over y, x, core), narrow: 4 (over z).
Axes of the slice: x: 2, y: 2, z: 4, core: 2. Of those that a mesh axis runs over, the one named last changes fastest.
Arguments:
- inputs: bfloat16 [10240, 768], P(('wide', 'narrow')), may hold values from -6 to 6
- memory: bfloat16 [32768, 768], P(('wide', 'narrow')), may hold values from -6 to 6
- targets: int32 [10240], P(('wide', 'narrow')), may hold values from 0 to 32127
- tgt_lengths: int32 [32, 2], P(('wide', 'narrow')), may hold values from 0 to 320, as said below
- src_lengths: int32 [32, 2], P(('wide', 'narrow')), may hold values from 0 to 1024, as said below
- self_gain: bfloat16 [768], P(('wide', 'narrow')), may hold values from 0.5 to 1.5
- self_query: bfloat16 [768, 768], P(('wide', 'narrow')), may hold values from -0.0546875 to 0.0546875
- self_key: bfloat16 [768, 768], P(('wide', 'narrow')), may hold values from -0.21875 to 0.21875
- self_value: bfloat16 [768, 768], P(('wide', 'narrow')), may hold values from -0.21875 to 0.21875
- self_out: bfloat16 [768, 768], P(('wide', 'narrow')), may hold values from -0.875 to 0.875
- cross_gain: bfloat16 [768], P(('wide', 'narrow')), may hold values from 0.5 to 1.5
- cross_query: bfloat16 [768, 768], P(('wide', 'narrow')), may hold values from -0.0546875 to 0.0546875
- cross_key: bfloat16 [768, 768], P(('wide', 'narrow')), may hold values from -0.21875 to 0.21875
- cross_value: bfloat16 [768, 768], P(('wide', 'narrow')), may hold values from -0.21875 to 0.21875
- cross_out: bfloat16 [768, 768], P(('wide', 'narrow')), may hold values from -0.875 to 0.875
- mlp_gain: bfloat16 [768], P(('wide', 'narrow')), may hold values from 0.5 to 1.5
- mlp_gate: bfloat16 [768, 2048], P(('wide', 'narrow')), may hold values from -0.21875 to 0.21875
- mlp_up: bfloat16 [768, 2048], P(('wide', 'narrow')), may hold values from -0.21875 to 0.21875
- mlp_down: bfloat16 [2048, 768], P(('wide', 'narrow')), may hold values from -0.125 to 0.125
- exit_gain: bfloat16 [768], P(('wide', 'narrow')), may hold values from 0.5 to 1.5
- embedding: bfloat16 [32128, 768], P('wide', 'narrow'), may hold values from -15 to 15
Outputs:
- activations: bfloat16 [10240, 768], P(('wide', 'narrow'))
- mean_loss: float32 [], replicated
- inputs_grad: float32 [10240, 768], P(('wide', 'narrow'))
- memory_grad: float32 [32768, 768], P(('wide', 'narrow'))
- self_gain_grad: float32 [768], P(('wide', 'narrow'))
- self_query_grad: float32 [768, 768], P(('wide', 'narrow'))
- self_key_grad: float32 [768, 768], P(('wide', 'narrow'))
- self_value_grad: float32 [768, 768], P(('wide', 'narrow'))
- self_out_grad: float32 [768, 768], P(('wide', 'narrow'))
- cross_gain_grad: float32 [768], P(('wide', 'narrow'))
- cross_query_grad: float32 [768, 768], P(('wide', 'narrow'))
- cross_key_grad: float32 [768, 768], P(('wide', 'narrow'))
- cross_value_grad: float32 [768, 768], P(('wide', 'narrow'))
- cross_out_grad: float32 [768, 768], P(('wide', 'narrow'))
- mlp_gain_grad: float32 [768], P(('wide', 'narrow'))
- mlp_gate_grad: float32 [768, 2048], P(('wide', 'narrow'))
- mlp_up_grad: float32 [768, 2048], P(('wide', 'narrow'))
- mlp_down_grad: float32 [2048, 768], P(('wide', 'narrow'))
- exit_gain_grad: float32 [768], P(('wide', 'narrow'))
- embedding_grad: float32 [32128, 768], P('wide', 'narrow')
The draws below stay inside these ranges and needn't reach their ends.
Inputs may be any that keep to these rules, and one draw needn't show every extreme that they name: `tgt_lengths`: row b describes bucket b (the device at that place in the order wide, narrow): it holds one pair or 2 pairs, a missing pair having length 0; a row sums to at least 1 and at most 320, and the last row holds one pair of exactly 320. `src_lengths`: source lengths of the same pairs: a pair has a source of length 1 or more exactly when it has a target; a row sums to at most 1024, and some row holds one source of exactly 1024.
All inputs are finite; a program needn't handle non-finite values.
Results may differ from the reference program's by a relative error of at most 0.034.
The reference program's roundings to bfloat16 on the way count: a program that leaves them out, or rounds other values in their place, can miss the bound.
Values may be sent and summed in bfloat16 or wider, within the bound.
No kernel may reach another device: no remote copies, remote signals or barrier semaphores. Data moves between devices by JAX's collectives and lax.ppermute only.
A program may use at most 320 MiB of HBM per device.

```python
import math
import jax
import jax.numpy as jnp
import numpy as np
from jax import lax

D = 768
HEADS = 12
HEAD = 64
FF = 2048
VOCAB = 32128
PAIRS = 2
TGT_DEV = 320
MEM_DEV = 1024
BUCKETS = 32
TOKENS = 10240
MEM_TOKENS = 32768


def bucket_plan(key):
    base_key = jax.random.fold_in(key, 11)
    subkeys = jax.random.split(base_key, 6)
    bucket_ids = jnp.arange(BUCKETS, dtype=jnp.int32)
    last_id = BUCKETS - 1
    quarter = TGT_DEV // 4
    ceiling = quarter + (TGT_DEV - quarter) * bucket_ids // max(BUCKETS - 1, 1)
    shorten = jax.random.randint(subkeys[2], (BUCKETS,), 0, TGT_DEV // 8 + 1)
    shorten = jnp.where((bucket_ids == 1) | (bucket_ids == last_id), 0, shorten)
    total = jnp.maximum(ceiling - shorten, 1)
    paired = jax.random.randint(subkeys[0], (BUCKETS,), 0, 2)
    paired = jnp.where(bucket_ids == 1, 1, paired)
    paired = jnp.where((bucket_ids == last_id) | (total < 2), 0, paired)
    lengthy = jax.random.randint(subkeys[1], (BUCKETS,), 0, 4) == 0
    lengthy = (lengthy | (bucket_ids == last_id)) & (paired == 0)
    split_at = jax.random.randint(subkeys[3], (BUCKETS,), 0, 1 << 20)
    first_len = 1 + split_at % jnp.maximum(total - 1, 1)
    sources = jax.random.randint(subkeys[5], (BUCKETS, 2), MEM_DEV // 16, MEM_DEV // 2)
    target_part = jnp.stack([jnp.where(paired == 1, first_len, total), jnp.where(paired == 1, total - first_len, 0)], axis=1)
    source_part = jnp.stack([jnp.where(lengthy, MEM_DEV, sources[:, 0]), jnp.where(paired == 1, sources[:, 1], 0)], axis=1)
    return (target_part.astype(jnp.int32), source_part.astype(jnp.int32))


def draw_tgt_lengths(key, part):
    return bucket_plan(key)[0]


def draw_src_lengths(key, part):
    return bucket_plan(key)[1]


def set_ends(values, stream_key, smallest, largest):
    longest = values.shape.index(max(values.shape))
    spots = []
    for shift in (0, 1):
        where = [jax.random.randint(jax.random.fold_in(stream_key, axis), (), 0, length) for axis, length in enumerate(values.shape)]
        where[longest] = (where[longest] + shift) % values.shape[longest]
        spots.append(tuple(where))
    return values.at[spots[0]].set(smallest).at[spots[1]].set(largest)


def block_levels(own_key, shape, cuts, smallest, top_value):
    loudness = 1.0
    for position, blocks in cuts:
        steps = jax.random.uniform(jax.random.fold_in(jax.random.fold_in(own_key, 6), position), (blocks,), jnp.float32, smallest / len(cuts), top_value / len(cuts))
        loudness = loudness * jnp.repeat(jnp.exp(steps), shape[position] // blocks).reshape((-1,) + (1,) * (len(shape) - 1 - position))
    return loudness


def cumulative_ranks(amount, slope):
    portions = [(1 << 20) // math.isqrt(grade ** slope) + 1 for grade in range(1, amount + 1)]
    deviation = 1 + sum(portions) // (1 << 30)
    return np.cumsum(np.array([max(1, weight // deviation) for weight in portions]))


def skewed_ids(key, extent, number_of, lean):
    table = cumulative_ranks(number_of, lean)
    ticket = jax.random.randint(jax.random.fold_in(key, 1), extent, 0, int(table[number_of - 1]))
    grade = jnp.searchsorted(jnp.asarray(table, jnp.int32), ticket, side="right")
    return jax.random.permutation(jax.random.fold_in(key, 2), number_of)[grade].astype(jnp.int32)


def bell_draw(stream_key, dims, spread, limit, cuts=(), held_as=jnp.bfloat16):
    drawn = spread * jax.random.normal(stream_key, dims, jnp.float32)
    if cuts:
        drawn = drawn * block_levels(stream_key, dims, cuts, -0.22, 0.18)
    return jnp.clip(drawn, -limit, limit).astype(held_as)


def setup_inputs(seed: int = 0) -> dict:
    seeds = jax.random.split(jax.random.key(seed), 22)
    inputs = bell_draw(seeds[0], (TOKENS, D), 1.0, 6.0, ((0, 32),))
    memory = bell_draw(seeds[1], (MEM_TOKENS, D), 1.0, 6.0, ((0, 32),))
    targets = set_ends(skewed_ids(seeds[2], (TOKENS,), VOCAB, 2), jax.random.fold_in(seeds[2], 3), 0, VOCAB - 1).astype(jnp.int32)
    tgt_lengths = draw_tgt_lengths(jax.random.fold_in(seeds[21], 71), 0)
    src_lengths = draw_src_lengths(jax.random.fold_in(seeds[21], 71), 0)
    self_gain = jnp.clip(1.0 + 0.1 * jax.random.normal(seeds[5], (D,), jnp.float32), 0.5, 1.5).astype(jnp.bfloat16)
    self_query = bell_draw(seeds[6], (D, D), (16 * D) ** -0.5, 0.0546875, ((0, 32),))
    self_key = bell_draw(seeds[7], (D, D), D ** -0.5, 0.21875, ((0, 32),))
    self_value = bell_draw(seeds[8], (D, D), D ** -0.5, 0.21875, ((0, 32),))
    self_out = bell_draw(seeds[9], (D, D), (D // 16) ** -0.5, 0.875, ((0, 32),))
    cross_gain = jnp.clip(1.0 + 0.1 * jax.random.normal(seeds[10], (D,), jnp.float32), 0.5, 1.5).astype(jnp.bfloat16)
    cross_query = bell_draw(seeds[11], (D, D), (16 * D) ** -0.5, 0.0546875, ((0, 32),))
    cross_key = bell_draw(seeds[12], (D, D), D ** -0.5, 0.21875, ((0, 32),))
    cross_value = bell_draw(seeds[13], (D, D), D ** -0.5, 0.21875, ((0, 32),))
    cross_out = bell_draw(seeds[14], (D, D), (D // 16) ** -0.5, 0.875, ((0, 32),))
    mlp_gain = jnp.clip(1.0 + 0.1 * jax.random.normal(seeds[15], (D,), jnp.float32), 0.5, 1.5).astype(jnp.bfloat16)
    mlp_gate = bell_draw(seeds[16], (D, FF), D ** -0.5, 0.21875, ((0, 32),))
    mlp_up = bell_draw(seeds[17], (D, FF), D ** -0.5, 0.21875, ((0, 32),))
    mlp_down = bell_draw(seeds[18], (FF, D), FF ** -0.5, 0.125, ((0, 32),))
    exit_gain = jnp.clip(1.0 + 0.1 * jax.random.normal(seeds[19], (D,), jnp.float32), 0.5, 1.5).astype(jnp.bfloat16)
    embedding = bell_draw(seeds[20], (VOCAB, D), 2.5, 15.0, ((0, 8), (1, 4)))
    return {"inputs": inputs, "memory": memory, "targets": targets, "tgt_lengths": tgt_lengths, "src_lengths": src_lengths, "self_gain": self_gain, "self_query": self_query, "self_key": self_key, "self_value": self_value, "self_out": self_out, "cross_gain": cross_gain, "cross_query": cross_query, "cross_key": cross_key, "cross_value": cross_value, "cross_out": cross_out, "mlp_gain": mlp_gain, "mlp_gate": mlp_gate, "mlp_up": mlp_up, "mlp_down": mlp_down, "exit_gain": exit_gain, "embedding": embedding}


@jax.custom_vjp
def low(v):
    return lax.optimization_barrier(v.astype(jnp.bfloat16)).astype(jnp.float32)

@jax.custom_vjp
def low_back(v):
    return v

def low_keep(v):
    return (low(v), None)

def low_pass(kept, grad):
    return (grad,)

def back_keep(v):
    return (v, None)

def back_low(kept, grad):
    return (low(grad),)
low.defvjp(low_keep, low_pass)
low_back.defvjp(back_keep, back_low)
EPSILON = 1e-06
NEGATIVE = -1e+30
HIGHEST = lax.Precision.HIGHEST

def rms_norm(values, norm_gain):
    return values * lax.rsqrt(lax.optimization_barrier(jnp.mean(values * values, axis=-1, keepdims=True)) + EPSILON) * norm_gain

def segments(lengths, length):
    boundary = jnp.cumsum(lengths)
    places = jnp.arange(length, dtype=jnp.int32)
    return lax.optimization_barrier(jnp.sum((places[:, None] >= boundary[None, :]).astype(jnp.int32), axis=1))

def matmul(left_side, right_side):
    return jnp.dot(left_side, right_side, precision=HIGHEST, preferred_element_type=jnp.float32)

def rounded(values):
    return low(low_back(values))

def attention(queries, key_rows, value_rows, allowed):
    query_heads = queries.reshape(queries.shape[0], HEADS, HEAD)
    key_heads = key_rows.reshape(key_rows.shape[0], HEADS, HEAD)
    value_heads = value_rows.reshape(value_rows.shape[0], HEADS, HEAD)
    scores = jnp.einsum('thd,shd->hts', query_heads, key_heads, precision=HIGHEST)
    scores = jnp.where(allowed[None], low_back(scores), NEGATIVE)
    log_total = jax.nn.logsumexp(scores, axis=-1, keepdims=True)
    weights_low = low(jnp.exp(scores - log_total))
    mixed = jnp.einsum('hts,shd->thd', weights_low, value_heads, precision=HIGHEST)
    return rounded(mixed.reshape(queries.shape[0], HEADS * HEAD))

def layer(params, stream_zero, memory_rows, target_ids, target_lengths, source_lengths):
    self_gain, self_query, self_key, self_value, self_out, cross_gain, cross_query, cross_key, cross_value, cross_out, mlp_gain, mlp_gate, mlp_up, mlp_down, exit_gain, embedding = params
    target_seg = segments(target_lengths, TGT_DEV)
    memory_seg = segments(source_lengths, MEM_DEV)
    places = jnp.arange(TGT_DEV, dtype=jnp.int32)
    self_mask = (target_seg[:, None] == target_seg[None, :]) & (places[None, :] <= places[:, None])
    cross_mask = (target_seg[:, None] == memory_seg[None, :]) | (target_seg[:, None] == PAIRS)
    normed_one = low(rms_norm(stream_zero, self_gain))
    query_one = rounded(matmul(normed_one, self_query))
    key_one = rounded(matmul(normed_one, self_key))
    value_one = rounded(matmul(normed_one, self_value))
    stream_one = stream_zero + low_back(matmul(attention(query_one, key_one, value_one, self_mask), self_out))
    normed_two = low(rms_norm(stream_one, cross_gain))
    query_two = rounded(matmul(normed_two, cross_query))
    key_two = rounded(matmul(memory_rows, cross_key))
    value_two = rounded(matmul(memory_rows, cross_value))
    stream_two = stream_one + low_back(matmul(attention(query_two, key_two, value_two, cross_mask), cross_out))
    normed_three = low(rms_norm(stream_two, mlp_gain))
    gate_pre = low_back(matmul(normed_three, mlp_gate))
    up_pre = low_back(matmul(normed_three, mlp_up))
    hidden = low(jax.nn.gelu(gate_pre, approximate=True) * up_pre)
    stream_three = stream_two + low_back(matmul(hidden, mlp_down))
    normed_four = low(rms_norm(stream_three, exit_gain))
    logits = low_back(jnp.dot(normed_four, embedding.T, precision=HIGHEST, preferred_element_type=jnp.float32)) * (1.0 / math.sqrt(D))
    log_total = jax.nn.logsumexp(logits, axis=-1)
    picked = jnp.take_along_axis(logits, target_ids[:, None], axis=1)[:, 0]
    loss_weight = (target_seg < PAIRS).astype(jnp.float32)
    return (jnp.sum(loss_weight * (log_total - picked)), stream_three)

def reference(inputs, memory, targets, tgt_lengths, src_lengths, self_gain, self_query, self_key, self_value, self_out, cross_gain, cross_query, cross_key, cross_value, cross_out, mlp_gain, mlp_gate, mlp_up, mlp_down, exit_gain, embedding):
    params = tuple((member.astype(jnp.float32) for member in (self_gain, self_query, self_key, self_value, self_out, cross_gain, cross_query, cross_key, cross_value, cross_out, mlp_gain, mlp_gate, mlp_up, mlp_down, exit_gain, embedding)))
    streams = inputs.astype(jnp.float32).reshape(BUCKETS, TGT_DEV, D)
    memories = memory.astype(jnp.float32).reshape(BUCKETS, MEM_DEV, D)
    target_rows = targets.reshape(BUCKETS, TGT_DEV)

    def bucket(running, bucket_items):
        gradients, loss_sum = running
        stream_zero, memory_rows, target_ids, target_lengths, source_lengths = bucket_items

        def loss_of(weights, stream_in, memory_in):
            return layer(weights, stream_in, memory_in, target_ids, target_lengths, source_lengths)
        bucket_loss, pullback, stream_out = jax.vjp(loss_of, params, stream_zero, memory_rows, has_aux=True)
        param_grads, stream_grad, memory_rows_grad = pullback(jnp.ones_like(bucket_loss))
        gradients = jax.tree.map(lambda left_side, right_side: left_side + right_side, gradients, param_grads)
        return ((gradients, loss_sum + bucket_loss), (stream_out, stream_grad, memory_rows_grad))
    initial = (jax.tree.map(jnp.zeros_like, params), jnp.zeros((), jnp.float32))
    (gradients, loss_sum), (outputs, input_grads, memory_grads) = lax.scan(bucket, initial, (streams, memories, target_rows, tgt_lengths, src_lengths))
    return (outputs.reshape(TOKENS, D).astype(jnp.bfloat16), loss_sum / TOKENS, input_grads.reshape(TOKENS, D), memory_grads.reshape(MEM_TOKENS, D), gradients[0], gradients[1], gradients[2], gradients[3], gradients[4], gradients[5], gradients[6], gradients[7], gradients[8], gradients[9], gradients[10], gradients[11], gradients[12], gradients[13], gradients[14], gradients[15])
```

```python
import functools
import math

import jax
import jax.numpy as jnp
from jax import lax
from jax.experimental import pallas as pl
from jax.experimental.pallas import tpu as pltpu
from jax.sharding import PartitionSpec as P

HEADS = 12
EPSILON = 1e-06
NEGATIVE = -1e30
F32 = jnp.float32
BF16 = jnp.bfloat16
LANES = 128
ROW_TILE = 256
VOCAB_TILE = 512
MIX = math.sqrt(2.0 / math.pi)
CUBE = 0.044715

VMEM = pl.BlockSpec(memory_space=pltpu.VMEM)
SMEM = pl.BlockSpec(memory_space=pltpu.SMEM)
ANY = pl.BlockSpec(memory_space=pl.ANY)
PARAMS = pltpu.CompilerParams(vmem_limit_bytes=60 * 2**20)


def nn(left, right):
    return lax.dot_general(left, right, (((1,), (0,)), ((), ())), preferred_element_type=F32)


def nt(left, right):
    return lax.dot_general(left, right, (((1,), (1,)), ((), ())), preferred_element_type=F32)


def tn(left, right):
    return lax.dot_general(left, right, (((0,), (0,)), ((), ())), preferred_element_type=F32)


def like(shape, kind):
    return jax.ShapeDtypeStruct(shape, kind)


def stage_masks(count):
    up = [1 << bit for bit in range(1, count.bit_length() - 1)]
    return up, up[::-1]


def stage_pairs(count):
    even, odd = stage_masks(count)
    return [[(v, v ^ (odd if v % 2 else even)[i]) for v in range(count)] for i in range(len(even))]


def flip_pairs(count):
    return [(v, v ^ 1) for v in range(count)]


def slot_tables(count):
    tables = []
    for masks in stage_masks(count):
        slots = [0]
        for mask in masks:
            slots = slots + [slot ^ mask for slot in slots]
        tables.append(slots)
    even, odd = tables
    return (
        even + [1 ^ slot for slot in odd],
        odd + [1 ^ slot for slot in even],
    )


def slot_places(wide, count):
    even, odd = slot_tables(count)
    table = jnp.where(wide % 2 == 0, jnp.array(even, jnp.int32), jnp.array(odd, jnp.int32))
    return wide ^ table


def gather_wide(block, count):
    held = block[None]
    for pairs in stage_pairs(count):
        held = jnp.concatenate([held, lax.ppermute(held, "wide", pairs)], axis=0)
    return held, lax.ppermute(held, "wide", flip_pairs(count))


def scatter_wide(mine, other, count):
    held = mine.astype(F32) + lax.ppermute(other, "wide", flip_pairs(count)).astype(F32)
    for pairs in stage_pairs(count)[::-1]:
        half = held.shape[0] // 2
        sent = lax.ppermute(held[half:].astype(BF16), "wide", pairs)
        held = held[:half] + sent.astype(F32)
    return held[0]


def narrow_pairs(count, step):
    return [(v, v ^ step) for v in range(count)]


def gather_narrow(block, narrow, count):
    pieces = [block] + [
        lax.ppermute(block, "narrow", narrow_pairs(count, step)) for step in range(1, count)
    ]
    stacked = jnp.stack(pieces)
    return [
        lax.dynamic_index_in_dim(stacked, narrow ^ place, 0, keepdims=False)
        for place in range(count)
    ]


def scatter_narrow(blocks, narrow, count):
    total = lax.dynamic_index_in_dim(blocks, narrow, 0, keepdims=False).astype(F32)
    for step in range(1, count):
        sent = lax.dynamic_index_in_dim(blocks, narrow ^ step, 0, keepdims=False)
        total = total + lax.ppermute(
            sent.astype(BF16), "narrow", narrow_pairs(count, step)
        ).astype(F32)
    return total


def weight_copies(places, mine, other, target, rows, sems):
    half = mine.shape[0]
    matrices = target.shape[0]
    copies = []
    for slot in range(2 * half):
        source = mine if slot < half else other
        start = pl.multiple_of(places[slot] * rows, 8)
        for matrix in range(matrices):
            copies.append(
                pltpu.make_async_copy(
                    source.at[slot % half, pl.ds(matrix * rows, rows), :],
                    target.at[matrix, pl.ds(start, rows), :],
                    sems.at[slot, matrix],
                )
            )
    return copies


def store_blocks(places, value_ref, matrix, rows, mine, other):
    half = mine.shape[0]
    for slot in range(2 * half):
        target = mine if slot < half else other
        start = pl.multiple_of(places[slot] * rows, 8)
        target[slot % half, pl.ds(matrix * rows, rows), :] = value_ref[pl.ds(start, rows), :]


def norm_scale(values):
    return lax.rsqrt(jnp.mean(values * values, axis=-1, keepdims=True) + EPSILON)


def norm_back(values, gain, grad):
    root = norm_scale(values)
    scaled = gain * grad
    gain_grad = jnp.sum(grad * values * root, axis=0, keepdims=True)
    inner = jnp.mean(scaled * values, axis=-1, keepdims=True)
    return root * scaled - values * (root * root * root) * inner, gain_grad


def query_segments(lengths, count):
    places = lax.broadcasted_iota(jnp.int32, (1, count), 1)
    segment = jnp.zeros((1, count), jnp.int32)
    edge = jnp.int32(0)
    for pair in range(lengths.shape[0]):
        edge = edge + lengths[pair]
        segment = segment + (places >= edge).astype(jnp.int32)
    return places, segment


def fill_self_bias(bias, lengths):
    count = bias.shape[1]
    places, segment = query_segments(lengths, count)
    low = jnp.zeros((1, count), jnp.int32)
    edge = jnp.int32(0)
    for pair in range(lengths.shape[0]):
        edge = edge + lengths[pair]
        low = jnp.where(segment == pair + 1, edge, low)
    keys = lax.broadcasted_iota(jnp.int32, bias.shape, 0)
    bias[...] = jnp.where((keys >= low) & (keys <= places), 0.0, NEGATIVE)


def fill_cross_bias(bias, lengths, sources):
    count = bias.shape[1]
    places, segment = query_segments(lengths, count)
    low = jnp.zeros((1, count), jnp.int32)
    high = jnp.full((1, count), bias.shape[0], jnp.int32)
    edge = jnp.int32(0)
    for pair in range(lengths.shape[0]):
        low = jnp.where(segment == pair, edge, low)
        edge = edge + sources[pair]
        high = jnp.where(segment == pair, edge, high)
    keys = lax.broadcasted_iota(jnp.int32, bias.shape, 0)
    bias[...] = jnp.where((keys >= low) & (keys < high), 0.0, NEGATIVE)


def first_half(width):
    return lax.broadcasted_iota(jnp.int32, (1, width), 1) < width // 2


def attend(queries, keys, values, bias, outputs, totals):
    width = 2 * (queries.shape[1] // HEADS)
    chosen = first_half(width)

    def pair_of_heads(pair, carry):
        columns = pl.ds(pl.multiple_of(pair * width, width), width)
        query = queries[:, columns]
        key = keys[:, columns]
        value = values[:, columns].T
        halves = []
        for side in range(2):
            own = jnp.where(chosen if side == 0 else ~chosen, query, 0)
            scores = nt(key, own) + bias[...]
            highest = jnp.max(scores, axis=0, keepdims=True)
            raised = jnp.exp(scores - highest)
            summed = jnp.sum(raised, axis=0, keepdims=True)
            weights = (raised * (1.0 / summed)).astype(BF16)
            totals[2 * pair + side] = highest + jnp.log(summed)
            halves.append(nn(value[side * width // 2 : (side + 1) * width // 2], weights))
        outputs[:, columns] = jnp.concatenate(halves, axis=0).T.astype(BF16)
        return carry

    lax.fori_loop(0, HEADS // 2, pair_of_heads, 0)


def attend_back(queries, keys, values, bias, totals, grads, query_low, key_low, value_low):
    width = 2 * (queries.shape[1] // HEADS)
    chosen = first_half(width)

    def pair_of_heads(pair, carry):
        columns = pl.ds(pl.multiple_of(pair * width, width), width)
        query = queries[:, columns]
        key = keys[:, columns]
        value = values[:, columns]
        grad = grads[:, columns]
        key_across = key.T
        query_parts, key_parts, value_parts = [], [], []
        for side in range(2):
            mine = chosen if side == 0 else ~chosen
            scores = nt(key, jnp.where(mine, query, 0)) + bias[...]
            probs = jnp.exp(scores - totals[2 * pair + side])
            prob_grad = nt(value, jnp.where(mine, grad, 0))
            value_parts.append(nn(probs.astype(BF16), grad))
            weighted = probs * prob_grad
            centre = jnp.sum(weighted, axis=0, keepdims=True)
            score_grad = (weighted - probs * centre).astype(BF16)
            key_parts.append(nn(score_grad, query))
            query_parts.append(
                nn(key_across[side * width // 2 : (side + 1) * width // 2], score_grad)
            )
        query_low[:, columns] = jnp.concatenate(query_parts, axis=0).T.astype(BF16)
        key_low[:, columns] = jnp.where(chosen, key_parts[0], key_parts[1]).astype(BF16)
        value_low[:, columns] = jnp.where(chosen, value_parts[0], value_parts[1]).astype(BF16)
        return carry

    lax.fori_loop(0, HEADS // 2, pair_of_heads, 0)


def self_forward_kernel(
    places, lengths, inputs, gain, mine, other,
    normed, query, key, value, attended, totals, stream,
    weights, bias, sems,
):
    copies = weight_copies(places, mine, other, weights, weights.shape[1] // (2 * mine.shape[0]), sems)
    for copy in copies:
        copy.start()
    values = inputs[...].astype(F32)
    fill_self_bias(bias, lengths)
    low = (values * norm_scale(values) * gain[...]).astype(BF16)
    normed[...] = low
    for copy in copies:
        copy.wait()
    query[...] = nn(low, weights[0]).astype(BF16)
    key[...] = nn(low, weights[1]).astype(BF16)
    value[...] = nn(low, weights[2]).astype(BF16)
    attend(query, key, value, bias, attended, totals)
    stream[...] = values + nn(attended[...], weights[3])


def memory_kernel(places, memory, mine, other, key, value, weights, sems):
    rows = weights.shape[1] // (2 * mine.shape[0])
    copies = weight_copies(
        places, mine.at[:, pl.ds(rows, 2 * rows), :], other.at[:, pl.ds(rows, 2 * rows), :],
        weights, rows, sems,
    )
    for copy in copies:
        copy.start()
    for copy in copies:
        copy.wait()
    key[...] = nn(memory[...], weights[0]).astype(BF16)
    value[...] = nn(memory[...], weights[1]).astype(BF16)


def cross_forward_kernel(
    places, lengths, sources, stream_in, gain, key, value, mine, other,
    normed, query, attended, totals, stream,
    weights, bias, sems,
):
    rows = weights.shape[1] // (2 * mine.shape[0])
    first = weight_copies(places, mine, other, weights.at[pl.ds(0, 1)], rows, sems.at[0])
    last = weight_copies(
        places, mine.at[:, pl.ds(3 * rows, rows), :], other.at[:, pl.ds(3 * rows, rows), :],
        weights.at[pl.ds(1, 1)], rows, sems.at[1],
    )
    for copy in first + last:
        copy.start()
    values = stream_in[...]
    fill_cross_bias(bias, lengths, sources)
    low = (values * norm_scale(values) * gain[...]).astype(BF16)
    normed[...] = low
    for copy in first + last:
        copy.wait()
    query[...] = nn(low, weights[0]).astype(BF16)
    attend(query, key, value, bias, attended, totals)
    stream[...] = values + nn(attended[...], weights[1])


def mlp_forward_kernel(
    places, stream_in, gain, exit_gain, mine, other, down_mine, down_other,
    normed, gate, up, hidden, stream, activations, exit_normed,
    weights, down, sems, down_sems,
):
    rows = weights.shape[1] // (2 * mine.shape[0])
    down_rows = down.shape[1] // (2 * mine.shape[0])
    first = weight_copies(places, mine, other, weights, rows, sems)
    last = weight_copies(places, down_mine, down_other, down, down_rows, down_sems)
    for copy in first + last:
        copy.start()
    values = stream_in[...]
    low = (values * norm_scale(values) * gain[...]).astype(BF16)
    normed[...] = low
    for copy in first:
        copy.wait()
    width = weights.shape[2]
    step = width // 4
    for part in range(4):
        columns = pl.ds(part * step, step)
        gate_pre = nn(low, weights[0, :, columns])
        up_pre = nn(low, weights[1, :, columns])
        gate[:, columns] = gate_pre
        up[:, columns] = up_pre
        bent = jnp.tanh(MIX * (gate_pre + CUBE * (gate_pre * gate_pre * gate_pre)))
        hidden[:, columns] = (0.5 * gate_pre * (1.0 + bent) * up_pre).astype(BF16)
    for copy in last:
        copy.wait()
    out = values + nn(hidden[...], down[0])
    stream[...] = out
    activations[...] = out.astype(BF16)
    exit_normed[...] = (out * norm_scale(out) * exit_gain[...]).astype(BF16)


def exit_scores_kernel(
    places, mine, other, targets, table, raised, across, stats,
    tokens, scores, sems, *, vocab, scale,
):
    half = mine.shape[0]
    rows = mine.shape[1]
    step = pl.program_id(0)
    tile = raised.shape[0]

    @pl.when(step == 0)
    def load():
        copies = []
        for slot in range(2 * half):
            source = mine if slot < half else other
            copies.append(
                pltpu.make_async_copy(
                    source.at[slot % half],
                    tokens.at[pl.ds(pl.multiple_of(places[slot] * rows, 8), rows), :],
                    sems.at[slot],
                )
            )
        for copy in copies:
            copy.start()
        for copy in copies:
            copy.wait()

    own = tokens[pl.ds(pl.multiple_of(step * tile, tile), tile), :]
    across[...] = own.T
    width = scores.shape[1]
    lanes = lax.broadcasted_iota(jnp.int32, (tile, VOCAB_TILE), 1)
    wanted = targets[...]
    highest = jnp.full((tile, 1), NEGATIVE, F32)
    picked = jnp.zeros((tile, 1), F32)
    for first in range(0, width, VOCAB_TILE):
        part = nn(own, table[:, first : first + VOCAB_TILE]) * scale
        if first + VOCAB_TILE > vocab:
            part = jnp.where(lanes < vocab - first, part, NEGATIVE)
        scores[:, first : first + VOCAB_TILE] = part
        highest = jnp.maximum(highest, jnp.max(part, axis=1, keepdims=True))
        picked = picked + jnp.sum(
            jnp.where(lanes == wanted - first, part, 0.0), axis=1, keepdims=True
        )
    summed = jnp.zeros((tile, 1), F32)
    for first in range(0, width, VOCAB_TILE):
        part = jnp.exp(scores[:, first : first + VOCAB_TILE] - highest)
        raised[:, first : first + VOCAB_TILE] = part.astype(BF16)
        summed = summed + jnp.sum(part, axis=1, keepdims=True)
    spot = lax.broadcasted_iota(jnp.int32, (tile, LANES), 1)
    packed = jnp.where(spot == 0, highest, jnp.where(spot == 1, summed, picked))
    stats[...] = packed.T[:8]


def exit_grads_kernel(
    table, raised, across, columns, targets, token_grad, table_grad, total, *, vocab,
):
    step = pl.program_id(0)
    tile = raised.shape[0]
    width = raised.shape[1]
    factors = jnp.concatenate(
        [columns[...], jnp.zeros((LANES - columns.shape[0], tile), F32)], axis=0
    ).T
    factor, at_target = factors[:, 0:1], factors[:, 1:2]
    wanted = targets[...]
    lanes = lax.broadcasted_iota(jnp.int32, (tile, VOCAB_TILE), 1)
    grad = jnp.zeros((tile, token_grad.shape[1]), F32)

    @pl.when(step == 0)
    def clear():
        total[...] = jnp.zeros_like(total)

    for first in range(0, width, VOCAB_TILE):
        chunk = slice(first, first + VOCAB_TILE)
        part = raised[:, chunk].astype(F32) * factor
        part = jnp.where(lanes == wanted - first, at_target, part).astype(BF16)
        grad = grad + nt(part, table[:, chunk])
        total[:, chunk] += nn(across[...], part)
    token_grad[...] = grad.astype(BF16)

    @pl.when(step == pl.num_programs(0) - 1)
    def finish():
        table_grad[...] = total[...].astype(BF16)


def mlp_backward_kernel(
    places, grad_in, stream_three, stream_two, gain, exit_gain, normed, gate, up, hidden,
    mine, other, down_mine, down_other,
    stream_grad, gains, grad_mine, grad_other, down_grad_mine, down_grad_other,
    weights, down, total, gate_low, up_low, result, down_result, sems, down_sems,
):
    rows = weights.shape[1] // (2 * mine.shape[0])
    down_rows = down.shape[1] // (2 * mine.shape[0])
    first = weight_copies(places, down_mine, down_other, down, down_rows, down_sems)
    last = weight_copies(places, mine, other, weights, rows, sems)
    for copy in first + last:
        copy.start()
    stream_back, exit_gain_grad = norm_back(stream_three[...], exit_gain[...], grad_in[...].astype(F32))
    branch = stream_back.astype(BF16)
    for copy in first + last:
        copy.wait()
    width = weights.shape[2]
    step = width // 4
    for part in range(4):
        columns = pl.ds(part * step, step)
        gate_pre = gate[:, columns]
        up_pre = up[:, columns]
        hidden_grad = nt(branch, down[0, columns, :])
        bent = jnp.tanh(MIX * (gate_pre + CUBE * (gate_pre * gate_pre * gate_pre)))
        slope = 0.5 * (1.0 + bent) + 0.5 * gate_pre * (1.0 - bent * bent) * (
            MIX * (1.0 + 3.0 * CUBE * gate_pre * gate_pre)
        )
        gate_low[:, columns] = (hidden_grad * up_pre * slope).astype(BF16)
        up_low[:, columns] = (hidden_grad * (0.5 * gate_pre * (1.0 + bent))).astype(BF16)
    normed_grad = nt(gate_low[...], weights[0]) + nt(up_low[...], weights[1])
    branch_in, gain_grad = norm_back(stream_two[...], gain[...], normed_grad)
    stream_grad[...] = stream_back + branch_in
    gains[...] = jnp.concatenate(
        [gain_grad, exit_gain_grad, jnp.zeros((6, gain_grad.shape[1]), F32)], axis=0
    )
    for matrix, low in enumerate((gate_low, up_low)):
        for part in range(4):
            columns = pl.ds(part * step, step)
            result[:, columns] = tn(normed[...], low[:, columns]).astype(BF16)
        store_blocks(places, result, matrix, rows, grad_mine, grad_other)
    for part in range(4):
        columns = pl.ds(part * step, step)
        down_result[columns, :] = tn(hidden[:, columns], branch).astype(BF16)
    store_blocks(places, down_result, 0, down_rows, down_grad_mine, down_grad_other)


def cross_backward_kernel(
    places, lengths, sources, grad_in, stream_in, gain, normed, memory,
    query, key, value, totals, attended, mine, other,
    stream_grad, gains, memory_grad, grad_mine, grad_other,
    weights, bias, result, branch, attended_grad, query_low, key_low, value_low, sems,
):
    rows = weights.shape[1] // (2 * mine.shape[0])
    copies = weight_copies(places, mine, other, weights, rows, sems)
    for copy in copies:
        copy.start()
    fill_cross_bias(bias, lengths, sources)
    branch[...] = grad_in[...].astype(BF16)
    for copy in copies:
        copy.wait()
    attended_grad[...] = nt(branch[...], weights[3]).astype(BF16)
    attend_back(
        query, key, value, bias, totals, attended_grad, query_low, key_low, value_low
    )
    normed_grad = nt(query_low[...], weights[0])
    branch_in, gain_grad = norm_back(stream_in[...], gain[...], normed_grad)
    stream_grad[...] = grad_in[...] + branch_in
    gains[...] = jnp.broadcast_to(gain_grad, gains.shape)
    memory_grad[...] = nt(key_low[...], weights[1]) + nt(value_low[...], weights[2])
    pairs = ((normed, query_low), (memory, key_low), (memory, value_low), (attended, branch))
    for matrix, (left, right) in enumerate(pairs):
        result[...] = tn(left[...], right[...]).astype(BF16)
        store_blocks(places, result, matrix, rows, grad_mine, grad_other)


def self_backward_kernel(
    places, lengths, grad_in, inputs, gain, normed,
    query, key, value, totals, attended, mine, other,
    stream_grad, gains, grad_mine, grad_other,
    weights, bias, result, branch, attended_grad, query_low, key_low, value_low, sems,
):
    rows = weights.shape[1] // (2 * mine.shape[0])
    copies = weight_copies(places, mine, other, weights, rows, sems)
    for copy in copies:
        copy.start()
    fill_self_bias(bias, lengths)
    branch[...] = grad_in[...].astype(BF16)
    for copy in copies:
        copy.wait()
    attended_grad[...] = nt(branch[...], weights[3]).astype(BF16)
    attend_back(
        query, key, value, bias, totals, attended_grad, query_low, key_low, value_low
    )
    normed_grad = (
        nt(query_low[...], weights[0])
        + nt(key_low[...], weights[1])
        + nt(value_low[...], weights[2])
    )
    branch_in, gain_grad = norm_back(inputs[...].astype(F32), gain[...], normed_grad)
    stream_grad[...] = grad_in[...] + branch_in
    gains[...] = jnp.broadcast_to(gain_grad, gains.shape)
    pairs = ((normed, query_low), (normed, key_low), (normed, value_low), (attended, branch))
    for matrix, (left, right) in enumerate(pairs):
        result[...] = tn(left[...], right[...]).astype(BF16)
        store_blocks(places, result, matrix, rows, grad_mine, grad_other)


def per_device(
    inputs,
    memory,
    targets,
    tgt_lengths,
    src_lengths,
    self_gain,
    self_query,
    self_key,
    self_value,
    self_out,
    cross_gain,
    cross_query,
    cross_key,
    cross_value,
    cross_out,
    mlp_gain,
    mlp_gate,
    mlp_up,
    mlp_down,
    exit_gain,
    embedding,
):
    tokens, model = inputs.shape
    slots = memory.shape[0]
    hidden_width = mlp_gate.shape[1]
    pair_slots = tgt_lengths.shape[1]
    wide_count = lax.axis_size("wide")
    narrow_count = lax.axis_size("narrow")
    wide = lax.axis_index("wide")
    narrow = lax.axis_index("narrow")
    half = wide_count // 2
    slot_total = tokens * wide_count * narrow_count
    scale = 1.0 / math.sqrt(model)
    places = slot_places(wide, wide_count)
    lengths, sources = tgt_lengths[0], src_lengths[0]
    shard = self_query.shape[0]
    rows = shard * narrow_count
    down_rows = mlp_down.shape[0] * narrow_count

    aligned = rows % 8 == 0
    kernel_places = places if aligned else jnp.arange(2, dtype=jnp.int32)
    kernel_count = wide_count if aligned else 2

    ids = jnp.arange(wide_count, dtype=jnp.int32)
    into_order = (places[None, :] == ids[:, None]).astype(BF16)

    def reorder(matrix, blocks):
        flat = blocks.reshape(wide_count, -1)
        return nn(matrix, flat).astype(BF16).reshape(blocks.shape)

    def collect(parts):
        across = [gather_narrow(part, narrow, narrow_count) for part in parts]
        block = jnp.concatenate([piece for pieces in across for piece in pieces], axis=0)
        mine, other = gather_wide(block, wide_count)
        if aligned:
            return mine, other
        ordered = reorder(into_order, jnp.concatenate([mine, other], axis=0))
        ordered = ordered.reshape(wide_count, len(parts), -1, block.shape[-1]).transpose(1, 0, 2, 3)
        ordered = ordered.reshape(len(parts), 2, -1, block.shape[-1]).transpose(1, 0, 2, 3)
        ordered = ordered.reshape(2, -1, block.shape[-1])
        return ordered[:1], ordered[1:]

    def spread(grad_mine, grad_other, matrices, part):
        if not aligned:
            ordered = jnp.concatenate([grad_mine, grad_other], axis=0)
            width = ordered.shape[-1]
            ordered = ordered.reshape(2, matrices, -1, width).transpose(1, 0, 2, 3)
            ordered = ordered.reshape(matrices, wide_count, -1, width).transpose(1, 0, 2, 3)
            ordered = reorder(into_order.T, ordered.reshape(wide_count, -1, width))
            grad_mine, grad_other = ordered[:half], ordered[half:]
        summed = scatter_wide(grad_mine, grad_other, wide_count)
        summed = summed.reshape(matrices, narrow_count, part, summed.shape[-1])
        return scatter_narrow(summed.transpose(1, 0, 2, 3), narrow, narrow_count)

    gain_rows = jnp.zeros((8, LANES), F32)
    for place, member in enumerate((self_gain, cross_gain, mlp_gain, exit_gain)):
        gain_rows = gain_rows.at[place, :shard].set(member.astype(F32))
    gain_across = jnp.stack(gather_narrow(gain_rows, narrow, narrow_count))
    gain_mine, gain_other = gather_wide(gain_across, wide_count)
    gain_all = jnp.concatenate([gain_mine, gain_other], axis=0)[:, :, :4, :shard]
    order = (places[None, :] == jnp.arange(wide_count)[:, None]).astype(F32)
    gain_all = jnp.sum(order[:, :, None, None, None] * gain_all[None], axis=1)
    gain_all = gain_all.transpose(2, 0, 1, 3).reshape(4, 1, model)

    self_mine, self_other = collect([self_query, self_key, self_value, self_out])
    cross_mine, cross_other = collect([cross_query, cross_key, cross_value, cross_out])
    gate_mine, gate_other = collect([mlp_gate, mlp_up])
    down_mine, down_other = collect([mlp_down])

    vocab = embedding.shape[0]
    padded = -(-vocab // VOCAB_TILE) * VOCAB_TILE
    turned = jnp.pad(embedding.T, ((0, 0), (0, padded - vocab)))
    table = lax.all_gather(turned, "narrow", axis=0, tiled=True)

    head_rows = like((HEADS, 1, tokens), F32)
    activation = like((tokens, model), BF16)
    stream_like = like((tokens, model), F32)
    matrix_sems = pltpu.SemaphoreType.DMA((kernel_count, 4))

    normed_one, query_one, key_one, value_one, attended_one, totals_one, stream_one = pl.pallas_call(
        self_forward_kernel,
        in_specs=[SMEM, SMEM, VMEM, VMEM, ANY, ANY],
        out_specs=[VMEM] * 7,
        out_shape=[activation] * 5 + [head_rows, stream_like],
        scratch_shapes=[
            pltpu.VMEM((4, model, model), BF16),
            pltpu.VMEM((tokens, tokens), F32),
            matrix_sems,
        ],
        compiler_params=PARAMS,
        name="self_forward",
    )(kernel_places, lengths, inputs, gain_all[0], self_mine, self_other)

    key_two, value_two = pl.pallas_call(
        memory_kernel,
        in_specs=[SMEM, VMEM, ANY, ANY],
        out_specs=[VMEM] * 2,
        out_shape=[like((slots, model), BF16)] * 2,
        scratch_shapes=[
            pltpu.VMEM((2, model, model), BF16),
            pltpu.SemaphoreType.DMA((kernel_count, 2)),
        ],
        compiler_params=PARAMS,
        name="memory_projection",
    )(kernel_places, memory, cross_mine, cross_other)

    normed_two, query_two, attended_two, totals_two, stream_two = pl.pallas_call(
        cross_forward_kernel,
        in_specs=[SMEM, SMEM, SMEM, VMEM, VMEM, VMEM, VMEM, ANY, ANY],
        out_specs=[VMEM] * 5,
        out_shape=[activation] * 3 + [head_rows, stream_like],
        scratch_shapes=[
            pltpu.VMEM((2, model, model), BF16),
            pltpu.VMEM((slots, tokens), F32),
            pltpu.SemaphoreType.DMA((2, kernel_count, 1)),
        ],
        compiler_params=PARAMS,
        name="cross_forward",
    )(kernel_places, lengths, sources, stream_one, gain_all[1], key_two, value_two, cross_mine, cross_other)

    wide_f32 = like((tokens, hidden_width), F32)
    wide_low = like((tokens, hidden_width), BF16)
    normed_three, gate_pre, up_pre, hidden, stream_three, activations, normed_four = pl.pallas_call(
        mlp_forward_kernel,
        in_specs=[SMEM, VMEM, VMEM, VMEM, ANY, ANY, ANY, ANY],
        out_specs=[VMEM] * 7,
        out_shape=[activation, wide_f32, wide_f32, wide_low, stream_like, activation, activation],
        scratch_shapes=[
            pltpu.VMEM((2, model, hidden_width), BF16),
            pltpu.VMEM((1, hidden_width, model), BF16),
            pltpu.SemaphoreType.DMA((kernel_count, 2)),
            pltpu.SemaphoreType.DMA((kernel_count, 1)),
        ],
        compiler_params=PARAMS,
        name="mlp_forward",
    )(kernel_places, stream_two, gain_all[2], gain_all[3], gate_mine, gate_other, down_mine, down_other)

    exit_mine, exit_other = gather_wide(normed_four, wide_count)
    group = tokens * wide_count
    tiles = group // ROW_TILE
    segment = jnp.sum(
        (jnp.arange(tokens, dtype=jnp.int32)[None, :]
         >= jnp.sum(jnp.where(jnp.arange(pair_slots)[None, :] <= jnp.arange(pair_slots)[:, None], lengths[None, :], 0), axis=1)[:, None]
         ).astype(jnp.int32),
        axis=0,
    )
    loss_weight = (segment < pair_slots).astype(F32)
    packed = jnp.concatenate(
        [loss_weight[None], targets.astype(F32)[None], jnp.zeros((6, tokens), F32)], axis=0
    )
    packed_mine, packed_other = gather_wide(packed, wide_count)
    packed_all = jnp.concatenate([packed_mine, packed_other], axis=0)[:, :2]
    packed_all = jnp.sum(order[:, :, None, None] * packed_all[None], axis=1)
    group_weight = packed_all[:, 0].reshape(group)
    group_targets = packed_all[:, 1].reshape(group).astype(jnp.int32) - wide * vocab
    group_targets = jnp.where(group_targets < vocab, group_targets, -1)
    target_column = group_targets[:, None]

    raised, tokens_across, stats = pl.pallas_call(
        functools.partial(exit_scores_kernel, vocab=vocab, scale=scale),
        grid=(tiles,),
        in_specs=[
            SMEM, ANY, ANY,
            pl.BlockSpec((ROW_TILE, 1), lambda i: (i, 0)),
            pl.BlockSpec((model, padded), lambda i: (0, 0)),
        ],
        out_specs=[
            pl.BlockSpec((ROW_TILE, padded), lambda i: (i, 0)),
            pl.BlockSpec((model, ROW_TILE), lambda i: (0, i)),
            pl.BlockSpec((8, ROW_TILE), lambda i: (0, i)),
        ],
        out_shape=[
            like((group, padded), BF16),
            like((model, group), BF16),
            like((8, group), F32),
        ],
        scratch_shapes=[
            pltpu.VMEM((group, model), BF16),
            pltpu.VMEM((ROW_TILE, padded), F32),
            pltpu.SemaphoreType.DMA((wide_count,)),
        ],
        compiler_params=PARAMS,
        name="exit_scores",
    )(places, exit_mine, exit_other, target_column, table)

    own_peak = stats[0]
    joint = stats
    for pairs in stage_pairs(wide_count) + [flip_pairs(wide_count)]:
        came = lax.ppermute(joint, "wide", pairs)
        peak = jnp.maximum(joint[0], came[0])
        summed = joint[1] * jnp.exp(joint[0] - peak) + came[1] * jnp.exp(came[0] - peak)
        joint = jnp.concatenate(
            [peak[None], summed[None], joint[2:3] + came[2:3], jnp.zeros((5, group), F32)], axis=0
        )
    log_total = joint[0] + jnp.log(joint[1])
    picked = joint[2]
    loss_part = jnp.sum(group_weight * (log_total - picked))
    loss_tile = jnp.full((8, LANES), loss_part, F32)
    loss_all = loss_tile
    for step in range(1, narrow_count):
        loss_all = loss_all + lax.ppermute(loss_tile, "narrow", narrow_pairs(narrow_count, step))
    mean_loss = loss_all[0, 0] / slot_total

    factor = jnp.exp(own_peak - log_total) * (group_weight * scale)
    at_target = (jnp.exp(picked - log_total) - 1.0) * (group_weight * scale)
    columns = jnp.concatenate(
        [factor[None], at_target[None], jnp.zeros((6, group), F32)], axis=0
    )
    token_grad, table_grad = pl.pallas_call(
        functools.partial(exit_grads_kernel, vocab=vocab),
        grid=(tiles,),
        in_specs=[
            pl.BlockSpec((model, padded), lambda i: (0, 0)),
            pl.BlockSpec((ROW_TILE, padded), lambda i: (i, 0)),
            pl.BlockSpec((model, ROW_TILE), lambda i: (0, i)),
            pl.BlockSpec((8, ROW_TILE), lambda i: (0, i)),
            pl.BlockSpec((ROW_TILE, 1), lambda i: (i, 0)),
        ],
        out_specs=[
            pl.BlockSpec((ROW_TILE, model), lambda i: (i, 0)),
            pl.BlockSpec((model, padded), lambda i: (0, 0)),
        ],
        out_shape=[like((group, model), BF16), like((model, padded), BF16)],
        scratch_shapes=[pltpu.VMEM((model, padded), F32)],
        compiler_params=PARAMS,
        name="exit_grads",
    )(table, raised, tokens_across, columns, target_column)

    table_sum = lax.psum_scatter(table_grad, "narrow", scatter_dimension=0, tiled=True)
    embedding_grad = table_sum.astype(F32).T[:vocab]

    blocks = token_grad.reshape(wide_count, tokens, model)
    relative = jnp.concatenate(
        [lax.dynamic_index_in_dim(blocks, places[slot], 0) for slot in range(wide_count)], axis=0
    )
    exit_grad = scatter_wide(relative[:half], relative[half:], wide_count)

    two_gains = like((8, model), F32)
    stream_two_grad, mlp_gains, gate_g_mine, gate_g_other, down_g_mine, down_g_other = pl.pallas_call(
        mlp_backward_kernel,
        in_specs=[SMEM] + [VMEM] * 9 + [ANY] * 4,
        out_specs=[VMEM] * 6,
        out_shape=[
            stream_like,
            two_gains,
            like(gate_mine.shape, BF16),
            like(gate_mine.shape, BF16),
            like(down_mine.shape, BF16),
            like(down_mine.shape, BF16),
        ],
        scratch_shapes=[
            pltpu.VMEM((2, model, hidden_width), BF16),
            pltpu.VMEM((1, hidden_width, model), BF16),
            pltpu.VMEM((8, LANES), F32),
            pltpu.VMEM((tokens, hidden_width), BF16),
            pltpu.VMEM((tokens, hidden_width), BF16),
            pltpu.VMEM((model, hidden_width), BF16),
            pltpu.VMEM((hidden_width, model), BF16),
            pltpu.SemaphoreType.DMA((kernel_count, 2)),
            pltpu.SemaphoreType.DMA((kernel_count, 1)),
        ],
        compiler_params=PARAMS,
        name="mlp_backward",
    )(
        kernel_places, exit_grad, stream_three, stream_two, gain_all[2], gain_all[3], normed_three,
        gate_pre, up_pre, hidden, gate_mine, gate_other, down_mine, down_other,
    )
    gate_sum = spread(gate_g_mine, gate_g_other, 2, shard)
    down_sum = spread(down_g_mine, down_g_other, 1, mlp_down.shape[0])

    low_rows = pltpu.VMEM((tokens, model), BF16)
    stream_one_grad, cross_gains, memory_grad, cross_g_mine, cross_g_other = pl.pallas_call(
        cross_backward_kernel,
        in_specs=[SMEM] * 3 + [VMEM] * 10 + [ANY] * 2,
        out_specs=[VMEM] * 5,
        out_shape=[
            stream_like,
            two_gains,
            like((slots, model), F32),
            like(cross_mine.shape, BF16),
            like(cross_mine.shape, BF16),
        ],
        scratch_shapes=[
            pltpu.VMEM((4, model, model), BF16),
            pltpu.VMEM((slots, tokens), F32),
            pltpu.VMEM((model, model), BF16),
            low_rows,
            low_rows,
            low_rows,
            pltpu.VMEM((slots, model), BF16),
            pltpu.VMEM((slots, model), BF16),
            matrix_sems,
        ],
        compiler_params=PARAMS,
        name="cross_backward",
    )(
        kernel_places, lengths, sources, stream_two_grad, stream_one, gain_all[1], normed_two, memory,
        query_two, key_two, value_two, totals_two, attended_two, cross_mine, cross_other,
    )
    cross_sum = spread(cross_g_mine, cross_g_other, 4, shard)

    inputs_grad, self_gains, self_g_mine, self_g_other = pl.pallas_call(
        self_backward_kernel,
        in_specs=[SMEM] * 2 + [VMEM] * 9 + [ANY] * 2,
        out_specs=[VMEM] * 4,
        out_shape=[
            stream_like,
            two_gains,
            like(self_mine.shape, BF16),
            like(self_mine.shape, BF16),
        ],
        scratch_shapes=[
            pltpu.VMEM((4, model, model), BF16),
            pltpu.VMEM((tokens, tokens), F32),
            pltpu.VMEM((model, model), BF16),
            low_rows,
            low_rows,
            low_rows,
            low_rows,
            low_rows,
            matrix_sems,
        ],
        compiler_params=PARAMS,
        name="self_backward",
    )(
        kernel_places, lengths, stream_one_grad, inputs, gain_all[0], normed_one,
        query_one, key_one, value_one, totals_one, attended_one, self_mine, self_other,
    )
    self_sum = spread(self_g_mine, self_g_other, 4, shard)

    gains = jnp.stack([self_gains[0], cross_gains[0], mlp_gains[0], mlp_gains[1]])
    gains = lax.psum(gains, ("wide", "narrow")).reshape(4, wide_count * narrow_count, shard)
    gains = lax.dynamic_index_in_dim(gains, wide * narrow_count + narrow, 1, keepdims=False)

    return (
        activations,
        mean_loss,
        inputs_grad,
        memory_grad,
        gains[0],
        self_sum[0],
        self_sum[1],
        self_sum[2],
        self_sum[3],
        gains[1],
        cross_sum[0],
        cross_sum[1],
        cross_sum[2],
        cross_sum[3],
        gains[2],
        gate_sum[0],
        gate_sum[1],
        down_sum[0],
        gains[3],
        embedding_grad,
    )


def solution(mesh):
    both = ("wide", "narrow")
    rows, flat = P(both, None), P(both)
    placed = (
        rows, rows, flat, rows, rows,
        flat, rows, rows, rows, rows,
        flat, rows, rows, rows, rows,
        flat, rows, rows, rows, flat,
        P("wide", "narrow"),
    )
    given = (
        rows, P(), rows, rows,
        flat, rows, rows, rows, rows,
        flat, rows, rows, rows, rows,
        flat, rows, rows, rows, flat,
        P("wide", "narrow"),
    )
    return jax.shard_map(
        per_device, mesh=mesh, in_specs=placed, out_specs=given, check_vma=False
    )
```

```python
import functools
import math

import jax
import jax.numpy as jnp
from jax import lax
from jax.experimental import pallas as pl
from jax.experimental.pallas import tpu as pltpu
from jax.sharding import PartitionSpec as P

HEADS = 12
EPSILON = 1e-06
NEGATIVE = -1e30
F32 = jnp.float32
BF16 = jnp.bfloat16
LANES = 128
ROW_TILE = 256
GRAD_TILE = 256
VOCAB_TILE = 512
MIX = math.sqrt(2.0 / math.pi)
CUBE = 0.044715
LOG2E = math.log2(math.e)
META_WIDE, META_TILES, META_LISTS = 0, 1, 2

VMEM = pl.BlockSpec(memory_space=pltpu.VMEM)
SMEM = pl.BlockSpec(memory_space=pltpu.SMEM)
ANY = pl.BlockSpec(memory_space=pl.ANY)
PARAMS = pltpu.CompilerParams(vmem_limit_bytes=60 * 2**20)


def work(gigaflops):
    return pl.CostEstimate(flops=gigaflops * 10**9, bytes_accessed=10**6, transcendentals=0)


def nn(left, right):
    return lax.dot_general(left, right, (((1,), (0,)), ((), ())), preferred_element_type=F32)


def nt(left, right):
    return lax.dot_general(left, right, (((1,), (1,)), ((), ())), preferred_element_type=F32)


def tn(left, right):
    return lax.dot_general(left, right, (((0,), (0,)), ((), ())), preferred_element_type=F32)


def like(shape, kind):
    return jax.ShapeDtypeStruct(shape, kind)


def stage_masks(count):
    up = [1 << bit for bit in range(1, count.bit_length() - 1)]
    return up, up[::-1]


def stage_pairs(count):
    even, odd = stage_masks(count)
    return [[(v, v ^ (odd if v % 2 else even)[i]) for v in range(count)] for i in range(len(even))]


def flip_pairs(count):
    return [(v, v ^ 1) for v in range(count)]


def slot_tables(count):
    tables = []
    for masks in stage_masks(count):
        slots = [0]
        for mask in masks:
            slots = slots + [slot ^ mask for slot in slots]
        tables.append(slots)
    even, odd = tables
    return (
        even + [1 ^ slot for slot in odd],
        odd + [1 ^ slot for slot in even],
    )


def slot_places(wide, count):
    even, odd = slot_tables(count)
    table = jnp.where(wide % 2 == 0, jnp.array(even, jnp.int32), jnp.array(odd, jnp.int32))
    return wide ^ table


def tie(value, *others):
    return lax.optimization_barrier((value, *others))[0]


def cross_core(value, count):
    return lax.ppermute(value, "wide", flip_pairs(count))


def gather_wide(block, count):
    held = block[None]
    *early, last = stage_pairs(count)
    for pairs in early:
        held = jnp.concatenate([held, lax.ppermute(held, "wide", pairs)], axis=0)
    came = lax.ppermute(held, "wide", last)
    return held, came, cross_core(held, count), cross_core(came, count)


def scatter_core(parts, count):
    sent, kept = cross_core(parts[3], count), cross_core(parts[2], count)
    return (parts[1], sent), (parts[0], kept)


def scatter_far(sent, kept, count):
    far = (sent[0].astype(F32) + sent[1].astype(F32)).astype(BF16)
    came = lax.ppermute(far, "wide", stage_pairs(count)[-1])
    return far, came, kept


def scatter_near(came, kept, count):
    held = kept[0].astype(F32) + kept[1].astype(F32) + came.astype(F32)
    *rest, last = stage_pairs(count)[-2::-1]
    for pairs in rest:
        half = held.shape[0] // 2
        sent = lax.ppermute(held[half:].astype(BF16), "wide", pairs)
        held = held[:half] + sent.astype(F32)
    far = held[1].astype(BF16)
    return far, lax.ppermute(far, "wide", last), held[0]


def scatter_wide(parts, count):
    far, came, kept = scatter_far(*scatter_core(parts, count), count)
    far, came, held = scatter_near(came, kept, count)
    return held + came.astype(F32)


def narrow_pairs(count, step):
    return [(v, v ^ step) for v in range(count)]


def gather_narrow(block, count):
    return [block] + [
        lax.ppermute(block, "narrow", narrow_pairs(count, step)) for step in range(1, count)
    ]


def pick(values, place, axis=0):
    return lax.dynamic_index_in_dim(values, place.astype(jnp.uint32), axis, keepdims=False)


def in_line_order(pieces, narrow):
    stacked = jnp.stack(pieces)
    return [pick(stacked, narrow ^ place) for place in range(stacked.shape[0])]


def scatter_narrow(blocks, narrow, count):
    total = pick(blocks, narrow)
    for step in range(1, count):
        sent = pick(blocks, narrow ^ step).astype(BF16)
        total = total + lax.ppermute(sent, "narrow", narrow_pairs(count, step)).astype(F32)
    return total


def weight_copies(places, parts, start, target, rows, sems):
    size = parts[0].shape[0]
    copies = []
    for slot in range(len(parts) * size):
        place = pl.multiple_of(places[slot] * rows, 8)
        for matrix in range(target.shape[0]):
            copies.append(
                pltpu.make_async_copy(
                    parts[slot // size].at[slot % size, pl.ds(start + matrix * rows, rows), :],
                    target.at[matrix, pl.ds(place, rows), :],
                    sems.at[slot, matrix],
                )
            )
    return copies


def store_blocks(places, value_ref, start, rows, parts):
    size = parts[0].shape[0]
    for slot in range(len(parts) * size):
        place = pl.multiple_of(places[slot] * rows, 8)
        parts[slot // size][slot % size, pl.ds(start, rows), :] = value_ref[pl.ds(place, rows), :]


def norm_scale(values):
    return lax.rsqrt(jnp.mean(values * values, axis=-1, keepdims=True) + EPSILON)


def norm_back(values, gain, grad):
    root = norm_scale(values)
    scaled = gain * grad
    gain_grad = jnp.sum(grad * values * root, axis=0, keepdims=True)
    inner = jnp.mean(scaled * values, axis=-1, keepdims=True)
    return root * scaled - values * (root * root * root) * inner, gain_grad


def query_segments(lengths, count):
    places = lax.broadcasted_iota(jnp.int32, (1, count), 1)
    segment = jnp.zeros((1, count), jnp.int32)
    edge = jnp.int32(0)
    for pair in range(lengths.shape[0]):
        edge = edge + lengths[pair]
        segment = segment + (places >= edge).astype(jnp.int32)
    return places, segment


def fill_self_bias(bias, lengths):
    count = bias.shape[1]
    places, segment = query_segments(lengths, count)
    low = jnp.zeros((1, count), jnp.int32)
    edge = jnp.int32(0)
    for pair in range(lengths.shape[0]):
        edge = edge + lengths[pair]
        low = jnp.where(segment == pair + 1, edge, low)
    keys = lax.broadcasted_iota(jnp.int32, bias.shape, 0)
    bias[...] = jnp.where((keys >= low) & (keys <= places), 0.0, NEGATIVE)


def fill_cross_bias(bias, lengths, sources):
    count = bias.shape[1]
    places, segment = query_segments(lengths, count)
    low = jnp.zeros((1, count), jnp.int32)
    high = jnp.full((1, count), bias.shape[0], jnp.int32)
    edge = jnp.int32(0)
    for pair in range(lengths.shape[0]):
        low = jnp.where(segment == pair, edge, low)
        edge = edge + sources[pair]
        high = jnp.where(segment == pair, edge, high)
    keys = lax.broadcasted_iota(jnp.int32, bias.shape, 0)
    bias[...] = jnp.where((keys >= low) & (keys < high), 0.0, NEGATIVE)


def first_half(width):
    return lax.broadcasted_iota(jnp.int32, (1, width), 1) < width // 2


def attend(queries, keys, values, bias, outputs, totals):
    width = 2 * (queries.shape[1] // HEADS)
    chosen = first_half(width)

    def pair_of_heads(pair, carry):
        columns = pl.ds(pl.multiple_of(pair * width, width), width)
        query = queries[:, columns]
        key = keys[:, columns]
        value = values[:, columns].T
        halves = []
        for side in range(2):
            own = jnp.where(chosen if side == 0 else ~chosen, query, 0)
            scores = nt(key, own) + bias[...]
            highest = jnp.max(scores, axis=0, keepdims=True)
            raised = jnp.exp(scores - highest)
            summed = jnp.sum(raised, axis=0, keepdims=True)
            weights = (raised * (1.0 / summed)).astype(BF16)
            totals[2 * pair + side] = highest + jnp.log(summed)
            halves.append(nn(value[side * width // 2 : (side + 1) * width // 2], weights))
        outputs[:, columns] = jnp.concatenate(halves, axis=0).T.astype(BF16)
        return carry

    lax.fori_loop(0, HEADS // 2, pair_of_heads, 0)


def attend_back(queries, keys, values, bias, totals, grads, query_low, key_low, value_low):
    width = 2 * (queries.shape[1] // HEADS)
    chosen = first_half(width)

    def pair_of_heads(pair, carry):
        columns = pl.ds(pl.multiple_of(pair * width, width), width)
        query = queries[:, columns]
        key = keys[:, columns]
        value = values[:, columns]
        grad = grads[:, columns]
        key_across = key.T
        query_parts, key_parts, value_parts = [], [], []
        for side in range(2):
            mine = chosen if side == 0 else ~chosen
            scores = nt(key, jnp.where(mine, query, 0)) + bias[...]
            probs = jnp.exp(scores - totals[2 * pair + side])
            prob_grad = nt(value, jnp.where(mine, grad, 0))
            value_parts.append(nn(probs.astype(BF16), grad))
            weighted = probs * prob_grad
            centre = jnp.sum(weighted, axis=0, keepdims=True)
            score_grad = (weighted - probs * centre).astype(BF16)
            key_parts.append(nn(score_grad, query))
            query_parts.append(
                nn(key_across[side * width // 2 : (side + 1) * width // 2], score_grad)
            )
        query_low[:, columns] = jnp.concatenate(query_parts, axis=0).T.astype(BF16)
        key_low[:, columns] = jnp.where(chosen, key_parts[0], key_parts[1]).astype(BF16)
        value_low[:, columns] = jnp.where(chosen, value_parts[0], value_parts[1]).astype(BF16)
        return carry

    lax.fori_loop(0, HEADS // 2, pair_of_heads, 0)


def block_rows(weights, parts):
    return weights.shape[1] // (len(parts) * parts[0].shape[0])


def join_kernel(*refs):
    start = 0
    for ref in refs[:-1]:
        refs[-1][start : start + ref.shape[0], :] = ref[...]
        start += ref.shape[0]


def join_rows(*members):
    if any(member.shape[0] % 8 for member in members):
        return jnp.concatenate(members, axis=0)
    rows = sum(member.shape[0] for member in members)
    return pl.pallas_call(
        join_kernel,
        in_specs=[VMEM] * len(members),
        out_specs=VMEM,
        out_shape=like((rows, members[0].shape[1]), members[0].dtype),
        cost_estimate=work(1),
        name="join_rows",
    )(*members)


def line_kernel(narrow, *refs, sizes):
    pieces, block = refs[:-1], refs[-1]
    start = 0
    for size in sizes:
        for step, piece in enumerate(pieces):
            place = pl.multiple_of(start * len(pieces) + (narrow[0] ^ step) * size, 8)
            block[pl.ds(place, size), :] = piece[start : start + size]
        start += size


def join_wide_kernel(*refs):
    block = refs[-1]
    width = block.shape[1]
    start, spot = 0, 0
    for ref in refs[:-1]:
        if ref.shape[1] == width:
            block[start : start + ref.shape[0], :] = ref[...]
            start += ref.shape[0]
    for ref in refs[:-1]:
        if ref.shape[1] != width:
            for first in range(0, ref.shape[1], LANES):
                top = start + spot // (width // LANES) * ref.shape[0]
                left = spot % (width // LANES) * LANES
                block[top : top + ref.shape[0], left : left + LANES] = ref[:, first : first + LANES]
                spot += 1
            size = ref.shape[0]
    while spot % (width // LANES):
        top = start + spot // (width // LANES) * size
        left = spot % (width // LANES) * LANES
        block[top : top + size, left : left + LANES] = jnp.zeros((size, LANES), BF16)
        spot += 1


def line_wide_kernel(narrow, *refs, sizes, wide_size):
    pieces, block, wide_block = refs[:-2], refs[-2], refs[-1]
    count, width = len(pieces), block.shape[1]
    start = 0
    for size in sizes:
        for step, piece in enumerate(pieces):
            place = pl.multiple_of(start * count + (narrow[0] ^ step) * size, 8)
            block[pl.ds(place, size), :] = piece[start : start + size]
        start += size
    matrices = wide_block.shape[0] // (count * wide_size)
    spot = 0
    for matrix in range(matrices):
        for first in range(0, wide_block.shape[1], LANES):
            top = start + spot // (width // LANES) * wide_size
            left = spot % (width // LANES) * LANES
            for step, piece in enumerate(pieces):
                place = pl.multiple_of((matrix * count + (narrow[0] ^ step)) * wide_size, 8)
                wide_block[pl.ds(place, wide_size), first : first + LANES] = piece[
                    top : top + wide_size, left : left + LANES
                ]
            spot += 1


def self_forward_kernel(
    places, lengths, inputs, *refs,
):
    parts = refs[:4]
    normed, query, key, value, attended, totals, stream, gains = refs[4:12]
    weights, gain_parts, bias, sems, gain_sems = refs[12:]
    size = parts[0].shape[0]
    rows = block_rows(weights, parts)
    gain_copies = [
        pltpu.make_async_copy(
            parts[slot // size].at[slot % size, pl.ds(4 * rows, gain_parts.shape[1]), :],
            gain_parts.at[slot],
            gain_sems.at[slot],
        )
        for slot in range(4 * size)
    ]
    copies = weight_copies(places, parts, 0, weights, rows, sems)
    for copy in gain_copies + copies:
        copy.start()
    values = inputs[...].astype(F32)
    fill_self_bias(bias, lengths)
    scaled = values * norm_scale(values)
    for copy in gain_copies:
        copy.wait()
    members = gain_parts[...].astype(F32).reshape(-1, 8, gains.shape[1])
    summed = members[0]
    for member in range(1, members.shape[0]):
        summed = summed + members[member]
    gains[...] = summed
    low = (scaled * summed[0:1]).astype(BF16)
    normed[...] = low
    for copy in copies:
        copy.wait()
    query[...] = nn(low, weights[0]).astype(BF16)
    key[...] = nn(low, weights[1]).astype(BF16)
    value[...] = nn(low, weights[2]).astype(BF16)
    attend(query, key, value, bias, attended, totals)
    stream[...] = values + nn(attended[...], weights[3])


def memory_kernel(places, memory, *refs):
    parts = refs[:4]
    key, value, weights, sems = refs[4:]
    rows = block_rows(weights, parts)
    copies = weight_copies(places, parts, rows, weights, rows, sems)
    for copy in copies:
        copy.start()
    for copy in copies:
        copy.wait()
    key[...] = nn(memory[...], weights[0]).astype(BF16)
    value[...] = nn(memory[...], weights[1]).astype(BF16)


def cross_forward_kernel(
    places, lengths, sources, stream_in, gains, key, value, *refs,
):
    parts = refs[:4]
    normed, query, attended, totals, stream, weights, bias, sems = refs[4:]
    rows = block_rows(weights, parts)
    copies = weight_copies(places, parts, 0, weights.at[pl.ds(0, 1)], rows, sems.at[0])
    copies += weight_copies(places, parts, 3 * rows, weights.at[pl.ds(1, 1)], rows, sems.at[1])
    for copy in copies:
        copy.start()
    values = stream_in[...]
    fill_cross_bias(bias, lengths, sources)
    low = (values * norm_scale(values) * gains[1:2]).astype(BF16)
    normed[...] = low
    for copy in copies:
        copy.wait()
    query[...] = nn(low, weights[0]).astype(BF16)
    attend(query, key, value, bias, attended, totals)
    stream[...] = values + nn(attended[...], weights[1])


def mlp_forward_kernel(
    places, stream_in, gains, side, *refs,
):
    parts, down_parts = refs[:4], refs[4:8]
    normed, gate, up, hidden, stream, activations, exit_normed = refs[8:15]
    weights, down, sems, down_sems = refs[15:]
    rows, down_rows = block_rows(weights, parts), block_rows(down, down_parts)
    first = weight_copies(places, parts, 0, weights, rows, sems)
    last = weight_copies(
        places, down_parts, down_parts[0].shape[1] - down_rows, down, down_rows, down_sems
    )
    for copy in first + last:
        copy.start()
    values = stream_in[...]
    low = (values * norm_scale(values) * gains[2:3]).astype(BF16)
    normed[...] = low
    for copy in first:
        copy.wait()
    width = weights.shape[2]
    step = width // 4
    for part in range(4):
        columns = pl.ds(part * step, step)
        gate_pre = nn(low, weights[0, :, columns])
        up_pre = nn(low, weights[1, :, columns])
        gate[:, columns] = gate_pre
        up[:, columns] = up_pre
        bent = jnp.tanh(MIX * (gate_pre + CUBE * (gate_pre * gate_pre * gate_pre)))
        hidden[:, columns] = (0.5 * gate_pre * (1.0 + bent) * up_pre).astype(BF16)
    for copy in last:
        copy.wait()
    out = values + nn(hidden[...], down[0])
    stream[...] = out
    activations[...] = out.astype(BF16)
    count = out.shape[0]
    exit_normed[:count] = (out * norm_scale(out) * gains[3:4]).astype(BF16)
    exit_normed[count:] = side[...]


def exit_scores_kernel(meta, slot_of, *refs, vocab, scale):
    parts = refs[:4]
    source, raised, across, stats = refs[4:8]
    table, tokens, columns, landed, scores, table_sem, sems = refs[8:]
    size = parts[0].shape[0]
    members = 4 * size
    ring = landed.shape[0]
    count = parts[0].shape[1] - 8
    step = pl.program_id(0)
    tile = raised.shape[0]
    starts, counts = META_LISTS, META_LISTS + members

    def fetch(member):
        slot = slot_of[member]
        for part in range(4):

            @pl.when(slot // size == part)
            def start():
                pltpu.make_async_copy(
                    parts[part].at[slot % size], landed.at[member % ring], sems.at[member % ring]
                ).start()

    @pl.when(step == 0)
    def load():
        whole = pltpu.make_async_copy(source, table, table_sem)
        for member in range(min(ring, members)):
            fetch(member)
        whole.start()
        tokens[...] = jnp.zeros_like(tokens)
        columns[...] = jnp.zeros_like(columns)
        lanes = -(-count // LANES) * LANES
        spots = lax.broadcasted_iota(jnp.int32, (1, lanes), 1)
        for member in range(members):
            pltpu.make_async_copy(
                parts[0].at[0], landed.at[member % ring], sems.at[member % ring]
            ).wait()
            begin = pl.multiple_of(meta[starts + member], 16)
            block = landed[member % ring]
            tokens[pl.ds(begin, count), :] = block[:count]
            side = block[count:, :lanes].astype(F32)
            wanted = side[0:1] * 256.0 + side[1:2]
            weight = jnp.where(spots < meta[counts + member], 1.0, 0.0)
            packed = jnp.concatenate(
                [weight, wanted, jnp.zeros((LANES - 2, lanes), F32)], axis=0
            )
            columns[pl.ds(begin, count), :] = packed.T[:count]
            if member + ring < members:
                fetch(member + ring)
        whole.wait()

    spot = lax.broadcasted_iota(jnp.int32, (tile, LANES), 1)

    @pl.when(step < meta[META_TILES])
    def compute():
        here = pl.ds(pl.multiple_of(step * tile, tile), tile)
        own = tokens[here, :]
        column = columns[here, :]
        across[...] = own.T
        width = scores.shape[1]
        lanes = lax.broadcasted_iota(jnp.int32, (tile, LANES), 1)
        wanted = column[:, 1:2].astype(jnp.int32) - meta[META_WIDE] * vocab
        wanted = jnp.where(wanted < vocab, wanted, -1)
        peaks = jnp.full((tile, LANES), NEGATIVE, F32)
        found = jnp.zeros((tile, LANES), F32)
        for first in range(0, width, VOCAB_TILE):
            part = nn(own, table[:, first : first + VOCAB_TILE])
            for inner in range(0, VOCAB_TILE, LANES):
                piece = part[:, inner : inner + LANES]
                offset = first + inner
                if offset + LANES > vocab:
                    piece = jnp.where(lanes < vocab - offset, piece, NEGATIVE)
                scores[:, offset : offset + LANES] = piece
                peaks = jnp.maximum(peaks, piece)
                found = found + jnp.where(lanes == wanted - offset, piece, 0.0)
        highest = jnp.max(peaks, axis=1, keepdims=True)
        sums = jnp.zeros((tile, LANES), F32)
        for offset in range(0, width, LANES):
            piece = jnp.exp2((scores[:, offset : offset + LANES] - highest) * (scale * LOG2E))
            raised[:, offset : offset + LANES] = piece.astype(BF16)
            sums = sums + piece
        summed = jnp.sum(sums, axis=1, keepdims=True)
        picked = jnp.sum(found, axis=1, keepdims=True)
        values = (highest * scale, summed, picked * scale, column[:, 0:1], column[:, 1:2])
        packed = jnp.zeros((tile, LANES), F32)
        for place, value in enumerate(values):
            packed = jnp.where(spot == place, value, packed)
        stats[...] = packed.T[:8]

    @pl.when(step >= meta[META_TILES])
    def skip():
        rows = lax.broadcasted_iota(jnp.int32, stats.shape, 0)
        stats[...] = jnp.where(rows == 1, 1.0, 0.0)


def exit_grads_kernel(meta, places, *refs, vocab):
    source, raised, across, factors = refs[:4]
    parts = refs[4:8]
    table_grad = refs[8]
    table, total, token_grad, landed, table_sem, sems = refs[9:]
    size = parts[0].shape[0]
    members = 4 * size
    count = parts[0].shape[1]
    starts, counts = META_LISTS, META_LISTS + members
    step = pl.program_id(0)
    tile = raised.shape[0]
    width = raised.shape[1]

    @pl.when(step == 0)
    def load():
        whole = pltpu.make_async_copy(source, table, table_sem)
        whole.start()
        total[...] = jnp.zeros_like(total)
        whole.wait()

    @pl.when(step < meta[META_TILES] // (tile // ROW_TILE))
    def compute():
        columns = jnp.concatenate(
            [factors[...], jnp.zeros((LANES - factors.shape[0], tile), F32)], axis=0
        ).T
        factor, at_target = columns[:, 0:1], columns[:, 1:2]
        wanted = columns[:, 2:3].astype(jnp.int32) - meta[META_WIDE] * vocab
        wanted = jnp.where(wanted < vocab, wanted, -1)
        lanes = lax.broadcasted_iota(jnp.int32, (tile, VOCAB_TILE), 1)
        grad = jnp.zeros((tile, token_grad.shape[1]), F32)
        for first in range(0, width, VOCAB_TILE):
            chunk = slice(first, first + VOCAB_TILE)
            part = raised[:, chunk].astype(F32) * factor
            part = jnp.where(lanes == wanted - first, at_target, part).astype(BF16)
            grad = grad + nt(part, table[:, chunk])
            total[:, chunk] += nn(across[...], part)
        token_grad[pl.ds(pl.multiple_of(step * tile, tile), tile), :] = grad.astype(BF16)

    @pl.when(step == pl.num_programs(0) - 1)
    def finish():
        copies = []
        spots = lax.broadcasted_iota(jnp.int32, (count, 1), 0)
        for slot in range(members):
            if slot >= 2:
                copies[slot - 2].wait()
            member = places[slot]
            begin = pl.multiple_of(meta[starts + member], 16)
            block = token_grad[pl.ds(begin, count), :].astype(F32)
            landed[slot % 2] = jnp.where(spots < meta[counts + member], block, 0.0).astype(BF16)
            copy = pltpu.make_async_copy(
                landed.at[slot % 2], parts[slot // size].at[slot % size], sems.at[slot % 2]
            )
            copy.start()
            copies.append(copy)
        table_grad[...] = total[...].astype(BF16)
        for copy in copies[-2:]:
            copy.wait()


def mlp_backward_kernel(
    places, grad_in, stream_three, stream_two, gain, normed, gate, up, hidden, *refs,
):
    parts, down_parts = refs[:4], refs[4:8]
    stream_grad, gains = refs[8:10]
    grad_parts, down_grad_parts = refs[10:14], refs[14:18]
    weights, down, gate_low, up_low, result, down_result, sems, down_sems = refs[18:]
    rows, down_rows = block_rows(weights, parts), block_rows(down, down_parts)
    copies = weight_copies(
        places, down_parts, down_parts[0].shape[1] - down_rows, down, down_rows, down_sems
    )
    copies += weight_copies(places, parts, 0, weights, rows, sems)
    for copy in copies:
        copy.start()
    stream_back, exit_gain_grad = norm_back(stream_three[...], gain[3:4], grad_in[...])
    branch = stream_back.astype(BF16)
    for copy in copies:
        copy.wait()
    width = weights.shape[2]
    step = width // 4
    for part in range(4):
        columns = pl.ds(part * step, step)
        gate_pre = gate[:, columns]
        up_pre = up[:, columns]
        hidden_grad = nt(branch, down[0, columns, :])
        bent = jnp.tanh(MIX * (gate_pre + CUBE * (gate_pre * gate_pre * gate_pre)))
        slope = 0.5 * (1.0 + bent) + 0.5 * gate_pre * (1.0 - bent * bent) * (
            MIX * (1.0 + 3.0 * CUBE * gate_pre * gate_pre)
        )
        gate_low[:, columns] = (hidden_grad * up_pre * slope).astype(BF16)
        up_low[:, columns] = (hidden_grad * (0.5 * gate_pre * (1.0 + bent))).astype(BF16)
    normed_grad = nt(gate_low[...], weights[0]) + nt(up_low[...], weights[1])
    branch_in, gain_grad = norm_back(stream_two[...], gain[2:3], normed_grad)
    stream_grad[...] = stream_back + branch_in
    gains[...] = jnp.concatenate(
        [gain_grad, exit_gain_grad, jnp.zeros((6, gain_grad.shape[1]), F32)], axis=0
    )
    for matrix, low in enumerate((gate_low, up_low)):
        for part in range(4):
            columns = pl.ds(part * step, step)
            result[:, columns] = tn(normed[...], low[:, columns]).astype(BF16)
        store_blocks(places, result, matrix * rows, rows, grad_parts)
    for part in range(4):
        columns = pl.ds(part * step, step)
        down_result[columns, :] = tn(hidden[:, columns], branch).astype(BF16)
    store_blocks(places, down_result, 0, down_rows, down_grad_parts)


def cross_attention_backward_kernel(
    places, lengths, sources, grad_in, query, key, value, totals, *refs,
):
    parts = refs[:4]
    branch, query_low, key_low, value_low, weights, bias, attended_grad, sems = refs[4:]
    rows = block_rows(weights, parts)
    copies = weight_copies(places, parts, 3 * rows, weights, rows, sems)
    for copy in copies:
        copy.start()
    fill_cross_bias(bias, lengths, sources)
    branch[...] = grad_in[...].astype(BF16)
    for copy in copies:
        copy.wait()
    attended_grad[...] = nt(branch[...], weights[0]).astype(BF16)
    attend_back(
        query, key, value, bias, totals, attended_grad, query_low, key_low, value_low
    )


def cross_backward_kernel(
    places, grad_in, stream_in, gain, normed, memory, attended,
    branch, query_low, key_low, value_low, *refs,
):
    parts = refs[:4]
    stream_grad, gains, memory_grad = refs[4:7]
    grad_parts = refs[7:11]
    weights, result, sems = refs[11:]
    rows = block_rows(weights, parts)
    copies = weight_copies(places, parts, 0, weights, rows, sems)
    for copy in copies:
        copy.start()
    pairs = ((normed, query_low), (memory, key_low), (memory, value_low), (attended, branch))
    for matrix, (left, right) in enumerate(pairs):
        result[...] = tn(left[...], right[...]).astype(BF16)
        store_blocks(places, result, matrix * rows, rows, grad_parts)
    for copy in copies:
        copy.wait()
    normed_grad = nt(query_low[...], weights[0])
    branch_in, gain_grad = norm_back(stream_in[...], gain[1:2], normed_grad)
    stream_grad[...] = grad_in[...] + branch_in
    gains[...] = jnp.broadcast_to(gain_grad, gains.shape)
    memory_grad[...] = nt(key_low[...], weights[1]) + nt(value_low[...], weights[2])


def self_attention_backward_kernel(
    places, lengths, grad_in, query, key, value, totals, *refs,
):
    parts = refs[:4]
    branch, query_low, key_low, value_low, weights, bias, attended_grad, sems = refs[4:]
    rows = block_rows(weights, parts)
    copies = weight_copies(places, parts, 3 * rows, weights, rows, sems)
    for copy in copies:
        copy.start()
    fill_self_bias(bias, lengths)
    branch[...] = grad_in[...].astype(BF16)
    for copy in copies:
        copy.wait()
    attended_grad[...] = nt(branch[...], weights[0]).astype(BF16)
    attend_back(
        query, key, value, bias, totals, attended_grad, query_low, key_low, value_low
    )


def self_backward_kernel(
    places, grad_in, inputs, gain, normed, attended, cross_gains, mlp_gains,
    branch, query_low, key_low, value_low, *refs,
):
    parts = refs[:4]
    stream_grad = refs[4]
    grad_parts = refs[5:9]
    weights, result, sems = refs[9:]
    rows = block_rows(weights, parts)
    copies = weight_copies(places, parts, 0, weights, rows, sems)
    for copy in copies:
        copy.start()
    pairs = ((normed, query_low), (normed, key_low), (normed, value_low), (attended, branch))
    for matrix, (left, right) in enumerate(pairs):
        result[...] = tn(left[...], right[...]).astype(BF16)
        store_blocks(places, result, matrix * rows, rows, grad_parts)
    for copy in copies:
        copy.wait()
    normed_grad = (
        nt(query_low[...], weights[0])
        + nt(key_low[...], weights[1])
        + nt(value_low[...], weights[2])
    )
    branch_in, gain_grad = norm_back(inputs[...].astype(F32), gain[0:1], normed_grad)
    stream_grad[...] = grad_in[...] + branch_in
    spot = lax.broadcasted_iota(jnp.int32, (8, gain_grad.shape[1]), 0)
    terms = jnp.where(spot == 0, gain_grad, 0.0)
    terms = jnp.where(spot == 1, cross_gains[0:1], terms)
    terms = jnp.where(spot == 2, mlp_gains[0:1], terms)
    terms = jnp.where(spot == 3, mlp_gains[1:2], terms).astype(BF16)
    for part in grad_parts:
        for slot in range(part.shape[0]):
            for start in range(4 * rows, part.shape[1], 8):
                part[slot, start : start + 8, :] = terms


def per_device(
    inputs,
    memory,
    targets,
    tgt_lengths,
    src_lengths,
    self_gain,
    self_query,
    self_key,
    self_value,
    self_out,
    cross_gain,
    cross_query,
    cross_key,
    cross_value,
    cross_out,
    mlp_gain,
    mlp_gate,
    mlp_up,
    mlp_down,
    exit_gain,
    embedding,
):
    tokens, model = inputs.shape
    slots = memory.shape[0]
    hidden_width = mlp_gate.shape[1]
    pair_slots = tgt_lengths.shape[1]
    wide_count = lax.axis_size("wide")
    narrow_count = lax.axis_size("narrow")
    wide = lax.axis_index("wide")
    narrow = lax.axis_index("narrow")
    slot_total = tokens * wide_count * narrow_count
    scale = 1.0 / math.sqrt(model)
    places = slot_places(wide, wide_count)
    lengths, sources = tgt_lengths[0], src_lengths[0]
    shard = self_query.shape[0]
    rows = shard * narrow_count
    down_rows = mlp_down.shape[0] * narrow_count

    aligned = rows % 8 == 0
    kernel_places = places if aligned else jnp.arange(4, dtype=jnp.int32)
    kernel_count = wide_count if aligned else 4
    ids = jnp.arange(wide_count, dtype=jnp.int32)
    order = places[None, :] == ids[:, None]

    def reorder(matrix, blocks):
        flat = blocks.reshape(wide_count, -1)
        return nn(matrix.astype(BF16), flat).astype(BF16).reshape(blocks.shape)

    def for_kernels(parts, sizes):
        if aligned:
            return parts
        whole, start, members = jnp.concatenate(parts, axis=0), 0, []
        for size in sizes:
            ordered = reorder(order, whole[:, start : start + size])
            members.append(ordered.reshape(4, -1, whole.shape[-1]))
            start += size
        return jnp.split(jnp.concatenate(members, axis=1), 4)

    def from_kernels(parts, sizes):
        if aligned:
            return parts
        whole, start, members = jnp.concatenate(parts, axis=0), 0, []
        for size in sizes:
            extent = size * wide_count // 4
            member = whole[:, start : start + extent].reshape(wide_count, size, -1)
            members.append(reorder(order.T, member))
            start += extent
        return jnp.split(jnp.concatenate(members, axis=1), 4)

    def line_block(pieces, sizes, *others):
        pieces = lax.optimization_barrier((*pieces, *others))[: len(pieces)]
        if all(size % 8 == 0 for size in sizes):
            return pl.pallas_call(
                functools.partial(line_kernel, sizes=sizes),
                in_specs=[SMEM] + [VMEM] * len(pieces),
                out_specs=VMEM,
                out_shape=like((pieces[0].shape[0] * len(pieces), pieces[0].shape[1]), BF16),
                compiler_params=PARAMS,
                cost_estimate=work(1),
                name="line_block",
            )(narrow[None], *pieces)
        ordered, start, members = in_line_order(pieces, narrow), 0, []
        for size in sizes:
            members += [piece[start : start + size] for piece in ordered]
            start += size
        return jnp.concatenate(members, axis=0)

    self_sizes, cross_sizes = [shard] * 4 + [8], [shard] * 4 + [mlp_down.shape[0]]
    gate_sizes = [shard] * 2
    count = jnp.sum(lengths)
    owner = wide * narrow_count + narrow
    gain_shards = jnp.stack([self_gain, cross_gain, mlp_gain, exit_gain])
    numbers = jnp.broadcast_to(
        jnp.stack([count // 16, count % 16])[:, None], (2, shard)
    ).astype(BF16)
    own_rows = jnp.concatenate([gain_shards, numbers, jnp.zeros((2, shard), BF16)], axis=0)
    own_rows = jnp.tile(own_rows, (1, model // shard))
    own_columns = jnp.arange(model, dtype=jnp.int32)[None, :] // shard == owner
    own_rows = jnp.where(own_columns, own_rows, 0)
    self_pack = join_rows(self_query, self_key, self_value, self_out, own_rows)
    members = (cross_query, cross_key, cross_value, cross_out, mlp_down)
    if aligned:
        wide_rows = -(-2 * hidden_width // model) * shard
        joined_pack = pl.pallas_call(
            join_wide_kernel,
            in_specs=[VMEM] * 7,
            out_specs=VMEM,
            out_shape=like((sum(cross_sizes) + wide_rows, model), BF16),
            compiler_params=PARAMS,
            cost_estimate=work(1),
            name="join_wide",
        )(*members, mlp_gate, mlp_up)
    side = jnp.stack([targets // 256, targets % 256]).astype(BF16)
    side = jnp.pad(side, ((0, 6), (0, model - tokens)))

    self_line = gather_narrow(self_pack, narrow_count)
    self_block = line_block(self_line, self_sizes)

    vocab = embedding.shape[0]
    padded = -(-vocab // VOCAB_TILE) * VOCAB_TILE
    turned = jnp.pad(embedding.T, ((0, 0), (0, padded - vocab)))
    table = lax.all_gather(tie(turned, *self_line), "narrow", axis=0, tiled=True)

    *early, last = stage_pairs(wide_count)

    def gather_early(block):
        held = block[None]
        for pairs in early:
            held = jnp.concatenate([held, lax.ppermute(held, "wide", pairs)], axis=0)
        return held

    if aligned:
        joined_line = gather_narrow(tie(joined_pack, *self_line), narrow_count)
    else:
        cross_line = gather_narrow(join_rows(*members), narrow_count)
        gate_line = gather_narrow(join_rows(mlp_gate, mlp_up), narrow_count)
    self_held = gather_early(self_block)
    self_came = lax.ppermute(self_held, "wide", last)
    if aligned:
        joined_line = lax.optimization_barrier((*joined_line, self_held))[:narrow_count]
        cross_block, gate_block = pl.pallas_call(
            functools.partial(line_wide_kernel, sizes=cross_sizes, wide_size=shard),
            in_specs=[SMEM] + [VMEM] * narrow_count,
            out_specs=[VMEM] * 2,
            out_shape=[
                like((sum(cross_sizes) * narrow_count, model), BF16),
                like((2 * rows, hidden_width), BF16),
            ],
            compiler_params=PARAMS,
            cost_estimate=work(1),
            name="line_wide",
        )(narrow[None], *joined_line)
    else:
        cross_block = line_block(cross_line, cross_sizes)
        gate_block = line_block(gate_line, gate_sizes)
    self_parts = (
        self_held, self_came, cross_core(self_held, wide_count), cross_core(self_came, wide_count)
    )
    cross_held = gather_early(tie(cross_block, self_came))
    cross_came = lax.ppermute(cross_held, "wide", last)

    head_rows = like((HEADS, 1, tokens), F32)
    activation = like((tokens, model), BF16)
    stream_like = like((tokens, model), F32)
    matrix_sems = pltpu.SemaphoreType.DMA((kernel_count, 4))
    one_matrix_sems = pltpu.SemaphoreType.DMA((kernel_count, 1))

    self_gathered = for_kernels(self_parts, [size * narrow_count for size in self_sizes])
    (
        normed_one, query_one, key_one, value_one, attended_one, totals_one, stream_one, gain_all,
    ) = pl.pallas_call(
        self_forward_kernel,
        in_specs=[SMEM, SMEM, VMEM] + [ANY] * 4,
        out_specs=[VMEM] * 8,
        out_shape=[activation] * 5 + [head_rows, stream_like, like((8, model), F32)],
        scratch_shapes=[
            pltpu.VMEM((4, model, model), BF16),
            pltpu.VMEM((kernel_count, 8 * narrow_count * wide_count // kernel_count, model), BF16),
            pltpu.VMEM((tokens, tokens), F32),
            matrix_sems,
            pltpu.SemaphoreType.DMA((kernel_count,)),
        ],
        compiler_params=PARAMS,
        cost_estimate=work(1),
        name="self_forward",
    )(kernel_places, lengths, tie(inputs, cross_held), *self_gathered)

    numbers = (gain_all[4] * 16.0 + gain_all[5]).reshape(wide_count, narrow_count, shard)[:, :, 0]
    numbers = jnp.sum(
        jnp.where(jnp.arange(narrow_count)[None, :] == narrow, numbers, 0.0), axis=1
    ).astype(jnp.int32)
    extents = (numbers + 15) // 16 * 16
    starts = jnp.sum(jnp.where(ids[None, :] < ids[:, None], extents[None, :], 0), axis=1)
    needed = (jnp.sum(extents) + GRAD_TILE - 1) // GRAD_TILE * (GRAD_TILE // ROW_TILE)
    meta = jnp.concatenate([jnp.stack([wide, needed]), starts, numbers])
    slot_of = jnp.sum(jnp.where(order, ids[None, :], 0), axis=1)

    cross_came = tie(cross_came, stream_one)
    cross_parts = (
        cross_held, cross_came, cross_core(cross_held, wide_count), cross_core(cross_came, wide_count)
    )
    gate_held = gather_early(tie(gate_block, cross_came))
    gate_came = lax.ppermute(gate_held, "wide", last)
    cross_gathered = for_kernels(cross_parts, [size * narrow_count for size in cross_sizes])

    key_two, value_two = pl.pallas_call(
        memory_kernel,
        in_specs=[SMEM, VMEM] + [ANY] * 4,
        out_specs=[VMEM] * 2,
        out_shape=[like((slots, model), BF16)] * 2,
        scratch_shapes=[
            pltpu.VMEM((2, model, model), BF16),
            pltpu.SemaphoreType.DMA((kernel_count, 2)),
        ],
        compiler_params=PARAMS,
        cost_estimate=work(1),
        name="memory_projection",
    )(kernel_places, memory, *cross_gathered)

    normed_two, query_two, attended_two, totals_two, stream_two = pl.pallas_call(
        cross_forward_kernel,
        in_specs=[SMEM, SMEM, SMEM, VMEM, VMEM, VMEM, VMEM] + [ANY] * 4,
        out_specs=[VMEM] * 5,
        out_shape=[activation] * 3 + [head_rows, stream_like],
        scratch_shapes=[
            pltpu.VMEM((2, model, model), BF16),
            pltpu.VMEM((slots, tokens), F32),
            pltpu.SemaphoreType.DMA((2, kernel_count, 1)),
        ],
        compiler_params=PARAMS,
        cost_estimate=work(1),
        name="cross_forward",
    )(
        kernel_places, lengths, sources, tie(stream_one, gate_held), gain_all, key_two, value_two,
        *cross_gathered,
    )

    gate_came = tie(gate_came, stream_two)
    gate_parts = (
        gate_held, gate_came, cross_core(gate_held, wide_count), cross_core(gate_came, wide_count)
    )
    gate_gathered = for_kernels(gate_parts, [size * narrow_count for size in gate_sizes])

    wide_f32 = like((tokens, hidden_width), F32)
    wide_low = like((tokens, hidden_width), BF16)
    normed_three, gate_pre, up_pre, hidden, stream_three, activations, normed_four = pl.pallas_call(
        mlp_forward_kernel,
        in_specs=[SMEM, VMEM, VMEM, VMEM] + [ANY] * 8,
        out_specs=[VMEM] * 7,
        out_shape=[
            activation, wide_f32, wide_f32, wide_low, stream_like, activation,
            like((tokens + 8, model), BF16),
        ],
        scratch_shapes=[
            pltpu.VMEM((2, model, hidden_width), BF16),
            pltpu.VMEM((1, hidden_width, model), BF16),
            pltpu.SemaphoreType.DMA((kernel_count, 2)),
            one_matrix_sems,
        ],
        compiler_params=PARAMS,
        cost_estimate=work(1),
        name="mlp_forward",
    )(kernel_places, stream_two, gain_all, side, *gate_gathered, *cross_gathered)

    exit_parts = gather_wide(normed_four, wide_count)
    group = tokens * wide_count
    tiles = -(-group // GRAD_TILE) * (GRAD_TILE // ROW_TILE)
    kept = lambda i, meta: jnp.minimum(i, meta[META_TILES] - 1)
    kept_grad = lambda i, meta: jnp.minimum(i, meta[META_TILES] * ROW_TILE // GRAD_TILE - 1)

    raised, tokens_across, stats = pl.pallas_call(
        functools.partial(exit_scores_kernel, vocab=vocab, scale=scale),
        grid_spec=pltpu.PrefetchScalarGridSpec(
            num_scalar_prefetch=2,
            grid=(tiles,),
            in_specs=[ANY] * 5,
            out_specs=[
                pl.BlockSpec((ROW_TILE, padded), lambda i, meta, slots: (kept(i, meta), 0)),
                pl.BlockSpec((model, ROW_TILE), lambda i, meta, slots: (0, kept(i, meta))),
                pl.BlockSpec((8, ROW_TILE), lambda i, meta, slots: (0, i)),
            ],
            scratch_shapes=[
                pltpu.VMEM((model, padded), BF16),
                pltpu.VMEM((tiles * ROW_TILE, model), BF16),
                pltpu.VMEM((tiles * ROW_TILE, LANES), F32),
                pltpu.VMEM((min(wide_count, 8), tokens + 8, model), BF16),
                pltpu.VMEM((ROW_TILE, padded), F32),
                pltpu.SemaphoreType.DMA,
                pltpu.SemaphoreType.DMA((min(wide_count, 8),)),
            ],
        ),
        out_shape=[
            like((tiles * ROW_TILE, padded), BF16),
            like((model, tiles * ROW_TILE), BF16),
            like((8, tiles * ROW_TILE), F32),
        ],
        compiler_params=PARAMS,
        cost_estimate=work(1),
        name="exit_scores",
    )(meta, slot_of, *exit_parts, table)

    own_peak = stats[0]
    joint = stats
    for pairs in stage_pairs(wide_count) + [flip_pairs(wide_count)]:
        came = lax.ppermute(joint, "wide", pairs)
        peak = jnp.maximum(joint[0], came[0])
        summed = joint[1] * jnp.exp(joint[0] - peak) + came[1] * jnp.exp(came[0] - peak)
        joint = jnp.concatenate([peak[None], summed[None], joint[2:3] + came[2:3], stats[3:]], axis=0)
    log_total = joint[0] + jnp.log(joint[1])
    picked, group_weight = joint[2], stats[3]
    loss_part = jnp.full((8, LANES), jnp.sum(group_weight * (log_total - picked)), F32)
    loss_all = loss_part
    for step in range(1, narrow_count):
        loss_all = loss_all + lax.ppermute(loss_part, "narrow", narrow_pairs(narrow_count, step))
    mean_loss = loss_all[0, 0] / slot_total

    factor = jnp.exp(own_peak - log_total) * (group_weight * scale)
    at_target = (jnp.exp(picked - log_total) - 1.0) * (group_weight * scale)
    factors = jnp.concatenate([factor[None], at_target[None], stats[4:5], stats[3:]], axis=0)
    token_part = like((wide_count // 4, tokens, model), BF16)
    *exit_grads, table_grad = pl.pallas_call(
        functools.partial(exit_grads_kernel, vocab=vocab),
        grid_spec=pltpu.PrefetchScalarGridSpec(
            num_scalar_prefetch=2,
            grid=(tiles * ROW_TILE // GRAD_TILE,),
            in_specs=[
                ANY,
                pl.BlockSpec((GRAD_TILE, padded), lambda i, meta, slots: (kept_grad(i, meta), 0)),
                pl.BlockSpec((model, GRAD_TILE), lambda i, meta, slots: (0, kept_grad(i, meta))),
                pl.BlockSpec((8, GRAD_TILE), lambda i, meta, slots: (0, i)),
            ],
            out_specs=[ANY] * 4 + [pl.BlockSpec((model, padded), lambda i, meta, slots: (0, 0))],
            scratch_shapes=[
                pltpu.VMEM((model, padded), BF16),
                pltpu.VMEM((model, padded), F32),
                pltpu.VMEM((tiles * ROW_TILE, model), BF16),
                pltpu.VMEM((2, tokens, model), BF16),
                pltpu.SemaphoreType.DMA,
                pltpu.SemaphoreType.DMA((2,)),
            ],
        ),
        out_shape=[token_part] * 4 + [like((model, padded), BF16)],
        compiler_params=PARAMS,
        cost_estimate=work(1),
        name="exit_grads",
    )(meta, places, table, raised, tokens_across, factors)

    table_sum = lax.psum_scatter(table_grad, "narrow", scatter_dimension=0, tiled=True)
    embedding_grad = table_sum.astype(F32).T[:vocab]
    exit_grad = scatter_wide(exit_grads, wide_count)

    gain_like = like((8, model), F32)
    stream_two_grad, mlp_gains, *mlp_grads = pl.pallas_call(
        mlp_backward_kernel,
        in_specs=[SMEM] + [VMEM] * 8 + [ANY] * 8,
        out_specs=[VMEM] * 10,
        out_shape=[stream_like, gain_like]
        + [like(part.shape, BF16) for part in gate_gathered]
        + [
            like((part.shape[0], hidden_width // kernel_count, model), BF16)
            for part in cross_gathered
        ],
        scratch_shapes=[
            pltpu.VMEM((2, model, hidden_width), BF16),
            pltpu.VMEM((1, hidden_width, model), BF16),
            pltpu.VMEM((tokens, hidden_width), BF16),
            pltpu.VMEM((tokens, hidden_width), BF16),
            pltpu.VMEM((model, hidden_width), BF16),
            pltpu.VMEM((hidden_width, model), BF16),
            pltpu.SemaphoreType.DMA((kernel_count, 2)),
            one_matrix_sems,
        ],
        compiler_params=PARAMS,
        cost_estimate=work(1),
        name="mlp_backward",
    )(
        kernel_places, exit_grad, stream_three, stream_two, gain_all, normed_three,
        gate_pre, up_pre, hidden, *gate_gathered, *cross_gathered,
    )
    gate_scatter = scatter_core(from_kernels(mlp_grads[:4], [rows, rows]), wide_count)
    down_scatter = scatter_core(from_kernels(mlp_grads[4:], [down_rows]), wide_count)

    low_like = like((slots, model), BF16)
    branch_two, query_two_low, key_two_low, value_two_low = pl.pallas_call(
        cross_attention_backward_kernel,
        in_specs=[SMEM] * 3 + [VMEM] * 5 + [ANY] * 4,
        out_specs=[VMEM] * 4,
        out_shape=[activation, activation, low_like, low_like],
        scratch_shapes=[
            pltpu.VMEM((1, model, model), BF16),
            pltpu.VMEM((slots, tokens), F32),
            pltpu.VMEM((tokens, model), BF16),
            one_matrix_sems,
        ],
        compiler_params=PARAMS,
        cost_estimate=work(1),
        name="cross_attention_backward",
    )(
        kernel_places, lengths, sources, stream_two_grad, query_two, key_two, value_two, totals_two,
        *cross_gathered,
    )

    def go_far(scatter, *others):
        (own, came), kept = scatter
        return scatter_far((own, tie(came, *others)), kept, wide_count)

    def go_near(state, *others):
        _, came, kept = state
        return scatter_near(tie(came, *others), kept, wide_count)

    gate_far = go_far(gate_scatter, query_two_low)
    down_far = go_far(down_scatter, query_two_low)

    cross_matrices = like((cross_gathered[0].shape[0], 4 * model // kernel_count, model), BF16)
    stream_one_grad, cross_gains, memory_grad, *cross_grads = pl.pallas_call(
        cross_backward_kernel,
        in_specs=[SMEM] + [VMEM] * 10 + [ANY] * 4,
        out_specs=[VMEM] * 7,
        out_shape=[stream_like, gain_like, like((slots, model), F32)] + [cross_matrices] * 4,
        scratch_shapes=[
            pltpu.VMEM((3, model, model), BF16),
            pltpu.VMEM((model, model), BF16),
            pltpu.SemaphoreType.DMA((kernel_count, 3)),
        ],
        compiler_params=PARAMS,
        cost_estimate=work(1),
        name="cross_backward",
    )(
        kernel_places, tie(stream_two_grad, gate_far[0], down_far[0]), stream_one, gain_all,
        normed_two, memory, attended_two, branch_two, query_two_low, key_two_low, value_two_low,
        *cross_gathered,
    )
    cross_scatter = scatter_core(from_kernels(cross_grads, [rows] * 4), wide_count)

    branch_one, query_one_low, key_one_low, value_one_low = pl.pallas_call(
        self_attention_backward_kernel,
        in_specs=[SMEM] * 2 + [VMEM] * 5 + [ANY] * 4,
        out_specs=[VMEM] * 4,
        out_shape=[activation] * 4,
        scratch_shapes=[
            pltpu.VMEM((1, model, model), BF16),
            pltpu.VMEM((tokens, tokens), F32),
            pltpu.VMEM((tokens, model), BF16),
            one_matrix_sems,
        ],
        compiler_params=PARAMS,
        cost_estimate=work(1),
        name="self_attention_backward",
    )(
        kernel_places, lengths, tie(stream_one_grad, loss_all), query_one, key_one, value_one, totals_one,
        *self_gathered,
    )
    gate_near = go_near(gate_far, query_one_low)
    down_near = go_near(down_far, query_one_low)
    cross_far = go_far(cross_scatter, query_one_low)

    inputs_grad, *self_grads = pl.pallas_call(
        self_backward_kernel,
        in_specs=[SMEM] + [VMEM] * 11 + [ANY] * 4,
        out_specs=[VMEM] * 5,
        out_shape=[stream_like] + [like(part.shape, BF16) for part in self_gathered],
        scratch_shapes=[
            pltpu.VMEM((3, model, model), BF16),
            pltpu.VMEM((model, model), BF16),
            pltpu.SemaphoreType.DMA((kernel_count, 3)),
        ],
        compiler_params=PARAMS,
        cost_estimate=work(1),
        name="self_backward",
    )(
        kernel_places, tie(stream_one_grad, gate_near[0], down_near[0], cross_far[0]), inputs,
        gain_all, normed_one, attended_one, cross_gains, mlp_gains, branch_one, query_one_low,
        key_one_low, value_one_low, *self_gathered,
    )
    extra = narrow_count * 8
    self_scatter = scatter_core(from_kernels(self_grads, [rows] * 4 + [extra]), wide_count)

    def finish(near, matrices, *others):
        _, came, held = near
        summed = held + tie(came, *others).astype(F32)
        width = summed.shape[-1]
        size = matrices * (summed.shape[0] // (matrices * 8 * narrow_count)) * 8 * narrow_count
        members = [
            summed[:size].reshape(matrices, narrow_count, -1, width).transpose(1, 0, 2, 3)
            .reshape(narrow_count, -1, width)
        ]
        if size < summed.shape[0]:
            members.append(summed[size:].reshape(narrow_count, -1, width))
        return scatter_narrow(jnp.concatenate(members, axis=1), narrow, narrow_count)

    gate_sum = finish(gate_near, 2, inputs_grad).reshape(2, shard, hidden_width)
    down_sum = finish(down_near, 1, inputs_grad)
    cross_near = go_near(cross_far, inputs_grad)
    self_far = go_far(self_scatter)
    cross_sum = finish(cross_near, 4).reshape(4, shard, model)
    self_sum = finish(go_near(self_far), 4)
    gains = pick(self_sum[4 * shard :].reshape(8, model // shard, shard), owner, 1)
    self_sum = self_sum[: 4 * shard].reshape(4, shard, model)

    return (
        activations,
        mean_loss,
        inputs_grad,
        memory_grad,
        gains[0],
        self_sum[0],
        self_sum[1],
        self_sum[2],
        self_sum[3],
        gains[1],
        cross_sum[0],
        cross_sum[1],
        cross_sum[2],
        cross_sum[3],
        gains[2],
        gate_sum[0],
        gate_sum[1],
        down_sum,
        gains[3],
        embedding_grad,
    )


def solution(mesh):
    both = ("wide", "narrow")
    rows, flat = P(both, None), P(both)
    placed = (
        rows, rows, flat, rows, rows,
        flat, rows, rows, rows, rows,
        flat, rows, rows, rows, rows,
        flat, rows, rows, rows, flat,
        P("wide", "narrow"),
    )
    given = (
        rows, P(), rows, rows,
        flat, rows, rows, rows, rows,
        flat, rows, rows, rows, rows,
        flat, rows, rows, rows, flat,
        P("wide", "narrow"),
    )
    return jax.shard_map(
        per_device, mesh=mesh, in_specs=placed, out_specs=given, check_vma=False
    )
```

```python
import functools
import math

import jax
import jax.numpy as jnp
from jax import lax
from jax.experimental import pallas as pl
from jax.experimental.pallas import tpu as pltpu
from jax.sharding import PartitionSpec as P

HEADS = 12
EPSILON = 1e-06
NEGATIVE = -1e30
F32 = jnp.float32
BF16 = jnp.bfloat16
LANES = 128
ROW_TILE = 256
GRAD_TILE = 256
VOCAB_TILE = 512
MIX = math.sqrt(2.0 / math.pi)
CUBE = 0.044715
LOG2E = math.log2(math.e)
META_WIDE, META_TILES, META_LISTS = 0, 1, 2

VMEM = pl.BlockSpec(memory_space=pltpu.VMEM)
SMEM = pl.BlockSpec(memory_space=pltpu.SMEM)
ANY = pl.BlockSpec(memory_space=pl.ANY)
PARAMS = pltpu.CompilerParams(vmem_limit_bytes=60 * 2**20)


def work(gigaflops):
    return pl.CostEstimate(flops=gigaflops * 10**9, bytes_accessed=10**6, transcendentals=0)


def nn(left, right):
    return lax.dot_general(left, right, (((1,), (0,)), ((), ())), preferred_element_type=F32)


def nt(left, right):
    return lax.dot_general(left, right, (((1,), (1,)), ((), ())), preferred_element_type=F32)


def tn(left, right):
    return lax.dot_general(left, right, (((0,), (0,)), ((), ())), preferred_element_type=F32)


def like(shape, kind):
    return jax.ShapeDtypeStruct(shape, kind)


def stage_masks(count):
    up = [1 << bit for bit in range(1, count.bit_length() - 1)]
    return up, up[::-1]


def stage_pairs(count):
    even, odd = stage_masks(count)
    return [[(v, v ^ (odd if v % 2 else even)[i]) for v in range(count)] for i in range(len(even))]


def flip_pairs(count):
    return [(v, v ^ 1) for v in range(count)]


def slot_tables(count):
    tables = []
    for masks in stage_masks(count):
        slots = [0]
        for mask in masks:
            slots = slots + [slot ^ mask for slot in slots]
        tables.append(slots)
    even, odd = tables
    return (
        even + [1 ^ slot for slot in odd],
        odd + [1 ^ slot for slot in even],
    )


def slot_places(wide, count):
    even, odd = slot_tables(count)
    table = jnp.where(wide % 2 == 0, jnp.array(even, jnp.int32), jnp.array(odd, jnp.int32))
    return wide ^ table


def tie(value, *others):
    return lax.optimization_barrier((value, *others))[0]


def cross_core(value, count):
    return lax.ppermute(value, "wide", flip_pairs(count))


def gather_wide(block, count):
    held = block[None]
    *early, last = stage_pairs(count)
    for pairs in early:
        held = jnp.concatenate([held, lax.ppermute(held, "wide", pairs)], axis=0)
    came = lax.ppermute(held, "wide", last)
    return held, came, cross_core(held, count), cross_core(came, count)


def scatter_core(parts, count):
    sent, kept = cross_core(parts[3], count), cross_core(parts[2], count)
    return (parts[1], sent), (parts[0], kept)


def scatter_far(sent, kept, count):
    far = sent[0] + sent[1]
    came = lax.ppermute(far, "wide", stage_pairs(count)[-1])
    return far, came, kept


def scatter_near(came, kept, count):
    *rest, last = stage_pairs(count)[-2::-1]
    terms = (*kept, came)
    if not rest:
        far = sum(term[1].astype(F32) for term in terms).astype(BF16)
        return far, lax.ppermute(far, "wide", last), sum(term[0].astype(F32) for term in terms)
    held = sum(term.astype(F32) for term in terms)
    for pairs in rest:
        half = held.shape[0] // 2
        sent = lax.ppermute(held[half:].astype(BF16), "wide", pairs)
        held = held[:half] + sent.astype(F32)
    far = held[1].astype(BF16)
    return far, lax.ppermute(far, "wide", last), held[0]


def scatter_wide(parts, count):
    far, came, kept = scatter_far(*scatter_core(parts, count), count)
    far, came, held = scatter_near(came, kept, count)
    return held + came.astype(F32)


def narrow_pairs(count, step):
    return [(v, v ^ step) for v in range(count)]


def gather_narrow(block, count):
    return [block] + [
        lax.ppermute(block, "narrow", narrow_pairs(count, step)) for step in range(1, count)
    ]


def pick(values, place, axis=0):
    return lax.dynamic_index_in_dim(values, place.astype(jnp.uint32), axis, keepdims=False)


def in_line_order(pieces, narrow):
    stacked = jnp.stack(pieces)
    return [pick(stacked, narrow ^ place) for place in range(stacked.shape[0])]


def scatter_narrow(blocks, narrow, count):
    return [pick(blocks, narrow)] + [
        lax.ppermute(pick(blocks, narrow ^ step).astype(BF16), "narrow", narrow_pairs(count, step))
        for step in range(1, count)
    ]


def add_terms(terms, *others):
    terms = lax.optimization_barrier((*terms, *others))[: len(terms)]
    return sum(term.astype(F32) for term in terms)


def weight_copies(places, parts, start, target, rows, sems):
    size = parts[0].shape[0]
    copies = []
    for slot in range(len(parts) * size):
        place = pl.multiple_of(places[slot] * rows, 8)
        for matrix in range(target.shape[0]):
            copies.append(
                pltpu.make_async_copy(
                    parts[slot // size].at[slot % size, pl.ds(start + matrix * rows, rows), :],
                    target.at[matrix, pl.ds(place, rows), :],
                    sems.at[slot, matrix],
                )
            )
    return copies


def block_copies(places, value, start, rows, parts, sems):
    size = parts[0].shape[0]
    copies = []
    for slot in range(len(parts) * size):
        place = pl.multiple_of(places[slot] * rows, 8)
        copies.append(
            pltpu.make_async_copy(
                value.at[pl.ds(place, rows), :],
                parts[slot // size].at[slot % size, pl.ds(start, rows), :],
                sems.at[slot],
            )
        )
    return copies


def send_off(copies, more):
    for copy in more:
        copy.start()
    copies += more


def norm_scale(values):
    return lax.rsqrt(jnp.mean(values * values, axis=-1, keepdims=True) + EPSILON)


def norm_back(values, gain, grad):
    root = norm_scale(values)
    scaled = gain * grad
    gain_grad = jnp.sum(grad * values * root, axis=0, keepdims=True)
    inner = jnp.mean(scaled * values, axis=-1, keepdims=True)
    return root * scaled - values * (root * root * root) * inner, gain_grad


def query_segments(lengths, count):
    places = lax.broadcasted_iota(jnp.int32, (1, count), 1)
    segment = jnp.zeros((1, count), jnp.int32)
    edge = jnp.int32(0)
    for pair in range(lengths.shape[0]):
        edge = edge + lengths[pair]
        segment = segment + (places >= edge).astype(jnp.int32)
    return places, segment


def fill_self_bias(bias, lengths):
    count = bias.shape[1] // 2
    places, segment = query_segments(lengths, count)
    low = jnp.zeros((1, count), jnp.int32)
    edge = jnp.int32(0)
    for pair in range(lengths.shape[0]):
        edge = edge + lengths[pair]
        low = jnp.where(segment == pair + 1, edge, low)
    keys = lax.broadcasted_iota(jnp.int32, (bias.shape[0], count), 0)
    one = jnp.where((keys >= low) & (keys <= places), 0.0, NEGATIVE)
    bias[...] = jnp.concatenate([one, one], axis=1)


def fill_cross_bias(bias, lengths, sources):
    count = bias.shape[1] // 2
    places, segment = query_segments(lengths, count)
    low = jnp.zeros((1, count), jnp.int32)
    high = jnp.full((1, count), bias.shape[0], jnp.int32)
    edge = jnp.int32(0)
    for pair in range(lengths.shape[0]):
        low = jnp.where(segment == pair, edge, low)
        edge = edge + sources[pair]
        high = jnp.where(segment == pair, edge, high)
    low = jnp.concatenate([low, low], axis=1)
    high = jnp.concatenate([high, high], axis=1)
    keys = lax.broadcasted_iota(jnp.int32, bias.shape, 0)
    bias[...] = jnp.where((keys >= low) & (keys < high), 0.0, NEGATIVE)


def first_half(width):
    return lax.broadcasted_iota(jnp.int32, (1, width), 1) < width // 2


def apart(values, chosen):
    return jnp.concatenate([jnp.where(chosen, values, 0), jnp.where(chosen, 0, values)], axis=0)


def together(values, chosen):
    count = values.shape[0] // 2
    return jnp.where(chosen, values[:count], values[count:])


def attend(queries, keys, values, bias, outputs, totals, unroll):
    width = 2 * (queries.shape[1] // HEADS)
    chosen = first_half(width)

    def pair_of_heads(pair, carry):
        columns = pl.ds(pl.multiple_of(pair * width, width), width)
        scores = nt(keys[:, columns], apart(queries[:, columns], chosen)) + bias[...]
        highest = jnp.max(scores, axis=0, keepdims=True)
        raised = jnp.exp(scores - highest)
        summed = jnp.sum(raised, axis=0, keepdims=True)
        totals[pair] = highest + jnp.log(summed)
        weights = (raised * (1.0 / summed)).astype(BF16)
        mixed = nn(values[:, columns].T, weights).T
        outputs[:, columns] = together(mixed, chosen).astype(BF16)
        return carry

    lax.fori_loop(0, HEADS // 2, pair_of_heads, 0, unroll=unroll)


def attend_back(
    queries, keys, values, bias, totals, grads, query_low, key_low, value_low, first, last
):
    width = 2 * (queries.shape[1] // HEADS)
    chosen = first_half(width)

    for pair in range(first, last):
        columns = slice(pair * width, (pair + 1) * width)
        result = slice((pair - first) * width, (pair - first + 1) * width)
        query, grad = apart(queries[:, columns], chosen), apart(grads[:, columns], chosen)
        key = keys[:, columns]
        probs = jnp.exp(nt(key, query) + bias[...] - totals[pair])
        prob_grad = nt(values[:, columns], grad)
        value_low[:, result] = nn(probs.astype(BF16), grad).astype(BF16)
        weighted = probs * prob_grad
        centre = jnp.sum(weighted, axis=0, keepdims=True)
        score_grad = (weighted - probs * centre).astype(BF16)
        key_low[:, result] = nn(score_grad, query).astype(BF16)
        query_low[:, result] = together(nn(key.T, score_grad).T, chosen).astype(BF16)


def block_rows(weights, parts):
    return weights.shape[1] // (len(parts) * parts[0].shape[0])


def join_kernel(*refs):
    start = 0
    for ref in refs[:-1]:
        refs[-1][start : start + ref.shape[0], :] = ref[...]
        start += ref.shape[0]


def join_self_kernel(owner, lengths, gains, *refs):
    join_kernel(*refs)
    pack = refs[-1]
    shard, width = gains.shape[1], pack.shape[1]
    total = jnp.int32(0)
    for pair in range(lengths.shape[0]):
        total = total + lengths[pair]
    spot = lax.broadcasted_iota(jnp.int32, (8, shard), 0)
    high, low = (total // 16).astype(F32), (total % 16).astype(F32)
    own = jnp.concatenate([gains[...].astype(F32), jnp.zeros((8 - gains.shape[0], shard), F32)], axis=0)
    own = jnp.where(spot == 4, high, jnp.where(spot == 5, low, own)).astype(BF16)
    row = lax.broadcasted_iota(jnp.int32, (shard, width), 0)
    column = lax.broadcasted_iota(jnp.int32, (shard, width), 1)
    spread = (row + owner[0] * shard == column).astype(BF16)
    pack[pack.shape[0] - 8 :, :] = nn(own, spread).astype(BF16)


def join_rows(*members):
    if any(member.shape[0] % 8 for member in members):
        return jnp.concatenate(members, axis=0)
    rows = sum(member.shape[0] for member in members)
    return pl.pallas_call(
        join_kernel,
        in_specs=[VMEM] * len(members),
        out_specs=VMEM,
        out_shape=like((rows, members[0].shape[1]), members[0].dtype),
        cost_estimate=work(1),
        name="join_rows",
    )(*members)


def line_kernel(narrow, *refs, sizes):
    pieces, block = refs[:-1], refs[-1]
    start = 0
    for size in sizes:
        for step, piece in enumerate(pieces):
            place = pl.multiple_of(start * len(pieces) + (narrow[0] ^ step) * size, 8)
            block[pl.ds(place, size), :] = piece[start : start + size]
        start += size


def join_wide_kernel(*refs):
    block = refs[-1]
    width = block.shape[1]
    start, spot = 0, 0
    for ref in refs[:-1]:
        if ref.shape[1] == width:
            block[start : start + ref.shape[0], :] = ref[...]
            start += ref.shape[0]
    for ref in refs[:-1]:
        if ref.shape[1] != width:
            for first in range(0, ref.shape[1], LANES):
                top = start + spot // (width // LANES) * ref.shape[0]
                left = spot % (width // LANES) * LANES
                block[top : top + ref.shape[0], left : left + LANES] = ref[:, first : first + LANES]
                spot += 1
            size = ref.shape[0]
    while spot % (width // LANES):
        top = start + spot // (width // LANES) * size
        left = spot % (width // LANES) * LANES
        block[top : top + size, left : left + LANES] = jnp.zeros((size, LANES), BF16)
        spot += 1


def line_wide_kernel(narrow, *refs, sizes, wide_size):
    pieces, block, wide_block = refs[:-2], refs[-2], refs[-1]
    count, width = len(pieces), block.shape[1]
    start = 0
    for size in sizes:
        for step, piece in enumerate(pieces):
            place = pl.multiple_of(start * count + (narrow[0] ^ step) * size, 8)
            block[pl.ds(place, size), :] = piece[start : start + size]
        start += size
    matrices = wide_block.shape[0] // (count * wide_size)
    spot = 0
    for matrix in range(matrices):
        for first in range(0, wide_block.shape[1], LANES):
            top = start + spot // (width // LANES) * wide_size
            left = spot % (width // LANES) * LANES
            for step, piece in enumerate(pieces):
                place = pl.multiple_of((matrix * count + (narrow[0] ^ step)) * wide_size, 8)
                wide_block[pl.ds(place, wide_size), first : first + LANES] = piece[
                    top : top + wide_size, left : left + LANES
                ]
            spot += 1


def self_forward_kernel(
    places, lengths, inputs, *refs,
):
    parts = refs[:4]
    normed, query, key, value, attended, totals, stream, gains = refs[4:12]
    weights, gain_parts, bias, sems, gain_sems = refs[12:]
    size = parts[0].shape[0]
    rows = block_rows(weights, parts)
    gain_copies = [
        pltpu.make_async_copy(
            parts[slot // size].at[slot % size, pl.ds(4 * rows, gain_parts.shape[1]), :],
            gain_parts.at[slot],
            gain_sems.at[slot],
        )
        for slot in range(4 * size)
    ]
    copies = weight_copies(places, parts, 0, weights, rows, sems)
    for copy in gain_copies + copies:
        copy.start()
    values = inputs[...].astype(F32)
    fill_self_bias(bias, lengths)
    scaled = values * norm_scale(values)
    for copy in gain_copies:
        copy.wait()
    members = gain_parts[...].astype(F32).reshape(-1, 8, gains.shape[1])
    summed = members[0]
    for member in range(1, members.shape[0]):
        summed = summed + members[member]
    gains[...] = summed
    low = (scaled * summed[0:1]).astype(BF16)
    normed[...] = low
    for copy in copies:
        copy.wait()
    query[...] = nn(low, weights[0]).astype(BF16)
    key[...] = nn(low, weights[1]).astype(BF16)
    value[...] = nn(low, weights[2]).astype(BF16)
    attend(query, key, value, bias, attended, totals, HEADS // 2)
    stream[...] = values + nn(attended[...], weights[3])


def memory_kernel(places, memory, *refs):
    parts = refs[:4]
    key, value, weights, sems = refs[4:]
    rows = block_rows(weights, parts)
    copies = weight_copies(places, parts, rows, weights, rows, sems)
    for copy in copies:
        copy.start()
    for copy in copies:
        copy.wait()
    key[...] = nn(memory[...], weights[0]).astype(BF16)
    value[...] = nn(memory[...], weights[1]).astype(BF16)


def cross_forward_kernel(
    places, lengths, sources, stream_in, gains, key, value, *refs,
):
    parts = refs[:4]
    normed, query, attended, totals, stream, weights, bias, sems = refs[4:]
    rows = block_rows(weights, parts)
    copies = weight_copies(places, parts, 0, weights.at[pl.ds(0, 1)], rows, sems.at[0])
    copies += weight_copies(places, parts, 3 * rows, weights.at[pl.ds(1, 1)], rows, sems.at[1])
    for copy in copies:
        copy.start()
    values = stream_in[...]
    fill_cross_bias(bias, lengths, sources)
    low = (values * norm_scale(values) * gains[1:2]).astype(BF16)
    normed[...] = low
    for copy in copies:
        copy.wait()
    query[...] = nn(low, weights[0]).astype(BF16)
    attend(query, key, value, bias, attended, totals, HEADS // 4)
    stream[...] = values + nn(attended[...], weights[1])


def mlp_forward_kernel(
    places, stream_in, gains, side, *refs,
):
    parts, down_parts = refs[:4], refs[4:8]
    normed, gate, up, hidden, stream, activations, exit_normed = refs[8:15]
    weights, down, sems, down_sems = refs[15:]
    rows, down_rows = block_rows(weights, parts), block_rows(down, down_parts)
    first = weight_copies(places, parts, 0, weights, rows, sems)
    last = weight_copies(
        places, down_parts, down_parts[0].shape[1] - down_rows, down, down_rows, down_sems
    )
    for copy in first + last:
        copy.start()
    values = stream_in[...]
    low = (values * norm_scale(values) * gains[2:3]).astype(BF16)
    normed[...] = low
    for copy in first:
        copy.wait()
    width = weights.shape[2]
    step = width // 4
    for part in range(4):
        columns = pl.ds(part * step, step)
        gate_pre = nn(low, weights[0, :, columns])
        up_pre = nn(low, weights[1, :, columns])
        gate[:, columns] = gate_pre
        up[:, columns] = up_pre
        bent = jnp.tanh(MIX * (gate_pre + CUBE * (gate_pre * gate_pre * gate_pre)))
        hidden[:, columns] = (0.5 * gate_pre * (1.0 + bent) * up_pre).astype(BF16)
    for copy in last:
        copy.wait()
    out = values + nn(hidden[...], down[0])
    stream[...] = out
    activations[...] = out.astype(BF16)
    count = out.shape[0]
    exit_normed[:count] = (out * norm_scale(out) * gains[3:4]).astype(BF16)
    exit_normed[count:] = side[...]


def exit_scores_kernel(meta, slot_of, *refs, vocab, scale):
    parts = refs[:4]
    source, raised, across, stats = refs[4:8]
    table, tokens, columns, landed, scores, table_sem, sems = refs[8:]
    size = parts[0].shape[0]
    members = 4 * size
    ring = landed.shape[0]
    count = parts[0].shape[1] - 8
    step = pl.program_id(0)
    tile = raised.shape[0]
    starts, counts = META_LISTS, META_LISTS + members

    def fetch(member):
        slot = slot_of[member]
        for part in range(4):

            @pl.when(slot // size == part)
            def start():
                pltpu.make_async_copy(
                    parts[part].at[slot % size], landed.at[member % ring], sems.at[member % ring]
                ).start()

    @pl.when(step == 0)
    def load():
        whole = pltpu.make_async_copy(source, table, table_sem)
        for member in range(min(ring, members)):
            fetch(member)
        whole.start()
        tokens[...] = jnp.zeros_like(tokens)
        columns[...] = jnp.zeros_like(columns)
        lanes = -(-count // LANES) * LANES
        spots = lax.broadcasted_iota(jnp.int32, (1, lanes), 1)
        for member in range(members):
            pltpu.make_async_copy(
                parts[0].at[0], landed.at[member % ring], sems.at[member % ring]
            ).wait()
            begin = pl.multiple_of(meta[starts + member], 16)
            block = landed[member % ring]
            tokens[pl.ds(begin, count), :] = block[:count]
            side = block[count:, :lanes].astype(F32)
            wanted = side[0:1] * 256.0 + side[1:2]
            weight = jnp.where(spots < meta[counts + member], 1.0, 0.0)
            packed = jnp.concatenate(
                [weight, wanted, jnp.zeros((LANES - 2, lanes), F32)], axis=0
            )
            columns[pl.ds(begin, count), :] = packed.T[:count]
            if member + ring < members:
                fetch(member + ring)
        whole.wait()

    spot = lax.broadcasted_iota(jnp.int32, (tile, LANES), 1)

    @pl.when(step < meta[META_TILES])
    def compute():
        here = pl.ds(pl.multiple_of(step * tile, tile), tile)
        own = tokens[here, :]
        column = columns[here, :]
        across[...] = own.T
        width = scores.shape[1]
        lanes = lax.broadcasted_iota(jnp.int32, (tile, LANES), 1)
        wanted = column[:, 1:2].astype(jnp.int32) - meta[META_WIDE] * vocab
        wanted = jnp.where(wanted < vocab, wanted, -1)
        peaks = jnp.full((tile, LANES), NEGATIVE, F32)
        found = jnp.zeros((tile, LANES), F32)
        for first in range(0, width, VOCAB_TILE):
            part = nn(own, table[:, first : first + VOCAB_TILE])
            for inner in range(0, VOCAB_TILE, LANES):
                piece = part[:, inner : inner + LANES]
                offset = first + inner
                if offset + LANES > vocab:
                    piece = jnp.where(lanes < vocab - offset, piece, NEGATIVE)
                scores[:, offset : offset + LANES] = piece
                peaks = jnp.maximum(peaks, piece)
                found = found + jnp.where(lanes == wanted - offset, piece, 0.0)
        highest = jnp.max(peaks, axis=1, keepdims=True)
        sums = jnp.zeros((tile, LANES), F32)
        for offset in range(0, width, LANES):
            piece = jnp.exp2((scores[:, offset : offset + LANES] - highest) * (scale * LOG2E))
            raised[:, offset : offset + LANES] = piece.astype(BF16)
            sums = sums + piece
        summed = jnp.sum(sums, axis=1, keepdims=True)
        picked = jnp.sum(found, axis=1, keepdims=True)
        values = (highest * scale, summed, picked * scale, column[:, 0:1], column[:, 1:2])
        packed = jnp.zeros((tile, LANES), F32)
        for place, value in enumerate(values):
            packed = jnp.where(spot == place, value, packed)
        stats[...] = packed.T[:8]

    @pl.when(step >= meta[META_TILES])
    def skip():
        rows = lax.broadcasted_iota(jnp.int32, stats.shape, 0)
        stats[...] = jnp.where(rows == 1, 1.0, 0.0)


def logit_grads(meta, raised, factors, first, width, vocab):
    tile = raised.shape[0]
    columns = jnp.concatenate(
        [factors[...], jnp.zeros((LANES - factors.shape[0], tile), F32)], axis=0
    ).T
    factor, at_target = columns[:, 0:1], columns[:, 1:2]
    wanted = columns[:, 2:3].astype(jnp.int32) - meta[META_WIDE] * vocab
    wanted = jnp.where(wanted < vocab, wanted, -1) - first
    lanes = lax.broadcasted_iota(jnp.int32, (tile, width), 1)

    def chunk(start):
        part = raised[:, start : start + width].astype(F32) * factor
        return jnp.where(lanes == wanted - start, at_target, part).astype(BF16)

    return chunk


def exit_tokens_kernel(meta, places, *refs, vocab):
    source, raised, factors = refs[:3]
    parts = refs[3:7]
    table, token_grad, landed, table_sem, sems = refs[7:]
    size = parts[0].shape[0]
    members = 4 * size
    count = parts[0].shape[1]
    starts, counts = META_LISTS, META_LISTS + members
    step = pl.program_id(0)
    tile = raised.shape[0]

    @pl.when(step == 0)
    def load():
        whole = pltpu.make_async_copy(source, table, table_sem)
        whole.start()
        whole.wait()

    @pl.when(step < meta[META_TILES])
    def compute():
        chunk = logit_grads(meta, raised, factors, 0, VOCAB_TILE, vocab)
        grad = jnp.zeros((tile, token_grad.shape[1]), F32)
        for first in range(0, raised.shape[1], VOCAB_TILE):
            grad = grad + nt(chunk(first), table[:, first : first + VOCAB_TILE])
        token_grad[pl.ds(pl.multiple_of(step * tile, tile), tile), :] = grad.astype(BF16)

    @pl.when(step == pl.num_programs(0) - 1)
    def finish():
        copies = []
        spots = lax.broadcasted_iota(jnp.int32, (count, 1), 0)
        for slot in range(members):
            if slot >= 2:
                copies[slot - 2].wait()
            member = places[slot]
            begin = pl.multiple_of(meta[starts + member], 16)
            block = token_grad[pl.ds(begin, count), :].astype(F32)
            landed[slot % 2] = jnp.where(spots < meta[counts + member], block, 0.0).astype(BF16)
            copy = pltpu.make_async_copy(
                landed.at[slot % 2], parts[slot // size].at[slot % size], sems.at[slot % 2]
            )
            copy.start()
            copies.append(copy)
        for copy in copies[-2:]:
            copy.wait()


def exit_table_kernel(meta, raised, across, factors, *refs, first, vocab):
    table_grad, total = refs[-2:]
    step = pl.program_id(0)
    width = min(VOCAB_TILE, raised.shape[1])

    @pl.when(step == 0)
    def clear():
        total[...] = jnp.zeros_like(total)

    @pl.when(step < meta[META_TILES])
    def compute():
        chunk = logit_grads(meta, raised, factors, first, width, vocab)
        for start in range(0, raised.shape[1], width):
            total[:, start : start + width] += nn(across[...], chunk(start))

    @pl.when(step == pl.num_programs(0) - 1)
    def finish():
        table_grad[...] = total[...].astype(BF16)


def mlp_backward_kernel(
    places, grad_in, stream_three, stream_two, gain, normed, gate, up, hidden, *refs,
):
    parts, down_parts = refs[:4], refs[4:8]
    stream_grad, gains = refs[8:10]
    grad_parts, down_grad_parts = refs[10:14], refs[14:18]
    weights, down, gate_low, up_low, result, down_result, sems, down_sems, out_sems = refs[18:]
    rows, down_rows = block_rows(weights, parts), block_rows(down, down_parts)
    first = weight_copies(
        places, down_parts, down_parts[0].shape[1] - down_rows, down, down_rows, down_sems
    )
    last = weight_copies(places, parts, 0, weights, rows, sems)
    for copy in first + last:
        copy.start()
    stream_back, exit_gain_grad = norm_back(stream_three[...], gain[3:4], grad_in[...])
    branch = stream_back.astype(BF16)
    for copy in first:
        copy.wait()
    width = weights.shape[2]
    step = width // 4
    normed_across = normed[...].T
    sent = []
    for part in range(4):
        columns = pl.ds(part * step, step)
        gate_pre = gate[:, columns]
        up_pre = up[:, columns]
        hidden_grad = nt(branch, down[0, columns, :])
        bent = jnp.tanh(MIX * (gate_pre + CUBE * (gate_pre * gate_pre * gate_pre)))
        slope = 0.5 * (1.0 + bent) + 0.5 * gate_pre * (1.0 - bent * bent) * (
            MIX * (1.0 + 3.0 * CUBE * gate_pre * gate_pre)
        )
        gate_low[:, columns] = (hidden_grad * up_pre * slope).astype(BF16)
        up_low[:, columns] = (hidden_grad * (0.5 * gate_pre * (1.0 + bent))).astype(BF16)
        result[0, :, columns] = nn(normed_across, gate_low[:, columns]).astype(BF16)
        result[1, :, columns] = nn(normed_across, up_low[:, columns]).astype(BF16)
    for matrix in range(2):
        send_off(
            sent,
            block_copies(
                places, result.at[matrix], matrix * rows, rows, grad_parts, out_sems.at[matrix]
            ),
        )
    for part in range(4):
        columns = pl.ds(part * step, step)
        down_result[columns, :] = nn(hidden[:, columns].T, branch).astype(BF16)
    send_off(
        sent, block_copies(places, down_result, 0, down_rows, down_grad_parts, out_sems.at[2])
    )
    for copy in last:
        copy.wait()
    normed_grad = nt(gate_low[...], weights[0]) + nt(up_low[...], weights[1])
    branch_in, gain_grad = norm_back(stream_two[...], gain[2:3], normed_grad)
    stream_grad[...] = stream_back + branch_in
    gains[...] = jnp.concatenate(
        [gain_grad, exit_gain_grad, jnp.zeros((6, gain_grad.shape[1]), F32)], axis=0
    )
    for copy in sent:
        copy.wait()


def cross_attention_first_kernel(
    places, lengths, sources, grad_in, query, key, value, totals, *refs,
):
    parts = refs[:4]
    branch, attended_grad, query_low, key_low, value_low, weights, bias, sems = refs[4:]
    rows = block_rows(weights, parts)
    copies = weight_copies(places, parts, 3 * rows, weights, rows, sems)
    for copy in copies:
        copy.start()
    fill_cross_bias(bias, lengths, sources)
    branch[...] = grad_in[...].astype(BF16)
    for copy in copies:
        copy.wait()
    attended_grad[...] = nt(branch[...], weights[0]).astype(BF16)
    attend_back(
        query, key, value, bias, totals, attended_grad, query_low, key_low, value_low,
        0, HEADS // 4,
    )


def cross_attention_last_kernel(
    lengths, sources, attended_grad, query, key, value, totals,
    first_query, first_key, first_value, query_low, key_low, value_low, bias,
):
    middle = first_query.shape[1]
    fill_cross_bias(bias, lengths, sources)
    attend_back(
        query, key, value, bias, totals, attended_grad,
        query_low.at[:, middle:], key_low.at[:, middle:], value_low.at[:, middle:],
        HEADS // 4, HEADS // 2,
    )
    query_low[:, :middle] = first_query[...]
    key_low[:, :middle] = first_key[...]
    value_low[:, :middle] = first_value[...]


def cross_backward_kernel(
    places, grad_in, stream_in, gain, normed, memory, attended, self_attended,
    branch, query_low, key_low, value_low, *refs,
):
    parts = refs[:4]
    stream_grad, gains, memory_grad, self_branch = refs[4:8]
    grad_parts = refs[8:12]
    weights, results, sems, out_sems = refs[12:]
    rows = block_rows(weights, parts)
    copies = weight_copies(places, parts, 0, weights, rows, sems)
    for copy in copies:
        copy.start()
    sent = []

    def weight_grad(matrix, left_across, right):
        results[matrix] = nn(left_across, right[...]).astype(BF16)
        send_off(
            sent,
            block_copies(
                places, results.at[matrix], matrix * rows, rows, grad_parts, out_sems.at[matrix]
            ),
        )

    memory_across = memory[...].T
    weight_grad(1, memory_across, key_low)
    weight_grad(2, memory_across, value_low)
    weight_grad(0, normed[...].T, query_low)
    weight_grad(3, attended[...].T, branch)
    for copy in copies:
        copy.wait()
    normed_grad = nt(query_low[...], weights[0])
    branch_in, gain_grad = norm_back(stream_in[...], gain[1:2], normed_grad)
    total = grad_in[...] + branch_in
    stream_grad[...] = total
    self_branch[...] = total.astype(BF16)
    weight_grad(4, self_attended[...].T, self_branch)
    gains[...] = jnp.broadcast_to(gain_grad, gains.shape)
    memory_grad[...] = nt(key_low[...], weights[1]) + nt(value_low[...], weights[2])
    for copy in sent:
        copy.wait()


def self_attention_backward_kernel(
    places, lengths, branch, query, key, value, totals, *refs,
):
    parts = refs[:4]
    query_low, key_low, value_low, weights, bias, attended_grad, sems = refs[4:]
    rows = block_rows(weights, parts)
    copies = weight_copies(places, parts, 3 * rows, weights, rows, sems)
    for copy in copies:
        copy.start()
    fill_self_bias(bias, lengths)
    for copy in copies:
        copy.wait()
    attended_grad[...] = nt(branch[...], weights[0]).astype(BF16)
    attend_back(
        query, key, value, bias, totals, attended_grad, query_low, key_low, value_low,
        0, HEADS // 2,
    )


def self_backward_kernel(
    places, grad_in, inputs, gain, normed, cross_gains, mlp_gains,
    query_low, key_low, value_low, *refs,
):
    parts = refs[:4]
    stream_grad = refs[4]
    grad_parts = refs[5:9]
    weights, results, terms, sems, out_sems, term_sems = refs[9:]
    rows = block_rows(weights, parts)
    size = grad_parts[0].shape[0]
    copies = weight_copies(places, parts, 0, weights, rows, sems)
    for copy in copies:
        copy.start()
    sent = []
    normed_across = normed[...].T
    for matrix, low in enumerate((query_low, key_low, value_low)):
        results[matrix] = nn(normed_across, low[...]).astype(BF16)
        send_off(
            sent,
            block_copies(
                places, results.at[matrix], matrix * rows, rows, grad_parts, out_sems.at[matrix]
            ),
        )
    for copy in copies:
        copy.wait()
    normed_grad = (
        nt(query_low[...], weights[0])
        + nt(key_low[...], weights[1])
        + nt(value_low[...], weights[2])
    )
    branch_in, gain_grad = norm_back(inputs[...].astype(F32), gain[0:1], normed_grad)
    stream_grad[...] = grad_in[...] + branch_in
    spot = lax.broadcasted_iota(jnp.int32, (8, gain_grad.shape[1]), 0)
    row = jnp.where(spot == 0, gain_grad, 0.0)
    row = jnp.where(spot == 1, cross_gains[0:1], row)
    row = jnp.where(spot == 2, mlp_gains[0:1], row)
    row = jnp.where(spot == 3, mlp_gains[1:2], row).astype(BF16)
    for start in range(0, terms.shape[0], 8):
        terms[start : start + 8] = row
    send_off(
        sent,
        [
            pltpu.make_async_copy(
                terms,
                grad_parts[slot // size].at[slot % size, pl.ds(3 * rows, terms.shape[0]), :],
                term_sems.at[slot],
            )
            for slot in range(4 * size)
        ],
    )
    for copy in sent:
        copy.wait()


def per_device(
    inputs,
    memory,
    targets,
    tgt_lengths,
    src_lengths,
    self_gain,
    self_query,
    self_key,
    self_value,
    self_out,
    cross_gain,
    cross_query,
    cross_key,
    cross_value,
    cross_out,
    mlp_gain,
    mlp_gate,
    mlp_up,
    mlp_down,
    exit_gain,
    embedding,
):
    tokens, model = inputs.shape
    slots = memory.shape[0]
    hidden_width = mlp_gate.shape[1]
    pair_slots = tgt_lengths.shape[1]
    wide_count = lax.axis_size("wide")
    narrow_count = lax.axis_size("narrow")
    wide = lax.axis_index("wide")
    narrow = lax.axis_index("narrow")
    slot_total = tokens * wide_count * narrow_count
    scale = 1.0 / math.sqrt(model)
    places = slot_places(wide, wide_count)
    lengths, sources = tgt_lengths[0], src_lengths[0]
    shard = self_query.shape[0]
    rows = shard * narrow_count
    down_rows = mlp_down.shape[0] * narrow_count

    aligned = rows % 8 == 0
    kernel_places = places if aligned else jnp.arange(4, dtype=jnp.int32)
    kernel_count = wide_count if aligned else 4
    ids = jnp.arange(wide_count, dtype=jnp.int32)
    order = places[None, :] == ids[:, None]

    def reorder(matrix, blocks):
        flat = blocks.reshape(wide_count, -1)
        return nn(matrix.astype(BF16), flat).astype(BF16).reshape(blocks.shape)

    def for_kernels(parts, sizes):
        if aligned:
            return parts
        whole, start, members = jnp.concatenate(parts, axis=0), 0, []
        for size in sizes:
            ordered = reorder(order, whole[:, start : start + size])
            members.append(ordered.reshape(4, -1, whole.shape[-1]))
            start += size
        return jnp.split(jnp.concatenate(members, axis=1), 4)

    def from_kernels(parts, sizes):
        if aligned:
            return parts
        whole, start, members = jnp.concatenate(parts, axis=0), 0, []
        for size in sizes:
            extent = size * wide_count // 4
            member = whole[:, start : start + extent].reshape(wide_count, size, -1)
            members.append(reorder(order.T, member))
            start += extent
        return jnp.split(jnp.concatenate(members, axis=1), 4)

    def line_block(pieces, sizes, *others):
        pieces = lax.optimization_barrier((*pieces, *others))[: len(pieces)]
        if all(size % 8 == 0 for size in sizes):
            return pl.pallas_call(
                functools.partial(line_kernel, sizes=sizes),
                in_specs=[SMEM] + [VMEM] * len(pieces),
                out_specs=VMEM,
                out_shape=like((pieces[0].shape[0] * len(pieces), pieces[0].shape[1]), BF16),
                compiler_params=PARAMS,
                cost_estimate=work(30),
                name="line_block",
            )(narrow[None], *pieces)
        ordered, start, members = in_line_order(pieces, narrow), 0, []
        for size in sizes:
            members += [piece[start : start + size] for piece in ordered]
            start += size
        return jnp.concatenate(members, axis=0)

    self_sizes, cross_sizes = [shard] * 4 + [8], [shard] * 4 + [mlp_down.shape[0]]
    gate_sizes = [shard] * 2
    count = jnp.sum(lengths)
    owner = wide * narrow_count + narrow
    gain_shards = jnp.stack([self_gain, cross_gain, mlp_gain, exit_gain])
    def join_self():
        return pl.pallas_call(
            join_self_kernel,
            in_specs=[SMEM] * 2 + [VMEM] * 5,
            out_specs=VMEM,
            out_shape=like((sum(self_sizes), model), BF16),
            cost_estimate=work(1),
            name="join_self",
        )(owner[None], lengths, gain_shards, self_query, self_key, self_value, self_out)

    numbers = jnp.broadcast_to(
        jnp.stack([count // 16, count % 16])[:, None], (2, shard)
    ).astype(BF16)
    own_rows = jnp.concatenate([gain_shards, numbers, jnp.zeros((2, shard), BF16)], axis=0)
    own_rows = jnp.tile(own_rows, (1, model // shard))
    own_columns = jnp.arange(model, dtype=jnp.int32)[None, :] // shard == owner
    own_rows = jnp.where(own_columns, own_rows, 0)
    self_pack = (
        join_self()
        if aligned
        else join_rows(self_query, self_key, self_value, self_out, own_rows)
    )
    members = (cross_query, cross_key, cross_value, cross_out, mlp_down)
    if aligned:
        wide_rows = -(-2 * hidden_width // model) * shard
        joined_pack = pl.pallas_call(
            join_wide_kernel,
            in_specs=[VMEM] * 7,
            out_specs=VMEM,
            out_shape=like((sum(cross_sizes) + wide_rows, model), BF16),
            compiler_params=PARAMS,
            cost_estimate=work(1),
            name="join_wide",
        )(*members, mlp_gate, mlp_up)
    side = jnp.stack([targets // 256, targets % 256]).astype(BF16)
    side = jnp.pad(side, ((0, 6), (0, model - tokens)))

    self_line = gather_narrow(self_pack, narrow_count)
    self_block = line_block(self_line, self_sizes)

    vocab = embedding.shape[0]
    padded = -(-vocab // VOCAB_TILE) * VOCAB_TILE
    turned = jnp.pad(embedding.T, ((0, 0), (0, padded - vocab)))
    table = lax.all_gather(tie(turned, *self_line), "narrow", axis=0, tiled=True)

    *early, last = stage_pairs(wide_count)

    def gather_early(block):
        held = block[None]
        for pairs in early:
            held = jnp.concatenate([held, lax.ppermute(held, "wide", pairs)], axis=0)
        return held

    if aligned:
        joined_line = gather_narrow(tie(joined_pack, *self_line), narrow_count)
    else:
        cross_line = gather_narrow(join_rows(*members), narrow_count)
        gate_line = gather_narrow(join_rows(mlp_gate, mlp_up), narrow_count)
    self_held = gather_early(self_block)
    if aligned:
        self_held = tie(self_held, joined_line[1])
    self_came = lax.ppermute(self_held, "wide", last)
    if aligned:
        joined_line = lax.optimization_barrier((*joined_line, self_held))[:narrow_count]
        cross_block, gate_block = pl.pallas_call(
            functools.partial(line_wide_kernel, sizes=cross_sizes, wide_size=shard),
            in_specs=[SMEM] + [VMEM] * narrow_count,
            out_specs=[VMEM] * 2,
            out_shape=[
                like((sum(cross_sizes) * narrow_count, model), BF16),
                like((2 * rows, hidden_width), BF16),
            ],
            compiler_params=PARAMS,
            cost_estimate=work(1),
            name="line_wide",
        )(narrow[None], *joined_line)
    else:
        cross_block = line_block(cross_line, cross_sizes)
        gate_block = line_block(gate_line, gate_sizes)
    self_parts = (
        self_held, self_came, cross_core(self_held, wide_count), cross_core(self_came, wide_count)
    )
    cross_held = gather_early(tie(cross_block, self_came))
    cross_came = lax.ppermute(cross_held, "wide", last)

    head_rows = like((HEADS // 2, 1, 2 * tokens), F32)
    activation = like((tokens, model), BF16)
    stream_like = like((tokens, model), F32)
    matrix_sems = pltpu.SemaphoreType.DMA((kernel_count, 4))
    one_matrix_sems = pltpu.SemaphoreType.DMA((kernel_count, 1))

    self_gathered = for_kernels(self_parts, [size * narrow_count for size in self_sizes])
    (
        normed_one, query_one, key_one, value_one, attended_one, totals_one, stream_one, gain_all,
    ) = pl.pallas_call(
        self_forward_kernel,
        in_specs=[SMEM, SMEM, VMEM] + [ANY] * 4,
        out_specs=[VMEM] * 8,
        out_shape=[activation] * 5 + [head_rows, stream_like, like((8, model), F32)],
        scratch_shapes=[
            pltpu.VMEM((4, model, model), BF16),
            pltpu.VMEM((kernel_count, 8 * narrow_count * wide_count // kernel_count, model), BF16),
            pltpu.VMEM((tokens, 2 * tokens), F32),
            matrix_sems,
            pltpu.SemaphoreType.DMA((kernel_count,)),
        ],
        compiler_params=PARAMS,
        cost_estimate=work(1),
        name="self_forward",
    )(kernel_places, lengths, tie(inputs, cross_held), *self_gathered)

    numbers = (gain_all[4] * 16.0 + gain_all[5]).reshape(wide_count, narrow_count, shard)[:, :, 0]
    numbers = jnp.sum(
        jnp.where(jnp.arange(narrow_count)[None, :] == narrow, numbers, 0.0), axis=1
    ).astype(jnp.int32)
    extents = (numbers + 15) // 16 * 16
    starts = jnp.sum(jnp.where(ids[None, :] < ids[:, None], extents[None, :], 0), axis=1)
    needed = (jnp.sum(extents) + GRAD_TILE - 1) // GRAD_TILE * (1)
    meta = jnp.concatenate([jnp.stack([wide, needed]), starts, numbers])
    slot_of = jnp.sum(jnp.where(order, ids[None, :], 0), axis=1)

    cross_came = tie(cross_came, stream_one)
    cross_parts = (
        cross_held, cross_came, cross_core(cross_held, wide_count), cross_core(cross_came, wide_count)
    )
    gate_held = gather_early(tie(gate_block, cross_came))
    gate_came = lax.ppermute(gate_held, "wide", last)
    cross_gathered = for_kernels(cross_parts, [size * narrow_count for size in cross_sizes])

    key_two, value_two = pl.pallas_call(
        memory_kernel,
        in_specs=[SMEM, VMEM] + [ANY] * 4,
        out_specs=[VMEM] * 2,
        out_shape=[like((slots, model), BF16)] * 2,
        scratch_shapes=[
            pltpu.VMEM((2, model, model), BF16),
            pltpu.SemaphoreType.DMA((kernel_count, 2)),
        ],
        compiler_params=PARAMS,
        cost_estimate=work(1),
        name="memory_projection",
    )(kernel_places, memory, *cross_gathered)

    normed_two, query_two, attended_two, totals_two, stream_two = pl.pallas_call(
        cross_forward_kernel,
        in_specs=[SMEM, SMEM, SMEM, VMEM, VMEM, VMEM, VMEM] + [ANY] * 4,
        out_specs=[VMEM] * 5,
        out_shape=[activation] * 3 + [head_rows, stream_like],
        scratch_shapes=[
            pltpu.VMEM((2, model, model), BF16),
            pltpu.VMEM((slots, 2 * tokens), F32),
            pltpu.SemaphoreType.DMA((2, kernel_count, 1)),
        ],
        compiler_params=PARAMS,
        cost_estimate=work(1),
        name="cross_forward",
    )(
        kernel_places, lengths, sources, tie(stream_one, gate_held), gain_all, key_two, value_two,
        *cross_gathered,
    )

    gate_came = tie(gate_came, stream_two)
    gate_parts = (
        gate_held, gate_came, cross_core(gate_held, wide_count), cross_core(gate_came, wide_count)
    )
    gate_gathered = for_kernels(gate_parts, [size * narrow_count for size in gate_sizes])

    wide_f32 = like((tokens, hidden_width), F32)
    wide_low = like((tokens, hidden_width), BF16)
    normed_three, gate_pre, up_pre, hidden, stream_three, activations, normed_four = pl.pallas_call(
        mlp_forward_kernel,
        in_specs=[SMEM, VMEM, VMEM, VMEM] + [ANY] * 8,
        out_specs=[VMEM] * 7,
        out_shape=[
            activation, wide_f32, wide_f32, wide_low, stream_like, activation,
            like((tokens + 8, model), BF16),
        ],
        scratch_shapes=[
            pltpu.VMEM((2, model, hidden_width), BF16),
            pltpu.VMEM((1, hidden_width, model), BF16),
            pltpu.SemaphoreType.DMA((kernel_count, 2)),
            one_matrix_sems,
        ],
        compiler_params=PARAMS,
        cost_estimate=work(1),
        name="mlp_forward",
    )(kernel_places, stream_two, gain_all, side, *gate_gathered, *cross_gathered)

    exit_parts = gather_wide(normed_four, wide_count)
    group = tokens * wide_count
    tiles = -(-group // GRAD_TILE) * (1)
    kept = lambda i, meta: jnp.minimum(i, meta[META_TILES] - 1)
    kept_grad = lambda i, meta: jnp.minimum(i, meta[META_TILES] * 1 - 1)

    raised, tokens_across, stats = pl.pallas_call(
        functools.partial(exit_scores_kernel, vocab=vocab, scale=scale),
        grid_spec=pltpu.PrefetchScalarGridSpec(
            num_scalar_prefetch=2,
            grid=(tiles,),
            in_specs=[ANY] * 5,
            out_specs=[
                pl.BlockSpec((ROW_TILE, padded), lambda i, meta, slots: (kept(i, meta), 0)),
                pl.BlockSpec((model, ROW_TILE), lambda i, meta, slots: (0, kept(i, meta))),
                pl.BlockSpec((8, ROW_TILE), lambda i, meta, slots: (0, i)),
            ],
            scratch_shapes=[
                pltpu.VMEM((model, padded), BF16),
                pltpu.VMEM((tiles * ROW_TILE, model), BF16),
                pltpu.VMEM((tiles * ROW_TILE, LANES), F32),
                pltpu.VMEM((min(wide_count, 8), tokens + 8, model), BF16),
                pltpu.VMEM((ROW_TILE, padded), F32),
                pltpu.SemaphoreType.DMA,
                pltpu.SemaphoreType.DMA((min(wide_count, 8),)),
            ],
        ),
        out_shape=[
            like((tiles * ROW_TILE, padded), BF16),
            like((model, tiles * ROW_TILE), BF16),
            like((8, tiles * ROW_TILE), F32),
        ],
        compiler_params=PARAMS,
        cost_estimate=work(52),
        name="exit_scores",
    )(meta, slot_of, *exit_parts, table)

    own_peak = stats[0]
    joint = stats
    for pairs in stage_pairs(wide_count) + [flip_pairs(wide_count)]:
        came = lax.ppermute(joint, "wide", pairs)
        peak = jnp.maximum(joint[0], came[0])
        summed = joint[1] * jnp.exp(joint[0] - peak) + came[1] * jnp.exp(came[0] - peak)
        joint = jnp.concatenate([peak[None], summed[None], joint[2:3] + came[2:3], stats[3:]], axis=0)
    log_total = joint[0] + jnp.log(joint[1])
    picked, group_weight = joint[2], stats[3]
    loss_part = jnp.full((8, LANES), jnp.sum(group_weight * (log_total - picked)), F32)

    factor = jnp.exp(own_peak - log_total) * (group_weight * scale)
    at_target = (jnp.exp(picked - log_total) - 1.0) * (group_weight * scale)
    factors = jnp.concatenate([factor[None], at_target[None], stats[4:5], stats[3:]], axis=0)
    token_part = like((wide_count // 4, tokens, model), BF16)
    exit_grads = pl.pallas_call(
        functools.partial(exit_tokens_kernel, vocab=vocab),
        grid_spec=pltpu.PrefetchScalarGridSpec(
            num_scalar_prefetch=2,
            grid=(tiles,),
            in_specs=[
                ANY,
                pl.BlockSpec((ROW_TILE, padded), lambda i, meta, slots: (kept(i, meta), 0)),
                pl.BlockSpec((8, ROW_TILE), lambda i, meta, slots: (0, i)),
            ],
            out_specs=[ANY] * 4,
            scratch_shapes=[
                pltpu.VMEM((model, padded), BF16),
                pltpu.VMEM((tiles * ROW_TILE, model), BF16),
                pltpu.VMEM((2, tokens, model), BF16),
                pltpu.SemaphoreType.DMA,
                pltpu.SemaphoreType.DMA((2,)),
            ],
        ),
        out_shape=[token_part] * 4,
        compiler_params=PARAMS,
        cost_estimate=work(50),
        name="exit_tokens",
    )(meta, places, table, raised, factors)

    half = padded // 2

    def table_half(side, factors, *before):
        return pl.pallas_call(
            functools.partial(exit_table_kernel, first=side * half, vocab=vocab),
            grid_spec=pltpu.PrefetchScalarGridSpec(
                num_scalar_prefetch=1,
                grid=(tiles,),
                in_specs=[
                    pl.BlockSpec((ROW_TILE, half), lambda i, meta: (kept(i, meta), side)),
                    pl.BlockSpec((model, ROW_TILE), lambda i, meta: (0, kept(i, meta))),
                    pl.BlockSpec((8, ROW_TILE), lambda i, meta: (0, i)),
                ]
                + [ANY] * len(before),
                out_specs=pl.BlockSpec((model, half), lambda i, meta: (0, side)),
                scratch_shapes=[pltpu.VMEM((model, half), F32)],
            ),
            out_shape=like((model, padded), BF16),
            input_output_aliases={4: 0} if before else {},
            compiler_params=PARAMS,
            cost_estimate=work(30),
            name="exit_table",
        )(meta, raised, tokens_across, factors, *before)

    exit_scatter = scatter_core(exit_grads, wide_count)
    half_grad = table_half(0, tie(factors, *exit_grads))
    (own, came), exit_kept = exit_scatter
    exit_far = scatter_far((own, tie(came, half_grad)), exit_kept, wide_count)
    table_grad = table_half(1, tie(factors, exit_far[0]), half_grad)
    table_sum = lax.psum_scatter(table_grad, "narrow", scatter_dimension=0, tiled=True)
    embedding_grad = table_sum.astype(F32).T[:vocab]
    exit_near = scatter_near(tie(exit_far[1], table_grad), exit_far[2], wide_count)
    exit_grad = exit_near[2] + exit_near[1].astype(F32)

    gain_like = like((8, model), F32)
    stream_two_grad, mlp_gains, *mlp_grads = pl.pallas_call(
        mlp_backward_kernel,
        in_specs=[SMEM] + [VMEM] * 8 + [ANY] * 8,
        out_specs=[VMEM] * 2 + [ANY] * 8,
        out_shape=[stream_like, gain_like]
        + [like(part.shape, BF16) for part in gate_gathered]
        + [
            like((part.shape[0], hidden_width // kernel_count, model), BF16)
            for part in cross_gathered
        ],
        scratch_shapes=[
            pltpu.VMEM((2, model, hidden_width), BF16),
            pltpu.VMEM((1, hidden_width, model), BF16),
            pltpu.VMEM((tokens, hidden_width), BF16),
            pltpu.VMEM((tokens, hidden_width), BF16),
            pltpu.VMEM((2, model, hidden_width), BF16),
            pltpu.VMEM((hidden_width, model), BF16),
            pltpu.SemaphoreType.DMA((kernel_count, 2)),
            one_matrix_sems,
            pltpu.SemaphoreType.DMA((3, kernel_count)),
        ],
        compiler_params=PARAMS,
        cost_estimate=work(40),
        name="mlp_backward",
    )(
        kernel_places, exit_grad, stream_three, stream_two, gain_all, normed_three,
        gate_pre, up_pre, hidden, *gate_gathered, *cross_gathered,
    )
    gate_scatter = scatter_core(from_kernels(mlp_grads[:4], [rows, rows]), wide_count)
    down_scatter = scatter_core(from_kernels(mlp_grads[4:], [down_rows]), wide_count)

    def go_far(scatter, *others):
        (own, came), kept = scatter
        return scatter_far((own, tie(came, *others)), kept, wide_count)

    def go_near(state, *others):
        _, came, kept = state
        return scatter_near(tie(came, *others), kept, wide_count)

    low_like = like((slots, model), BF16)
    middle = 2 * (HEADS // 4) * (model // HEADS)
    low_half = like((slots, middle), BF16)
    branch_two, attended_grad, *first_lows = pl.pallas_call(
        cross_attention_first_kernel,
        in_specs=[SMEM] * 3 + [VMEM] * 5 + [ANY] * 4,
        out_specs=[VMEM] * 5,
        out_shape=[activation, activation, like((tokens, middle), BF16), low_half, low_half],
        scratch_shapes=[
            pltpu.VMEM((1, model, model), BF16),
            pltpu.VMEM((slots, 2 * tokens), F32),
            one_matrix_sems,
        ],
        compiler_params=PARAMS,
        cost_estimate=work(20),
        name="cross_attention_first",
    )(
        kernel_places, lengths, sources, stream_two_grad, query_two, key_two, value_two, totals_two,
        *cross_gathered,
    )
    gate_far = go_far(gate_scatter, first_lows[0])
    down_far = go_far(down_scatter, first_lows[0])
    query_two_low, key_two_low, value_two_low = pl.pallas_call(
        cross_attention_last_kernel,
        in_specs=[SMEM] * 2 + [VMEM] * 8,
        out_specs=[VMEM] * 3,
        out_shape=[activation, low_like, low_like],
        scratch_shapes=[pltpu.VMEM((slots, 2 * tokens), F32)],
        compiler_params=PARAMS,
        cost_estimate=work(20),
        name="cross_attention_last",
    )(
        lengths, sources, tie(attended_grad, gate_far[0], down_far[0]), query_two, key_two,
        value_two, totals_two, *first_lows,
    )

    cross_matrices = like((cross_gathered[0].shape[0], 5 * model // kernel_count, model), BF16)
    stream_one_grad, cross_gains, memory_grad, branch_one, *cross_grads = pl.pallas_call(
        cross_backward_kernel,
        in_specs=[SMEM] + [VMEM] * 11 + [ANY] * 4,
        out_specs=[VMEM] * 4 + [ANY] * 4,
        out_shape=[stream_like, gain_like, like((slots, model), F32), activation]
        + [cross_matrices] * 4,
        scratch_shapes=[
            pltpu.VMEM((3, model, model), BF16),
            pltpu.VMEM((5, model, model), BF16),
            pltpu.SemaphoreType.DMA((kernel_count, 3)),
            pltpu.SemaphoreType.DMA((5, kernel_count)),
        ],
        compiler_params=PARAMS,
        cost_estimate=work(34),
        name="cross_backward",
    )(
        kernel_places, stream_two_grad, stream_one, gain_all,
        normed_two, memory, attended_two, attended_one, branch_two,
        query_two_low, key_two_low, value_two_low, *cross_gathered,
    )
    cross_scatter = scatter_core(from_kernels(cross_grads, [rows] * 5), wide_count)

    gate_near = go_near(gate_far, branch_one)
    down_near = go_near(down_far, branch_one)
    query_one_low, key_one_low, value_one_low = pl.pallas_call(
        self_attention_backward_kernel,
        in_specs=[SMEM] * 2 + [VMEM] * 5 + [ANY] * 4,
        out_specs=[VMEM] * 3,
        out_shape=[activation] * 3,
        scratch_shapes=[
            pltpu.VMEM((1, model, model), BF16),
            pltpu.VMEM((tokens, 2 * tokens), F32),
            pltpu.VMEM((tokens, model), BF16),
            one_matrix_sems,
        ],
        compiler_params=PARAMS,
        cost_estimate=work(18),
        name="self_attention_backward",
    )(
        kernel_places, lengths, tie(branch_one, gate_near[0], down_near[0]), query_one, key_one, value_one, totals_one,
        *self_gathered,
    )
    def line_blocks(near, matrices, *others):
        _, came, held = near
        summed = held + tie(came, *others).astype(F32)
        width = summed.shape[-1]
        size = matrices * (summed.shape[0] // (matrices * 8 * narrow_count)) * 8 * narrow_count
        members = [
            summed[:size].reshape(matrices, narrow_count, -1, width).transpose(1, 0, 2, 3)
            .reshape(narrow_count, -1, width)
        ]
        if size < summed.shape[0]:
            members.append(summed[size:].reshape(narrow_count, -1, width))
        return jnp.concatenate(members, axis=1)

    def line_first(near, matrices, *others):
        blocks = line_blocks(near, matrices, *others)
        steps = range(0, narrow_count, 2)
        sent = jnp.stack([pick(blocks, narrow ^ (step + 1)) for step in steps]).astype(BF16)
        came = lax.ppermute(sent, "narrow", narrow_pairs(narrow_count, 1))
        return sent, came, [pick(blocks, narrow ^ step) for step in steps]

    def line_second(state, *others):
        _, came, kept = state
        came = tie(came, *others).astype(F32)
        terms = [kept[0] + came[0]]
        for place in range(1, len(kept)):
            sent = (kept[place] + came[place]).astype(BF16)
            terms.append(lax.ppermute(sent, "narrow", narrow_pairs(narrow_count, 2 * place)))
        return terms

    cross_far = go_far(cross_scatter, query_one_low)
    gate_line = line_first(gate_near, 2, query_one_low)

    extra = narrow_count * 8
    spare = extra * wide_count // kernel_count
    inputs_grad, *self_grads = pl.pallas_call(
        self_backward_kernel,
        in_specs=[SMEM] + [VMEM] * 9 + [ANY] * 4,
        out_specs=[VMEM] + [ANY] * 4,
        out_shape=[stream_like]
        + [like((part.shape[0], 3 * model // kernel_count + spare, model), BF16) for part in self_gathered],
        scratch_shapes=[
            pltpu.VMEM((3, model, model), BF16),
            pltpu.VMEM((3, model, model), BF16),
            pltpu.VMEM((spare, model), BF16),
            pltpu.SemaphoreType.DMA((kernel_count, 3)),
            pltpu.SemaphoreType.DMA((3, kernel_count)),
            pltpu.SemaphoreType.DMA((kernel_count,)),
        ],
        compiler_params=PARAMS,
        cost_estimate=work(20),
        name="self_backward",
    )(
        kernel_places, tie(stream_one_grad, gate_line[0], cross_far[0]), inputs,
        gain_all, normed_one, cross_gains, mlp_gains, query_one_low, key_one_low, value_one_low,
        *self_gathered,
    )
    self_scatter = scatter_core(from_kernels(self_grads, [rows] * 3 + [extra]), wide_count)

    cross_near = go_near(cross_far, inputs_grad)
    self_far = go_far(self_scatter, cross_near[0])
    down_line = line_first(down_near, 1, self_far[0])
    self_near = go_near(self_far, down_line[0], embedding_grad)
    gate_terms = line_second(gate_line, self_near[0])
    down_terms = line_second(down_line, self_near[0])
    cross_line = line_first(cross_near, 5, self_near[0])
    self_terms = scatter_narrow(line_blocks(self_near, 3), narrow, narrow_count)
    cross_terms = line_second(cross_line, self_terms[0])
    gate_sum = add_terms(gate_terms, self_terms[0]).reshape(2, shard, hidden_width)
    down_sum = add_terms(down_terms, self_terms[0])
    cross_sum = add_terms(cross_terms).reshape(5, shard, model)
    self_sum = add_terms(self_terms)
    gains = pick(self_sum[3 * shard :].reshape(8, model // shard, shard), owner, 1)
    self_sum = self_sum[: 3 * shard].reshape(3, shard, model)

    loss_part = tie(loss_part, self_near[0])
    loss_all = loss_part
    for step in range(1, narrow_count):
        loss_all = loss_all + lax.ppermute(loss_part, "narrow", narrow_pairs(narrow_count, step))
    mean_loss = loss_all[0, 0] / slot_total

    return (
        activations,
        mean_loss,
        inputs_grad,
        memory_grad,
        gains[0],
        self_sum[0],
        self_sum[1],
        self_sum[2],
        cross_sum[4],
        gains[1],
        cross_sum[0],
        cross_sum[1],
        cross_sum[2],
        cross_sum[3],
        gains[2],
        gate_sum[0],
        gate_sum[1],
        down_sum,
        gains[3],
        embedding_grad,
    )


def solution(mesh):
    both = ("wide", "narrow")
    rows, flat = P(both, None), P(both)
    placed = (
        rows, rows, flat, rows, rows,
        flat, rows, rows, rows, rows,
        flat, rows, rows, rows, rows,
        flat, rows, rows, rows, flat,
        P("wide", "narrow"),
    )
    given = (
        rows, P(), rows, rows,
        flat, rows, rows, rows, rows,
        flat, rows, rows, rows, rows,
        flat, rows, rows, rows, flat,
        P("wide", "narrow"),
    )
    return jax.shard_map(
        per_device, mesh=mesh, in_specs=placed, out_specs=given, check_vma=False
    )
```

```python
import functools
import math

import jax
import jax.numpy as jnp
from jax import lax
from jax.experimental import pallas as pl
from jax.experimental.pallas import tpu as pltpu
from jax.sharding import PartitionSpec as P

HEADS = 12
EPSILON = 1e-06
NEGATIVE = -1e30
F32 = jnp.float32
BF16 = jnp.bfloat16
LANES = 128
ROW_TILE = 256
VOCAB_TILE = 512
MIX = math.sqrt(2.0 / math.pi)
CUBE = 0.044715
LOG2E = math.log2(math.e)
META_WIDE, META_TILES, META_LISTS = 0, 1, 2

VMEM = pl.BlockSpec(memory_space=pltpu.VMEM)
SMEM = pl.BlockSpec(memory_space=pltpu.SMEM)
ANY = pl.BlockSpec(memory_space=pl.ANY)
PARAMS = pltpu.CompilerParams(vmem_limit_bytes=60 * 2**20)


def work(gigaflops):
    return pl.CostEstimate(flops=gigaflops * 10**9, bytes_accessed=10**6, transcendentals=0)


def nn(left, right):
    return lax.dot_general(left, right, (((1,), (0,)), ((), ())), preferred_element_type=F32)


def nt(left, right):
    return lax.dot_general(left, right, (((1,), (1,)), ((), ())), preferred_element_type=F32)


def tn(left, right):
    return lax.dot_general(left, right, (((0,), (0,)), ((), ())), preferred_element_type=F32)


def like(shape, kind):
    return jax.ShapeDtypeStruct(shape, kind)


def stage_masks(count):
    up = [1 << bit for bit in range(1, count.bit_length() - 1)]
    return up, up[::-1]


def stage_pairs(count):
    even, odd = stage_masks(count)
    return [[(v, v ^ (odd if v % 2 else even)[i]) for v in range(count)] for i in range(len(even))]


def flip_pairs(count):
    return [(v, v ^ 1) for v in range(count)]


def slot_tables(count):
    tables = []
    for masks in stage_masks(count):
        slots = [0]
        for mask in masks:
            slots = slots + [slot ^ mask for slot in slots]
        tables.append(slots)
    even, odd = tables
    return (
        even + [1 ^ slot for slot in odd],
        odd + [1 ^ slot for slot in even],
    )


def slot_places(wide, count):
    even, odd = slot_tables(count)
    table = jnp.where(wide % 2 == 0, jnp.array(even, jnp.int32), jnp.array(odd, jnp.int32))
    return wide ^ table


def tie(value, *others):
    return lax.optimization_barrier((value, *others))[0]


def cross_core(value, count):
    return lax.ppermute(value, "wide", flip_pairs(count))


def gather_wide(block, count):
    held = block[None]
    *early, last = stage_pairs(count)
    for pairs in early:
        held = jnp.concatenate([held, lax.ppermute(held, "wide", pairs)], axis=0)
    came = lax.ppermute(held, "wide", last)
    return held, came, cross_core(held, count), cross_core(came, count)


def scatter_core(parts, count):
    sent, kept = cross_core(parts[3], count), cross_core(parts[2], count)
    return (parts[1], sent), (parts[0], kept)


def scatter_far(sent, kept, count):
    far = sent[0] + sent[1]
    came = lax.ppermute(far, "wide", stage_pairs(count)[-1])
    return far, came, kept


def scatter_near(came, kept, count):
    *rest, last = stage_pairs(count)[-2::-1]
    terms = (*kept, came)
    if not rest:
        far = sum(term[1].astype(F32) for term in terms).astype(BF16)
        return far, lax.ppermute(far, "wide", last), sum(term[0].astype(F32) for term in terms)
    held = sum(term.astype(F32) for term in terms)
    for pairs in rest:
        half = held.shape[0] // 2
        sent = lax.ppermute(held[half:].astype(BF16), "wide", pairs)
        held = held[:half] + sent.astype(F32)
    far = held[1].astype(BF16)
    return far, lax.ppermute(far, "wide", last), held[0]


def scatter_wide(parts, count):
    far, came, kept = scatter_far(*scatter_core(parts, count), count)
    far, came, held = scatter_near(came, kept, count)
    return held + came.astype(F32)


def narrow_pairs(count, step):
    return [(v, v ^ step) for v in range(count)]


def gather_narrow(block, count):
    return [block] + [
        lax.ppermute(block, "narrow", narrow_pairs(count, step)) for step in range(1, count)
    ]


def pick(values, place, axis=0):
    return lax.dynamic_index_in_dim(values, place.astype(jnp.uint32), axis, keepdims=False)


def in_line_order(pieces, narrow):
    stacked = jnp.stack(pieces)
    return [pick(stacked, narrow ^ place) for place in range(stacked.shape[0])]


def scatter_narrow(blocks, narrow, count):
    return [pick(blocks, narrow)] + [
        lax.ppermute(pick(blocks, narrow ^ step).astype(BF16), "narrow", narrow_pairs(count, step))
        for step in range(1, count)
    ]


def add_terms(terms, *others):
    terms = lax.optimization_barrier((*terms, *others))[: len(terms)]
    return sum(term.astype(F32) for term in terms)


def weight_copies(places, parts, start, target, rows, sems):
    size = parts[0].shape[0]
    copies = []
    for slot in range(len(parts) * size):
        place = pl.multiple_of(places[slot] * rows, 8)
        for matrix in range(target.shape[0]):
            copies.append(
                pltpu.make_async_copy(
                    parts[slot // size].at[slot % size, pl.ds(start + matrix * rows, rows), :],
                    target.at[matrix, pl.ds(place, rows), :],
                    sems.at[slot, matrix],
                )
            )
    return copies


def block_copies(places, value, start, rows, parts, sems):
    size = parts[0].shape[0]
    copies = []
    for slot in range(len(parts) * size):
        place = pl.multiple_of(places[slot] * rows, 8)
        copies.append(
            pltpu.make_async_copy(
                value.at[pl.ds(place, rows), :],
                parts[slot // size].at[slot % size, pl.ds(start, rows), :],
                sems.at[slot],
            )
        )
    return copies


def send_off(copies, more):
    for copy in more:
        copy.start()
    copies += more


def norm_scale(values):
    return lax.rsqrt(jnp.mean(values * values, axis=-1, keepdims=True) + EPSILON)


def norm_back(values, gain, grad):
    root = norm_scale(values)
    scaled = gain * grad
    gain_grad = jnp.sum(grad * values * root, axis=0, keepdims=True)
    inner = jnp.mean(scaled * values, axis=-1, keepdims=True)
    return root * scaled - values * (root * root * root) * inner, gain_grad


def query_segments(lengths, count):
    places = lax.broadcasted_iota(jnp.int32, (1, count), 1)
    segment = jnp.zeros((1, count), jnp.int32)
    edge = jnp.int32(0)
    for pair in range(lengths.shape[0]):
        edge = edge + lengths[pair]
        segment = segment + (places >= edge).astype(jnp.int32)
    return places, segment


def fill_self_bias(bias, lengths):
    count = bias.shape[1] // 2
    places, segment = query_segments(lengths, count)
    low = jnp.zeros((1, count), jnp.int32)
    edge = jnp.int32(0)
    for pair in range(lengths.shape[0]):
        edge = edge + lengths[pair]
        low = jnp.where(segment == pair + 1, edge, low)
    keys = lax.broadcasted_iota(jnp.int32, (bias.shape[0], count), 0)
    one = jnp.where((keys >= low) & (keys <= places), 0.0, NEGATIVE)
    bias[...] = jnp.concatenate([one, one], axis=1)


def fill_cross_bias(bias, lengths, sources):
    count = bias.shape[1] // 2
    places, segment = query_segments(lengths, count)
    low = jnp.zeros((1, count), jnp.int32)
    high = jnp.full((1, count), bias.shape[0], jnp.int32)
    edge = jnp.int32(0)
    for pair in range(lengths.shape[0]):
        low = jnp.where(segment == pair, edge, low)
        edge = edge + sources[pair]
        high = jnp.where(segment == pair, edge, high)
    low = jnp.concatenate([low, low], axis=1)
    high = jnp.concatenate([high, high], axis=1)
    keys = lax.broadcasted_iota(jnp.int32, bias.shape, 0)
    bias[...] = jnp.where((keys >= low) & (keys < high), 0.0, NEGATIVE)


def first_half(width):
    return lax.broadcasted_iota(jnp.int32, (1, width), 1) < width // 2


def apart(values, chosen):
    return jnp.concatenate([jnp.where(chosen, values, 0), jnp.where(chosen, 0, values)], axis=0)


def together(values, chosen):
    count = values.shape[0] // 2
    return jnp.where(chosen, values[:count], values[count:])


def attend(queries, keys, values, bias, outputs, totals, unroll):
    width = 2 * (queries.shape[1] // HEADS)
    chosen = first_half(width)

    def pair_of_heads(pair, carry):
        columns = pl.ds(pl.multiple_of(pair * width, width), width)
        scores = nt(keys[:, columns], apart(queries[:, columns], chosen)) + bias[...]
        highest = jnp.max(scores, axis=0, keepdims=True)
        raised = jnp.exp(scores - highest)
        summed = jnp.sum(raised, axis=0, keepdims=True)
        totals[pair] = highest + jnp.log(summed)
        weights = (raised * (1.0 / summed)).astype(BF16)
        mixed = nn(values[:, columns].T, weights).T
        outputs[:, columns] = together(mixed, chosen).astype(BF16)
        return carry

    lax.fori_loop(0, HEADS // 2, pair_of_heads, 0, unroll=unroll)


def attend_back(
    queries, keys, values, bias, totals, grads, query_low, key_low, value_low, first, last
):
    width = 2 * (queries.shape[1] // HEADS)
    chosen = first_half(width)

    for pair in range(first, last):
        columns = slice(pair * width, (pair + 1) * width)
        result = slice((pair - first) * width, (pair - first + 1) * width)
        query, grad = apart(queries[:, columns], chosen), apart(grads[:, columns], chosen)
        key = keys[:, columns]
        probs = jnp.exp(nt(key, query) + bias[...] - totals[pair])
        prob_grad = nt(values[:, columns], grad)
        value_low[:, result] = nn(probs.astype(BF16), grad).astype(BF16)
        weighted = probs * prob_grad
        centre = jnp.sum(weighted, axis=0, keepdims=True)
        score_grad = (weighted - probs * centre).astype(BF16)
        key_low[:, result] = nn(score_grad, query).astype(BF16)
        query_low[:, result] = together(nn(key.T, score_grad).T, chosen).astype(BF16)


def block_rows(weights, parts):
    return weights.shape[1] // (len(parts) * parts[0].shape[0])


def join_kernel(*refs):
    start = 0
    for ref in refs[:-1]:
        refs[-1][start : start + ref.shape[0], :] = ref[...]
        start += ref.shape[0]


def join_self_kernel(owner, lengths, gains, *refs):
    join_kernel(*refs)
    pack = refs[-1]
    shard, width = gains.shape[1], pack.shape[1]
    total = jnp.int32(0)
    for pair in range(lengths.shape[0]):
        total = total + lengths[pair]
    spot = lax.broadcasted_iota(jnp.int32, (8, shard), 0)
    high, low = (total // 16).astype(F32), (total % 16).astype(F32)
    own = jnp.concatenate([gains[...].astype(F32), jnp.zeros((8 - gains.shape[0], shard), F32)], axis=0)
    own = jnp.where(spot == 4, high, jnp.where(spot == 5, low, own)).astype(BF16)
    row = lax.broadcasted_iota(jnp.int32, (shard, width), 0)
    column = lax.broadcasted_iota(jnp.int32, (shard, width), 1)
    spread = (row + owner[0] * shard == column).astype(BF16)
    pack[pack.shape[0] - 8 :, :] = nn(own, spread).astype(BF16)


def join_rows(*members):
    if any(member.shape[0] % 8 for member in members):
        return jnp.concatenate(members, axis=0)
    rows = sum(member.shape[0] for member in members)
    return pl.pallas_call(
        join_kernel,
        in_specs=[VMEM] * len(members),
        out_specs=VMEM,
        out_shape=like((rows, members[0].shape[1]), members[0].dtype),
        cost_estimate=work(1),
        name="join_rows",
    )(*members)


def line_kernel(narrow, *refs, sizes):
    pieces, block = refs[:-1], refs[-1]
    start = 0
    for size in sizes:
        for step, piece in enumerate(pieces):
            place = pl.multiple_of(start * len(pieces) + (narrow[0] ^ step) * size, 8)
            block[pl.ds(place, size), :] = piece[start : start + size]
        start += size


def join_wide_kernel(*refs):
    block = refs[-1]
    width = block.shape[1]
    start, spot = 0, 0
    for ref in refs[:-1]:
        if ref.shape[1] == width:
            block[start : start + ref.shape[0], :] = ref[...]
            start += ref.shape[0]
    for ref in refs[:-1]:
        if ref.shape[1] != width:
            for first in range(0, ref.shape[1], LANES):
                top = start + spot // (width // LANES) * ref.shape[0]
                left = spot % (width // LANES) * LANES
                block[top : top + ref.shape[0], left : left + LANES] = ref[:, first : first + LANES]
                spot += 1
            size = ref.shape[0]
    while spot % (width // LANES):
        top = start + spot // (width // LANES) * size
        left = spot % (width // LANES) * LANES
        block[top : top + size, left : left + LANES] = jnp.zeros((size, LANES), BF16)
        spot += 1


def line_wide_kernel(narrow, even, odd, block, wide_block, *, sizes, wide_size):
    pieces = [(odd if step % 2 else even).at[step // 2] for step in range(2 * even.shape[0])]
    count, width = len(pieces), block.shape[1]
    start = 0
    for size in sizes:
        for step, piece in enumerate(pieces):
            place = pl.multiple_of(start * count + (narrow[0] ^ step) * size, 8)
            block[pl.ds(place, size), :] = piece[start : start + size]
        start += size
    matrices = wide_block.shape[0] // (count * wide_size)
    spot = 0
    for matrix in range(matrices):
        for first in range(0, wide_block.shape[1], LANES):
            top = start + spot // (width // LANES) * wide_size
            left = spot % (width // LANES) * LANES
            for step, piece in enumerate(pieces):
                place = pl.multiple_of((matrix * count + (narrow[0] ^ step)) * wide_size, 8)
                wide_block[pl.ds(place, wide_size), first : first + LANES] = piece[
                    top : top + wide_size, left : left + LANES
                ]
            spot += 1


def self_forward_kernel(
    places, lengths, inputs, *refs,
):
    parts = refs[:4]
    normed, query, key, value, attended, totals, stream, gains = refs[4:12]
    weights, gain_parts, bias, sems, gain_sems = refs[12:]
    size = parts[0].shape[0]
    rows = block_rows(weights, parts)
    gain_copies = [
        pltpu.make_async_copy(
            parts[slot // size].at[slot % size, pl.ds(4 * rows, gain_parts.shape[1]), :],
            gain_parts.at[slot],
            gain_sems.at[slot],
        )
        for slot in range(4 * size)
    ]
    copies = weight_copies(places, parts, 0, weights, rows, sems)
    for copy in gain_copies + copies:
        copy.start()
    values = inputs[...].astype(F32)
    fill_self_bias(bias, lengths)
    scaled = values * norm_scale(values)
    for copy in gain_copies:
        copy.wait()
    members = gain_parts[...].astype(F32).reshape(-1, 8, gains.shape[1])
    summed = members[0]
    for member in range(1, members.shape[0]):
        summed = summed + members[member]
    gains[...] = summed
    low = (scaled * summed[0:1]).astype(BF16)
    normed[...] = low
    for copy in copies:
        copy.wait()
    query[...] = nn(low, weights[0]).astype(BF16)
    key[...] = nn(low, weights[1]).astype(BF16)
    value[...] = nn(low, weights[2]).astype(BF16)
    attend(query, key, value, bias, attended, totals, HEADS // 2)
    stream[...] = values + nn(attended[...], weights[3])


def memory_kernel(places, memory, *refs):
    parts = refs[:4]
    key, value, weights, sems = refs[4:]
    rows = block_rows(weights, parts)
    copies = weight_copies(places, parts, rows, weights, rows, sems)
    for copy in copies:
        copy.start()
    for copy in copies:
        copy.wait()
    key[...] = nn(memory[...], weights[0]).astype(BF16)
    value[...] = nn(memory[...], weights[1]).astype(BF16)


def cross_forward_kernel(
    places, lengths, sources, stream_in, gains, key, value, *refs,
):
    parts = refs[:4]
    normed, query, attended, totals, stream, weights, bias, sems = refs[4:]
    rows = block_rows(weights, parts)
    copies = weight_copies(places, parts, 0, weights.at[pl.ds(0, 1)], rows, sems.at[0])
    copies += weight_copies(places, parts, 3 * rows, weights.at[pl.ds(1, 1)], rows, sems.at[1])
    for copy in copies:
        copy.start()
    values = stream_in[...]
    fill_cross_bias(bias, lengths, sources)
    low = (values * norm_scale(values) * gains[1:2]).astype(BF16)
    normed[...] = low
    for copy in copies:
        copy.wait()
    query[...] = nn(low, weights[0]).astype(BF16)
    attend(query, key, value, bias, attended, totals, HEADS // 4)
    stream[...] = values + nn(attended[...], weights[1])


def mlp_forward_kernel(
    places, stream_in, gains, side, *refs,
):
    parts, down_parts = refs[:4], refs[4:8]
    normed, gate, up, hidden, stream, activations, exit_normed = refs[8:15]
    weights, down, sems, down_sems = refs[15:]
    rows, down_rows = block_rows(weights, parts), block_rows(down, down_parts)
    first = weight_copies(places, parts, 0, weights, rows, sems)
    last = weight_copies(
        places, down_parts, down_parts[0].shape[1] - down_rows, down, down_rows, down_sems
    )
    for copy in first + last:
        copy.start()
    values = stream_in[...]
    low = (values * norm_scale(values) * gains[2:3]).astype(BF16)
    normed[...] = low
    for copy in first:
        copy.wait()
    width = weights.shape[2]
    step = width // 4
    for part in range(4):
        columns = pl.ds(part * step, step)
        gate_pre = nn(low, weights[0, :, columns])
        up_pre = nn(low, weights[1, :, columns])
        gate[:, columns] = gate_pre
        up[:, columns] = up_pre
        bent = jnp.tanh(MIX * (gate_pre + CUBE * (gate_pre * gate_pre * gate_pre)))
        hidden[:, columns] = (0.5 * gate_pre * (1.0 + bent) * up_pre).astype(BF16)
    for copy in last:
        copy.wait()
    out = values + nn(hidden[...], down[0])
    stream[...] = out
    activations[...] = out.astype(BF16)
    count = out.shape[0]
    exit_normed[:count] = (out * norm_scale(out) * gains[3:4]).astype(BF16)
    exit_normed[count:] = side[...]


def exit_scores_kernel(meta, slot_of, *refs, vocab, scale):
    parts = refs[:4]
    source, raised, across, stats = refs[4:8]
    table, tokens, columns, landed, scores, table_sem, sems = refs[8:]
    size = parts[0].shape[0]
    members = 4 * size
    ring = landed.shape[0]
    count = parts[0].shape[1] - 8
    step = pl.program_id(0)
    tile = raised.shape[0]
    starts, counts = META_LISTS, META_LISTS + members

    def fetch(member):
        slot = slot_of[member]
        for part in range(4):

            @pl.when(slot // size == part)
            def start():
                pltpu.make_async_copy(
                    parts[part].at[slot % size], landed.at[member % ring], sems.at[member % ring]
                ).start()

    @pl.when(step == 0)
    def load():
        whole = pltpu.make_async_copy(source, table, table_sem)
        for member in range(min(ring, members)):
            fetch(member)
        whole.start()
        tokens[...] = jnp.zeros_like(tokens)
        columns[...] = jnp.zeros_like(columns)
        lanes = -(-count // LANES) * LANES
        spots = lax.broadcasted_iota(jnp.int32, (1, lanes), 1)
        for member in range(members):
            pltpu.make_async_copy(
                parts[0].at[0], landed.at[member % ring], sems.at[member % ring]
            ).wait()
            begin = pl.multiple_of(meta[starts + member], 16)
            block = landed[member % ring]
            tokens[pl.ds(begin, count), :] = block[:count]
            side = block[count:, :lanes].astype(F32)
            wanted = side[0:1] * 256.0 + side[1:2]
            weight = jnp.where(spots < meta[counts + member], 1.0, 0.0)
            packed = jnp.concatenate(
                [weight, wanted, jnp.zeros((LANES - 2, lanes), F32)], axis=0
            )
            columns[pl.ds(begin, count), :] = packed.T[:count]
            if member + ring < members:
                fetch(member + ring)
        whole.wait()

    spot = lax.broadcasted_iota(jnp.int32, (tile, LANES), 1)

    @pl.when(step < meta[META_TILES])
    def compute():
        here = pl.ds(pl.multiple_of(step * tile, tile), tile)
        own = tokens[here, :]
        column = columns[here, :]
        across[...] = own.T
        width = scores.shape[1]
        lanes = lax.broadcasted_iota(jnp.int32, (tile, LANES), 1)
        wanted = column[:, 1:2].astype(jnp.int32) - meta[META_WIDE] * vocab
        wanted = jnp.where(wanted < vocab, wanted, -1)
        peaks = jnp.full((tile, LANES), NEGATIVE, F32)
        found = jnp.zeros((tile, LANES), F32)
        for first in range(0, width, VOCAB_TILE):
            part = nn(own, table[:, first : first + VOCAB_TILE])
            for inner in range(0, VOCAB_TILE, LANES):
                piece = part[:, inner : inner + LANES]
                offset = first + inner
                if offset + LANES > vocab:
                    piece = jnp.where(lanes < vocab - offset, piece, NEGATIVE)
                scores[:, offset : offset + LANES] = piece
                peaks = jnp.maximum(peaks, piece)
                found = found + jnp.where(lanes == wanted - offset, piece, 0.0)
        highest = jnp.max(peaks, axis=1, keepdims=True)
        sums = jnp.zeros((tile, LANES), F32)
        for offset in range(0, width, LANES):
            piece = jnp.exp2((scores[:, offset : offset + LANES] - highest) * (scale * LOG2E))
            raised[:, offset : offset + LANES] = piece.astype(BF16)
            sums = sums + piece
        summed = jnp.sum(sums, axis=1, keepdims=True)
        picked = jnp.sum(found, axis=1, keepdims=True)
        values = (highest * scale, summed, picked * scale, column[:, 0:1], column[:, 1:2])
        packed = jnp.zeros((tile, LANES), F32)
        for place, value in enumerate(values):
            packed = jnp.where(spot == place, value, packed)
        stats[...] = packed.T[:8]

    @pl.when(step >= meta[META_TILES])
    def skip():
        rows = lax.broadcasted_iota(jnp.int32, stats.shape, 0)
        stats[...] = jnp.where(rows == 1, 1.0, 0.0)


def logit_grads(meta, raised, factors, first, width, vocab):
    tile = raised.shape[0]
    columns = jnp.concatenate(
        [factors[...], jnp.zeros((LANES - factors.shape[0], tile), F32)], axis=0
    ).T
    factor, at_target = columns[:, 0:1], columns[:, 1:2]
    wanted = columns[:, 2:3].astype(jnp.int32) - meta[META_WIDE] * vocab
    wanted = jnp.where(wanted < vocab, wanted, -1) - first
    lanes = lax.broadcasted_iota(jnp.int32, (tile, width), 1)

    def chunk(start):
        part = raised[:, start : start + width].astype(F32) * factor
        return jnp.where(lanes == wanted - start, at_target, part).astype(BF16)

    return chunk


def exit_tokens_kernel(meta, places, *refs, vocab):
    source, raised, factors = refs[:3]
    parts = refs[3:7]
    table, token_grad, landed, table_sem, sems = refs[7:]
    size = parts[0].shape[0]
    members = 4 * size
    count = parts[0].shape[1]
    starts, counts = META_LISTS, META_LISTS + members
    step = pl.program_id(0)
    tile = raised.shape[0]

    @pl.when(step == 0)
    def load():
        whole = pltpu.make_async_copy(source, table, table_sem)
        whole.start()
        whole.wait()

    @pl.when(step < meta[META_TILES])
    def compute():
        chunk = logit_grads(meta, raised, factors, 0, VOCAB_TILE, vocab)
        grad = jnp.zeros((tile, token_grad.shape[1]), F32)
        for first in range(0, raised.shape[1], VOCAB_TILE):
            grad = grad + nt(chunk(first), table[:, first : first + VOCAB_TILE])
        token_grad[pl.ds(pl.multiple_of(step * tile, tile), tile), :] = grad.astype(BF16)

    @pl.when(step == pl.num_programs(0) - 1)
    def finish():
        copies = []
        spots = lax.broadcasted_iota(jnp.int32, (count, 1), 0)
        for slot in range(members):
            if slot >= 2:
                copies[slot - 2].wait()
            member = places[slot]
            begin = pl.multiple_of(meta[starts + member], 16)
            block = token_grad[pl.ds(begin, count), :].astype(F32)
            landed[slot % 2] = jnp.where(spots < meta[counts + member], block, 0.0).astype(BF16)
            copy = pltpu.make_async_copy(
                landed.at[slot % 2], parts[slot // size].at[slot % size], sems.at[slot % 2]
            )
            copy.start()
            copies.append(copy)
        for copy in copies[-2:]:
            copy.wait()


def exit_table_kernel(meta, raised, across, factors, *refs, first, vocab):
    table_grad, total = refs[-2:]
    step = pl.program_id(0)
    width = min(VOCAB_TILE, raised.shape[1])

    @pl.when(step == 0)
    def clear():
        total[...] = jnp.zeros_like(total)

    def compute(raised, across, factors):
        chunk = logit_grads(meta, raised, factors, first, width, vocab)
        for start in range(0, raised.shape[1], width):
            total[:, start : start + width] += nn(across[...], chunk(start))

    @pl.when(2 * step + 1 < meta[META_TILES])
    def both():
        compute(raised, across, factors)

    @pl.when(2 * step + 1 == meta[META_TILES])
    def one():
        half = raised.shape[0] // 2
        compute(raised.at[:half], across.at[:, :half], factors.at[:, :half])

    @pl.when(step == pl.num_programs(0) - 1)
    def finish():
        table_grad[...] = total[...].astype(BF16)


def mlp_backward_kernel(
    places, grad_in, stream_three, stream_two, gain, normed, gate, up, hidden, *refs,
):
    parts, down_parts = refs[:4], refs[4:8]
    stream_grad, gains = refs[8:10]
    grad_parts, down_grad_parts = refs[10:14], refs[14:18]
    weights, down, gate_low, up_low, result, down_result, sems, down_sems, out_sems = refs[18:]
    rows, down_rows = block_rows(weights, parts), block_rows(down, down_parts)
    first = weight_copies(
        places, down_parts, down_parts[0].shape[1] - down_rows, down, down_rows, down_sems
    )
    last = weight_copies(places, parts, 0, weights, rows, sems)
    for copy in first + last:
        copy.start()
    stream_back, exit_gain_grad = norm_back(stream_three[...], gain[3:4], grad_in[...])
    branch = stream_back.astype(BF16)
    for copy in first:
        copy.wait()
    width = weights.shape[2]
    step = width // 4
    normed_across = normed[...].T
    sent = []
    for part in range(4):
        columns = pl.ds(part * step, step)
        gate_pre = gate[:, columns]
        up_pre = up[:, columns]
        hidden_grad = nt(branch, down[0, columns, :])
        bent = jnp.tanh(MIX * (gate_pre + CUBE * (gate_pre * gate_pre * gate_pre)))
        slope = 0.5 * (1.0 + bent) + 0.5 * gate_pre * (1.0 - bent * bent) * (
            MIX * (1.0 + 3.0 * CUBE * gate_pre * gate_pre)
        )
        gate_low[:, columns] = (hidden_grad * up_pre * slope).astype(BF16)
        up_low[:, columns] = (hidden_grad * (0.5 * gate_pre * (1.0 + bent))).astype(BF16)
        result[0, :, columns] = nn(normed_across, gate_low[:, columns]).astype(BF16)
        result[1, :, columns] = nn(normed_across, up_low[:, columns]).astype(BF16)
    for matrix in range(2):
        send_off(
            sent,
            block_copies(
                places, result.at[matrix], matrix * rows, rows, grad_parts, out_sems.at[matrix]
            ),
        )
    for part in range(4):
        columns = pl.ds(part * step, step)
        down_result[columns, :] = nn(hidden[:, columns].T, branch).astype(BF16)
    send_off(
        sent, block_copies(places, down_result, 0, down_rows, down_grad_parts, out_sems.at[2])
    )
    for copy in last:
        copy.wait()
    normed_grad = nt(gate_low[...], weights[0]) + nt(up_low[...], weights[1])
    branch_in, gain_grad = norm_back(stream_two[...], gain[2:3], normed_grad)
    stream_grad[...] = stream_back + branch_in
    gains[...] = jnp.concatenate(
        [gain_grad, exit_gain_grad, jnp.zeros((6, gain_grad.shape[1]), F32)], axis=0
    )
    for copy in sent:
        copy.wait()


def cross_attention_first_kernel(
    places, lengths, sources, grad_in, query, key, value, totals, *refs,
):
    parts = refs[:4]
    branch, attended_grad, query_low, key_low, value_low, weights, bias, sems = refs[4:]
    rows = block_rows(weights, parts)
    copies = weight_copies(places, parts, 3 * rows, weights, rows, sems)
    for copy in copies:
        copy.start()
    fill_cross_bias(bias, lengths, sources)
    branch[...] = grad_in[...].astype(BF16)
    for copy in copies:
        copy.wait()
    attended_grad[...] = nt(branch[...], weights[0]).astype(BF16)
    attend_back(
        query, key, value, bias, totals, attended_grad, query_low, key_low, value_low,
        0, HEADS // 4,
    )


def cross_attention_last_kernel(
    lengths, sources, attended_grad, query, key, value, totals,
    first_query, first_key, first_value, query_low, key_low, value_low, bias,
):
    middle = first_query.shape[1]
    fill_cross_bias(bias, lengths, sources)
    attend_back(
        query, key, value, bias, totals, attended_grad,
        query_low.at[:, middle:], key_low.at[:, middle:], value_low.at[:, middle:],
        HEADS // 4, HEADS // 2,
    )
    query_low[:, :middle] = first_query[...]
    key_low[:, :middle] = first_key[...]
    value_low[:, :middle] = first_value[...]


def cross_backward_kernel(
    places, grad_in, stream_in, gain, normed, memory, attended, self_attended,
    branch, query_low, key_low, value_low, *refs,
):
    parts = refs[:4]
    stream_grad, gains, memory_grad, self_branch = refs[4:8]
    grad_parts = refs[8:12]
    weights, results, sems, out_sems = refs[12:]
    rows = block_rows(weights, parts)
    copies = weight_copies(places, parts, 0, weights, rows, sems)
    for copy in copies:
        copy.start()
    sent = []

    def weight_grad(matrix, left_across, right):
        results[matrix] = nn(left_across, right[...]).astype(BF16)
        send_off(
            sent,
            block_copies(
                places, results.at[matrix], matrix * rows, rows, grad_parts, out_sems.at[matrix]
            ),
        )

    memory_across = memory[...].T
    weight_grad(1, memory_across, key_low)
    weight_grad(2, memory_across, value_low)
    weight_grad(0, normed[...].T, query_low)
    weight_grad(3, attended[...].T, branch)
    for copy in copies:
        copy.wait()
    normed_grad = nt(query_low[...], weights[0])
    branch_in, gain_grad = norm_back(stream_in[...], gain[1:2], normed_grad)
    total = grad_in[...] + branch_in
    stream_grad[...] = total
    self_branch[...] = total.astype(BF16)
    weight_grad(4, self_attended[...].T, self_branch)
    gains[...] = jnp.broadcast_to(gain_grad, gains.shape)
    memory_grad[...] = nt(key_low[...], weights[1]) + nt(value_low[...], weights[2])
    for copy in sent:
        copy.wait()


def self_attention_backward_kernel(
    places, lengths, branch, query, key, value, totals, *refs,
):
    parts = refs[:4]
    query_low, key_low, value_low, weights, bias, attended_grad, sems = refs[4:]
    rows = block_rows(weights, parts)
    copies = weight_copies(places, parts, 3 * rows, weights, rows, sems)
    for copy in copies:
        copy.start()
    fill_self_bias(bias, lengths)
    for copy in copies:
        copy.wait()
    attended_grad[...] = nt(branch[...], weights[0]).astype(BF16)
    attend_back(
        query, key, value, bias, totals, attended_grad, query_low, key_low, value_low,
        0, HEADS // 2,
    )


def self_backward_kernel(
    places, grad_in, inputs, gain, normed, cross_gains, mlp_gains,
    query_low, key_low, value_low, *refs,
):
    parts = refs[:4]
    stream_grad = refs[4]
    grad_parts = refs[5:9]
    weights, results, terms, sems, out_sems, term_sems = refs[9:]
    rows = block_rows(weights, parts)
    size = grad_parts[0].shape[0]
    copies = weight_copies(places, parts, 0, weights, rows, sems)
    for copy in copies:
        copy.start()
    sent = []
    normed_across = normed[...].T
    for matrix, low in enumerate((query_low, key_low, value_low)):
        results[matrix] = nn(normed_across, low[...]).astype(BF16)
        send_off(
            sent,
            block_copies(
                places, results.at[matrix], matrix * rows, rows, grad_parts, out_sems.at[matrix]
            ),
        )
    for copy in copies:
        copy.wait()
    normed_grad = (
        nt(query_low[...], weights[0])
        + nt(key_low[...], weights[1])
        + nt(value_low[...], weights[2])
    )
    branch_in, gain_grad = norm_back(inputs[...].astype(F32), gain[0:1], normed_grad)
    stream_grad[...] = grad_in[...] + branch_in
    spot = lax.broadcasted_iota(jnp.int32, (8, gain_grad.shape[1]), 0)
    row = jnp.where(spot == 0, gain_grad, 0.0)
    row = jnp.where(spot == 1, cross_gains[0:1], row)
    row = jnp.where(spot == 2, mlp_gains[0:1], row)
    row = jnp.where(spot == 3, mlp_gains[1:2], row).astype(BF16)
    for start in range(0, terms.shape[0], 8):
        terms[start : start + 8] = row
    send_off(
        sent,
        [
            pltpu.make_async_copy(
                terms,
                grad_parts[slot // size].at[slot % size, pl.ds(3 * rows, terms.shape[0]), :],
                term_sems.at[slot],
            )
            for slot in range(4 * size)
        ],
    )
    for copy in sent:
        copy.wait()


def per_device(
    inputs,
    memory,
    targets,
    tgt_lengths,
    src_lengths,
    self_gain,
    self_query,
    self_key,
    self_value,
    self_out,
    cross_gain,
    cross_query,
    cross_key,
    cross_value,
    cross_out,
    mlp_gain,
    mlp_gate,
    mlp_up,
    mlp_down,
    exit_gain,
    embedding,
):
    tokens, model = inputs.shape
    slots = memory.shape[0]
    hidden_width = mlp_gate.shape[1]
    pair_slots = tgt_lengths.shape[1]
    wide_count = lax.axis_size("wide")
    narrow_count = lax.axis_size("narrow")
    wide = lax.axis_index("wide")
    narrow = lax.axis_index("narrow")
    slot_total = tokens * wide_count * narrow_count
    scale = 1.0 / math.sqrt(model)
    places = slot_places(wide, wide_count)
    lengths, sources = tgt_lengths[0], src_lengths[0]
    shard = self_query.shape[0]
    rows = shard * narrow_count
    down_rows = mlp_down.shape[0] * narrow_count

    aligned = rows % 8 == 0
    kernel_places = places if aligned else jnp.arange(4, dtype=jnp.int32)
    kernel_count = wide_count if aligned else 4
    ids = jnp.arange(wide_count, dtype=jnp.int32)
    order = places[None, :] == ids[:, None]

    def reorder(matrix, blocks):
        flat = blocks.reshape(wide_count, -1)
        return nn(matrix.astype(BF16), flat).astype(BF16).reshape(blocks.shape)

    def for_kernels(parts, sizes):
        if aligned:
            return parts
        whole, start, members = jnp.concatenate(parts, axis=0), 0, []
        for size in sizes:
            ordered = reorder(order, whole[:, start : start + size])
            members.append(ordered.reshape(4, -1, whole.shape[-1]))
            start += size
        return jnp.split(jnp.concatenate(members, axis=1), 4)

    def from_kernels(parts, sizes):
        if aligned:
            return parts
        whole, start, members = jnp.concatenate(parts, axis=0), 0, []
        for size in sizes:
            extent = size * wide_count // 4
            member = whole[:, start : start + extent].reshape(wide_count, size, -1)
            members.append(reorder(order.T, member))
            start += extent
        return jnp.split(jnp.concatenate(members, axis=1), 4)

    def line_block(pieces, sizes, *others):
        pieces = lax.optimization_barrier((*pieces, *others))[: len(pieces)]
        if all(size % 8 == 0 for size in sizes):
            return pl.pallas_call(
                functools.partial(line_kernel, sizes=sizes),
                in_specs=[SMEM] + [VMEM] * len(pieces),
                out_specs=VMEM,
                out_shape=like((pieces[0].shape[0] * len(pieces), pieces[0].shape[1]), BF16),
                compiler_params=PARAMS,
                cost_estimate=work(30),
                name="line_block",
            )(narrow[None], *pieces)
        ordered, start, members = in_line_order(pieces, narrow), 0, []
        for size in sizes:
            members += [piece[start : start + size] for piece in ordered]
            start += size
        return jnp.concatenate(members, axis=0)

    self_sizes, cross_sizes = [shard] * 4 + [8], [shard] * 4 + [mlp_down.shape[0]]
    gate_sizes = [shard] * 2
    count = jnp.sum(lengths)
    owner = wide * narrow_count + narrow
    gain_shards = jnp.stack([self_gain, cross_gain, mlp_gain, exit_gain])
    def join_self():
        return pl.pallas_call(
            join_self_kernel,
            in_specs=[SMEM] * 2 + [VMEM] * 5,
            out_specs=VMEM,
            out_shape=like((sum(self_sizes), model), BF16),
            cost_estimate=work(1),
            name="join_self",
        )(owner[None], lengths, gain_shards, self_query, self_key, self_value, self_out)

    numbers = jnp.broadcast_to(
        jnp.stack([count // 16, count % 16])[:, None], (2, shard)
    ).astype(BF16)
    own_rows = jnp.concatenate([gain_shards, numbers, jnp.zeros((2, shard), BF16)], axis=0)
    own_rows = jnp.tile(own_rows, (1, model // shard))
    own_columns = jnp.arange(model, dtype=jnp.int32)[None, :] // shard == owner
    own_rows = jnp.where(own_columns, own_rows, 0)
    self_pack = (
        join_self()
        if aligned
        else join_rows(self_query, self_key, self_value, self_out, own_rows)
    )
    members = (cross_query, cross_key, cross_value, cross_out, mlp_down)
    if aligned:
        wide_rows = -(-2 * hidden_width // model) * shard
        joined_pack = pl.pallas_call(
            join_wide_kernel,
            in_specs=[VMEM] * 7,
            out_specs=VMEM,
            out_shape=like((sum(cross_sizes) + wide_rows, model), BF16),
            compiler_params=PARAMS,
            cost_estimate=work(1),
            name="join_wide",
        )(*members, mlp_gate, mlp_up)
    side = jnp.stack([targets // 256, targets % 256]).astype(BF16)
    side = jnp.pad(side, ((0, 6), (0, model - tokens)))

    self_line = gather_narrow(self_pack, narrow_count)
    self_block = line_block(self_line, self_sizes)

    vocab = embedding.shape[0]
    padded = -(-vocab // VOCAB_TILE) * VOCAB_TILE
    turned = jnp.pad(embedding.T, ((0, 0), (0, padded - vocab)))
    table = lax.all_gather(tie(turned, *self_line), "narrow", axis=0, tiled=True)

    *early, last = stage_pairs(wide_count)

    def gather_early(block):
        held = block[None]
        for pairs in early:
            held = jnp.concatenate([held, lax.ppermute(held, "wide", pairs)], axis=0)
        return held

    if aligned:
        joined_even = tie(joined_pack, *self_line)
        joined_even = jnp.stack(
            [joined_even]
            + [
                lax.ppermute(joined_even, "narrow", narrow_pairs(narrow_count, step))
                for step in range(2, narrow_count, 2)
            ]
        )
        joined_odd = lax.ppermute(joined_even, "narrow", narrow_pairs(narrow_count, 1))
    else:
        cross_line = gather_narrow(join_rows(*members), narrow_count)
        gate_line = gather_narrow(join_rows(mlp_gate, mlp_up), narrow_count)
    self_held = gather_early(self_block)
    if aligned:
        self_held = tie(self_held, joined_even)
    self_came = lax.ppermute(self_held, "wide", last)
    if aligned:
        joined_odd = tie(joined_odd, self_held)
        cross_block, gate_block = pl.pallas_call(
            functools.partial(line_wide_kernel, sizes=cross_sizes, wide_size=shard),
            in_specs=[SMEM] + [VMEM] * 2,
            out_specs=[VMEM] * 2,
            out_shape=[
                like((sum(cross_sizes) * narrow_count, model), BF16),
                like((2 * rows, hidden_width), BF16),
            ],
            compiler_params=PARAMS,
            cost_estimate=work(1),
            name="line_wide",
        )(narrow[None], joined_even, joined_odd)
    else:
        cross_block = line_block(cross_line, cross_sizes)
        gate_block = line_block(gate_line, gate_sizes)
    self_parts = (
        self_held, self_came, cross_core(self_held, wide_count), cross_core(self_came, wide_count)
    )
    cross_held = gather_early(tie(cross_block, self_came))
    cross_came = lax.ppermute(cross_held, "wide", last)

    head_rows = like((HEADS // 2, 1, 2 * tokens), F32)
    activation = like((tokens, model), BF16)
    stream_like = like((tokens, model), F32)
    matrix_sems = pltpu.SemaphoreType.DMA((kernel_count, 4))
    one_matrix_sems = pltpu.SemaphoreType.DMA((kernel_count, 1))

    self_gathered = for_kernels(self_parts, [size * narrow_count for size in self_sizes])
    (
        normed_one, query_one, key_one, value_one, attended_one, totals_one, stream_one, gain_all,
    ) = pl.pallas_call(
        self_forward_kernel,
        in_specs=[SMEM, SMEM, VMEM] + [ANY] * 4,
        out_specs=[VMEM] * 8,
        out_shape=[activation] * 5 + [head_rows, stream_like, like((8, model), F32)],
        scratch_shapes=[
            pltpu.VMEM((4, model, model), BF16),
            pltpu.VMEM((kernel_count, 8 * narrow_count * wide_count // kernel_count, model), BF16),
            pltpu.VMEM((tokens, 2 * tokens), F32),
            matrix_sems,
            pltpu.SemaphoreType.DMA((kernel_count,)),
        ],
        compiler_params=PARAMS,
        cost_estimate=work(1),
        name="self_forward",
    )(kernel_places, lengths, tie(inputs, cross_held), *self_gathered)

    numbers = (gain_all[4] * 16.0 + gain_all[5]).reshape(wide_count, narrow_count, shard)[:, :, 0]
    numbers = jnp.sum(
        jnp.where(jnp.arange(narrow_count)[None, :] == narrow, numbers, 0.0), axis=1
    ).astype(jnp.int32)
    extents = (numbers + 15) // 16 * 16
    starts = jnp.sum(jnp.where(ids[None, :] < ids[:, None], extents[None, :], 0), axis=1)
    needed = (jnp.sum(extents) + ROW_TILE - 1) // ROW_TILE
    meta = jnp.concatenate([jnp.stack([wide, needed]), starts, numbers])
    slot_of = jnp.sum(jnp.where(order, ids[None, :], 0), axis=1)

    cross_came = tie(cross_came, stream_one)
    cross_parts = (
        cross_held, cross_came, cross_core(cross_held, wide_count), cross_core(cross_came, wide_count)
    )
    gate_held = gather_early(tie(gate_block, cross_came))
    gate_came = lax.ppermute(gate_held, "wide", last)
    cross_gathered = for_kernels(cross_parts, [size * narrow_count for size in cross_sizes])

    key_two, value_two = pl.pallas_call(
        memory_kernel,
        in_specs=[SMEM, VMEM] + [ANY] * 4,
        out_specs=[VMEM] * 2,
        out_shape=[like((slots, model), BF16)] * 2,
        scratch_shapes=[
            pltpu.VMEM((2, model, model), BF16),
            pltpu.SemaphoreType.DMA((kernel_count, 2)),
        ],
        compiler_params=PARAMS,
        cost_estimate=work(1),
        name="memory_projection",
    )(kernel_places, memory, *cross_gathered)

    normed_two, query_two, attended_two, totals_two, stream_two = pl.pallas_call(
        cross_forward_kernel,
        in_specs=[SMEM, SMEM, SMEM, VMEM, VMEM, VMEM, VMEM] + [ANY] * 4,
        out_specs=[VMEM] * 5,
        out_shape=[activation] * 3 + [head_rows, stream_like],
        scratch_shapes=[
            pltpu.VMEM((2, model, model), BF16),
            pltpu.VMEM((slots, 2 * tokens), F32),
            pltpu.SemaphoreType.DMA((2, kernel_count, 1)),
        ],
        compiler_params=PARAMS,
        cost_estimate=work(1),
        name="cross_forward",
    )(
        kernel_places, lengths, sources, tie(stream_one, gate_held), gain_all, key_two, value_two,
        *cross_gathered,
    )

    gate_came = tie(gate_came, stream_two)
    gate_parts = (
        gate_held, gate_came, cross_core(gate_held, wide_count), cross_core(gate_came, wide_count)
    )
    gate_gathered = for_kernels(gate_parts, [size * narrow_count for size in gate_sizes])

    wide_f32 = like((tokens, hidden_width), F32)
    wide_low = like((tokens, hidden_width), BF16)
    normed_three, gate_pre, up_pre, hidden, stream_three, activations, normed_four = pl.pallas_call(
        mlp_forward_kernel,
        in_specs=[SMEM, VMEM, VMEM, VMEM] + [ANY] * 8,
        out_specs=[VMEM] * 7,
        out_shape=[
            activation, wide_f32, wide_f32, wide_low, stream_like, activation,
            like((tokens + 8, model), BF16),
        ],
        scratch_shapes=[
            pltpu.VMEM((2, model, hidden_width), BF16),
            pltpu.VMEM((1, hidden_width, model), BF16),
            pltpu.SemaphoreType.DMA((kernel_count, 2)),
            one_matrix_sems,
        ],
        compiler_params=PARAMS,
        cost_estimate=work(1),
        name="mlp_forward",
    )(kernel_places, stream_two, gain_all, side, *gate_gathered, *cross_gathered)

    exit_parts = gather_wide(normed_four, wide_count)
    group = tokens * wide_count
    tiles = -(-group // (2 * ROW_TILE)) * 2
    kept = lambda i, meta: jnp.minimum(i, meta[META_TILES] - 1)
    kept_pair = lambda i, meta: jnp.minimum(i, (meta[META_TILES] - 1) // 2)

    raised, tokens_across, stats = pl.pallas_call(
        functools.partial(exit_scores_kernel, vocab=vocab, scale=scale),
        grid_spec=pltpu.PrefetchScalarGridSpec(
            num_scalar_prefetch=2,
            grid=(tiles,),
            in_specs=[ANY] * 5,
            out_specs=[
                pl.BlockSpec((ROW_TILE, padded), lambda i, meta, slots: (kept(i, meta), 0)),
                pl.BlockSpec((model, ROW_TILE), lambda i, meta, slots: (0, kept(i, meta))),
                pl.BlockSpec((8, ROW_TILE), lambda i, meta, slots: (0, i)),
            ],
            scratch_shapes=[
                pltpu.VMEM((model, padded), BF16),
                pltpu.VMEM((tiles * ROW_TILE, model), BF16),
                pltpu.VMEM((tiles * ROW_TILE, LANES), F32),
                pltpu.VMEM((min(wide_count, 8), tokens + 8, model), BF16),
                pltpu.VMEM((ROW_TILE, padded), F32),
                pltpu.SemaphoreType.DMA,
                pltpu.SemaphoreType.DMA((min(wide_count, 8),)),
            ],
        ),
        out_shape=[
            like((tiles * ROW_TILE, padded), BF16),
            like((model, tiles * ROW_TILE), BF16),
            like((8, tiles * ROW_TILE), F32),
        ],
        compiler_params=PARAMS,
        cost_estimate=work(52),
        name="exit_scores",
    )(meta, slot_of, *exit_parts, table)

    own_peak = stats[0]
    joint = stats
    for pairs in stage_pairs(wide_count) + [flip_pairs(wide_count)]:
        came = lax.ppermute(joint, "wide", pairs)
        peak = jnp.maximum(joint[0], came[0])
        summed = joint[1] * jnp.exp(joint[0] - peak) + came[1] * jnp.exp(came[0] - peak)
        joint = jnp.concatenate([peak[None], summed[None], joint[2:3] + came[2:3], stats[3:]], axis=0)
    log_total = joint[0] + jnp.log(joint[1])
    picked, group_weight = joint[2], stats[3]
    loss_part = jnp.full((8, LANES), jnp.sum(group_weight * (log_total - picked)), F32)

    factor = jnp.exp(own_peak - log_total) * (group_weight * scale)
    at_target = (jnp.exp(picked - log_total) - 1.0) * (group_weight * scale)
    factors = jnp.concatenate([factor[None], at_target[None], stats[4:5], stats[3:]], axis=0)
    token_part = like((wide_count // 4, tokens, model), BF16)
    exit_grads = pl.pallas_call(
        functools.partial(exit_tokens_kernel, vocab=vocab),
        grid_spec=pltpu.PrefetchScalarGridSpec(
            num_scalar_prefetch=2,
            grid=(tiles,),
            in_specs=[
                ANY,
                pl.BlockSpec((ROW_TILE, padded), lambda i, meta, slots: (kept(i, meta), 0)),
                pl.BlockSpec((8, ROW_TILE), lambda i, meta, slots: (0, i)),
            ],
            out_specs=[ANY] * 4,
            scratch_shapes=[
                pltpu.VMEM((model, padded), BF16),
                pltpu.VMEM((tiles * ROW_TILE, model), BF16),
                pltpu.VMEM((2, tokens, model), BF16),
                pltpu.SemaphoreType.DMA,
                pltpu.SemaphoreType.DMA((2,)),
            ],
        ),
        out_shape=[token_part] * 4,
        compiler_params=PARAMS,
        cost_estimate=work(50),
        name="exit_tokens",
    )(meta, places, table, raised, factors)

    half = padded // 2

    def table_half(side, factors, *before):
        return pl.pallas_call(
            functools.partial(exit_table_kernel, first=side * half, vocab=vocab),
            grid_spec=pltpu.PrefetchScalarGridSpec(
                num_scalar_prefetch=1,
                grid=(tiles // 2,),
                in_specs=[
                    pl.BlockSpec((2 * ROW_TILE, half), lambda i, meta: (kept_pair(i, meta), side)),
                    pl.BlockSpec((model, 2 * ROW_TILE), lambda i, meta: (0, kept_pair(i, meta))),
                    pl.BlockSpec((8, 2 * ROW_TILE), lambda i, meta: (0, i)),
                ]
                + [ANY] * len(before),
                out_specs=pl.BlockSpec((model, half), lambda i, meta: (0, side)),
                scratch_shapes=[pltpu.VMEM((model, half), F32)],
            ),
            out_shape=like((model, padded), BF16),
            input_output_aliases={4: 0} if before else {},
            compiler_params=PARAMS,
            cost_estimate=work(15),
            name="exit_table",
        )(meta, raised, tokens_across, factors, *before)

    exit_scatter = scatter_core(exit_grads, wide_count)
    half_grad = table_half(0, tie(factors, *exit_grads))
    (own, came), exit_kept = exit_scatter
    exit_far = scatter_far((own, tie(came, half_grad)), exit_kept, wide_count)
    table_grad = table_half(1, tie(factors, exit_far[0]), half_grad)
    table_sum = lax.psum_scatter(table_grad, "narrow", scatter_dimension=0, tiled=True)
    embedding_grad = table_sum.astype(F32).T[:vocab]
    exit_near = scatter_near(tie(exit_far[1], table_grad), exit_far[2], wide_count)
    exit_grad = exit_near[2] + exit_near[1].astype(F32)

    gain_like = like((8, model), F32)
    stream_two_grad, mlp_gains, *mlp_grads = pl.pallas_call(
        mlp_backward_kernel,
        in_specs=[SMEM] + [VMEM] * 8 + [ANY] * 8,
        out_specs=[VMEM] * 2 + [ANY] * 8,
        out_shape=[stream_like, gain_like]
        + [like(part.shape, BF16) for part in gate_gathered]
        + [
            like((part.shape[0], hidden_width // kernel_count, model), BF16)
            for part in cross_gathered
        ],
        scratch_shapes=[
            pltpu.VMEM((2, model, hidden_width), BF16),
            pltpu.VMEM((1, hidden_width, model), BF16),
            pltpu.VMEM((tokens, hidden_width), BF16),
            pltpu.VMEM((tokens, hidden_width), BF16),
            pltpu.VMEM((2, model, hidden_width), BF16),
            pltpu.VMEM((hidden_width, model), BF16),
            pltpu.SemaphoreType.DMA((kernel_count, 2)),
            one_matrix_sems,
            pltpu.SemaphoreType.DMA((3, kernel_count)),
        ],
        compiler_params=PARAMS,
        cost_estimate=work(15),
        name="mlp_backward",
    )(
        kernel_places, exit_grad, stream_three, stream_two, gain_all, normed_three,
        gate_pre, up_pre, hidden, *gate_gathered, *cross_gathered,
    )
    gate_scatter = scatter_core(from_kernels(mlp_grads[:4], [rows, rows]), wide_count)
    down_scatter = scatter_core(from_kernels(mlp_grads[4:], [down_rows]), wide_count)

    def go_far(scatter, *others):
        (own, came), kept = scatter
        return scatter_far((own, tie(came, *others)), kept, wide_count)

    def go_near(state, *others):
        _, came, kept = state
        return scatter_near(tie(came, *others), kept, wide_count)

    low_like = like((slots, model), BF16)
    middle = 2 * (HEADS // 4) * (model // HEADS)
    low_half = like((slots, middle), BF16)
    branch_two, attended_grad, *first_lows = pl.pallas_call(
        cross_attention_first_kernel,
        in_specs=[SMEM] * 3 + [VMEM] * 5 + [ANY] * 4,
        out_specs=[VMEM] * 5,
        out_shape=[activation, activation, like((tokens, middle), BF16), low_half, low_half],
        scratch_shapes=[
            pltpu.VMEM((1, model, model), BF16),
            pltpu.VMEM((slots, 2 * tokens), F32),
            one_matrix_sems,
        ],
        compiler_params=PARAMS,
        cost_estimate=work(16),
        name="cross_attention_first",
    )(
        kernel_places, lengths, sources, stream_two_grad, query_two, key_two, value_two, totals_two,
        *cross_gathered,
    )
    gate_far = go_far(gate_scatter, first_lows[0])
    down_far = go_far(down_scatter, first_lows[0])
    query_two_low, key_two_low, value_two_low = pl.pallas_call(
        cross_attention_last_kernel,
        in_specs=[SMEM] * 2 + [VMEM] * 8,
        out_specs=[VMEM] * 3,
        out_shape=[activation, low_like, low_like],
        scratch_shapes=[pltpu.VMEM((slots, 2 * tokens), F32)],
        compiler_params=PARAMS,
        cost_estimate=work(16),
        name="cross_attention_last",
    )(
        lengths, sources, tie(attended_grad, gate_far[0], down_far[0]), query_two, key_two,
        value_two, totals_two, *first_lows,
    )

    loss_part = tie(loss_part, query_two_low)
    loss_all = loss_part
    for step in range(1, narrow_count):
        loss_all = loss_all + lax.ppermute(loss_part, "narrow", narrow_pairs(narrow_count, step))
    mean_loss = loss_all[0, 0] / slot_total
    cross_matrices = like((cross_gathered[0].shape[0], 5 * model // kernel_count, model), BF16)
    stream_one_grad, cross_gains, memory_grad, branch_one, *cross_grads = pl.pallas_call(
        cross_backward_kernel,
        in_specs=[SMEM] + [VMEM] * 11 + [ANY] * 4,
        out_specs=[VMEM] * 4 + [ANY] * 4,
        out_shape=[stream_like, gain_like, like((slots, model), F32), activation]
        + [cross_matrices] * 4,
        scratch_shapes=[
            pltpu.VMEM((3, model, model), BF16),
            pltpu.VMEM((5, model, model), BF16),
            pltpu.SemaphoreType.DMA((kernel_count, 3)),
            pltpu.SemaphoreType.DMA((5, kernel_count)),
        ],
        compiler_params=PARAMS,
        cost_estimate=work(20),
        name="cross_backward",
    )(
        kernel_places, stream_two_grad, stream_one, gain_all,
        normed_two, memory, attended_two, attended_one, branch_two,
        query_two_low, key_two_low, value_two_low, *cross_gathered,
    )
    cross_scatter = scatter_core(from_kernels(cross_grads, [rows] * 5), wide_count)

    gate_near = go_near(gate_far, branch_one)
    down_near = go_near(down_far, branch_one)
    query_one_low, key_one_low, value_one_low = pl.pallas_call(
        self_attention_backward_kernel,
        in_specs=[SMEM] * 2 + [VMEM] * 5 + [ANY] * 4,
        out_specs=[VMEM] * 3,
        out_shape=[activation] * 3,
        scratch_shapes=[
            pltpu.VMEM((1, model, model), BF16),
            pltpu.VMEM((tokens, 2 * tokens), F32),
            pltpu.VMEM((tokens, model), BF16),
            one_matrix_sems,
        ],
        compiler_params=PARAMS,
        cost_estimate=work(10),
        name="self_attention_backward",
    )(
        kernel_places, lengths, tie(branch_one, gate_near[0], down_near[0], loss_all), query_one, key_one, value_one, totals_one,
        *self_gathered,
    )
    def line_blocks(near, matrices, *others):
        _, came, held = near
        summed = held + tie(came, *others).astype(F32)
        width = summed.shape[-1]
        size = matrices * (summed.shape[0] // (matrices * 8 * narrow_count)) * 8 * narrow_count
        members = [
            summed[:size].reshape(matrices, narrow_count, -1, width).transpose(1, 0, 2, 3)
            .reshape(narrow_count, -1, width)
        ]
        if size < summed.shape[0]:
            members.append(summed[size:].reshape(narrow_count, -1, width))
        return jnp.concatenate(members, axis=1)

    def line_first(near, matrices, *others):
        blocks = line_blocks(near, matrices, *others)
        steps = range(0, narrow_count, 2)
        sent = jnp.stack([pick(blocks, narrow ^ (step + 1)) for step in steps]).astype(BF16)
        came = lax.ppermute(sent, "narrow", narrow_pairs(narrow_count, 1))
        return sent, came, [pick(blocks, narrow ^ step) for step in steps]

    def line_second(state, *others):
        _, came, kept = state
        came = tie(came, *others).astype(F32)
        terms = [kept[0] + came[0]]
        for place in range(1, len(kept)):
            sent = (kept[place] + came[place]).astype(BF16)
            terms.append(lax.ppermute(sent, "narrow", narrow_pairs(narrow_count, 2 * place)))
        return terms

    cross_far = go_far(cross_scatter, query_one_low)
    gate_line = line_first(gate_near, 2, query_one_low)

    extra = narrow_count * 8
    spare = extra * wide_count // kernel_count
    inputs_grad, *self_grads = pl.pallas_call(
        self_backward_kernel,
        in_specs=[SMEM] + [VMEM] * 9 + [ANY] * 4,
        out_specs=[VMEM] + [ANY] * 4,
        out_shape=[stream_like]
        + [like((part.shape[0], 3 * model // kernel_count + spare, model), BF16) for part in self_gathered],
        scratch_shapes=[
            pltpu.VMEM((3, model, model), BF16),
            pltpu.VMEM((3, model, model), BF16),
            pltpu.VMEM((spare, model), BF16),
            pltpu.SemaphoreType.DMA((kernel_count, 3)),
            pltpu.SemaphoreType.DMA((3, kernel_count)),
            pltpu.SemaphoreType.DMA((kernel_count,)),
        ],
        compiler_params=PARAMS,
        cost_estimate=work(12),
        name="self_backward",
    )(
        kernel_places, tie(stream_one_grad, gate_line[0], cross_far[0]), inputs,
        gain_all, normed_one, cross_gains, mlp_gains, query_one_low, key_one_low, value_one_low,
        *self_gathered,
    )
    self_scatter = scatter_core(from_kernels(self_grads, [rows] * 3 + [extra]), wide_count)

    cross_near = go_near(cross_far, inputs_grad)
    self_far = go_far(self_scatter, cross_near[0])
    down_line = line_first(down_near, 1, self_far[0])
    gate_terms = line_second(gate_line, self_far[0])
    cross_line = line_first(cross_near, 5, down_line[0], gate_terms[0], embedding_grad)
    self_near = go_near(self_far, cross_line[0])
    down_terms = line_second(down_line, self_near[0])
    gate_sum = add_terms(gate_terms, self_near[0]).reshape(2, shard, hidden_width)
    cross_terms = line_second(cross_line, down_terms[0], gate_sum)
    self_terms = scatter_narrow(
        line_blocks(self_near, 3, cross_terms[0]), narrow, narrow_count
    )
    down_sum = add_terms(down_terms, self_terms[0])
    cross_sum = add_terms(cross_terms, self_terms[0]).reshape(5, shard, model)
    self_sum = add_terms(self_terms)
    gains = pick(self_sum[3 * shard :].reshape(8, model // shard, shard), owner, 1)
    self_sum = self_sum[: 3 * shard].reshape(3, shard, model)

    return (
        activations,
        mean_loss,
        inputs_grad,
        memory_grad,
        gains[0],
        self_sum[0],
        self_sum[1],
        self_sum[2],
        cross_sum[4],
        gains[1],
        cross_sum[0],
        cross_sum[1],
        cross_sum[2],
        cross_sum[3],
        gains[2],
        gate_sum[0],
        gate_sum[1],
        down_sum,
        gains[3],
        embedding_grad,
    )


def solution(mesh):
    both = ("wide", "narrow")
    rows, flat = P(both, None), P(both)
    placed = (
        rows, rows, flat, rows, rows,
        flat, rows, rows, rows, rows,
        flat, rows, rows, rows, rows,
        flat, rows, rows, rows, flat,
        P("wide", "narrow"),
    )
    given = (
        rows, P(), rows, rows,
        flat, rows, rows, rows, rows,
        flat, rows, rows, rows, rows,
        flat, rows, rows, rows, flat,
        P("wide", "narrow"),
    )
    return jax.shard_map(
        per_device, mesh=mesh, in_specs=placed, out_specs=given, check_vma=False
    )
```

```python
import functools
import math

import jax
import jax.numpy as jnp
from jax import lax
from jax.experimental import pallas as pl
from jax.experimental.pallas import tpu as pltpu
from jax.sharding import PartitionSpec as P

HEADS = 12
EPSILON = 1e-06
NEGATIVE = -1e30
F32 = jnp.float32
BF16 = jnp.bfloat16
LANES = 128
ROW_TILE = 256
VOCAB_TILE = 512
MIX = math.sqrt(2.0 / math.pi)
CUBE = 0.044715
LOG2E = math.log2(math.e)
META_WIDE, META_TILES, META_LISTS = 0, 1, 2

VMEM = pl.BlockSpec(memory_space=pltpu.VMEM)
SMEM = pl.BlockSpec(memory_space=pltpu.SMEM)
ANY = pl.BlockSpec(memory_space=pl.ANY)
PARAMS = pltpu.CompilerParams(vmem_limit_bytes=60 * 2**20)


def work(gigaflops):
    return pl.CostEstimate(flops=gigaflops * 10**9, bytes_accessed=10**6, transcendentals=0)


def nn(left, right):
    return lax.dot_general(left, right, (((1,), (0,)), ((), ())), preferred_element_type=F32)


def nt(left, right):
    return lax.dot_general(left, right, (((1,), (1,)), ((), ())), preferred_element_type=F32)


def tn(left, right):
    return lax.dot_general(left, right, (((0,), (0,)), ((), ())), preferred_element_type=F32)


def like(shape, kind):
    return jax.ShapeDtypeStruct(shape, kind)


def stage_masks(count):
    up = [1 << bit for bit in range(1, count.bit_length() - 1)]
    return up, up[::-1]


def stage_pairs(count):
    even, odd = stage_masks(count)
    return [[(v, v ^ (odd if v % 2 else even)[i]) for v in range(count)] for i in range(len(even))]


def flip_pairs(count):
    return [(v, v ^ 1) for v in range(count)]


def slot_tables(count):
    tables = []
    for masks in stage_masks(count):
        slots = [0]
        for mask in masks:
            slots = slots + [slot ^ mask for slot in slots]
        tables.append(slots)
    even, odd = tables
    return (
        even + [1 ^ slot for slot in odd],
        odd + [1 ^ slot for slot in even],
    )


def slot_places(wide, count):
    even, odd = slot_tables(count)
    table = jnp.where(wide % 2 == 0, jnp.array(even, jnp.int32), jnp.array(odd, jnp.int32))
    return wide ^ table


def tie(value, *others):
    return lax.optimization_barrier((value, *others))[0]


def cross_core(value, count):
    return lax.ppermute(value, "wide", flip_pairs(count))


def gather_wide(block, count):
    held = block[None]
    *early, last = stage_pairs(count)
    for pairs in early:
        held = jnp.concatenate([held, lax.ppermute(held, "wide", pairs)], axis=0)
    came = lax.ppermute(held, "wide", last)
    return held, came, cross_core(held, count), cross_core(came, count)


def scatter_core(parts, count):
    sent, kept = cross_core(parts[3], count), cross_core(parts[2], count)
    return (parts[1], sent), (parts[0], kept)


def scatter_far(sent, kept, count):
    far = sent[0] + sent[1]
    came = lax.ppermute(far, "wide", stage_pairs(count)[-1])
    return far, came, kept


def scatter_near(came, kept, count):
    *rest, last = stage_pairs(count)[-2::-1]
    terms = (*kept, came)
    if not rest:
        far = sum(term[1].astype(F32) for term in terms).astype(BF16)
        return far, lax.ppermute(far, "wide", last), sum(term[0].astype(F32) for term in terms)
    held = sum(term.astype(F32) for term in terms)
    for pairs in rest:
        half = held.shape[0] // 2
        sent = lax.ppermute(held[half:].astype(BF16), "wide", pairs)
        held = held[:half] + sent.astype(F32)
    far = held[1].astype(BF16)
    return far, lax.ppermute(far, "wide", last), held[0]


def scatter_wide(parts, count):
    far, came, kept = scatter_far(*scatter_core(parts, count), count)
    far, came, held = scatter_near(came, kept, count)
    return held + came.astype(F32)


def narrow_pairs(count, step):
    return [(v, v ^ step) for v in range(count)]


def gather_narrow(block, count):
    return [block] + [
        lax.ppermute(block, "narrow", narrow_pairs(count, step)) for step in range(1, count)
    ]


def pick(values, place, axis=0):
    return lax.dynamic_index_in_dim(values, place.astype(jnp.uint32), axis, keepdims=False)


def in_line_order(pieces, narrow):
    stacked = jnp.stack(pieces)
    return [pick(stacked, narrow ^ place) for place in range(stacked.shape[0])]


def scatter_narrow(blocks, narrow, count):
    return [pick(blocks, narrow)] + [
        lax.ppermute(pick(blocks, narrow ^ step).astype(BF16), "narrow", narrow_pairs(count, step))
        for step in range(1, count)
    ]


def add_terms(terms, *others):
    terms = lax.optimization_barrier((*terms, *others))[: len(terms)]
    return sum(term.astype(F32) for term in terms)


def weight_copies(places, parts, start, target, rows, sems):
    size = parts[0].shape[0]
    copies = []
    for slot in range(len(parts) * size):
        place = pl.multiple_of(places[slot] * rows, 8)
        for matrix in range(target.shape[0]):
            copies.append(
                pltpu.make_async_copy(
                    parts[slot // size].at[slot % size, pl.ds(start + matrix * rows, rows), :],
                    target.at[matrix, pl.ds(place, rows), :],
                    sems.at[slot, matrix],
                )
            )
    return copies


def block_copies(places, value, start, rows, parts, sems):
    size = parts[0].shape[0]
    copies = []
    for slot in range(len(parts) * size):
        place = pl.multiple_of(places[slot] * rows, 8)
        copies.append(
            pltpu.make_async_copy(
                value.at[pl.ds(place, rows), :],
                parts[slot // size].at[slot % size, pl.ds(start, rows), :],
                sems.at[slot],
            )
        )
    return copies


def send_off(copies, more):
    for copy in more:
        copy.start()
    copies += more


def norm_scale(values):
    return lax.rsqrt(jnp.mean(values * values, axis=-1, keepdims=True) + EPSILON)


def norm_back(values, gain, grad):
    root = norm_scale(values)
    scaled = gain * grad
    gain_grad = jnp.sum(grad * values * root, axis=0, keepdims=True)
    inner = jnp.mean(scaled * values, axis=-1, keepdims=True)
    return root * scaled - values * (root * root * root) * inner, gain_grad


def query_segments(lengths, count):
    places = lax.broadcasted_iota(jnp.int32, (1, count), 1)
    segment = jnp.zeros((1, count), jnp.int32)
    edge = jnp.int32(0)
    for pair in range(lengths.shape[0]):
        edge = edge + lengths[pair]
        segment = segment + (places >= edge).astype(jnp.int32)
    return places, segment


def fill_self_bias(bias, lengths):
    count = bias.shape[1] // 2
    places, segment = query_segments(lengths, count)
    low = jnp.zeros((1, count), jnp.int32)
    edge = jnp.int32(0)
    for pair in range(lengths.shape[0]):
        edge = edge + lengths[pair]
        low = jnp.where(segment == pair + 1, edge, low)
    keys = lax.broadcasted_iota(jnp.int32, (bias.shape[0], count), 0)
    one = jnp.where((keys >= low) & (keys <= places), 0.0, NEGATIVE)
    bias[...] = jnp.concatenate([one, one], axis=1)


def fill_cross_bias(bias, lengths, sources):
    count = bias.shape[1] // 2
    places, segment = query_segments(lengths, count)
    low = jnp.zeros((1, count), jnp.int32)
    high = jnp.full((1, count), bias.shape[0], jnp.int32)
    edge = jnp.int32(0)
    for pair in range(lengths.shape[0]):
        low = jnp.where(segment == pair, edge, low)
        edge = edge + sources[pair]
        high = jnp.where(segment == pair, edge, high)
    low = jnp.concatenate([low, low], axis=1)
    high = jnp.concatenate([high, high], axis=1)
    keys = lax.broadcasted_iota(jnp.int32, bias.shape, 0)
    bias[...] = jnp.where((keys >= low) & (keys < high), 0.0, NEGATIVE)


def first_half(width):
    return lax.broadcasted_iota(jnp.int32, (1, width), 1) < width // 2


def apart(values, chosen):
    return jnp.concatenate([jnp.where(chosen, values, 0), jnp.where(chosen, 0, values)], axis=0)


def together(values, chosen):
    count = values.shape[0] // 2
    return jnp.where(chosen, values[:count], values[count:])


def attend(queries, keys, values, bias, outputs, totals, unroll):
    width = 2 * (queries.shape[1] // HEADS)
    chosen = first_half(width)

    def pair_of_heads(pair, carry):
        columns = pl.ds(pl.multiple_of(pair * width, width), width)
        scores = nt(keys[:, columns], apart(queries[:, columns], chosen)) + bias[...]
        highest = jnp.max(scores, axis=0, keepdims=True)
        raised = jnp.exp(scores - highest)
        summed = jnp.sum(raised, axis=0, keepdims=True)
        totals[pair] = highest + jnp.log(summed)
        weights = (raised * (1.0 / summed)).astype(BF16)
        mixed = nn(values[:, columns].T, weights).T
        outputs[:, columns] = together(mixed, chosen).astype(BF16)
        return carry

    lax.fori_loop(0, HEADS // 2, pair_of_heads, 0, unroll=unroll)


def attend_back(
    queries, keys, values, bias, totals, grads, query_low, key_low, value_low, first, last
):
    width = 2 * (queries.shape[1] // HEADS)
    chosen = first_half(width)

    for pair in range(first, last):
        columns = slice(pair * width, (pair + 1) * width)
        result = slice((pair - first) * width, (pair - first + 1) * width)
        query, grad = apart(queries[:, columns], chosen), apart(grads[:, columns], chosen)
        key = keys[:, columns]
        probs = jnp.exp(nt(key, query) + bias[...] - totals[pair])
        prob_grad = nt(values[:, columns], grad)
        value_low[:, result] = nn(probs.astype(BF16), grad).astype(BF16)
        weighted = probs * prob_grad
        centre = jnp.sum(weighted, axis=0, keepdims=True)
        score_grad = (weighted - probs * centre).astype(BF16)
        key_low[:, result] = nn(score_grad, query).astype(BF16)
        query_low[:, result] = together(nn(key.T, score_grad).T, chosen).astype(BF16)


def block_rows(weights, parts):
    return weights.shape[1] // (len(parts) * parts[0].shape[0])


def join_kernel(*refs):
    start = 0
    for ref in refs[:-1]:
        refs[-1][start : start + ref.shape[0], :] = ref[...]
        start += ref.shape[0]


def join_self_kernel(owner, lengths, gains, *refs):
    join_kernel(*refs)
    pack = refs[-1]
    shard, width = gains.shape[1], pack.shape[1]
    total = jnp.int32(0)
    for pair in range(lengths.shape[0]):
        total = total + lengths[pair]
    spot = lax.broadcasted_iota(jnp.int32, (8, shard), 0)
    high, low = (total // 16).astype(F32), (total % 16).astype(F32)
    own = jnp.concatenate([gains[...].astype(F32), jnp.zeros((8 - gains.shape[0], shard), F32)], axis=0)
    own = jnp.where(spot == 4, high, jnp.where(spot == 5, low, own)).astype(BF16)
    row = lax.broadcasted_iota(jnp.int32, (shard, width), 0)
    column = lax.broadcasted_iota(jnp.int32, (shard, width), 1)
    spread = (row + owner[0] * shard == column).astype(BF16)
    pack[pack.shape[0] - 8 :, :] = nn(own, spread).astype(BF16)


def join_rows(*members):
    if any(member.shape[0] % 8 for member in members):
        return jnp.concatenate(members, axis=0)
    rows = sum(member.shape[0] for member in members)
    return pl.pallas_call(
        join_kernel,
        in_specs=[VMEM] * len(members),
        out_specs=VMEM,
        out_shape=like((rows, members[0].shape[1]), members[0].dtype),
        cost_estimate=work(1),
        name="join_rows",
    )(*members)


def line_kernel(narrow, *refs, sizes):
    pieces, block = refs[:-1], refs[-1]
    start = 0
    for size in sizes:
        for step, piece in enumerate(pieces):
            place = pl.multiple_of(start * len(pieces) + (narrow[0] ^ step) * size, 8)
            block[pl.ds(place, size), :] = piece[start : start + size]
        start += size


def line_pair_kernel(narrow, even, odd, block, *, sizes):
    pieces = [(odd if step % 2 else even).at[step // 2] for step in range(2 * even.shape[0])]
    start = 0
    for size in sizes:
        for step, piece in enumerate(pieces):
            place = pl.multiple_of(start * len(pieces) + (narrow[0] ^ step) * size, 8)
            block[pl.ds(place, size), :] = piece[start : start + size]
        start += size


def self_forward_kernel(
    places, lengths, inputs, *refs,
):
    parts = refs[:4]
    normed, query, key, value, attended, totals, stream, gains = refs[4:12]
    weights, gain_parts, bias, sems, gain_sems = refs[12:]
    size = parts[0].shape[0]
    rows = block_rows(weights, parts)
    gain_copies = [
        pltpu.make_async_copy(
            parts[slot // size].at[slot % size, pl.ds(4 * rows, gain_parts.shape[1]), :],
            gain_parts.at[slot],
            gain_sems.at[slot],
        )
        for slot in range(4 * size)
    ]
    copies = weight_copies(places, parts, 0, weights, rows, sems)
    for copy in gain_copies + copies:
        copy.start()
    values = inputs[...].astype(F32)
    fill_self_bias(bias, lengths)
    scaled = values * norm_scale(values)
    for copy in gain_copies:
        copy.wait()
    members = gain_parts[...].astype(F32).reshape(-1, 8, gains.shape[1])
    summed = members[0]
    for member in range(1, members.shape[0]):
        summed = summed + members[member]
    gains[...] = summed
    low = (scaled * summed[0:1]).astype(BF16)
    normed[...] = low
    for copy in copies:
        copy.wait()
    query[...] = nn(low, weights[0]).astype(BF16)
    key[...] = nn(low, weights[1]).astype(BF16)
    value[...] = nn(low, weights[2]).astype(BF16)
    attend(query, key, value, bias, attended, totals, HEADS // 2)
    stream[...] = values + nn(attended[...], weights[3])


def memory_kernel(places, memory, *refs):
    parts = refs[:4]
    key, value, weights, sems = refs[4:]
    rows = block_rows(weights, parts)
    copies = weight_copies(places, parts, rows, weights, rows, sems)
    for copy in copies:
        copy.start()
    for copy in copies:
        copy.wait()
    key[...] = nn(memory[...], weights[0]).astype(BF16)
    value[...] = nn(memory[...], weights[1]).astype(BF16)


def cross_forward_kernel(
    places, lengths, sources, stream_in, gains, key, value, *refs,
):
    parts = refs[:4]
    normed, query, attended, totals, stream, weights, bias, sems = refs[4:]
    rows = block_rows(weights, parts)
    copies = weight_copies(places, parts, 0, weights.at[pl.ds(0, 1)], rows, sems.at[0])
    copies += weight_copies(places, parts, 3 * rows, weights.at[pl.ds(1, 1)], rows, sems.at[1])
    for copy in copies:
        copy.start()
    values = stream_in[...]
    fill_cross_bias(bias, lengths, sources)
    low = (values * norm_scale(values) * gains[1:2]).astype(BF16)
    normed[...] = low
    for copy in copies:
        copy.wait()
    query[...] = nn(low, weights[0]).astype(BF16)
    attend(query, key, value, bias, attended, totals, HEADS // 4)
    stream[...] = values + nn(attended[...], weights[1])


def mlp_forward_kernel(
    places, stream_in, gains, side, *refs,
):
    parts, down_parts = refs[:4], refs[4:8]
    normed, gate, up, hidden, stream, activations, exit_normed = refs[8:15]
    weights, down, sems, down_sems = refs[15:]
    rows, down_rows = block_rows(weights, parts), block_rows(down, down_parts)
    first = weight_copies(places, parts, 0, weights, rows, sems)
    last = weight_copies(
        places, down_parts, down_parts[0].shape[1] - down_rows, down, down_rows, down_sems
    )
    for copy in first + last:
        copy.start()
    values = stream_in[...]
    low = (values * norm_scale(values) * gains[2:3]).astype(BF16)
    normed[...] = low
    for copy in first:
        copy.wait()
    width = weights.shape[2]
    step = width // 4
    for part in range(4):
        columns = pl.ds(part * step, step)
        gate_pre = nn(low, weights[0, :, columns])
        up_pre = nn(low, weights[1, :, columns])
        gate[:, columns] = gate_pre
        up[:, columns] = up_pre
        bent = jnp.tanh(MIX * (gate_pre + CUBE * (gate_pre * gate_pre * gate_pre)))
        hidden[:, columns] = (0.5 * gate_pre * (1.0 + bent) * up_pre).astype(BF16)
    for copy in last:
        copy.wait()
    out = values + nn(hidden[...], down[0])
    stream[...] = out
    activations[...] = out.astype(BF16)
    count = out.shape[0]
    exit_normed[:count] = (out * norm_scale(out) * gains[3:4]).astype(BF16)
    exit_normed[count:] = side[...]


def exit_scores_kernel(meta, slot_of, *refs, vocab, scale):
    parts = refs[:4]
    source, raised, across, stats = refs[4:8]
    table, tokens, columns, landed, scores, table_sem, sems = refs[8:]
    size = parts[0].shape[0]
    members = 4 * size
    ring = landed.shape[0]
    count = parts[0].shape[1] - 8
    step = pl.program_id(0)
    tile = raised.shape[0]
    starts, counts = META_LISTS, META_LISTS + members

    def fetch(member):
        slot = slot_of[member]
        for part in range(4):

            @pl.when(slot // size == part)
            def start():
                pltpu.make_async_copy(
                    parts[part].at[slot % size], landed.at[member % ring], sems.at[member % ring]
                ).start()

    @pl.when(step == 0)
    def load():
        whole = pltpu.make_async_copy(source, table, table_sem)
        for member in range(min(ring, members)):
            fetch(member)
        whole.start()
        tokens[...] = jnp.zeros_like(tokens)
        columns[...] = jnp.zeros_like(columns)
        lanes = -(-count // LANES) * LANES
        spots = lax.broadcasted_iota(jnp.int32, (1, lanes), 1)
        for member in range(members):
            pltpu.make_async_copy(
                parts[0].at[0], landed.at[member % ring], sems.at[member % ring]
            ).wait()
            begin = pl.multiple_of(meta[starts + member], 16)
            block = landed[member % ring]
            tokens[pl.ds(begin, count), :] = block[:count]
            side = block[count:, :lanes].astype(F32)
            wanted = side[0:1] * 256.0 + side[1:2]
            weight = jnp.where(spots < meta[counts + member], 1.0, 0.0)
            packed = jnp.concatenate(
                [weight, wanted, jnp.zeros((LANES - 2, lanes), F32)], axis=0
            )
            columns[pl.ds(begin, count), :] = packed.T[:count]
            if member + ring < members:
                fetch(member + ring)
        whole.wait()

    spot = lax.broadcasted_iota(jnp.int32, (tile, LANES), 1)

    @pl.when(step < meta[META_TILES])
    def compute():
        here = pl.ds(pl.multiple_of(step * tile, tile), tile)
        own = tokens[here, :]
        column = columns[here, :]
        across[...] = own.T
        width = scores.shape[1]
        lanes = lax.broadcasted_iota(jnp.int32, (tile, LANES), 1)
        wanted = column[:, 1:2].astype(jnp.int32) - meta[META_WIDE] * vocab
        wanted = jnp.where(wanted < vocab, wanted, -1)
        peaks = jnp.full((tile, LANES), NEGATIVE, F32)
        found = jnp.zeros((tile, LANES), F32)
        for first in range(0, width, VOCAB_TILE):
            part = nn(own, table[:, first : first + VOCAB_TILE])
            for inner in range(0, VOCAB_TILE, LANES):
                piece = part[:, inner : inner + LANES]
                offset = first + inner
                if offset + LANES > vocab:
                    piece = jnp.where(lanes < vocab - offset, piece, NEGATIVE)
                scores[:, offset : offset + LANES] = piece
                peaks = jnp.maximum(peaks, piece)
                found = found + jnp.where(lanes == wanted - offset, piece, 0.0)
        highest = jnp.max(peaks, axis=1, keepdims=True)
        sums = jnp.zeros((tile, LANES), F32)
        for offset in range(0, width, LANES):
            piece = jnp.exp2((scores[:, offset : offset + LANES] - highest) * (scale * LOG2E))
            raised[:, offset : offset + LANES] = piece.astype(BF16)
            sums = sums + piece
        summed = jnp.sum(sums, axis=1, keepdims=True)
        picked = jnp.sum(found, axis=1, keepdims=True)
        values = (highest * scale, summed, picked * scale, column[:, 0:1], column[:, 1:2])
        packed = jnp.zeros((tile, LANES), F32)
        for place, value in enumerate(values):
            packed = jnp.where(spot == place, value, packed)
        stats[...] = packed.T[:8]

    @pl.when(step >= meta[META_TILES])
    def skip():
        rows = lax.broadcasted_iota(jnp.int32, stats.shape, 0)
        stats[...] = jnp.where(rows == 1, 1.0, 0.0)


def logit_grads(meta, raised, factors, first, width, vocab):
    tile = raised.shape[0]
    columns = jnp.concatenate(
        [factors[...], jnp.zeros((LANES - factors.shape[0], tile), F32)], axis=0
    ).T
    factor, at_target = columns[:, 0:1], columns[:, 1:2]
    wanted = columns[:, 2:3].astype(jnp.int32) - meta[META_WIDE] * vocab
    wanted = jnp.where(wanted < vocab, wanted, -1) - first
    lanes = lax.broadcasted_iota(jnp.int32, (tile, width), 1)

    def chunk(start):
        part = raised[:, start : start + width].astype(F32) * factor
        return jnp.where(lanes == wanted - start, at_target, part).astype(BF16)

    return chunk


def exit_tokens_kernel(meta, places, *refs, vocab):
    source, raised, factors = refs[:3]
    parts = refs[3:7]
    table, token_grad, landed, table_sem, sems = refs[7:]
    size = parts[0].shape[0]
    members = 4 * size
    count = parts[0].shape[1]
    starts, counts = META_LISTS, META_LISTS + members
    step = pl.program_id(0)
    tile = raised.shape[0]

    @pl.when(step == 0)
    def load():
        whole = pltpu.make_async_copy(source, table, table_sem)
        whole.start()
        whole.wait()

    @pl.when(step < meta[META_TILES])
    def compute():
        chunk = logit_grads(meta, raised, factors, 0, VOCAB_TILE, vocab)
        grad = jnp.zeros((tile, token_grad.shape[1]), F32)
        for first in range(0, raised.shape[1], VOCAB_TILE):
            grad = grad + nt(chunk(first), table[:, first : first + VOCAB_TILE])
        token_grad[pl.ds(pl.multiple_of(step * tile, tile), tile), :] = grad.astype(BF16)

    @pl.when(step == pl.num_programs(0) - 1)
    def finish():
        copies = []
        spots = lax.broadcasted_iota(jnp.int32, (count, 1), 0)
        for slot in range(members):
            if slot >= 2:
                copies[slot - 2].wait()
            member = places[slot]
            begin = pl.multiple_of(meta[starts + member], 16)
            block = token_grad[pl.ds(begin, count), :].astype(F32)
            landed[slot % 2] = jnp.where(spots < meta[counts + member], block, 0.0).astype(BF16)
            copy = pltpu.make_async_copy(
                landed.at[slot % 2], parts[slot // size].at[slot % size], sems.at[slot % 2]
            )
            copy.start()
            copies.append(copy)
        for copy in copies[-2:]:
            copy.wait()


def exit_table_kernel(meta, raised, across, factors, *refs, first, vocab):
    table_grad, total = refs[-2:]
    step = pl.program_id(0)
    width = min(VOCAB_TILE, raised.shape[1])

    @pl.when(step == 0)
    def clear():
        total[...] = jnp.zeros_like(total)

    def compute(raised, across, factors):
        chunk = logit_grads(meta, raised, factors, first, width, vocab)
        for start in range(0, raised.shape[1], width):
            total[:, start : start + width] += nn(across[...], chunk(start))

    @pl.when(2 * step + 1 < meta[META_TILES])
    def both():
        compute(raised, across, factors)

    @pl.when(2 * step + 1 == meta[META_TILES])
    def one():
        half = raised.shape[0] // 2
        compute(raised.at[:half], across.at[:, :half], factors.at[:, :half])

    @pl.when(step == pl.num_programs(0) - 1)
    def finish():
        table_grad[...] = total[...].astype(BF16)


def mlp_backward_kernel(
    places, grad_in, stream_three, stream_two, gain, normed, gate, up, hidden, *refs,
):
    parts, down_parts = refs[:4], refs[4:8]
    stream_grad, gains = refs[8:10]
    grad_parts, down_grad_parts = refs[10:14], refs[14:18]
    weights, down, gate_low, up_low, result, down_result, sems, down_sems, out_sems = refs[18:]
    rows, down_rows = block_rows(weights, parts), block_rows(down, down_parts)
    first = weight_copies(
        places, down_parts, down_parts[0].shape[1] - down_rows, down, down_rows, down_sems
    )
    last = weight_copies(places, parts, 0, weights, rows, sems)
    for copy in first + last:
        copy.start()
    stream_back, exit_gain_grad = norm_back(stream_three[...], gain[3:4], grad_in[...])
    branch = stream_back.astype(BF16)
    for copy in first:
        copy.wait()
    width = weights.shape[2]
    step = width // 4
    normed_across = normed[...].T
    sent = []
    for part in range(4):
        columns = pl.ds(part * step, step)
        gate_pre = gate[:, columns]
        up_pre = up[:, columns]
        hidden_grad = nt(branch, down[0, columns, :])
        bent = jnp.tanh(MIX * (gate_pre + CUBE * (gate_pre * gate_pre * gate_pre)))
        slope = 0.5 * (1.0 + bent) + 0.5 * gate_pre * (1.0 - bent * bent) * (
            MIX * (1.0 + 3.0 * CUBE * gate_pre * gate_pre)
        )
        gate_low[:, columns] = (hidden_grad * up_pre * slope).astype(BF16)
        up_low[:, columns] = (hidden_grad * (0.5 * gate_pre * (1.0 + bent))).astype(BF16)
        result[0, :, columns] = nn(normed_across, gate_low[:, columns]).astype(BF16)
        result[1, :, columns] = nn(normed_across, up_low[:, columns]).astype(BF16)
    for matrix in range(2):
        send_off(
            sent,
            block_copies(
                places, result.at[matrix], matrix * rows, rows, grad_parts, out_sems.at[matrix]
            ),
        )
    for part in range(4):
        columns = pl.ds(part * step, step)
        down_result[columns, :] = nn(hidden[:, columns].T, branch).astype(BF16)
    send_off(
        sent, block_copies(places, down_result, 0, down_rows, down_grad_parts, out_sems.at[2])
    )
    for copy in last:
        copy.wait()
    normed_grad = nt(gate_low[...], weights[0]) + nt(up_low[...], weights[1])
    branch_in, gain_grad = norm_back(stream_two[...], gain[2:3], normed_grad)
    stream_grad[...] = stream_back + branch_in
    gains[...] = jnp.concatenate(
        [gain_grad, exit_gain_grad, jnp.zeros((6, gain_grad.shape[1]), F32)], axis=0
    )
    for copy in sent:
        copy.wait()


def cross_attention_first_kernel(
    places, lengths, sources, grad_in, query, key, value, totals, *refs,
):
    parts = refs[:4]
    branch, attended_grad, query_low, key_low, value_low, weights, bias, sems = refs[4:]
    rows = block_rows(weights, parts)
    copies = weight_copies(places, parts, 3 * rows, weights, rows, sems)
    for copy in copies:
        copy.start()
    fill_cross_bias(bias, lengths, sources)
    branch[...] = grad_in[...].astype(BF16)
    for copy in copies:
        copy.wait()
    attended_grad[...] = nt(branch[...], weights[0]).astype(BF16)
    attend_back(
        query, key, value, bias, totals, attended_grad, query_low, key_low, value_low,
        0, HEADS // 4,
    )


def cross_attention_last_kernel(
    lengths, sources, attended_grad, query, key, value, totals,
    first_query, first_key, first_value, query_low, key_low, value_low, bias,
):
    middle = first_query.shape[1]
    fill_cross_bias(bias, lengths, sources)
    attend_back(
        query, key, value, bias, totals, attended_grad,
        query_low.at[:, middle:], key_low.at[:, middle:], value_low.at[:, middle:],
        HEADS // 4, HEADS // 2,
    )
    query_low[:, :middle] = first_query[...]
    key_low[:, :middle] = first_key[...]
    value_low[:, :middle] = first_value[...]


def cross_backward_kernel(
    places, grad_in, stream_in, gain, normed, memory, attended, self_attended,
    branch, query_low, key_low, value_low, *refs,
):
    parts = refs[:4]
    stream_grad, gains, memory_grad, self_branch = refs[4:8]
    grad_parts = refs[8:12]
    weights, results, sems, out_sems = refs[12:]
    rows = block_rows(weights, parts)
    copies = weight_copies(places, parts, 0, weights, rows, sems)
    for copy in copies:
        copy.start()
    sent = []

    def weight_grad(matrix, left_across, right):
        results[matrix] = nn(left_across, right[...]).astype(BF16)
        send_off(
            sent,
            block_copies(
                places, results.at[matrix], matrix * rows, rows, grad_parts, out_sems.at[matrix]
            ),
        )

    memory_across = memory[...].T
    weight_grad(1, memory_across, key_low)
    weight_grad(2, memory_across, value_low)
    weight_grad(0, normed[...].T, query_low)
    weight_grad(3, attended[...].T, branch)
    for copy in copies:
        copy.wait()
    normed_grad = nt(query_low[...], weights[0])
    branch_in, gain_grad = norm_back(stream_in[...], gain[1:2], normed_grad)
    total = grad_in[...] + branch_in
    stream_grad[...] = total
    self_branch[...] = total.astype(BF16)
    weight_grad(4, self_attended[...].T, self_branch)
    gains[...] = jnp.broadcast_to(gain_grad, gains.shape)
    memory_grad[...] = nt(key_low[...], weights[1]) + nt(value_low[...], weights[2])
    for copy in sent:
        copy.wait()


def self_attention_backward_kernel(
    places, lengths, branch, query, key, value, totals, *refs,
):
    parts = refs[:4]
    query_low, key_low, value_low, weights, bias, attended_grad, sems = refs[4:]
    rows = block_rows(weights, parts)
    copies = weight_copies(places, parts, 3 * rows, weights, rows, sems)
    for copy in copies:
        copy.start()
    fill_self_bias(bias, lengths)
    for copy in copies:
        copy.wait()
    attended_grad[...] = nt(branch[...], weights[0]).astype(BF16)
    attend_back(
        query, key, value, bias, totals, attended_grad, query_low, key_low, value_low,
        0, HEADS // 2,
    )


def self_backward_kernel(
    places, grad_in, inputs, gain, normed, cross_gains, mlp_gains,
    query_low, key_low, value_low, *refs,
):
    parts = refs[:4]
    stream_grad = refs[4]
    grad_parts = refs[5:9]
    weights, results, terms, sems, out_sems, term_sems = refs[9:]
    rows = block_rows(weights, parts)
    size = grad_parts[0].shape[0]
    copies = weight_copies(places, parts, 0, weights, rows, sems)
    for copy in copies:
        copy.start()
    sent = []
    normed_across = normed[...].T
    for matrix, low in enumerate((query_low, key_low, value_low)):
        results[matrix] = nn(normed_across, low[...]).astype(BF16)
        send_off(
            sent,
            block_copies(
                places, results.at[matrix], matrix * rows, rows, grad_parts, out_sems.at[matrix]
            ),
        )
    for copy in copies:
        copy.wait()
    normed_grad = (
        nt(query_low[...], weights[0])
        + nt(key_low[...], weights[1])
        + nt(value_low[...], weights[2])
    )
    branch_in, gain_grad = norm_back(inputs[...].astype(F32), gain[0:1], normed_grad)
    stream_grad[...] = grad_in[...] + branch_in
    spot = lax.broadcasted_iota(jnp.int32, (8, gain_grad.shape[1]), 0)
    row = jnp.where(spot == 0, gain_grad, 0.0)
    row = jnp.where(spot == 1, cross_gains[0:1], row)
    row = jnp.where(spot == 2, mlp_gains[0:1], row)
    row = jnp.where(spot == 3, mlp_gains[1:2], row).astype(BF16)
    for start in range(0, terms.shape[0], 8):
        terms[start : start + 8] = row
    send_off(
        sent,
        [
            pltpu.make_async_copy(
                terms,
                grad_parts[slot // size].at[slot % size, pl.ds(3 * rows, terms.shape[0]), :],
                term_sems.at[slot],
            )
            for slot in range(4 * size)
        ],
    )
    for copy in sent:
        copy.wait()


def per_device(
    inputs,
    memory,
    targets,
    tgt_lengths,
    src_lengths,
    self_gain,
    self_query,
    self_key,
    self_value,
    self_out,
    cross_gain,
    cross_query,
    cross_key,
    cross_value,
    cross_out,
    mlp_gain,
    mlp_gate,
    mlp_up,
    mlp_down,
    exit_gain,
    embedding,
):
    tokens, model = inputs.shape
    slots = memory.shape[0]
    hidden_width = mlp_gate.shape[1]
    pair_slots = tgt_lengths.shape[1]
    wide_count = lax.axis_size("wide")
    narrow_count = lax.axis_size("narrow")
    wide = lax.axis_index("wide")
    narrow = lax.axis_index("narrow")
    slot_total = tokens * wide_count * narrow_count
    scale = 1.0 / math.sqrt(model)
    places = slot_places(wide, wide_count)
    lengths, sources = tgt_lengths[0], src_lengths[0]
    shard = self_query.shape[0]
    rows = shard * narrow_count
    down_rows = mlp_down.shape[0] * narrow_count

    aligned = rows % 8 == 0
    kernel_places = places if aligned else jnp.arange(4, dtype=jnp.int32)
    kernel_count = wide_count if aligned else 4
    ids = jnp.arange(wide_count, dtype=jnp.int32)
    order = places[None, :] == ids[:, None]

    def reorder(matrix, blocks):
        flat = blocks.reshape(wide_count, -1)
        return nn(matrix.astype(BF16), flat).astype(BF16).reshape(blocks.shape)

    def for_kernels(parts, sizes):
        if aligned:
            return parts
        whole, start, members = jnp.concatenate(parts, axis=0), 0, []
        for size in sizes:
            ordered = reorder(order, whole[:, start : start + size])
            members.append(ordered.reshape(4, -1, whole.shape[-1]))
            start += size
        return jnp.split(jnp.concatenate(members, axis=1), 4)

    def from_kernels(parts, sizes):
        if aligned:
            return parts
        whole, start, members = jnp.concatenate(parts, axis=0), 0, []
        for size in sizes:
            extent = size * wide_count // 4
            member = whole[:, start : start + extent].reshape(wide_count, size, -1)
            members.append(reorder(order.T, member))
            start += extent
        return jnp.split(jnp.concatenate(members, axis=1), 4)

    def line_block(pieces, sizes, *others):
        pieces = lax.optimization_barrier((*pieces, *others))[: len(pieces)]
        if all(size % 8 == 0 for size in sizes):
            return pl.pallas_call(
                functools.partial(line_kernel, sizes=sizes),
                in_specs=[SMEM] + [VMEM] * len(pieces),
                out_specs=VMEM,
                out_shape=like((pieces[0].shape[0] * len(pieces), pieces[0].shape[1]), BF16),
                compiler_params=PARAMS,
                cost_estimate=work(30),
                name="line_block",
            )(narrow[None], *pieces)
        ordered, start, members = in_line_order(pieces, narrow), 0, []
        for size in sizes:
            members += [piece[start : start + size] for piece in ordered]
            start += size
        return jnp.concatenate(members, axis=0)

    self_sizes, cross_sizes = [shard] * 4 + [8], [shard] * 4 + [mlp_down.shape[0]]
    gate_sizes = [shard] * 2
    count = jnp.sum(lengths)
    owner = wide * narrow_count + narrow
    gain_shards = jnp.stack([self_gain, cross_gain, mlp_gain, exit_gain])
    def join_self():
        return pl.pallas_call(
            join_self_kernel,
            in_specs=[SMEM] * 2 + [VMEM] * 5,
            out_specs=VMEM,
            out_shape=like((sum(self_sizes), model), BF16),
            cost_estimate=work(1),
            name="join_self",
        )(owner[None], lengths, gain_shards, self_query, self_key, self_value, self_out)

    numbers = jnp.broadcast_to(
        jnp.stack([count // 16, count % 16])[:, None], (2, shard)
    ).astype(BF16)
    own_rows = jnp.concatenate([gain_shards, numbers, jnp.zeros((2, shard), BF16)], axis=0)
    own_rows = jnp.tile(own_rows, (1, model // shard))
    own_columns = jnp.arange(model, dtype=jnp.int32)[None, :] // shard == owner
    own_rows = jnp.where(own_columns, own_rows, 0)
    self_pack = (
        join_self()
        if aligned
        else join_rows(self_query, self_key, self_value, self_out, own_rows)
    )
    members = (cross_query, cross_key, cross_value, cross_out, mlp_down)
    side = jnp.stack([targets // 256, targets % 256]).astype(BF16)
    side = jnp.pad(side, ((0, 6), (0, model - tokens)))

    self_line = gather_narrow(self_pack, narrow_count)
    self_block = line_block(self_line, self_sizes)

    vocab = embedding.shape[0]
    padded = -(-vocab // VOCAB_TILE) * VOCAB_TILE
    turned = jnp.pad(embedding.T, ((0, 0), (0, padded - vocab)))
    table = lax.all_gather(tie(turned, *self_line), "narrow", axis=0, tiled=True)

    *early, last = stage_pairs(wide_count)

    def gather_early(block, *others):
        held = block[None]
        for pairs in early:
            came = lax.ppermute(held, "wide", pairs)
            if others:
                came = tie(came, *others)
            held = jnp.concatenate([held, came], axis=0)
        return held

    cross_pack, gate_pack = join_rows(*members), join_rows(mlp_gate, mlp_up)

    def line_even(pack):
        return jnp.stack(
            [pack]
            + [
                lax.ppermute(pack, "narrow", narrow_pairs(narrow_count, step))
                for step in range(2, narrow_count, 2)
            ]
        )

    def line_odd(even):
        return lax.ppermute(even, "narrow", narrow_pairs(narrow_count, 1))

    def line_pair(even, odd, sizes):
        return pl.pallas_call(
            functools.partial(line_pair_kernel, sizes=sizes),
            in_specs=[SMEM] + [VMEM] * 2,
            out_specs=VMEM,
            out_shape=like((narrow_count * even.shape[1], even.shape[2]), BF16),
            compiler_params=PARAMS,
            cost_estimate=work(1),
            name="line_pair",
        )(narrow[None], even, odd)

    self_held = gather_early(self_block)
    if aligned:
        cross_even = line_even(tie(cross_pack, *self_line))
        cross_odd = line_odd(cross_even)
        gate_even = line_even(tie(gate_pack, cross_even))
        gate_odd = line_odd(gate_even)
        self_held = tie(self_held, cross_even)
        cross_block = line_pair(cross_even, tie(cross_odd, self_held), cross_sizes)
    else:
        cross_block = line_block(gather_narrow(cross_pack, narrow_count), cross_sizes)
        gate_block = line_block(gather_narrow(gate_pack, narrow_count), gate_sizes)
    self_came = lax.ppermute(self_held, "wide", last)
    self_parts = (
        self_held, self_came, cross_core(self_held, wide_count), cross_core(self_came, wide_count)
    )
    cross_block = tie(cross_block, self_came)
    if aligned:
        cross_block = tie(cross_block, gate_even)
    cross_held = gather_early(cross_block)
    if aligned:
        cross_held = tie(cross_held, gate_odd)
        gate_block = line_pair(gate_even, gate_odd, gate_sizes)
    cross_came = lax.ppermute(cross_held, "wide", last)

    head_rows = like((HEADS // 2, 1, 2 * tokens), F32)
    activation = like((tokens, model), BF16)
    stream_like = like((tokens, model), F32)
    matrix_sems = pltpu.SemaphoreType.DMA((kernel_count, 4))
    one_matrix_sems = pltpu.SemaphoreType.DMA((kernel_count, 1))

    self_gathered = for_kernels(self_parts, [size * narrow_count for size in self_sizes])
    (
        normed_one, query_one, key_one, value_one, attended_one, totals_one, stream_one, gain_all,
    ) = pl.pallas_call(
        self_forward_kernel,
        in_specs=[SMEM, SMEM, VMEM] + [ANY] * 4,
        out_specs=[VMEM] * 8,
        out_shape=[activation] * 5 + [head_rows, stream_like, like((8, model), F32)],
        scratch_shapes=[
            pltpu.VMEM((4, model, model), BF16),
            pltpu.VMEM((kernel_count, 8 * narrow_count * wide_count // kernel_count, model), BF16),
            pltpu.VMEM((tokens, 2 * tokens), F32),
            matrix_sems,
            pltpu.SemaphoreType.DMA((kernel_count,)),
        ],
        compiler_params=PARAMS,
        cost_estimate=work(1),
        name="self_forward",
    )(kernel_places, lengths, tie(inputs, cross_held), *self_gathered)

    numbers = (gain_all[4] * 16.0 + gain_all[5]).reshape(wide_count, narrow_count, shard)[:, :, 0]
    numbers = jnp.sum(
        jnp.where(jnp.arange(narrow_count)[None, :] == narrow, numbers, 0.0), axis=1
    ).astype(jnp.int32)
    extents = (numbers + 15) // 16 * 16
    starts = jnp.sum(jnp.where(ids[None, :] < ids[:, None], extents[None, :], 0), axis=1)
    needed = (jnp.sum(extents) + ROW_TILE - 1) // ROW_TILE
    meta = jnp.concatenate([jnp.stack([wide, needed]), starts, numbers])
    slot_of = jnp.sum(jnp.where(order, ids[None, :], 0), axis=1)

    cross_came = tie(cross_came, stream_one)
    cross_parts = (
        cross_held, cross_came, cross_core(cross_held, wide_count), cross_core(cross_came, wide_count)
    )
    cross_gathered = for_kernels(cross_parts, [size * narrow_count for size in cross_sizes])

    key_two, value_two = pl.pallas_call(
        memory_kernel,
        in_specs=[SMEM, VMEM] + [ANY] * 4,
        out_specs=[VMEM] * 2,
        out_shape=[like((slots, model), BF16)] * 2,
        scratch_shapes=[
            pltpu.VMEM((2, model, model), BF16),
            pltpu.SemaphoreType.DMA((kernel_count, 2)),
        ],
        compiler_params=PARAMS,
        cost_estimate=work(1),
        name="memory_projection",
    )(kernel_places, memory, *cross_gathered)

    gate_held = gather_early(tie(gate_block, cross_came), key_two)
    gate_came = lax.ppermute(gate_held, "wide", last)

    normed_two, query_two, attended_two, totals_two, stream_two = pl.pallas_call(
        cross_forward_kernel,
        in_specs=[SMEM, SMEM, SMEM, VMEM, VMEM, VMEM, VMEM] + [ANY] * 4,
        out_specs=[VMEM] * 5,
        out_shape=[activation] * 3 + [head_rows, stream_like],
        scratch_shapes=[
            pltpu.VMEM((2, model, model), BF16),
            pltpu.VMEM((slots, 2 * tokens), F32),
            pltpu.SemaphoreType.DMA((2, kernel_count, 1)),
        ],
        compiler_params=PARAMS,
        cost_estimate=work(1),
        name="cross_forward",
    )(
        kernel_places, lengths, sources, tie(stream_one, gate_held), gain_all, key_two, value_two,
        *cross_gathered,
    )

    gate_came = tie(gate_came, stream_two)
    gate_parts = (
        gate_held, gate_came, cross_core(gate_held, wide_count), cross_core(gate_came, wide_count)
    )
    gate_gathered = for_kernels(gate_parts, [size * narrow_count for size in gate_sizes])

    wide_f32 = like((tokens, hidden_width), F32)
    wide_low = like((tokens, hidden_width), BF16)
    normed_three, gate_pre, up_pre, hidden, stream_three, activations, normed_four = pl.pallas_call(
        mlp_forward_kernel,
        in_specs=[SMEM, VMEM, VMEM, VMEM] + [ANY] * 8,
        out_specs=[VMEM] * 7,
        out_shape=[
            activation, wide_f32, wide_f32, wide_low, stream_like, activation,
            like((tokens + 8, model), BF16),
        ],
        scratch_shapes=[
            pltpu.VMEM((2, model, hidden_width), BF16),
            pltpu.VMEM((1, hidden_width, model), BF16),
            pltpu.SemaphoreType.DMA((kernel_count, 2)),
            one_matrix_sems,
        ],
        compiler_params=PARAMS,
        cost_estimate=work(1),
        name="mlp_forward",
    )(kernel_places, stream_two, gain_all, side, *gate_gathered, *cross_gathered)

    exit_held = gather_early(normed_four)
    exit_came = tie(lax.ppermute(exit_held, "wide", last), table)
    exit_parts = (
        exit_held, exit_came, cross_core(exit_held, wide_count), cross_core(exit_came, wide_count)
    )
    group = tokens * wide_count
    tiles = -(-group // (2 * ROW_TILE)) * 2
    kept = lambda i, meta: jnp.minimum(i, meta[META_TILES] - 1)
    kept_pair = lambda i, meta: jnp.minimum(i, (meta[META_TILES] - 1) // 2)

    raised, tokens_across, stats = pl.pallas_call(
        functools.partial(exit_scores_kernel, vocab=vocab, scale=scale),
        grid_spec=pltpu.PrefetchScalarGridSpec(
            num_scalar_prefetch=2,
            grid=(tiles,),
            in_specs=[ANY] * 5,
            out_specs=[
                pl.BlockSpec((ROW_TILE, padded), lambda i, meta, slots: (kept(i, meta), 0)),
                pl.BlockSpec((model, ROW_TILE), lambda i, meta, slots: (0, kept(i, meta))),
                pl.BlockSpec((8, ROW_TILE), lambda i, meta, slots: (0, i)),
            ],
            scratch_shapes=[
                pltpu.VMEM((model, padded), BF16),
                pltpu.VMEM((tiles * ROW_TILE, model), BF16),
                pltpu.VMEM((tiles * ROW_TILE, LANES), F32),
                pltpu.VMEM((min(wide_count, 8), tokens + 8, model), BF16),
                pltpu.VMEM((ROW_TILE, padded), F32),
                pltpu.SemaphoreType.DMA,
                pltpu.SemaphoreType.DMA((min(wide_count, 8),)),
            ],
        ),
        out_shape=[
            like((tiles * ROW_TILE, padded), BF16),
            like((model, tiles * ROW_TILE), BF16),
            like((8, tiles * ROW_TILE), F32),
        ],
        compiler_params=PARAMS,
        cost_estimate=work(52),
        name="exit_scores",
    )(meta, slot_of, *exit_parts, table)

    own_peak = stats[0]
    joint = stats
    for pairs in stage_pairs(wide_count) + [flip_pairs(wide_count)]:
        came = lax.ppermute(joint, "wide", pairs)
        peak = jnp.maximum(joint[0], came[0])
        summed = joint[1] * jnp.exp(joint[0] - peak) + came[1] * jnp.exp(came[0] - peak)
        joint = jnp.concatenate([peak[None], summed[None], joint[2:3] + came[2:3], stats[3:]], axis=0)
    log_total = joint[0] + jnp.log(joint[1])
    picked, group_weight = joint[2], stats[3]
    loss_part = jnp.full((8, LANES), jnp.sum(group_weight * (log_total - picked)), F32)

    factor = jnp.exp(own_peak - log_total) * (group_weight * scale)
    at_target = (jnp.exp(picked - log_total) - 1.0) * (group_weight * scale)
    factors = jnp.concatenate([factor[None], at_target[None], stats[4:5], stats[3:]], axis=0)
    token_part = like((wide_count // 4, tokens, model), BF16)
    exit_grads = pl.pallas_call(
        functools.partial(exit_tokens_kernel, vocab=vocab),
        grid_spec=pltpu.PrefetchScalarGridSpec(
            num_scalar_prefetch=2,
            grid=(tiles,),
            in_specs=[
                ANY,
                pl.BlockSpec((ROW_TILE, padded), lambda i, meta, slots: (kept(i, meta), 0)),
                pl.BlockSpec((8, ROW_TILE), lambda i, meta, slots: (0, i)),
            ],
            out_specs=[ANY] * 4,
            scratch_shapes=[
                pltpu.VMEM((model, padded), BF16),
                pltpu.VMEM((tiles * ROW_TILE, model), BF16),
                pltpu.VMEM((2, tokens, model), BF16),
                pltpu.SemaphoreType.DMA,
                pltpu.SemaphoreType.DMA((2,)),
            ],
        ),
        out_shape=[token_part] * 4,
        compiler_params=PARAMS,
        cost_estimate=work(50),
        name="exit_tokens",
    )(meta, places, table, raised, factors)

    half = padded // 2

    def table_half(side, factors, *before):
        return pl.pallas_call(
            functools.partial(exit_table_kernel, first=side * half, vocab=vocab),
            grid_spec=pltpu.PrefetchScalarGridSpec(
                num_scalar_prefetch=1,
                grid=(tiles // 2,),
                in_specs=[
                    pl.BlockSpec((2 * ROW_TILE, half), lambda i, meta: (kept_pair(i, meta), side)),
                    pl.BlockSpec((model, 2 * ROW_TILE), lambda i, meta: (0, kept_pair(i, meta))),
                    pl.BlockSpec((8, 2 * ROW_TILE), lambda i, meta: (0, i)),
                ]
                + [ANY] * len(before),
                out_specs=pl.BlockSpec((model, half), lambda i, meta: (0, side)),
                scratch_shapes=[pltpu.VMEM((model, half), F32)],
            ),
            out_shape=like((model, padded), BF16),
            input_output_aliases={4: 0} if before else {},
            compiler_params=PARAMS,
            cost_estimate=work(15),
            name="exit_table",
        )(meta, raised, tokens_across, factors, *before)

    exit_scatter = scatter_core(exit_grads, wide_count)
    half_grad = table_half(0, tie(factors, *exit_grads))
    (own, came), exit_kept = exit_scatter
    exit_far = scatter_far((own, tie(came, half_grad)), exit_kept, wide_count)
    table_grad = table_half(1, tie(factors, exit_far[0]), half_grad)
    table_sum = lax.psum_scatter(table_grad, "narrow", scatter_dimension=0, tiled=True)
    embedding_grad = table_sum.astype(F32).T[:vocab]
    exit_near = scatter_near(tie(exit_far[1], table_grad), exit_far[2], wide_count)
    exit_grad = exit_near[2] + exit_near[1].astype(F32)

    gain_like = like((8, model), F32)
    stream_two_grad, mlp_gains, *mlp_grads = pl.pallas_call(
        mlp_backward_kernel,
        in_specs=[SMEM] + [VMEM] * 8 + [ANY] * 8,
        out_specs=[VMEM] * 2 + [ANY] * 8,
        out_shape=[stream_like, gain_like]
        + [like(part.shape, BF16) for part in gate_gathered]
        + [
            like((part.shape[0], hidden_width // kernel_count, model), BF16)
            for part in cross_gathered
        ],
        scratch_shapes=[
            pltpu.VMEM((2, model, hidden_width), BF16),
            pltpu.VMEM((1, hidden_width, model), BF16),
            pltpu.VMEM((tokens, hidden_width), BF16),
            pltpu.VMEM((tokens, hidden_width), BF16),
            pltpu.VMEM((2, model, hidden_width), BF16),
            pltpu.VMEM((hidden_width, model), BF16),
            pltpu.SemaphoreType.DMA((kernel_count, 2)),
            one_matrix_sems,
            pltpu.SemaphoreType.DMA((3, kernel_count)),
        ],
        compiler_params=PARAMS,
        cost_estimate=work(15),
        name="mlp_backward",
    )(
        kernel_places, exit_grad, stream_three, stream_two, gain_all, normed_three,
        gate_pre, up_pre, hidden, *gate_gathered, *cross_gathered,
    )
    gate_scatter = scatter_core(from_kernels(mlp_grads[:4], [rows, rows]), wide_count)
    down_scatter = scatter_core(from_kernels(mlp_grads[4:], [down_rows]), wide_count)

    def go_far(scatter, *others):
        (own, came), kept = scatter
        return scatter_far((own, tie(came, *others)), kept, wide_count)

    def go_near(state, *others):
        _, came, kept = state
        return scatter_near(tie(came, *others), kept, wide_count)

    low_like = like((slots, model), BF16)
    middle = 2 * (HEADS // 4) * (model // HEADS)
    low_half = like((slots, middle), BF16)
    branch_two, attended_grad, *first_lows = pl.pallas_call(
        cross_attention_first_kernel,
        in_specs=[SMEM] * 3 + [VMEM] * 5 + [ANY] * 4,
        out_specs=[VMEM] * 5,
        out_shape=[activation, activation, like((tokens, middle), BF16), low_half, low_half],
        scratch_shapes=[
            pltpu.VMEM((1, model, model), BF16),
            pltpu.VMEM((slots, 2 * tokens), F32),
            one_matrix_sems,
        ],
        compiler_params=PARAMS,
        cost_estimate=work(16),
        name="cross_attention_first",
    )(
        kernel_places, lengths, sources, stream_two_grad, query_two, key_two, value_two, totals_two,
        *cross_gathered,
    )
    gate_far = go_far(gate_scatter, first_lows[0])
    down_far = go_far(down_scatter, first_lows[0])
    query_two_low, key_two_low, value_two_low = pl.pallas_call(
        cross_attention_last_kernel,
        in_specs=[SMEM] * 2 + [VMEM] * 8,
        out_specs=[VMEM] * 3,
        out_shape=[activation, low_like, low_like],
        scratch_shapes=[pltpu.VMEM((slots, 2 * tokens), F32)],
        compiler_params=PARAMS,
        cost_estimate=work(16),
        name="cross_attention_last",
    )(
        lengths, sources, tie(attended_grad, gate_far[0], down_far[0]), query_two, key_two,
        value_two, totals_two, *first_lows,
    )

    loss_part = tie(loss_part, query_two_low)
    loss_all = loss_part
    for step in range(1, narrow_count):
        loss_all = loss_all + lax.ppermute(loss_part, "narrow", narrow_pairs(narrow_count, step))
    mean_loss = loss_all[0, 0] / slot_total
    cross_matrices = like((cross_gathered[0].shape[0], 5 * model // kernel_count, model), BF16)
    stream_one_grad, cross_gains, memory_grad, branch_one, *cross_grads = pl.pallas_call(
        cross_backward_kernel,
        in_specs=[SMEM] + [VMEM] * 11 + [ANY] * 4,
        out_specs=[VMEM] * 4 + [ANY] * 4,
        out_shape=[stream_like, gain_like, like((slots, model), F32), activation]
        + [cross_matrices] * 4,
        scratch_shapes=[
            pltpu.VMEM((3, model, model), BF16),
            pltpu.VMEM((5, model, model), BF16),
            pltpu.SemaphoreType.DMA((kernel_count, 3)),
            pltpu.SemaphoreType.DMA((5, kernel_count)),
        ],
        compiler_params=PARAMS,
        cost_estimate=work(20),
        name="cross_backward",
    )(
        kernel_places, stream_two_grad, stream_one, gain_all,
        normed_two, memory, attended_two, attended_one, branch_two,
        query_two_low, key_two_low, value_two_low, *cross_gathered,
    )
    cross_scatter = scatter_core(from_kernels(cross_grads, [rows] * 5), wide_count)

    gate_near = go_near(gate_far, branch_one)
    down_near = go_near(down_far, branch_one)
    query_one_low, key_one_low, value_one_low = pl.pallas_call(
        self_attention_backward_kernel,
        in_specs=[SMEM] * 2 + [VMEM] * 5 + [ANY] * 4,
        out_specs=[VMEM] * 3,
        out_shape=[activation] * 3,
        scratch_shapes=[
            pltpu.VMEM((1, model, model), BF16),
            pltpu.VMEM((tokens, 2 * tokens), F32),
            pltpu.VMEM((tokens, model), BF16),
            one_matrix_sems,
        ],
        compiler_params=PARAMS,
        cost_estimate=work(10),
        name="self_attention_backward",
    )(
        kernel_places, lengths, tie(branch_one, gate_near[0], down_near[0], loss_all), query_one, key_one, value_one, totals_one,
        *self_gathered,
    )
    def line_blocks(near, matrices, *others):
        _, came, held = near
        summed = held + tie(came, *others).astype(F32)
        width = summed.shape[-1]
        size = matrices * (summed.shape[0] // (matrices * 8 * narrow_count)) * 8 * narrow_count
        members = [
            summed[:size].reshape(matrices, narrow_count, -1, width).transpose(1, 0, 2, 3)
            .reshape(narrow_count, -1, width)
        ]
        if size < summed.shape[0]:
            members.append(summed[size:].reshape(narrow_count, -1, width))
        return jnp.concatenate(members, axis=1)

    def line_first(near, matrices, *others):
        blocks = line_blocks(near, matrices, *others)
        steps = range(0, narrow_count, 2)
        sent = jnp.stack([pick(blocks, narrow ^ (step + 1)) for step in steps]).astype(BF16)
        came = lax.ppermute(sent, "narrow", narrow_pairs(narrow_count, 1))
        return sent, came, [pick(blocks, narrow ^ step) for step in steps]

    def line_second(state, *others):
        _, came, kept = state
        came = tie(came, *others).astype(F32)
        terms = [kept[0] + came[0]]
        for place in range(1, len(kept)):
            sent = (kept[place] + came[place]).astype(BF16)
            terms.append(lax.ppermute(sent, "narrow", narrow_pairs(narrow_count, 2 * place)))
        return terms

    cross_far = go_far(cross_scatter, query_one_low)
    gate_line = line_first(gate_near, 2, query_one_low)

    extra = narrow_count * 8
    spare = extra * wide_count // kernel_count
    inputs_grad, *self_grads = pl.pallas_call(
        self_backward_kernel,
        in_specs=[SMEM] + [VMEM] * 9 + [ANY] * 4,
        out_specs=[VMEM] + [ANY] * 4,
        out_shape=[stream_like]
        + [like((part.shape[0], 3 * model // kernel_count + spare, model), BF16) for part in self_gathered],
        scratch_shapes=[
            pltpu.VMEM((3, model, model), BF16),
            pltpu.VMEM((3, model, model), BF16),
            pltpu.VMEM((spare, model), BF16),
            pltpu.SemaphoreType.DMA((kernel_count, 3)),
            pltpu.SemaphoreType.DMA((3, kernel_count)),
            pltpu.SemaphoreType.DMA((kernel_count,)),
        ],
        compiler_params=PARAMS,
        cost_estimate=work(12),
        name="self_backward",
    )(
        kernel_places, tie(stream_one_grad, gate_line[0], cross_far[0]), inputs,
        gain_all, normed_one, cross_gains, mlp_gains, query_one_low, key_one_low, value_one_low,
        *self_gathered,
    )
    self_scatter = scatter_core(from_kernels(self_grads, [rows] * 3 + [extra]), wide_count)

    cross_near = go_near(cross_far, inputs_grad)
    self_far = go_far(self_scatter, cross_near[0])
    down_line = line_first(down_near, 1, self_far[0])
    gate_terms = line_second(gate_line, self_far[0])
    cross_line = line_first(cross_near, 5, down_line[0], gate_terms[0], embedding_grad)
    self_near = go_near(self_far, cross_line[0])
    down_terms = line_second(down_line, self_near[0])
    gate_sum = add_terms(gate_terms, self_near[0]).reshape(2, shard, hidden_width)
    cross_terms = line_second(cross_line, down_terms[0], gate_sum)
    self_terms = scatter_narrow(
        line_blocks(self_near, 3, cross_terms[0]), narrow, narrow_count
    )
    down_sum = add_terms(down_terms, self_terms[0])
    cross_sum = add_terms(cross_terms, self_terms[0]).reshape(5, shard, model)
    self_sum = add_terms(self_terms)
    gains = pick(self_sum[3 * shard :].reshape(8, model // shard, shard), owner, 1)
    self_sum = self_sum[: 3 * shard].reshape(3, shard, model)

    return (
        activations,
        mean_loss,
        inputs_grad,
        memory_grad,
        gains[0],
        self_sum[0],
        self_sum[1],
        self_sum[2],
        cross_sum[4],
        gains[1],
        cross_sum[0],
        cross_sum[1],
        cross_sum[2],
        cross_sum[3],
        gains[2],
        gate_sum[0],
        gate_sum[1],
        down_sum,
        gains[3],
        embedding_grad,
    )


def solution(mesh):
    both = ("wide", "narrow")
    rows, flat = P(both, None), P(both)
    placed = (
        rows, rows, flat, rows, rows,
        flat, rows, rows, rows, rows,
        flat, rows, rows, rows, rows,
        flat, rows, rows, rows, flat,
        P("wide", "narrow"),
    )
    given = (
        rows, P(), rows, rows,
        flat, rows, rows, rows, rows,
        flat, rows, rows, rows, rows,
        flat, rows, rows, rows, flat,
        P("wide", "narrow"),
    )
    return jax.shard_map(
        per_device, mesh=mesh, in_specs=placed, out_specs=given, check_vma=False
    )
```

```python
import functools
import math

import jax
import jax.numpy as jnp
from jax import lax
from jax.experimental import pallas as pl
from jax.experimental.pallas import tpu as pltpu
from jax.sharding import PartitionSpec as P

HEADS = 12
EPSILON = 1e-06
NEGATIVE = -1e30
F32 = jnp.float32
BF16 = jnp.bfloat16
LANES = 128
ROW_TILE = 256
VOCAB_TILE = 512
MIX = math.sqrt(2.0 / math.pi)
CUBE = 0.044715
LOG2E = math.log2(math.e)
META_WIDE, META_TILES, META_LISTS = 0, 1, 2

VMEM = pl.BlockSpec(memory_space=pltpu.VMEM)
SMEM = pl.BlockSpec(memory_space=pltpu.SMEM)
ANY = pl.BlockSpec(memory_space=pl.ANY)
PARAMS = pltpu.CompilerParams(vmem_limit_bytes=60 * 2**20)


def work(gigaflops):
    return pl.CostEstimate(flops=gigaflops * 10**9, bytes_accessed=10**6, transcendentals=0)


def nn(left, right):
    return lax.dot_general(left, right, (((1,), (0,)), ((), ())), preferred_element_type=F32)


def nt(left, right):
    return lax.dot_general(left, right, (((1,), (1,)), ((), ())), preferred_element_type=F32)


def tn(left, right):
    return lax.dot_general(left, right, (((0,), (0,)), ((), ())), preferred_element_type=F32)


def like(shape, kind):
    return jax.ShapeDtypeStruct(shape, kind)


def stage_masks(count):
    up = [1 << bit for bit in range(1, count.bit_length() - 1)]
    return up, up[::-1]


def stage_pairs(count):
    even, odd = stage_masks(count)
    return [[(v, v ^ (odd if v % 2 else even)[i]) for v in range(count)] for i in range(len(even))]


def flip_pairs(count):
    return [(v, v ^ 1) for v in range(count)]


def slot_tables(count):
    tables = []
    for masks in stage_masks(count):
        slots = [0]
        for mask in masks:
            slots = slots + [slot ^ mask for slot in slots]
        tables.append(slots)
    even, odd = tables
    return (
        even + [1 ^ slot for slot in odd],
        odd + [1 ^ slot for slot in even],
    )


def slot_places(wide, count):
    even, odd = slot_tables(count)
    table = jnp.where(wide % 2 == 0, jnp.array(even, jnp.int32), jnp.array(odd, jnp.int32))
    return wide ^ table


def tie(value, *others):
    return lax.optimization_barrier((value, *others))[0]


def cross_core(value, count):
    return lax.ppermute(value, "wide", flip_pairs(count))


def gather_wide(block, count):
    held = block[None]
    *early, last = stage_pairs(count)
    for pairs in early:
        held = jnp.concatenate([held, lax.ppermute(held, "wide", pairs)], axis=0)
    came = lax.ppermute(held, "wide", last)
    return held, came, cross_core(held, count), cross_core(came, count)


def scatter_core(parts, count):
    sent, kept = cross_core(parts[3], count), cross_core(parts[2], count)
    return (parts[1], sent), (parts[0], kept)


def scatter_far(sent, kept, count):
    far = sent[0] + sent[1]
    came = lax.ppermute(far, "wide", stage_pairs(count)[-1])
    return far, came, kept


def scatter_near(came, kept, count):
    *rest, last = stage_pairs(count)[-2::-1]
    terms = (*kept, came)
    if not rest:
        far = sum(term[1].astype(F32) for term in terms).astype(BF16)
        return far, lax.ppermute(far, "wide", last), sum(term[0].astype(F32) for term in terms)
    held = sum(term.astype(F32) for term in terms)
    for pairs in rest:
        half = held.shape[0] // 2
        sent = lax.ppermute(held[half:].astype(BF16), "wide", pairs)
        held = held[:half] + sent.astype(F32)
    far = held[1].astype(BF16)
    return far, lax.ppermute(far, "wide", last), held[0]


def scatter_wide(parts, count):
    far, came, kept = scatter_far(*scatter_core(parts, count), count)
    far, came, held = scatter_near(came, kept, count)
    return held + came.astype(F32)


def narrow_pairs(count, step):
    return [(v, v ^ step) for v in range(count)]


def gather_narrow(block, count):
    return [block] + [
        lax.ppermute(block, "narrow", narrow_pairs(count, step)) for step in range(1, count)
    ]


def pick(values, place, axis=0):
    return lax.dynamic_index_in_dim(values, place.astype(jnp.uint32), axis, keepdims=False)


def in_line_order(pieces, narrow):
    stacked = jnp.stack(pieces)
    return [pick(stacked, narrow ^ place) for place in range(stacked.shape[0])]


def scatter_narrow(blocks, narrow, count):
    return [pick(blocks, narrow)] + [
        lax.ppermute(pick(blocks, narrow ^ step).astype(BF16), "narrow", narrow_pairs(count, step))
        for step in range(1, count)
    ]


def add_terms(terms, *others):
    terms = lax.optimization_barrier((*terms, *others))[: len(terms)]
    return sum(term.astype(F32) for term in terms)


def weight_copies(places, parts, start, target, rows, sems):
    size = parts[0].shape[0]
    copies = []
    for slot in range(len(parts) * size):
        place = pl.multiple_of(places[slot] * rows, 8)
        for matrix in range(target.shape[0]):
            copies.append(
                pltpu.make_async_copy(
                    parts[slot // size].at[slot % size, pl.ds(start + matrix * rows, rows), :],
                    target.at[matrix, pl.ds(place, rows), :],
                    sems.at[slot, matrix],
                )
            )
    return copies


def block_copies(places, value, start, rows, parts, sems):
    size = parts[0].shape[0]
    copies = []
    for slot in range(len(parts) * size):
        place = pl.multiple_of(places[slot] * rows, 8)
        copies.append(
            pltpu.make_async_copy(
                value.at[pl.ds(place, rows), :],
                parts[slot // size].at[slot % size, pl.ds(start, rows), :],
                sems.at[slot],
            )
        )
    return copies


def fetch(sources, targets, sems):
    copies = [
        pltpu.make_async_copy(source, target, sems.at[place])
        for place, (source, target) in enumerate(zip(sources, targets))
    ]
    for copy in copies:
        copy.start()
    return copies


def send_off(copies, more):
    for copy in more:
        copy.start()
    copies += more


def norm_scale(values):
    return lax.rsqrt(jnp.mean(values * values, axis=-1, keepdims=True) + EPSILON)


def norm_back(values, gain, grad):
    root = norm_scale(values)
    scaled = gain * grad
    gain_grad = jnp.sum(grad * values * root, axis=0, keepdims=True)
    inner = jnp.mean(scaled * values, axis=-1, keepdims=True)
    return root * scaled - values * (root * root * root) * inner, gain_grad


def query_segments(lengths, count):
    places = lax.broadcasted_iota(jnp.int32, (1, count), 1)
    segment = jnp.zeros((1, count), jnp.int32)
    edge = jnp.int32(0)
    for pair in range(lengths.shape[0]):
        edge = edge + lengths[pair]
        segment = segment + (places >= edge).astype(jnp.int32)
    return places, segment


def fill_self_bias(bias, lengths):
    count = bias.shape[1] // 2
    places, segment = query_segments(lengths, count)
    low = jnp.zeros((1, count), jnp.int32)
    edge = jnp.int32(0)
    for pair in range(lengths.shape[0]):
        edge = edge + lengths[pair]
        low = jnp.where(segment == pair + 1, edge, low)
    keys = lax.broadcasted_iota(jnp.int32, (bias.shape[0], count), 0)
    one = jnp.where((keys >= low) & (keys <= places), 0.0, NEGATIVE)
    bias[...] = jnp.concatenate([one, one], axis=1)


def fill_cross_bias(bias, lengths, sources):
    count = bias.shape[1] // 2
    places, segment = query_segments(lengths, count)
    low = jnp.zeros((1, count), jnp.int32)
    high = jnp.full((1, count), bias.shape[0], jnp.int32)
    edge = jnp.int32(0)
    for pair in range(lengths.shape[0]):
        low = jnp.where(segment == pair, edge, low)
        edge = edge + sources[pair]
        high = jnp.where(segment == pair, edge, high)
    low = jnp.concatenate([low, low], axis=1)
    high = jnp.concatenate([high, high], axis=1)
    keys = lax.broadcasted_iota(jnp.int32, bias.shape, 0)
    bias[...] = jnp.where((keys >= low) & (keys < high), 0.0, NEGATIVE)


def first_half(width):
    return lax.broadcasted_iota(jnp.int32, (1, width), 1) < width // 2


def apart(values, chosen):
    return jnp.concatenate([jnp.where(chosen, values, 0), jnp.where(chosen, 0, values)], axis=0)


def together(values, chosen):
    count = values.shape[0] // 2
    return jnp.where(chosen, values[:count], values[count:])


def attend(queries, keys, values, bias, outputs, totals, unroll):
    width = 2 * (queries.shape[1] // HEADS)
    chosen = first_half(width)

    def pair_of_heads(pair, carry):
        columns = pl.ds(pl.multiple_of(pair * width, width), width)
        scores = nt(keys[:, columns], apart(queries[:, columns], chosen)) + bias[...]
        highest = jnp.max(scores, axis=0, keepdims=True)
        raised = jnp.exp(scores - highest)
        summed = jnp.sum(raised, axis=0, keepdims=True)
        totals[pair] = highest + jnp.log(summed)
        weights = (raised * (1.0 / summed)).astype(BF16)
        mixed = nn(values[:, columns].T, weights).T
        outputs[:, columns] = together(mixed, chosen).astype(BF16)
        return carry

    lax.fori_loop(0, HEADS // 2, pair_of_heads, 0, unroll=unroll)


def attend_back(
    queries, keys, values, bias, totals, grads, query_low, key_low, value_low, first, last
):
    width = 2 * (queries.shape[1] // HEADS)
    chosen = first_half(width)

    for pair in range(first, last):
        columns = slice(pair * width, (pair + 1) * width)
        result = slice((pair - first) * width, (pair - first + 1) * width)
        query, grad = apart(queries[:, columns], chosen), apart(grads[:, columns], chosen)
        key = keys[:, columns]
        probs = jnp.exp(nt(key, query) + bias[...] - totals[pair])
        prob_grad = nt(values[:, columns], grad)
        value_low[:, result] = nn(probs.astype(BF16), grad).astype(BF16)
        weighted = probs * prob_grad
        centre = jnp.sum(weighted, axis=0, keepdims=True)
        score_grad = (weighted - probs * centre).astype(BF16)
        key_low[:, result] = nn(score_grad, query).astype(BF16)
        query_low[:, result] = together(nn(key.T, score_grad).T, chosen).astype(BF16)


def block_rows(weights, parts):
    return weights.shape[1] // (len(parts) * parts[0].shape[0])


def join_kernel(*refs):
    start = 0
    for ref in refs[:-1]:
        refs[-1][start : start + ref.shape[0], :] = ref[...]
        start += ref.shape[0]


def join_self_kernel(owner, lengths, gains, *refs):
    join_kernel(*refs)
    pack = refs[-1]
    shard, width = gains.shape[1], pack.shape[1]
    total = jnp.int32(0)
    for pair in range(lengths.shape[0]):
        total = total + lengths[pair]
    spot = lax.broadcasted_iota(jnp.int32, (8, shard), 0)
    high, low = (total // 16).astype(F32), (total % 16).astype(F32)
    own = jnp.concatenate([gains[...].astype(F32), jnp.zeros((8 - gains.shape[0], shard), F32)], axis=0)
    own = jnp.where(spot == 4, high, jnp.where(spot == 5, low, own)).astype(BF16)
    row = lax.broadcasted_iota(jnp.int32, (shard, width), 0)
    column = lax.broadcasted_iota(jnp.int32, (shard, width), 1)
    spread = (row + owner[0] * shard == column).astype(BF16)
    pack[pack.shape[0] - 8 :, :] = nn(own, spread).astype(BF16)


def join_rows(*members):
    if any(member.shape[0] % 8 for member in members):
        return jnp.concatenate(members, axis=0)
    rows = sum(member.shape[0] for member in members)
    return pl.pallas_call(
        join_kernel,
        in_specs=[VMEM] * len(members),
        out_specs=VMEM,
        out_shape=like((rows, members[0].shape[1]), members[0].dtype),
        cost_estimate=work(1),
        name="join_rows",
    )(*members)


def line_kernel(narrow, *refs, sizes):
    pieces, block = refs[:-1], refs[-1]
    start = 0
    for size in sizes:
        for step, piece in enumerate(pieces):
            place = pl.multiple_of(start * len(pieces) + (narrow[0] ^ step) * size, 8)
            block[pl.ds(place, size), :] = piece[start : start + size]
        start += size


def line_pair_kernel(narrow, even, odd, block, *, sizes):
    pieces = [(odd if step % 2 else even).at[step // 2] for step in range(2 * even.shape[0])]
    start = 0
    for size in sizes:
        for step, piece in enumerate(pieces):
            place = pl.multiple_of(start * len(pieces) + (narrow[0] ^ step) * size, 8)
            block[pl.ds(place, size), :] = piece[start : start + size]
        start += size


def self_forward_kernel(
    places, lengths, inputs, *refs,
):
    parts = refs[:4]
    normed, query, key, value, attended, totals, stream, gains = refs[4:12]
    weights, gain_parts, bias, sems, gain_sems = refs[12:]
    size = parts[0].shape[0]
    rows = block_rows(weights, parts)
    gain_copies = [
        pltpu.make_async_copy(
            parts[slot // size].at[slot % size, pl.ds(4 * rows, gain_parts.shape[1]), :],
            gain_parts.at[slot],
            gain_sems.at[slot],
        )
        for slot in range(4 * size)
    ]
    copies = weight_copies(places, parts, 0, weights, rows, sems)
    for copy in gain_copies + copies:
        copy.start()
    values = inputs[...].astype(F32)
    fill_self_bias(bias, lengths)
    scaled = values * norm_scale(values)
    for copy in gain_copies:
        copy.wait()
    members = gain_parts[...].astype(F32).reshape(-1, 8, gains.shape[1])
    summed = members[0]
    for member in range(1, members.shape[0]):
        summed = summed + members[member]
    gains[...] = summed
    low = (scaled * summed[0:1]).astype(BF16)
    normed[...] = low
    for copy in copies:
        copy.wait()
    query[...] = nn(low, weights[0]).astype(BF16)
    key[...] = nn(low, weights[1]).astype(BF16)
    value[...] = nn(low, weights[2]).astype(BF16)
    attend(query, key, value, bias, attended, totals, HEADS // 2)
    stream[...] = values + nn(attended[...], weights[3])


def memory_kernel(places, memory, *refs):
    parts = refs[:4]
    key, value, weights, sems = refs[4:]
    rows = block_rows(weights, parts)
    copies = weight_copies(places, parts, rows, weights, rows, sems)
    for copy in copies:
        copy.start()
    for copy in copies:
        copy.wait()
    key[...] = nn(memory[...], weights[0]).astype(BF16)
    value[...] = nn(memory[...], weights[1]).astype(BF16)


def cross_forward_kernel(
    places, lengths, sources, stream_in, gains, key, value, *refs,
):
    parts = refs[:4]
    normed, query, attended, totals, stream, weights, bias, sems = refs[4:]
    rows = block_rows(weights, parts)
    copies = weight_copies(places, parts, 0, weights.at[pl.ds(0, 1)], rows, sems.at[0])
    copies += weight_copies(places, parts, 3 * rows, weights.at[pl.ds(1, 1)], rows, sems.at[1])
    for copy in copies:
        copy.start()
    values = stream_in[...]
    fill_cross_bias(bias, lengths, sources)
    low = (values * norm_scale(values) * gains[1:2]).astype(BF16)
    normed[...] = low
    for copy in copies:
        copy.wait()
    query[...] = nn(low, weights[0]).astype(BF16)
    attend(query, key, value, bias, attended, totals, HEADS // 4)
    stream[...] = values + nn(attended[...], weights[1])


def mlp_forward_kernel(
    places, stream_in, gains, side, *refs,
):
    parts, down_parts = refs[:4], refs[4:8]
    normed, gate, up, hidden, stream, activations, exit_normed = refs[8:15]
    weights, down, sems, down_sems = refs[15:]
    rows, down_rows = block_rows(weights, parts), block_rows(down, down_parts)
    first = weight_copies(places, parts, 0, weights, rows, sems)
    last = weight_copies(
        places, down_parts, down_parts[0].shape[1] - down_rows, down, down_rows, down_sems
    )
    for copy in first + last:
        copy.start()
    values = stream_in[...]
    low = (values * norm_scale(values) * gains[2:3]).astype(BF16)
    normed[...] = low
    for copy in first:
        copy.wait()
    width = weights.shape[2]
    step = width // 4
    for part in range(4):
        columns = pl.ds(part * step, step)
        gate_pre = nn(low, weights[0, :, columns])
        up_pre = nn(low, weights[1, :, columns])
        gate[:, columns] = gate_pre
        up[:, columns] = up_pre
        bent = jnp.tanh(MIX * (gate_pre + CUBE * (gate_pre * gate_pre * gate_pre)))
        hidden[:, columns] = (0.5 * gate_pre * (1.0 + bent) * up_pre).astype(BF16)
    for copy in last:
        copy.wait()
    out = values + nn(hidden[...], down[0])
    stream[...] = out
    activations[...] = out.astype(BF16)
    count = out.shape[0]
    exit_normed[:count] = (out * norm_scale(out) * gains[3:4]).astype(BF16)
    exit_normed[count:] = side[...]


def exit_scores_kernel(meta, slot_of, *refs, vocab, scale):
    parts = refs[:4]
    source, raised, across, stats = refs[4:8]
    table, tokens, columns, landed, scores, table_sem, sems = refs[8:]
    size = parts[0].shape[0]
    members = 4 * size
    ring = landed.shape[0]
    count = parts[0].shape[1] - 8
    step = pl.program_id(0)
    tile = raised.shape[0]
    starts, counts = META_LISTS, META_LISTS + members

    def fetch(member):
        slot = slot_of[member]
        for part in range(4):

            @pl.when(slot // size == part)
            def start():
                pltpu.make_async_copy(
                    parts[part].at[slot % size], landed.at[member % ring], sems.at[member % ring]
                ).start()

    @pl.when(step == 0)
    def load():
        whole = pltpu.make_async_copy(source, table, table_sem)
        for member in range(min(ring, members)):
            fetch(member)
        whole.start()
        tokens[...] = jnp.zeros_like(tokens)
        columns[...] = jnp.zeros_like(columns)
        lanes = -(-count // LANES) * LANES
        spots = lax.broadcasted_iota(jnp.int32, (1, lanes), 1)
        for member in range(members):
            pltpu.make_async_copy(
                parts[0].at[0], landed.at[member % ring], sems.at[member % ring]
            ).wait()
            begin = pl.multiple_of(meta[starts + member], 16)
            block = landed[member % ring]
            tokens[pl.ds(begin, count), :] = block[:count]
            side = block[count:, :lanes].astype(F32)
            wanted = side[0:1] * 256.0 + side[1:2]
            weight = jnp.where(spots < meta[counts + member], 1.0, 0.0)
            packed = jnp.concatenate(
                [weight, wanted, jnp.zeros((LANES - 2, lanes), F32)], axis=0
            )
            columns[pl.ds(begin, count), :] = packed.T[:count]
            if member + ring < members:
                fetch(member + ring)
        whole.wait()

    spot = lax.broadcasted_iota(jnp.int32, (tile, LANES), 1)

    @pl.when(step < meta[META_TILES])
    def compute():
        here = pl.ds(pl.multiple_of(step * tile, tile), tile)
        own = tokens[here, :]
        column = columns[here, :]
        across[...] = own.T
        width = scores.shape[1]
        lanes = lax.broadcasted_iota(jnp.int32, (tile, LANES), 1)
        wanted = column[:, 1:2].astype(jnp.int32) - meta[META_WIDE] * vocab
        wanted = jnp.where(wanted < vocab, wanted, -1)
        peaks = jnp.full((tile, LANES), NEGATIVE, F32)
        found = jnp.zeros((tile, LANES), F32)
        for first in range(0, width, VOCAB_TILE):
            part = nn(own, table[:, first : first + VOCAB_TILE])
            for inner in range(0, VOCAB_TILE, LANES):
                piece = part[:, inner : inner + LANES]
                offset = first + inner
                if offset + LANES > vocab:
                    piece = jnp.where(lanes < vocab - offset, piece, NEGATIVE)
                scores[:, offset : offset + LANES] = piece
                peaks = jnp.maximum(peaks, piece)
                found = found + jnp.where(lanes == wanted - offset, piece, 0.0)
        highest = jnp.max(peaks, axis=1, keepdims=True)
        sums = jnp.zeros((tile, LANES), F32)
        for offset in range(0, width, LANES):
            piece = jnp.exp2((scores[:, offset : offset + LANES] - highest) * (scale * LOG2E))
            raised[:, offset : offset + LANES] = piece.astype(BF16)
            sums = sums + piece
        summed = jnp.sum(sums, axis=1, keepdims=True)
        picked = jnp.sum(found, axis=1, keepdims=True)
        values = (highest * scale, summed, picked * scale, column[:, 0:1], column[:, 1:2])
        packed = jnp.zeros((tile, LANES), F32)
        for place, value in enumerate(values):
            packed = jnp.where(spot == place, value, packed)
        stats[...] = packed.T[:8]

    @pl.when(step >= meta[META_TILES])
    def skip():
        rows = lax.broadcasted_iota(jnp.int32, stats.shape, 0)
        stats[...] = jnp.where(rows == 1, 1.0, 0.0)


def logit_grads(meta, raised, factors, first, width, vocab):
    tile = raised.shape[0]
    columns = jnp.concatenate(
        [factors[...], jnp.zeros((LANES - factors.shape[0], tile), F32)], axis=0
    ).T
    factor, at_target = columns[:, 0:1], columns[:, 1:2]
    wanted = columns[:, 2:3].astype(jnp.int32) - meta[META_WIDE] * vocab
    wanted = jnp.where(wanted < vocab, wanted, -1) - first
    lanes = lax.broadcasted_iota(jnp.int32, (tile, width), 1)

    def chunk(start):
        part = raised[:, start : start + width].astype(F32) * factor
        return jnp.where(lanes == wanted - start, at_target, part).astype(BF16)

    return chunk


def exit_tokens_kernel(meta, places, *refs, vocab):
    source, raised, factors = refs[:3]
    parts = refs[3:7]
    table, token_grad, landed, table_sem, sems = refs[7:]
    size = parts[0].shape[0]
    members = 4 * size
    count = parts[0].shape[1]
    starts, counts = META_LISTS, META_LISTS + members
    step = pl.program_id(0)
    tile = raised.shape[0]

    @pl.when(step == 0)
    def load():
        whole = pltpu.make_async_copy(source, table, table_sem)
        whole.start()
        whole.wait()

    @pl.when(step < meta[META_TILES])
    def compute():
        chunk = logit_grads(meta, raised, factors, 0, VOCAB_TILE, vocab)
        grad = jnp.zeros((tile, token_grad.shape[1]), F32)
        for first in range(0, raised.shape[1], VOCAB_TILE):
            grad = grad + nt(chunk(first), table[:, first : first + VOCAB_TILE])
        token_grad[pl.ds(pl.multiple_of(step * tile, tile), tile), :] = grad.astype(BF16)

    @pl.when(step == pl.num_programs(0) - 1)
    def finish():
        copies = []
        spots = lax.broadcasted_iota(jnp.int32, (count, 1), 0)
        for slot in range(members):
            if slot >= 2:
                copies[slot - 2].wait()
            member = places[slot]
            begin = pl.multiple_of(meta[starts + member], 16)
            block = token_grad[pl.ds(begin, count), :].astype(F32)
            landed[slot % 2] = jnp.where(spots < meta[counts + member], block, 0.0).astype(BF16)
            copy = pltpu.make_async_copy(
                landed.at[slot % 2], parts[slot // size].at[slot % size], sems.at[slot % 2]
            )
            copy.start()
            copies.append(copy)
        for copy in copies[-2:]:
            copy.wait()


def exit_table_kernel(meta, raised, across, factors, *refs, first, vocab):
    table_grad, total = refs[-2:]
    step = pl.program_id(0)
    width = min(VOCAB_TILE, raised.shape[1])

    @pl.when(step == 0)
    def clear():
        total[...] = jnp.zeros_like(total)

    def compute(raised, across, factors):
        chunk = logit_grads(meta, raised, factors, first, width, vocab)
        for start in range(0, raised.shape[1], width):
            total[:, start : start + width] += nn(across[...], chunk(start))

    @pl.when(2 * step + 1 < meta[META_TILES])
    def both():
        compute(raised, across, factors)

    @pl.when(2 * step + 1 == meta[META_TILES])
    def one():
        half = raised.shape[0] // 2
        compute(raised.at[:half], across.at[:, :half], factors.at[:, :half])

    @pl.when(step == pl.num_programs(0) - 1)
    def finish():
        table_grad[...] = total[...].astype(BF16)


def mlp_backward_kernel(
    places, grad_in, stream_three, gain, *refs,
):
    far, refs = refs[:5], refs[5:]
    parts, down_parts = refs[:4], refs[4:8]
    stream_grad, gains = refs[8:10]
    grad_parts, down_grad_parts = refs[10:14], refs[14:18]
    weights, down, gate_low, up_low, result, down_result, sems, down_sems, out_sems = refs[18:27]
    gate, up, normed, hidden, stream_two = refs[27:32]
    rows, down_rows = block_rows(weights, parts), block_rows(down, down_parts)
    first = weight_copies(
        places, down_parts, down_parts[0].shape[1] - down_rows, down, down_rows, down_sems
    )
    last = weight_copies(places, parts, 0, weights, rows, sems)
    for copy in first:
        copy.start()
    near = fetch(far, refs[27:32], refs[32])
    for copy in last:
        copy.start()
    stream_back, exit_gain_grad = norm_back(stream_three[...], gain[3:4], grad_in[...])
    branch = stream_back.astype(BF16)
    for copy in first + near[:3]:
        copy.wait()
    width = weights.shape[2]
    step = width // 4
    normed_across = normed[...].T
    sent = []
    for part in range(4):
        columns = pl.ds(part * step, step)
        gate_pre = gate[:, columns]
        up_pre = up[:, columns]
        hidden_grad = nt(branch, down[0, columns, :])
        bent = jnp.tanh(MIX * (gate_pre + CUBE * (gate_pre * gate_pre * gate_pre)))
        slope = 0.5 * (1.0 + bent) + 0.5 * gate_pre * (1.0 - bent * bent) * (
            MIX * (1.0 + 3.0 * CUBE * gate_pre * gate_pre)
        )
        gate_low[:, columns] = (hidden_grad * up_pre * slope).astype(BF16)
        up_low[:, columns] = (hidden_grad * (0.5 * gate_pre * (1.0 + bent))).astype(BF16)
        result[0, :, columns] = nn(normed_across, gate_low[:, columns]).astype(BF16)
        result[1, :, columns] = nn(normed_across, up_low[:, columns]).astype(BF16)
    for matrix in range(2):
        send_off(
            sent,
            block_copies(
                places, result.at[matrix], matrix * rows, rows, grad_parts, out_sems.at[matrix]
            ),
        )
    near[3].wait()
    for part in range(4):
        columns = pl.ds(part * step, step)
        down_result[columns, :] = nn(hidden[:, columns].T, branch).astype(BF16)
    send_off(
        sent, block_copies(places, down_result, 0, down_rows, down_grad_parts, out_sems.at[2])
    )
    for copy in last + near[4:]:
        copy.wait()
    normed_grad = nt(gate_low[...], weights[0]) + nt(up_low[...], weights[1])
    branch_in, gain_grad = norm_back(stream_two[...], gain[2:3], normed_grad)
    stream_grad[...] = stream_back + branch_in
    gains[...] = jnp.concatenate(
        [gain_grad, exit_gain_grad, jnp.zeros((6, gain_grad.shape[1]), F32)], axis=0
    )
    for copy in sent:
        copy.wait()


def cross_attention_first_kernel(
    places, lengths, sources, grad_in, query, key, value, totals, *refs,
):
    parts = refs[:4]
    branch, attended_grad, query_low, key_low, value_low, weights, bias, sems = refs[4:]
    rows = block_rows(weights, parts)
    copies = weight_copies(places, parts, 3 * rows, weights, rows, sems)
    for copy in copies:
        copy.start()
    fill_cross_bias(bias, lengths, sources)
    branch[...] = grad_in[...].astype(BF16)
    for copy in copies:
        copy.wait()
    attended_grad[...] = nt(branch[...], weights[0]).astype(BF16)
    attend_back(
        query, key, value, bias, totals, attended_grad, query_low, key_low, value_low,
        0, HEADS // 4,
    )


def cross_attention_last_kernel(
    lengths, sources, attended_grad, query, key, value, totals,
    first_query, first_key, first_value, query_low, key_low, value_low, bias,
):
    middle = first_query.shape[1]
    fill_cross_bias(bias, lengths, sources)
    attend_back(
        query, key, value, bias, totals, attended_grad,
        query_low.at[:, middle:], key_low.at[:, middle:], value_low.at[:, middle:],
        HEADS // 4, HEADS // 2,
    )
    query_low[:, :middle] = first_query[...]
    key_low[:, :middle] = first_key[...]
    value_low[:, :middle] = first_value[...]


def cross_backward_kernel(
    places, gain, memory, key_low, *refs,
):
    far, refs = refs[:8], refs[8:]
    parts = refs[:4]
    stream_grad, gains, memory_grad, self_branch = refs[4:8]
    grad_parts = refs[8:12]
    weights, results, sems, out_sems = refs[12:16]
    value_low, normed, query_low, attended, branch, stream_in, grad_in, self_attended = refs[16:24]
    near = fetch(far, refs[16:24], refs[24])
    rows = block_rows(weights, parts)
    copies = weight_copies(places, parts, 0, weights, rows, sems)
    for copy in copies:
        copy.start()
    sent = []

    def weight_grad(matrix, left_across, right):
        results[matrix] = nn(left_across, right[...]).astype(BF16)
        send_off(
            sent,
            block_copies(
                places, results.at[matrix], matrix * rows, rows, grad_parts, out_sems.at[matrix]
            ),
        )

    memory_across = memory[...].T
    weight_grad(1, memory_across, key_low)
    near[0].wait()
    weight_grad(2, memory_across, value_low)
    for copy in near[1:]:
        copy.wait()
    weight_grad(0, normed[...].T, query_low)
    weight_grad(3, attended[...].T, branch)
    for copy in copies:
        copy.wait()
    normed_grad = nt(query_low[...], weights[0])
    branch_in, gain_grad = norm_back(stream_in[...], gain[1:2], normed_grad)
    total = grad_in[...] + branch_in
    stream_grad[...] = total
    self_branch[...] = total.astype(BF16)
    weight_grad(4, self_attended[...].T, self_branch)
    gains[...] = jnp.broadcast_to(gain_grad, gains.shape)
    memory_grad[...] = nt(key_low[...], weights[1]) + nt(value_low[...], weights[2])
    for copy in sent:
        copy.wait()


def self_attention_backward_kernel(
    places, lengths, branch, query, key, value, totals, *refs,
):
    parts = refs[:4]
    query_low, key_low, value_low, weights, bias, attended_grad, sems = refs[4:]
    rows = block_rows(weights, parts)
    copies = weight_copies(places, parts, 3 * rows, weights, rows, sems)
    for copy in copies:
        copy.start()
    fill_self_bias(bias, lengths)
    for copy in copies:
        copy.wait()
    attended_grad[...] = nt(branch[...], weights[0]).astype(BF16)
    attend_back(
        query, key, value, bias, totals, attended_grad, query_low, key_low, value_low,
        0, HEADS // 2,
    )


def self_backward_kernel(
    places, grad_in, inputs, gain, normed, cross_gains, mlp_gains,
    query_low, key_low, value_low, *refs,
):
    parts = refs[:4]
    stream_grad = refs[4]
    grad_parts = refs[5:9]
    weights, results, terms, sems, out_sems, term_sems = refs[9:]
    rows = block_rows(weights, parts)
    size = grad_parts[0].shape[0]
    copies = weight_copies(places, parts, 0, weights, rows, sems)
    for copy in copies:
        copy.start()
    sent = []
    normed_across = normed[...].T
    for matrix, low in enumerate((query_low, key_low, value_low)):
        results[matrix] = nn(normed_across, low[...]).astype(BF16)
        send_off(
            sent,
            block_copies(
                places, results.at[matrix], matrix * rows, rows, grad_parts, out_sems.at[matrix]
            ),
        )
    for copy in copies:
        copy.wait()
    normed_grad = (
        nt(query_low[...], weights[0])
        + nt(key_low[...], weights[1])
        + nt(value_low[...], weights[2])
    )
    branch_in, gain_grad = norm_back(inputs[...].astype(F32), gain[0:1], normed_grad)
    stream_grad[...] = grad_in[...] + branch_in
    spot = lax.broadcasted_iota(jnp.int32, (8, gain_grad.shape[1]), 0)
    row = jnp.where(spot == 0, gain_grad, 0.0)
    row = jnp.where(spot == 1, cross_gains[0:1], row)
    row = jnp.where(spot == 2, mlp_gains[0:1], row)
    row = jnp.where(spot == 3, mlp_gains[1:2], row).astype(BF16)
    for start in range(0, terms.shape[0], 8):
        terms[start : start + 8] = row
    send_off(
        sent,
        [
            pltpu.make_async_copy(
                terms,
                grad_parts[slot // size].at[slot % size, pl.ds(3 * rows, terms.shape[0]), :],
                term_sems.at[slot],
            )
            for slot in range(4 * size)
        ],
    )
    for copy in sent:
        copy.wait()


def per_device(
    inputs,
    memory,
    targets,
    tgt_lengths,
    src_lengths,
    self_gain,
    self_query,
    self_key,
    self_value,
    self_out,
    cross_gain,
    cross_query,
    cross_key,
    cross_value,
    cross_out,
    mlp_gain,
    mlp_gate,
    mlp_up,
    mlp_down,
    exit_gain,
    embedding,
):
    tokens, model = inputs.shape
    slots = memory.shape[0]
    hidden_width = mlp_gate.shape[1]
    pair_slots = tgt_lengths.shape[1]
    wide_count = lax.axis_size("wide")
    narrow_count = lax.axis_size("narrow")
    wide = lax.axis_index("wide")
    narrow = lax.axis_index("narrow")
    slot_total = tokens * wide_count * narrow_count
    scale = 1.0 / math.sqrt(model)
    places = slot_places(wide, wide_count)
    lengths, sources = tgt_lengths[0], src_lengths[0]
    shard = self_query.shape[0]
    rows = shard * narrow_count
    down_rows = mlp_down.shape[0] * narrow_count

    aligned = rows % 8 == 0
    kernel_places = places if aligned else jnp.arange(4, dtype=jnp.int32)
    kernel_count = wide_count if aligned else 4
    ids = jnp.arange(wide_count, dtype=jnp.int32)
    order = places[None, :] == ids[:, None]

    def reorder(matrix, blocks):
        flat = blocks.reshape(wide_count, -1)
        return nn(matrix.astype(BF16), flat).astype(BF16).reshape(blocks.shape)

    def for_kernels(parts, sizes):
        if aligned:
            return parts
        whole, start, members = jnp.concatenate(parts, axis=0), 0, []
        for size in sizes:
            ordered = reorder(order, whole[:, start : start + size])
            members.append(ordered.reshape(4, -1, whole.shape[-1]))
            start += size
        return jnp.split(jnp.concatenate(members, axis=1), 4)

    def from_kernels(parts, sizes):
        if aligned:
            return parts
        whole, start, members = jnp.concatenate(parts, axis=0), 0, []
        for size in sizes:
            extent = size * wide_count // 4
            member = whole[:, start : start + extent].reshape(wide_count, size, -1)
            members.append(reorder(order.T, member))
            start += extent
        return jnp.split(jnp.concatenate(members, axis=1), 4)

    def line_block(pieces, sizes, *others):
        pieces = lax.optimization_barrier((*pieces, *others))[: len(pieces)]
        if all(size % 8 == 0 for size in sizes):
            return pl.pallas_call(
                functools.partial(line_kernel, sizes=sizes),
                in_specs=[SMEM] + [VMEM] * len(pieces),
                out_specs=VMEM,
                out_shape=like((pieces[0].shape[0] * len(pieces), pieces[0].shape[1]), BF16),
                compiler_params=PARAMS,
                cost_estimate=work(30),
                name="line_block",
            )(narrow[None], *pieces)
        ordered, start, members = in_line_order(pieces, narrow), 0, []
        for size in sizes:
            members += [piece[start : start + size] for piece in ordered]
            start += size
        return jnp.concatenate(members, axis=0)

    self_sizes, cross_sizes = [shard] * 4 + [8], [shard] * 4 + [mlp_down.shape[0]]
    gate_sizes = [shard] * 2
    count = jnp.sum(lengths)
    owner = wide * narrow_count + narrow
    gain_shards = jnp.stack([self_gain, cross_gain, mlp_gain, exit_gain])
    def join_self():
        return pl.pallas_call(
            join_self_kernel,
            in_specs=[SMEM] * 2 + [VMEM] * 5,
            out_specs=VMEM,
            out_shape=like((sum(self_sizes), model), BF16),
            cost_estimate=work(1),
            name="join_self",
        )(owner[None], lengths, gain_shards, self_query, self_key, self_value, self_out)

    numbers = jnp.broadcast_to(
        jnp.stack([count // 16, count % 16])[:, None], (2, shard)
    ).astype(BF16)
    own_rows = jnp.concatenate([gain_shards, numbers, jnp.zeros((2, shard), BF16)], axis=0)
    own_rows = jnp.tile(own_rows, (1, model // shard))
    own_columns = jnp.arange(model, dtype=jnp.int32)[None, :] // shard == owner
    own_rows = jnp.where(own_columns, own_rows, 0)
    self_pack = (
        join_self()
        if aligned
        else join_rows(self_query, self_key, self_value, self_out, own_rows)
    )
    members = (cross_query, cross_key, cross_value, cross_out, mlp_down)
    side = jnp.stack([targets // 256, targets % 256]).astype(BF16)
    side = jnp.pad(side, ((0, 6), (0, model - tokens)))

    self_line = gather_narrow(self_pack, narrow_count)
    self_block = line_block(self_line, self_sizes)

    vocab = embedding.shape[0]
    padded = -(-vocab // VOCAB_TILE) * VOCAB_TILE
    turned = jnp.pad(embedding.T, ((0, 0), (0, padded - vocab)))
    table = lax.all_gather(tie(turned, *self_line), "narrow", axis=0, tiled=True)

    *early, last = stage_pairs(wide_count)

    def gather_early(block, *others):
        held = block[None]
        for pairs in early:
            came = lax.ppermute(held, "wide", pairs)
            if others:
                came = tie(came, *others)
            held = jnp.concatenate([held, came], axis=0)
        return held

    cross_pack, gate_pack = join_rows(*members), join_rows(mlp_gate, mlp_up)

    def line_even(pack):
        return jnp.stack(
            [pack]
            + [
                lax.ppermute(pack, "narrow", narrow_pairs(narrow_count, step))
                for step in range(2, narrow_count, 2)
            ]
        )

    def line_odd(even):
        return lax.ppermute(even, "narrow", narrow_pairs(narrow_count, 1))

    def line_pair(even, odd, sizes):
        return pl.pallas_call(
            functools.partial(line_pair_kernel, sizes=sizes),
            in_specs=[SMEM] + [VMEM] * 2,
            out_specs=VMEM,
            out_shape=like((narrow_count * even.shape[1], even.shape[2]), BF16),
            compiler_params=PARAMS,
            cost_estimate=work(1),
            name="line_pair",
        )(narrow[None], even, odd)

    self_held = gather_early(self_block)
    if aligned:
        cross_even = line_even(tie(cross_pack, *self_line))
        cross_odd = line_odd(cross_even)
        gate_even = line_even(tie(gate_pack, cross_even))
        gate_odd = line_odd(gate_even)
        self_held = tie(self_held, cross_even)
        cross_block = line_pair(cross_even, tie(cross_odd, self_held), cross_sizes)
    else:
        cross_block = line_block(gather_narrow(cross_pack, narrow_count), cross_sizes)
        gate_block = line_block(gather_narrow(gate_pack, narrow_count), gate_sizes)
    self_came = lax.ppermute(self_held, "wide", last)
    self_parts = (
        self_held, self_came, cross_core(self_held, wide_count), cross_core(self_came, wide_count)
    )
    cross_block = tie(cross_block, self_came)
    if aligned:
        cross_block = tie(cross_block, gate_even)
    cross_held = gather_early(cross_block)
    if aligned:
        cross_held = tie(cross_held, gate_odd)
        gate_block = line_pair(gate_even, gate_odd, gate_sizes)
    cross_came = lax.ppermute(cross_held, "wide", last)

    head_rows = like((HEADS // 2, 1, 2 * tokens), F32)
    activation = like((tokens, model), BF16)
    stream_like = like((tokens, model), F32)
    matrix_sems = pltpu.SemaphoreType.DMA((kernel_count, 4))
    one_matrix_sems = pltpu.SemaphoreType.DMA((kernel_count, 1))

    self_gathered = for_kernels(self_parts, [size * narrow_count for size in self_sizes])
    (
        normed_one, query_one, key_one, value_one, attended_one, totals_one, stream_one, gain_all,
    ) = pl.pallas_call(
        self_forward_kernel,
        in_specs=[SMEM, SMEM, VMEM] + [ANY] * 4,
        out_specs=[VMEM] * 8,
        out_shape=[activation] * 5 + [head_rows, stream_like, like((8, model), F32)],
        scratch_shapes=[
            pltpu.VMEM((4, model, model), BF16),
            pltpu.VMEM((kernel_count, 8 * narrow_count * wide_count // kernel_count, model), BF16),
            pltpu.VMEM((tokens, 2 * tokens), F32),
            matrix_sems,
            pltpu.SemaphoreType.DMA((kernel_count,)),
        ],
        compiler_params=PARAMS,
        cost_estimate=work(1),
        name="self_forward",
    )(kernel_places, lengths, tie(inputs, cross_held), *self_gathered)

    numbers = (gain_all[4] * 16.0 + gain_all[5]).reshape(wide_count, narrow_count, shard)[:, :, 0]
    numbers = jnp.sum(
        jnp.where(jnp.arange(narrow_count)[None, :] == narrow, numbers, 0.0), axis=1
    ).astype(jnp.int32)
    extents = (numbers + 15) // 16 * 16
    starts = jnp.sum(jnp.where(ids[None, :] < ids[:, None], extents[None, :], 0), axis=1)
    needed = (jnp.sum(extents) + ROW_TILE - 1) // ROW_TILE
    meta = jnp.concatenate([jnp.stack([wide, needed]), starts, numbers])
    slot_of = jnp.sum(jnp.where(order, ids[None, :], 0), axis=1)

    cross_came = tie(cross_came, stream_one)
    cross_parts = (
        cross_held, cross_came, cross_core(cross_held, wide_count), cross_core(cross_came, wide_count)
    )
    cross_gathered = for_kernels(cross_parts, [size * narrow_count for size in cross_sizes])

    key_two, value_two = pl.pallas_call(
        memory_kernel,
        in_specs=[SMEM, VMEM] + [ANY] * 4,
        out_specs=[VMEM] * 2,
        out_shape=[like((slots, model), BF16)] * 2,
        scratch_shapes=[
            pltpu.VMEM((2, model, model), BF16),
            pltpu.SemaphoreType.DMA((kernel_count, 2)),
        ],
        compiler_params=PARAMS,
        cost_estimate=work(1),
        name="memory_projection",
    )(kernel_places, memory, *cross_gathered)

    gate_held = gather_early(tie(gate_block, cross_came), key_two)
    gate_came = lax.ppermute(gate_held, "wide", last)

    normed_two, query_two, attended_two, totals_two, stream_two = pl.pallas_call(
        cross_forward_kernel,
        in_specs=[SMEM, SMEM, SMEM, VMEM, VMEM, VMEM, VMEM] + [ANY] * 4,
        out_specs=[VMEM] * 5,
        out_shape=[activation] * 3 + [head_rows, stream_like],
        scratch_shapes=[
            pltpu.VMEM((2, model, model), BF16),
            pltpu.VMEM((slots, 2 * tokens), F32),
            pltpu.SemaphoreType.DMA((2, kernel_count, 1)),
        ],
        compiler_params=PARAMS,
        cost_estimate=work(1),
        name="cross_forward",
    )(
        kernel_places, lengths, sources, tie(stream_one, gate_held), gain_all, key_two, value_two,
        *cross_gathered,
    )

    gate_came = tie(gate_came, stream_two)
    gate_parts = (
        gate_held, gate_came, cross_core(gate_held, wide_count), cross_core(gate_came, wide_count)
    )
    gate_gathered = for_kernels(gate_parts, [size * narrow_count for size in gate_sizes])

    wide_f32 = like((tokens, hidden_width), F32)
    wide_low = like((tokens, hidden_width), BF16)
    normed_three, gate_pre, up_pre, hidden, stream_three, activations, normed_four = pl.pallas_call(
        mlp_forward_kernel,
        in_specs=[SMEM, VMEM, VMEM, VMEM] + [ANY] * 8,
        out_specs=[VMEM] * 7,
        out_shape=[
            activation, wide_f32, wide_f32, wide_low, stream_like, activation,
            like((tokens + 8, model), BF16),
        ],
        scratch_shapes=[
            pltpu.VMEM((2, model, hidden_width), BF16),
            pltpu.VMEM((1, hidden_width, model), BF16),
            pltpu.SemaphoreType.DMA((kernel_count, 2)),
            one_matrix_sems,
        ],
        compiler_params=PARAMS,
        cost_estimate=work(1),
        name="mlp_forward",
    )(kernel_places, stream_two, gain_all, side, *gate_gathered, *cross_gathered)

    exit_held = gather_early(normed_four)
    exit_came = tie(lax.ppermute(exit_held, "wide", last), table)
    exit_parts = (
        exit_held, exit_came, cross_core(exit_held, wide_count), cross_core(exit_came, wide_count)
    )
    group = tokens * wide_count
    tiles = -(-group // (2 * ROW_TILE)) * 2
    kept = lambda i, meta: jnp.minimum(i, meta[META_TILES] - 1)
    kept_pair = lambda i, meta: jnp.minimum(i, (meta[META_TILES] - 1) // 2)

    raised, tokens_across, stats = pl.pallas_call(
        functools.partial(exit_scores_kernel, vocab=vocab, scale=scale),
        grid_spec=pltpu.PrefetchScalarGridSpec(
            num_scalar_prefetch=2,
            grid=(tiles,),
            in_specs=[ANY] * 5,
            out_specs=[
                pl.BlockSpec((ROW_TILE, padded), lambda i, meta, slots: (kept(i, meta), 0)),
                pl.BlockSpec((model, ROW_TILE), lambda i, meta, slots: (0, kept(i, meta))),
                pl.BlockSpec((8, ROW_TILE), lambda i, meta, slots: (0, i)),
            ],
            scratch_shapes=[
                pltpu.VMEM((model, padded), BF16),
                pltpu.VMEM((tiles * ROW_TILE, model), BF16),
                pltpu.VMEM((tiles * ROW_TILE, LANES), F32),
                pltpu.VMEM((min(wide_count, 8), tokens + 8, model), BF16),
                pltpu.VMEM((ROW_TILE, padded), F32),
                pltpu.SemaphoreType.DMA,
                pltpu.SemaphoreType.DMA((min(wide_count, 8),)),
            ],
        ),
        out_shape=[
            like((tiles * ROW_TILE, padded), BF16),
            like((model, tiles * ROW_TILE), BF16),
            like((8, tiles * ROW_TILE), F32),
        ],
        compiler_params=PARAMS,
        cost_estimate=work(52),
        name="exit_scores",
    )(meta, slot_of, *exit_parts, table)

    own_peak = stats[0]
    joint = stats
    for pairs in stage_pairs(wide_count) + [flip_pairs(wide_count)]:
        came = lax.ppermute(joint, "wide", pairs)
        peak = jnp.maximum(joint[0], came[0])
        summed = joint[1] * jnp.exp(joint[0] - peak) + came[1] * jnp.exp(came[0] - peak)
        joint = jnp.concatenate([peak[None], summed[None], joint[2:3] + came[2:3], stats[3:]], axis=0)
    log_total = joint[0] + jnp.log(joint[1])
    picked, group_weight = joint[2], stats[3]
    loss_part = jnp.full((8, LANES), jnp.sum(group_weight * (log_total - picked)), F32)

    factor = jnp.exp(own_peak - log_total) * (group_weight * scale)
    at_target = (jnp.exp(picked - log_total) - 1.0) * (group_weight * scale)
    factors = jnp.concatenate([factor[None], at_target[None], stats[4:5], stats[3:]], axis=0)
    token_part = like((wide_count // 4, tokens, model), BF16)
    exit_grads = pl.pallas_call(
        functools.partial(exit_tokens_kernel, vocab=vocab),
        grid_spec=pltpu.PrefetchScalarGridSpec(
            num_scalar_prefetch=2,
            grid=(tiles,),
            in_specs=[
                ANY,
                pl.BlockSpec((ROW_TILE, padded), lambda i, meta, slots: (kept(i, meta), 0)),
                pl.BlockSpec((8, ROW_TILE), lambda i, meta, slots: (0, i)),
            ],
            out_specs=[ANY] * 4,
            scratch_shapes=[
                pltpu.VMEM((model, padded), BF16),
                pltpu.VMEM((tiles * ROW_TILE, model), BF16),
                pltpu.VMEM((2, tokens, model), BF16),
                pltpu.SemaphoreType.DMA,
                pltpu.SemaphoreType.DMA((2,)),
            ],
        ),
        out_shape=[token_part] * 4,
        compiler_params=PARAMS,
        cost_estimate=work(50),
        name="exit_tokens",
    )(meta, places, table, raised, factors)

    half = padded // 2

    def table_half(side, factors, *before):
        return pl.pallas_call(
            functools.partial(exit_table_kernel, first=side * half, vocab=vocab),
            grid_spec=pltpu.PrefetchScalarGridSpec(
                num_scalar_prefetch=1,
                grid=(tiles // 2,),
                in_specs=[
                    pl.BlockSpec((2 * ROW_TILE, half), lambda i, meta: (kept_pair(i, meta), side)),
                    pl.BlockSpec((model, 2 * ROW_TILE), lambda i, meta: (0, kept_pair(i, meta))),
                    pl.BlockSpec((8, 2 * ROW_TILE), lambda i, meta: (0, i)),
                ]
                + [ANY] * len(before),
                out_specs=pl.BlockSpec((model, half), lambda i, meta: (0, side)),
                scratch_shapes=[pltpu.VMEM((model, half), F32)],
            ),
            out_shape=like((model, padded), BF16),
            input_output_aliases={4: 0} if before else {},
            compiler_params=PARAMS,
            cost_estimate=work(15),
            name="exit_table",
        )(meta, raised, tokens_across, factors, *before)

    exit_scatter = scatter_core(exit_grads, wide_count)
    half_grad = table_half(0, tie(factors, *exit_grads))
    (own, came), exit_kept = exit_scatter
    exit_far = scatter_far((own, tie(came, half_grad)), exit_kept, wide_count)
    table_grad = table_half(1, tie(factors, exit_far[0]), half_grad)
    table_sum = lax.psum_scatter(table_grad, "narrow", scatter_dimension=0, tiled=True)
    embedding_grad = table_sum.astype(F32).T[:vocab]
    exit_near = scatter_near(tie(exit_far[1], table_grad), exit_far[2], wide_count)
    exit_grad = exit_near[2] + exit_near[1].astype(F32)

    gain_like = like((8, model), F32)
    stream_two_grad, mlp_gains, *mlp_grads = pl.pallas_call(
        mlp_backward_kernel,
        in_specs=[SMEM] + [VMEM] * 3 + [ANY] * 13,
        out_specs=[VMEM] * 2 + [ANY] * 8,
        out_shape=[stream_like, gain_like]
        + [like(part.shape, BF16) for part in gate_gathered]
        + [
            like((part.shape[0], hidden_width // kernel_count, model), BF16)
            for part in cross_gathered
        ],
        scratch_shapes=[
            pltpu.VMEM((2, model, hidden_width), BF16),
            pltpu.VMEM((1, hidden_width, model), BF16),
            pltpu.VMEM((tokens, hidden_width), BF16),
            pltpu.VMEM((tokens, hidden_width), BF16),
            pltpu.VMEM((2, model, hidden_width), BF16),
            pltpu.VMEM((hidden_width, model), BF16),
            pltpu.SemaphoreType.DMA((kernel_count, 2)),
            one_matrix_sems,
            pltpu.SemaphoreType.DMA((3, kernel_count)),
            pltpu.VMEM((tokens, hidden_width), F32),
            pltpu.VMEM((tokens, hidden_width), F32),
            pltpu.VMEM((tokens, model), BF16),
            pltpu.VMEM((tokens, hidden_width), BF16),
            pltpu.VMEM((tokens, model), F32),
            pltpu.SemaphoreType.DMA((5,)),
        ],
        compiler_params=PARAMS,
        cost_estimate=work(15),
        name="mlp_backward",
    )(
        kernel_places, exit_grad, stream_three, gain_all, gate_pre, up_pre, normed_three, hidden,
        stream_two, *gate_gathered, *cross_gathered,
    )
    gate_scatter = scatter_core(from_kernels(mlp_grads[:4], [rows, rows]), wide_count)
    down_scatter = scatter_core(from_kernels(mlp_grads[4:], [down_rows]), wide_count)

    def go_far(scatter, *others):
        (own, came), kept = scatter
        return scatter_far((own, tie(came, *others)), kept, wide_count)

    def go_near(state, *others):
        _, came, kept = state
        return scatter_near(tie(came, *others), kept, wide_count)

    low_like = like((slots, model), BF16)
    middle = 2 * (HEADS // 4) * (model // HEADS)
    low_half = like((slots, middle), BF16)
    branch_two, attended_grad, *first_lows = pl.pallas_call(
        cross_attention_first_kernel,
        in_specs=[SMEM] * 3 + [VMEM] * 5 + [ANY] * 4,
        out_specs=[VMEM] * 5,
        out_shape=[activation, activation, like((tokens, middle), BF16), low_half, low_half],
        scratch_shapes=[
            pltpu.VMEM((1, model, model), BF16),
            pltpu.VMEM((slots, 2 * tokens), F32),
            one_matrix_sems,
        ],
        compiler_params=PARAMS,
        cost_estimate=work(16),
        name="cross_attention_first",
    )(
        kernel_places, lengths, sources, stream_two_grad, query_two, key_two, value_two, totals_two,
        *cross_gathered,
    )
    gate_far = go_far(gate_scatter, first_lows[0])
    down_far = go_far(down_scatter, first_lows[0])
    query_two_low, key_two_low, value_two_low = pl.pallas_call(
        cross_attention_last_kernel,
        in_specs=[SMEM] * 2 + [VMEM] * 8,
        out_specs=[VMEM] * 3,
        out_shape=[activation, low_like, low_like],
        scratch_shapes=[pltpu.VMEM((slots, 2 * tokens), F32)],
        compiler_params=PARAMS,
        cost_estimate=work(16),
        name="cross_attention_last",
    )(
        lengths, sources, tie(attended_grad, gate_far[0], down_far[0]), query_two, key_two,
        value_two, totals_two, *first_lows,
    )

    loss_part = tie(loss_part, query_two_low)
    loss_all = loss_part
    for step in range(1, narrow_count):
        loss_all = loss_all + lax.ppermute(loss_part, "narrow", narrow_pairs(narrow_count, step))
    mean_loss = loss_all[0, 0] / slot_total
    cross_matrices = like((cross_gathered[0].shape[0], 5 * model // kernel_count, model), BF16)
    stream_one_grad, cross_gains, memory_grad, branch_one, *cross_grads = pl.pallas_call(
        cross_backward_kernel,
        in_specs=[SMEM] + [VMEM] * 3 + [ANY] * 12,
        out_specs=[VMEM] * 4 + [ANY] * 4,
        out_shape=[stream_like, gain_like, like((slots, model), F32), activation]
        + [cross_matrices] * 4,
        scratch_shapes=[
            pltpu.VMEM((3, model, model), BF16),
            pltpu.VMEM((5, model, model), BF16),
            pltpu.SemaphoreType.DMA((kernel_count, 3)),
            pltpu.SemaphoreType.DMA((5, kernel_count)),
            pltpu.VMEM((slots, model), BF16),
            pltpu.VMEM((tokens, model), BF16),
            pltpu.VMEM((tokens, model), BF16),
            pltpu.VMEM((tokens, model), BF16),
            pltpu.VMEM((tokens, model), BF16),
            pltpu.VMEM((tokens, model), F32),
            pltpu.VMEM((tokens, model), F32),
            pltpu.VMEM((tokens, model), BF16),
            pltpu.SemaphoreType.DMA((8,)),
        ],
        compiler_params=PARAMS,
        cost_estimate=work(20),
        name="cross_backward",
    )(
        kernel_places, gain_all, memory, key_two_low, value_two_low, normed_two, query_two_low,
        attended_two, branch_two, stream_one, stream_two_grad, attended_one, *cross_gathered,
    )
    cross_scatter = scatter_core(from_kernels(cross_grads, [rows] * 5), wide_count)

    gate_near = go_near(gate_far, branch_one)
    down_near = go_near(down_far, branch_one)
    query_one_low, key_one_low, value_one_low = pl.pallas_call(
        self_attention_backward_kernel,
        in_specs=[SMEM] * 2 + [VMEM] * 5 + [ANY] * 4,
        out_specs=[VMEM] * 3,
        out_shape=[activation] * 3,
        scratch_shapes=[
            pltpu.VMEM((1, model, model), BF16),
            pltpu.VMEM((tokens, 2 * tokens), F32),
            pltpu.VMEM((tokens, model), BF16),
            one_matrix_sems,
        ],
        compiler_params=PARAMS,
        cost_estimate=work(10),
        name="self_attention_backward",
    )(
        kernel_places, lengths, tie(branch_one, gate_near[0], down_near[0], loss_all), query_one, key_one, value_one, totals_one,
        *self_gathered,
    )
    def line_blocks(near, matrices, *others):
        _, came, held = near
        summed = held + tie(came, *others).astype(F32)
        width = summed.shape[-1]
        size = matrices * (summed.shape[0] // (matrices * 8 * narrow_count)) * 8 * narrow_count
        members = [
            summed[:size].reshape(matrices, narrow_count, -1, width).transpose(1, 0, 2, 3)
            .reshape(narrow_count, -1, width)
        ]
        if size < summed.shape[0]:
            members.append(summed[size:].reshape(narrow_count, -1, width))
        return jnp.concatenate(members, axis=1)

    def line_first(near, matrices, *others):
        blocks = line_blocks(near, matrices, *others)
        steps = range(0, narrow_count, 2)
        sent = jnp.stack([pick(blocks, narrow ^ (step + 1)) for step in steps]).astype(BF16)
        came = lax.ppermute(sent, "narrow", narrow_pairs(narrow_count, 1))
        return sent, came, [pick(blocks, narrow ^ step) for step in steps]

    def line_second(state, *others):
        _, came, kept = state
        came = tie(came, *others).astype(F32)
        terms = [kept[0] + came[0]]
        for place in range(1, len(kept)):
            sent = (kept[place] + came[place]).astype(BF16)
            terms.append(lax.ppermute(sent, "narrow", narrow_pairs(narrow_count, 2 * place)))
        return terms

    cross_far = go_far(cross_scatter, query_one_low)
    gate_line = line_first(gate_near, 2, query_one_low)

    extra = narrow_count * 8
    spare = extra * wide_count // kernel_count
    inputs_grad, *self_grads = pl.pallas_call(
        self_backward_kernel,
        in_specs=[SMEM] + [VMEM] * 9 + [ANY] * 4,
        out_specs=[VMEM] + [ANY] * 4,
        out_shape=[stream_like]
        + [like((part.shape[0], 3 * model // kernel_count + spare, model), BF16) for part in self_gathered],
        scratch_shapes=[
            pltpu.VMEM((3, model, model), BF16),
            pltpu.VMEM((3, model, model), BF16),
            pltpu.VMEM((spare, model), BF16),
            pltpu.SemaphoreType.DMA((kernel_count, 3)),
            pltpu.SemaphoreType.DMA((3, kernel_count)),
            pltpu.SemaphoreType.DMA((kernel_count,)),
        ],
        compiler_params=PARAMS,
        cost_estimate=work(12),
        name="self_backward",
    )(
        kernel_places, tie(stream_one_grad, gate_line[0], cross_far[0]), inputs,
        gain_all, normed_one, cross_gains, mlp_gains, query_one_low, key_one_low, value_one_low,
        *self_gathered,
    )
    self_scatter = scatter_core(from_kernels(self_grads, [rows] * 3 + [extra]), wide_count)

    cross_near = go_near(cross_far, inputs_grad)
    self_far = go_far(self_scatter, cross_near[0])
    down_line = line_first(down_near, 1, self_far[0])
    gate_terms = line_second(gate_line, self_far[0])
    cross_line = line_first(cross_near, 5, down_line[0], gate_terms[0], embedding_grad)
    self_near = go_near(self_far, cross_line[0])
    down_terms = line_second(down_line, self_near[0])
    gate_sum = add_terms(gate_terms, self_near[0]).reshape(2, shard, hidden_width)
    cross_terms = line_second(cross_line, down_terms[0], gate_sum)
    self_terms = scatter_narrow(
        line_blocks(self_near, 3, cross_terms[0]), narrow, narrow_count
    )
    down_sum = add_terms(down_terms, self_terms[0])
    cross_sum = add_terms(cross_terms, self_terms[0]).reshape(5, shard, model)
    self_sum = add_terms(self_terms)
    gains = pick(self_sum[3 * shard :].reshape(8, model // shard, shard), owner, 1)
    self_sum = self_sum[: 3 * shard].reshape(3, shard, model)

    return (
        activations,
        mean_loss,
        inputs_grad,
        memory_grad,
        gains[0],
        self_sum[0],
        self_sum[1],
        self_sum[2],
        cross_sum[4],
        gains[1],
        cross_sum[0],
        cross_sum[1],
        cross_sum[2],
        cross_sum[3],
        gains[2],
        gate_sum[0],
        gate_sum[1],
        down_sum,
        gains[3],
        embedding_grad,
    )


def solution(mesh):
    both = ("wide", "narrow")
    rows, flat = P(both, None), P(both)
    placed = (
        rows, rows, flat, rows, rows,
        flat, rows, rows, rows, rows,
        flat, rows, rows, rows, rows,
        flat, rows, rows, rows, flat,
        P("wide", "narrow"),
    )
    given = (
        rows, P(), rows, rows,
        flat, rows, rows, rows, rows,
        flat, rows, rows, rows, rows,
        flat, rows, rows, rows, flat,
        P("wide", "narrow"),
    )
    return jax.shard_map(
        per_device, mesh=mesh, in_specs=placed, out_specs=given, check_vma=False
    )
```

```python
import functools
import math

import jax
import jax.numpy as jnp
from jax import lax
from jax.experimental import pallas as pl
from jax.experimental.pallas import tpu as pltpu
from jax.sharding import PartitionSpec as P

HEADS = 12
EPSILON = 1e-06
NEGATIVE = -1e30
F32 = jnp.float32
BF16 = jnp.bfloat16
LANES = 128
ROW_TILE = 256
VOCAB_TILE = 512
MIX = math.sqrt(2.0 / math.pi)
CUBE = 0.044715
LOG2E = math.log2(math.e)
META_WIDE, META_TILES, META_LISTS = 0, 1, 2

VMEM = pl.BlockSpec(memory_space=pltpu.VMEM)
SMEM = pl.BlockSpec(memory_space=pltpu.SMEM)
ANY = pl.BlockSpec(memory_space=pl.ANY)
PARAMS = pltpu.CompilerParams(vmem_limit_bytes=60 * 2**20)


def work(gigaflops):
    return pl.CostEstimate(flops=gigaflops * 10**9, bytes_accessed=10**6, transcendentals=0)


def nn(left, right):
    return lax.dot_general(left, right, (((1,), (0,)), ((), ())), preferred_element_type=F32)


def nt(left, right):
    return lax.dot_general(left, right, (((1,), (1,)), ((), ())), preferred_element_type=F32)


def tn(left, right):
    return lax.dot_general(left, right, (((0,), (0,)), ((), ())), preferred_element_type=F32)


def like(shape, kind):
    return jax.ShapeDtypeStruct(shape, kind)


def stage_masks(count):
    up = [1 << bit for bit in range(1, count.bit_length() - 1)]
    return up, up[::-1]


def stage_pairs(count):
    even, odd = stage_masks(count)
    return [[(v, v ^ (odd if v % 2 else even)[i]) for v in range(count)] for i in range(len(even))]


def flip_pairs(count):
    return [(v, v ^ 1) for v in range(count)]


def slot_tables(count):
    tables = []
    for masks in stage_masks(count):
        slots = [0]
        for mask in masks:
            slots = slots + [slot ^ mask for slot in slots]
        tables.append(slots)
    even, odd = tables
    return (
        even + [1 ^ slot for slot in odd],
        odd + [1 ^ slot for slot in even],
    )


def slot_places(wide, count):
    even, odd = slot_tables(count)
    table = jnp.where(wide % 2 == 0, jnp.array(even, jnp.int32), jnp.array(odd, jnp.int32))
    return wide ^ table


def tie(value, *others):
    return lax.optimization_barrier((value, *others))[0]


def cross_core(value, count):
    return lax.ppermute(value, "wide", flip_pairs(count))


def gather_wide(block, count):
    held = block[None]
    *early, last = stage_pairs(count)
    for pairs in early:
        held = jnp.concatenate([held, lax.ppermute(held, "wide", pairs)], axis=0)
    came = lax.ppermute(held, "wide", last)
    return held, came, cross_core(held, count), cross_core(came, count)


def scatter_core(parts, count):
    sent, kept = cross_core(parts[3], count), cross_core(parts[2], count)
    return (parts[1], sent), (parts[0], kept)


def scatter_far(sent, kept, count):
    far = sent[0] + sent[1]
    came = lax.ppermute(far, "wide", stage_pairs(count)[-1])
    return far, came, kept


def scatter_near(came, kept, count):
    *rest, last = stage_pairs(count)[-2::-1]
    terms = (*kept, came)
    if not rest:
        far = sum(term[1].astype(F32) for term in terms).astype(BF16)
        return far, lax.ppermute(far, "wide", last), sum(term[0].astype(F32) for term in terms)
    held = sum(term.astype(F32) for term in terms)
    for pairs in rest:
        half = held.shape[0] // 2
        sent = lax.ppermute(held[half:].astype(BF16), "wide", pairs)
        held = held[:half] + sent.astype(F32)
    far = held[1].astype(BF16)
    return far, lax.ppermute(far, "wide", last), held[0]


def scatter_wide(parts, count):
    far, came, kept = scatter_far(*scatter_core(parts, count), count)
    far, came, held = scatter_near(came, kept, count)
    return held + came.astype(F32)


def narrow_pairs(count, step):
    return [(v, v ^ step) for v in range(count)]


def gather_narrow(block, count):
    return [block] + [
        lax.ppermute(block, "narrow", narrow_pairs(count, step)) for step in range(1, count)
    ]


def pick(values, place, axis=0):
    return lax.dynamic_index_in_dim(values, place.astype(jnp.uint32), axis, keepdims=False)


def in_line_order(pieces, narrow):
    stacked = jnp.stack(pieces)
    return [pick(stacked, narrow ^ place) for place in range(stacked.shape[0])]


def scatter_narrow(blocks, narrow, count):
    return [pick(blocks, narrow)] + [
        lax.ppermute(pick(blocks, narrow ^ step).astype(BF16), "narrow", narrow_pairs(count, step))
        for step in range(1, count)
    ]


def add_terms(terms, *others):
    terms = lax.optimization_barrier((*terms, *others))[: len(terms)]
    return sum(term.astype(F32) for term in terms)


def weight_copies(places, parts, start, target, rows, sems):
    size = parts[0].shape[0]
    copies = []
    for slot in range(len(parts) * size):
        place = pl.multiple_of(places[slot] * rows, 8)
        for matrix in range(target.shape[0]):
            copies.append(
                pltpu.make_async_copy(
                    parts[slot // size].at[slot % size, pl.ds(start + matrix * rows, rows), :],
                    target.at[matrix, pl.ds(place, rows), :],
                    sems.at[slot, matrix],
                )
            )
    return copies


def block_copies(places, value, start, rows, parts, sems):
    size = parts[0].shape[0]
    copies = []
    for slot in range(len(parts) * size):
        place = pl.multiple_of(places[slot] * rows, 8)
        copies.append(
            pltpu.make_async_copy(
                value.at[pl.ds(place, rows), :],
                parts[slot // size].at[slot % size, pl.ds(start, rows), :],
                sems.at[slot],
            )
        )
    return copies


def fetch(sources, targets, sems):
    copies = [
        pltpu.make_async_copy(source, target, sems.at[place])
        for place, (source, target) in enumerate(zip(sources, targets))
    ]
    for copy in copies:
        copy.start()
    return copies


def send_off(copies, more):
    for copy in more:
        copy.start()
    copies += more


def norm_scale(values):
    return lax.rsqrt(jnp.mean(values * values, axis=-1, keepdims=True) + EPSILON)


def norm_back(values, gain, grad):
    root = norm_scale(values)
    scaled = gain * grad
    gain_grad = jnp.sum(grad * values * root, axis=0, keepdims=True)
    inner = jnp.mean(scaled * values, axis=-1, keepdims=True)
    return root * scaled - values * (root * root * root) * inner, gain_grad


def query_segments(lengths, count):
    places = lax.broadcasted_iota(jnp.int32, (1, count), 1)
    segment = jnp.zeros((1, count), jnp.int32)
    edge = jnp.int32(0)
    for pair in range(lengths.shape[0]):
        edge = edge + lengths[pair]
        segment = segment + (places >= edge).astype(jnp.int32)
    return places, segment


def fill_self_bias(bias, lengths):
    count = bias.shape[1] // 2
    places, segment = query_segments(lengths, count)
    low = jnp.zeros((1, count), jnp.int32)
    edge = jnp.int32(0)
    for pair in range(lengths.shape[0]):
        edge = edge + lengths[pair]
        low = jnp.where(segment == pair + 1, edge, low)
    keys = lax.broadcasted_iota(jnp.int32, (bias.shape[0], count), 0)
    one = jnp.where((keys >= low) & (keys <= places), 0.0, NEGATIVE)
    bias[...] = jnp.concatenate([one, one], axis=1)


def fill_cross_bias(bias, lengths, sources):
    count = bias.shape[1] // 2
    places, segment = query_segments(lengths, count)
    low = jnp.zeros((1, count), jnp.int32)
    high = jnp.full((1, count), bias.shape[0], jnp.int32)
    edge = jnp.int32(0)
    for pair in range(lengths.shape[0]):
        low = jnp.where(segment == pair, edge, low)
        edge = edge + sources[pair]
        high = jnp.where(segment == pair, edge, high)
    low = jnp.concatenate([low, low], axis=1)
    high = jnp.concatenate([high, high], axis=1)
    keys = lax.broadcasted_iota(jnp.int32, bias.shape, 0)
    bias[...] = jnp.where((keys >= low) & (keys < high), 0.0, NEGATIVE)


def first_half(width):
    return lax.broadcasted_iota(jnp.int32, (1, width), 1) < width // 2


def apart(values, chosen):
    return jnp.concatenate([jnp.where(chosen, values, 0), jnp.where(chosen, 0, values)], axis=0)


def together(values, chosen):
    count = values.shape[0] // 2
    return jnp.where(chosen, values[:count], values[count:])


def attend(queries, keys, values, bias, outputs, totals, unroll):
    width = 2 * (queries.shape[1] // HEADS)
    chosen = first_half(width)

    def pair_of_heads(pair, carry):
        columns = pl.ds(pl.multiple_of(pair * width, width), width)
        scores = nt(keys[:, columns], apart(queries[:, columns], chosen)) + bias[...]
        highest = jnp.max(scores, axis=0, keepdims=True)
        raised = jnp.exp(scores - highest)
        summed = jnp.sum(raised, axis=0, keepdims=True)
        totals[pair] = highest + jnp.log(summed)
        weights = (raised * (1.0 / summed)).astype(BF16)
        mixed = nn(values[:, columns].T, weights).T
        outputs[:, columns] = together(mixed, chosen).astype(BF16)
        return carry

    lax.fori_loop(0, HEADS // 2, pair_of_heads, 0, unroll=unroll)


def attend_back(
    queries, keys, values, bias, totals, grads, query_low, key_low, value_low, first, last
):
    width = 2 * (queries.shape[1] // HEADS)
    chosen = first_half(width)

    for pair in range(first, last):
        columns = slice(pair * width, (pair + 1) * width)
        result = slice((pair - first) * width, (pair - first + 1) * width)
        query, grad = apart(queries[:, columns], chosen), apart(grads[:, columns], chosen)
        key = keys[:, columns]
        probs = jnp.exp(nt(key, query) + bias[...] - totals[pair])
        prob_grad = nt(values[:, columns], grad)
        value_low[:, result] = nn(probs.astype(BF16), grad).astype(BF16)
        weighted = probs * prob_grad
        centre = jnp.sum(weighted, axis=0, keepdims=True)
        score_grad = (weighted - probs * centre).astype(BF16)
        key_low[:, result] = nn(score_grad, query).astype(BF16)
        query_low[:, result] = together(nn(key.T, score_grad).T, chosen).astype(BF16)


def block_rows(weights, parts):
    return weights.shape[1] // (len(parts) * parts[0].shape[0])


def join_kernel(*refs):
    start = 0
    for ref in refs[:-1]:
        refs[-1][start : start + ref.shape[0], :] = ref[...]
        start += ref.shape[0]


def join_self_kernel(owner, lengths, gains, *refs):
    join_kernel(*refs)
    pack = refs[-1]
    shard, width = gains.shape[1], pack.shape[1]
    total = jnp.int32(0)
    for pair in range(lengths.shape[0]):
        total = total + lengths[pair]
    spot = lax.broadcasted_iota(jnp.int32, (8, shard), 0)
    high, low = (total // 16).astype(F32), (total % 16).astype(F32)
    own = jnp.concatenate([gains[...].astype(F32), jnp.zeros((8 - gains.shape[0], shard), F32)], axis=0)
    own = jnp.where(spot == 4, high, jnp.where(spot == 5, low, own)).astype(BF16)
    row = lax.broadcasted_iota(jnp.int32, (shard, width), 0)
    column = lax.broadcasted_iota(jnp.int32, (shard, width), 1)
    spread = (row + owner[0] * shard == column).astype(BF16)
    pack[pack.shape[0] - 8 :, :] = nn(own, spread).astype(BF16)


def join_rows(*members):
    if any(member.shape[0] % 8 for member in members):
        return jnp.concatenate(members, axis=0)
    rows = sum(member.shape[0] for member in members)
    return pl.pallas_call(
        join_kernel,
        in_specs=[VMEM] * len(members),
        out_specs=VMEM,
        out_shape=like((rows, members[0].shape[1]), members[0].dtype),
        cost_estimate=work(1),
        name="join_rows",
    )(*members)


def line_kernel(narrow, *refs, sizes):
    pieces, block = refs[:-1], refs[-1]
    start = 0
    for size in sizes:
        for step, piece in enumerate(pieces):
            place = pl.multiple_of(start * len(pieces) + (narrow[0] ^ step) * size, 8)
            block[pl.ds(place, size), :] = piece[start : start + size]
        start += size


def line_pair_kernel(narrow, even, odd, block, *, sizes):
    pieces = [(odd if step % 2 else even).at[step // 2] for step in range(2 * even.shape[0])]
    start = 0
    for size in sizes:
        for step, piece in enumerate(pieces):
            place = pl.multiple_of(start * len(pieces) + (narrow[0] ^ step) * size, 8)
            block[pl.ds(place, size), :] = piece[start : start + size]
        start += size


def self_forward_kernel(
    places, lengths, inputs, *refs,
):
    parts = refs[:4]
    normed, query, key, value, attended, totals, stream, gains = refs[4:12]
    weights, gain_parts, bias, sems, gain_sems = refs[12:]
    size = parts[0].shape[0]
    rows = block_rows(weights, parts)
    gain_copies = [
        pltpu.make_async_copy(
            parts[slot // size].at[slot % size, pl.ds(4 * rows, gain_parts.shape[1]), :],
            gain_parts.at[slot],
            gain_sems.at[slot],
        )
        for slot in range(4 * size)
    ]
    copies = weight_copies(places, parts, 0, weights, rows, sems)
    for copy in gain_copies + copies:
        copy.start()
    values = inputs[...].astype(F32)
    fill_self_bias(bias, lengths)
    scaled = values * norm_scale(values)
    for copy in gain_copies:
        copy.wait()
    members = gain_parts[...].astype(F32).reshape(-1, 8, gains.shape[1])
    summed = members[0]
    for member in range(1, members.shape[0]):
        summed = summed + members[member]
    gains[...] = summed
    low = (scaled * summed[0:1]).astype(BF16)
    normed[...] = low
    for copy in copies:
        copy.wait()
    query[...] = nn(low, weights[0]).astype(BF16)
    key[...] = nn(low, weights[1]).astype(BF16)
    value[...] = nn(low, weights[2]).astype(BF16)
    attend(query, key, value, bias, attended, totals, HEADS // 2)
    stream[...] = values + nn(attended[...], weights[3])


def memory_kernel(places, memory, *refs):
    parts = refs[:4]
    key, value, weights, sems = refs[4:]
    rows = block_rows(weights, parts)
    copies = weight_copies(places, parts, rows, weights, rows, sems)
    for copy in copies:
        copy.start()
    for copy in copies:
        copy.wait()
    key[...] = nn(memory[...], weights[0]).astype(BF16)
    value[...] = nn(memory[...], weights[1]).astype(BF16)


def cross_forward_kernel(
    places, lengths, sources, stream_in, gains, key, value, *refs,
):
    parts = refs[:4]
    normed, query, attended, totals, stream, weights, bias, sems = refs[4:]
    rows = block_rows(weights, parts)
    copies = weight_copies(places, parts, 0, weights.at[pl.ds(0, 1)], rows, sems.at[0])
    copies += weight_copies(places, parts, 3 * rows, weights.at[pl.ds(1, 1)], rows, sems.at[1])
    for copy in copies:
        copy.start()
    values = stream_in[...]
    fill_cross_bias(bias, lengths, sources)
    low = (values * norm_scale(values) * gains[1:2]).astype(BF16)
    normed[...] = low
    for copy in copies:
        copy.wait()
    query[...] = nn(low, weights[0]).astype(BF16)
    attend(query, key, value, bias, attended, totals, HEADS // 4)
    stream[...] = values + nn(attended[...], weights[1])


def mlp_forward_kernel(
    places, stream_in, gains, side, *refs,
):
    parts, down_parts = refs[:4], refs[4:8]
    normed, gate, up, hidden, stream, activations, exit_normed = refs[8:15]
    weights, down, sems, down_sems = refs[15:]
    rows, down_rows = block_rows(weights, parts), block_rows(down, down_parts)
    first = weight_copies(places, parts, 0, weights, rows, sems)
    last = weight_copies(
        places, down_parts, down_parts[0].shape[1] - down_rows, down, down_rows, down_sems
    )
    for copy in first + last:
        copy.start()
    values = stream_in[...]
    low = (values * norm_scale(values) * gains[2:3]).astype(BF16)
    normed[...] = low
    for copy in first:
        copy.wait()
    width = weights.shape[2]
    step = width // 4
    for part in range(4):
        columns = pl.ds(part * step, step)
        gate_pre = nn(low, weights[0, :, columns])
        up_pre = nn(low, weights[1, :, columns])
        gate[:, columns] = gate_pre
        up[:, columns] = up_pre
        bent = jnp.tanh(MIX * (gate_pre + CUBE * (gate_pre * gate_pre * gate_pre)))
        hidden[:, columns] = (0.5 * gate_pre * (1.0 + bent) * up_pre).astype(BF16)
    for copy in last:
        copy.wait()
    out = values + nn(hidden[...], down[0])
    stream[...] = out
    activations[...] = out.astype(BF16)
    count = out.shape[0]
    exit_normed[:count] = (out * norm_scale(out) * gains[3:4]).astype(BF16)
    exit_normed[count:] = side[...]


def exit_scores_kernel(meta, slot_of, *refs, vocab, scale):
    parts = refs[:4]
    source, raised, across, stats = refs[4:8]
    table, tokens, columns, landed, scores, table_sem, sems = refs[8:]
    size = parts[0].shape[0]
    members = 4 * size
    ring = landed.shape[0]
    count = parts[0].shape[1] - 8
    step = pl.program_id(0)
    tile = raised.shape[0]
    starts, counts = META_LISTS, META_LISTS + members

    def fetch(member):
        slot = slot_of[member]
        for part in range(4):

            @pl.when(slot // size == part)
            def start():
                pltpu.make_async_copy(
                    parts[part].at[slot % size], landed.at[member % ring], sems.at[member % ring]
                ).start()

    @pl.when(step == 0)
    def load():
        whole = pltpu.make_async_copy(source, table, table_sem)
        for member in range(min(ring, members)):
            fetch(member)
        whole.start()
        tokens[...] = jnp.zeros_like(tokens)
        columns[...] = jnp.zeros_like(columns)
        lanes = -(-count // LANES) * LANES
        spots = lax.broadcasted_iota(jnp.int32, (1, lanes), 1)
        for member in range(members):
            pltpu.make_async_copy(
                parts[0].at[0], landed.at[member % ring], sems.at[member % ring]
            ).wait()
            begin = pl.multiple_of(meta[starts + member], 16)
            block = landed[member % ring]
            tokens[pl.ds(begin, count), :] = block[:count]
            side = block[count:, :lanes].astype(F32)
            wanted = side[0:1] * 256.0 + side[1:2]
            weight = jnp.where(spots < meta[counts + member], 1.0, 0.0)
            packed = jnp.concatenate(
                [weight, wanted, jnp.zeros((LANES - 2, lanes), F32)], axis=0
            )
            columns[pl.ds(begin, count), :] = packed.T[:count]
            if member + ring < members:
                fetch(member + ring)
        whole.wait()

    spot = lax.broadcasted_iota(jnp.int32, (tile, LANES), 1)

    @pl.when(step < meta[META_TILES])
    def compute():
        here = pl.ds(pl.multiple_of(step * tile, tile), tile)
        own = tokens[here, :]
        column = columns[here, :]
        across[...] = own.T
        width = scores.shape[1]
        lanes = lax.broadcasted_iota(jnp.int32, (tile, LANES), 1)
        wanted = column[:, 1:2].astype(jnp.int32) - meta[META_WIDE] * vocab
        wanted = jnp.where(wanted < vocab, wanted, -1)
        peaks = jnp.full((tile, LANES), NEGATIVE, F32)
        found = jnp.zeros((tile, LANES), F32)
        for first in range(0, width, VOCAB_TILE):
            part = nn(own, table[:, first : first + VOCAB_TILE])
            for inner in range(0, VOCAB_TILE, LANES):
                piece = part[:, inner : inner + LANES]
                offset = first + inner
                if offset + LANES > vocab:
                    piece = jnp.where(lanes < vocab - offset, piece, NEGATIVE)
                scores[:, offset : offset + LANES] = piece
                peaks = jnp.maximum(peaks, piece)
                found = found + jnp.where(lanes == wanted - offset, piece, 0.0)
        highest = jnp.max(peaks, axis=1, keepdims=True)
        sums = jnp.zeros((tile, LANES), F32)
        for offset in range(0, width, LANES):
            piece = jnp.exp2((scores[:, offset : offset + LANES] - highest) * (scale * LOG2E))
            raised[:, offset : offset + LANES] = piece.astype(BF16)
            sums = sums + piece
        summed = jnp.sum(sums, axis=1, keepdims=True)
        picked = jnp.sum(found, axis=1, keepdims=True)
        values = (highest * scale, summed, picked * scale, column[:, 0:1], column[:, 1:2])
        packed = jnp.zeros((tile, LANES), F32)
        for place, value in enumerate(values):
            packed = jnp.where(spot == place, value, packed)
        stats[...] = packed.T[:8]

    @pl.when(step >= meta[META_TILES])
    def skip():
        rows = lax.broadcasted_iota(jnp.int32, stats.shape, 0)
        stats[...] = jnp.where(rows == 1, 1.0, 0.0)


def logit_grads(meta, raised, factors, first, width, vocab):
    tile = raised.shape[0]
    columns = jnp.concatenate(
        [factors[...], jnp.zeros((LANES - factors.shape[0], tile), F32)], axis=0
    ).T
    factor, at_target = columns[:, 0:1], columns[:, 1:2]
    wanted = columns[:, 2:3].astype(jnp.int32) - meta[META_WIDE] * vocab
    wanted = jnp.where(wanted < vocab, wanted, -1) - first
    lanes = lax.broadcasted_iota(jnp.int32, (tile, width), 1)

    def chunk(start):
        part = raised[:, start : start + width].astype(F32) * factor
        return jnp.where(lanes == wanted - start, at_target, part).astype(BF16)

    return chunk


def exit_tokens_kernel(meta, places, *refs, vocab):
    source, raised, factors = refs[:3]
    parts = refs[3:7]
    table, token_grad, landed, table_sem, sems = refs[7:]
    size = parts[0].shape[0]
    members = 4 * size
    count = parts[0].shape[1]
    starts, counts = META_LISTS, META_LISTS + members
    step = pl.program_id(0)
    tile = raised.shape[0]

    @pl.when(step == 0)
    def load():
        whole = pltpu.make_async_copy(source, table, table_sem)
        whole.start()
        whole.wait()

    @pl.when(step < meta[META_TILES])
    def compute():
        chunk = logit_grads(meta, raised, factors, 0, VOCAB_TILE, vocab)
        grad = jnp.zeros((tile, token_grad.shape[1]), F32)
        for first in range(0, raised.shape[1], VOCAB_TILE):
            grad = grad + nt(chunk(first), table[:, first : first + VOCAB_TILE])
        token_grad[pl.ds(pl.multiple_of(step * tile, tile), tile), :] = grad.astype(BF16)

    @pl.when(step == pl.num_programs(0) - 1)
    def finish():
        copies = []
        spots = lax.broadcasted_iota(jnp.int32, (count, 1), 0)
        for slot in range(members):
            if slot >= 2:
                copies[slot - 2].wait()
            member = places[slot]
            begin = pl.multiple_of(meta[starts + member], 16)
            block = token_grad[pl.ds(begin, count), :].astype(F32)
            landed[slot % 2] = jnp.where(spots < meta[counts + member], block, 0.0).astype(BF16)
            copy = pltpu.make_async_copy(
                landed.at[slot % 2], parts[slot // size].at[slot % size], sems.at[slot % 2]
            )
            copy.start()
            copies.append(copy)
        for copy in copies[-2:]:
            copy.wait()


def exit_table_kernel(meta, raised, across, factors, *refs, first, vocab):
    table_grad, total = refs[-2:]
    step = pl.program_id(0)
    width = min(VOCAB_TILE, raised.shape[1])

    @pl.when(step == 0)
    def clear():
        total[...] = jnp.zeros_like(total)

    def compute(raised, across, factors):
        chunk = logit_grads(meta, raised, factors, first, width, vocab)
        for start in range(0, raised.shape[1], width):
            total[:, start : start + width] += nn(across[...], chunk(start))

    @pl.when(2 * step + 1 < meta[META_TILES])
    def both():
        compute(raised, across, factors)

    @pl.when(2 * step + 1 == meta[META_TILES])
    def one():
        half = raised.shape[0] // 2
        compute(raised.at[:half], across.at[:, :half], factors.at[:, :half])

    @pl.when(step == pl.num_programs(0) - 1)
    def finish():
        table_grad[...] = total[...].astype(BF16)


def mlp_backward_kernel(
    places, grad_in, stream_three, gain, *refs,
):
    far, refs = refs[:5], refs[5:]
    parts, down_parts = refs[:4], refs[4:8]
    stream_grad, gains = refs[8:10]
    grad_parts, down_grad_parts = refs[10:14], refs[14:18]
    weights, down, gate_low, up_low, result, down_result, sems, down_sems, out_sems = refs[18:27]
    gate, up, normed, hidden, stream_two = refs[27:32]
    rows, down_rows = block_rows(weights, parts), block_rows(down, down_parts)
    first = weight_copies(
        places, down_parts, down_parts[0].shape[1] - down_rows, down, down_rows, down_sems
    )
    last = weight_copies(places, parts, 0, weights, rows, sems)
    for copy in first:
        copy.start()
    near = fetch(far, refs[27:32], refs[32])
    for copy in last:
        copy.start()
    stream_back, exit_gain_grad = norm_back(stream_three[...], gain[3:4], grad_in[...])
    branch = stream_back.astype(BF16)
    for copy in first + near[:3]:
        copy.wait()
    width = weights.shape[2]
    step = width // 4
    normed_across = normed[...].T
    sent = []
    for part in range(4):
        columns = pl.ds(part * step, step)
        gate_pre = gate[:, columns]
        up_pre = up[:, columns]
        hidden_grad = nt(branch, down[0, columns, :])
        bent = jnp.tanh(MIX * (gate_pre + CUBE * (gate_pre * gate_pre * gate_pre)))
        slope = 0.5 * (1.0 + bent) + 0.5 * gate_pre * (1.0 - bent * bent) * (
            MIX * (1.0 + 3.0 * CUBE * gate_pre * gate_pre)
        )
        gate_low[:, columns] = (hidden_grad * up_pre * slope).astype(BF16)
        up_low[:, columns] = (hidden_grad * (0.5 * gate_pre * (1.0 + bent))).astype(BF16)
        result[0, :, columns] = nn(normed_across, gate_low[:, columns]).astype(BF16)
        result[1, :, columns] = nn(normed_across, up_low[:, columns]).astype(BF16)
    for matrix in range(2):
        send_off(
            sent,
            block_copies(
                places, result.at[matrix], matrix * rows, rows, grad_parts, out_sems.at[matrix]
            ),
        )
    near[3].wait()
    for part in range(4):
        columns = pl.ds(part * step, step)
        down_result[columns, :] = nn(hidden[:, columns].T, branch).astype(BF16)
    send_off(
        sent, block_copies(places, down_result, 0, down_rows, down_grad_parts, out_sems.at[2])
    )
    for copy in last + near[4:]:
        copy.wait()
    normed_grad = nt(gate_low[...], weights[0]) + nt(up_low[...], weights[1])
    branch_in, gain_grad = norm_back(stream_two[...], gain[2:3], normed_grad)
    stream_grad[...] = stream_back + branch_in
    gains[...] = jnp.concatenate(
        [gain_grad, exit_gain_grad, jnp.zeros((6, gain_grad.shape[1]), F32)], axis=0
    )
    for copy in sent:
        copy.wait()


def cross_attention_first_kernel(
    places, lengths, sources, grad_in, query, key, value, totals, *refs,
):
    parts = refs[:4]
    branch, attended_grad, query_low, key_low, value_low, weights, bias, sems = refs[4:]
    rows = block_rows(weights, parts)
    copies = weight_copies(places, parts, 3 * rows, weights, rows, sems)
    for copy in copies:
        copy.start()
    fill_cross_bias(bias, lengths, sources)
    branch[...] = grad_in[...].astype(BF16)
    for copy in copies:
        copy.wait()
    attended_grad[...] = nt(branch[...], weights[0]).astype(BF16)
    attend_back(
        query, key, value, bias, totals, attended_grad, query_low, key_low, value_low,
        0, HEADS // 4,
    )


def cross_attention_last_kernel(
    lengths, sources, attended_grad, query, key, value, totals,
    first_query, first_key, first_value, query_low, key_low, value_low, bias,
):
    middle = first_query.shape[1]
    fill_cross_bias(bias, lengths, sources)
    attend_back(
        query, key, value, bias, totals, attended_grad,
        query_low.at[:, middle:], key_low.at[:, middle:], value_low.at[:, middle:],
        HEADS // 4, HEADS // 2,
    )
    query_low[:, :middle] = first_query[...]
    key_low[:, :middle] = first_key[...]
    value_low[:, :middle] = first_value[...]


def cross_backward_kernel(
    places, gain, memory, key_low, *refs,
):
    far, refs = refs[:8], refs[8:]
    parts = refs[:4]
    stream_grad, gains, memory_grad, self_branch = refs[4:8]
    grad_parts = refs[8:12]
    weights, results, sems, out_sems = refs[12:16]
    value_low, normed, query_low, attended, branch, stream_in, grad_in, self_attended = refs[16:24]
    near = fetch(far, refs[16:24], refs[24])
    rows = block_rows(weights, parts)
    copies = weight_copies(places, parts, 0, weights, rows, sems)
    for copy in copies:
        copy.start()
    sent = []

    def weight_grad(matrix, left_across, right):
        results[matrix] = nn(left_across, right[...]).astype(BF16)
        send_off(
            sent,
            block_copies(
                places, results.at[matrix], matrix * rows, rows, grad_parts, out_sems.at[matrix]
            ),
        )

    memory_across = memory[...].T
    weight_grad(1, memory_across, key_low)
    near[0].wait()
    weight_grad(2, memory_across, value_low)
    for copy in near[1:]:
        copy.wait()
    weight_grad(0, normed[...].T, query_low)
    weight_grad(3, attended[...].T, branch)
    for copy in copies:
        copy.wait()
    normed_grad = nt(query_low[...], weights[0])
    branch_in, gain_grad = norm_back(stream_in[...], gain[1:2], normed_grad)
    total = grad_in[...] + branch_in
    stream_grad[...] = total
    self_branch[...] = total.astype(BF16)
    weight_grad(4, self_attended[...].T, self_branch)
    gains[...] = jnp.broadcast_to(gain_grad, gains.shape)
    memory_grad[...] = nt(key_low[...], weights[1]) + nt(value_low[...], weights[2])
    for copy in sent:
        copy.wait()


def self_attention_backward_kernel(
    places, lengths, branch, query, key, value, totals, *refs,
):
    parts = refs[:4]
    query_low, key_low, value_low, weights, bias, attended_grad, sems = refs[4:]
    rows = block_rows(weights, parts)
    copies = weight_copies(places, parts, 3 * rows, weights, rows, sems)
    for copy in copies:
        copy.start()
    fill_self_bias(bias, lengths)
    for copy in copies:
        copy.wait()
    attended_grad[...] = nt(branch[...], weights[0]).astype(BF16)
    attend_back(
        query, key, value, bias, totals, attended_grad, query_low, key_low, value_low,
        0, HEADS // 2,
    )


def self_backward_kernel(
    places, gain, normed, cross_gains, mlp_gains, query_low, *refs,
):
    far, refs = refs[:4], refs[4:]
    parts = refs[:4]
    stream_grad = refs[4]
    grad_parts = refs[5:9]
    weights, results, terms, sems, out_sems, term_sems = refs[9:15]
    key_low, value_low, grad_in, inputs = refs[15:19]
    near = fetch(far, refs[15:19], refs[19])
    rows = block_rows(weights, parts)
    size = grad_parts[0].shape[0]
    copies = weight_copies(places, parts, 0, weights, rows, sems)
    for copy in copies:
        copy.start()
    sent = []
    normed_across = normed[...].T
    for matrix, low in enumerate((query_low, key_low, value_low)):
        if matrix:
            near[matrix - 1].wait()
        results[matrix] = nn(normed_across, low[...]).astype(BF16)
        send_off(
            sent,
            block_copies(
                places, results.at[matrix], matrix * rows, rows, grad_parts, out_sems.at[matrix]
            ),
        )
    for copy in copies + near[2:]:
        copy.wait()
    normed_grad = (
        nt(query_low[...], weights[0])
        + nt(key_low[...], weights[1])
        + nt(value_low[...], weights[2])
    )
    branch_in, gain_grad = norm_back(inputs[...].astype(F32), gain[0:1], normed_grad)
    stream_grad[...] = grad_in[...] + branch_in
    spot = lax.broadcasted_iota(jnp.int32, (8, gain_grad.shape[1]), 0)
    row = jnp.where(spot == 0, gain_grad, 0.0)
    row = jnp.where(spot == 1, cross_gains[0:1], row)
    row = jnp.where(spot == 2, mlp_gains[0:1], row)
    row = jnp.where(spot == 3, mlp_gains[1:2], row).astype(BF16)
    for start in range(0, terms.shape[0], 8):
        terms[start : start + 8] = row
    send_off(
        sent,
        [
            pltpu.make_async_copy(
                terms,
                grad_parts[slot // size].at[slot % size, pl.ds(3 * rows, terms.shape[0]), :],
                term_sems.at[slot],
            )
            for slot in range(4 * size)
        ],
    )
    for copy in sent:
        copy.wait()


def per_device(
    inputs,
    memory,
    targets,
    tgt_lengths,
    src_lengths,
    self_gain,
    self_query,
    self_key,
    self_value,
    self_out,
    cross_gain,
    cross_query,
    cross_key,
    cross_value,
    cross_out,
    mlp_gain,
    mlp_gate,
    mlp_up,
    mlp_down,
    exit_gain,
    embedding,
):
    tokens, model = inputs.shape
    slots = memory.shape[0]
    hidden_width = mlp_gate.shape[1]
    pair_slots = tgt_lengths.shape[1]
    wide_count = lax.axis_size("wide")
    narrow_count = lax.axis_size("narrow")
    wide = lax.axis_index("wide")
    narrow = lax.axis_index("narrow")
    slot_total = tokens * wide_count * narrow_count
    scale = 1.0 / math.sqrt(model)
    places = slot_places(wide, wide_count)
    lengths, sources = tgt_lengths[0], src_lengths[0]
    shard = self_query.shape[0]
    rows = shard * narrow_count
    down_rows = mlp_down.shape[0] * narrow_count

    aligned = rows % 8 == 0
    kernel_places = places if aligned else jnp.arange(4, dtype=jnp.int32)
    kernel_count = wide_count if aligned else 4
    ids = jnp.arange(wide_count, dtype=jnp.int32)
    order = places[None, :] == ids[:, None]

    def reorder(matrix, blocks):
        flat = blocks.reshape(wide_count, -1)
        return nn(matrix.astype(BF16), flat).astype(BF16).reshape(blocks.shape)

    def for_kernels(parts, sizes):
        if aligned:
            return parts
        whole, start, members = jnp.concatenate(parts, axis=0), 0, []
        for size in sizes:
            ordered = reorder(order, whole[:, start : start + size])
            members.append(ordered.reshape(4, -1, whole.shape[-1]))
            start += size
        return jnp.split(jnp.concatenate(members, axis=1), 4)

    def from_kernels(parts, sizes):
        if aligned:
            return parts
        whole, start, members = jnp.concatenate(parts, axis=0), 0, []
        for size in sizes:
            extent = size * wide_count // 4
            member = whole[:, start : start + extent].reshape(wide_count, size, -1)
            members.append(reorder(order.T, member))
            start += extent
        return jnp.split(jnp.concatenate(members, axis=1), 4)

    def line_block(pieces, sizes, *others):
        pieces = lax.optimization_barrier((*pieces, *others))[: len(pieces)]
        if all(size % 8 == 0 for size in sizes):
            return pl.pallas_call(
                functools.partial(line_kernel, sizes=sizes),
                in_specs=[SMEM] + [VMEM] * len(pieces),
                out_specs=VMEM,
                out_shape=like((pieces[0].shape[0] * len(pieces), pieces[0].shape[1]), BF16),
                compiler_params=PARAMS,
                cost_estimate=work(30),
                name="line_block",
            )(narrow[None], *pieces)
        ordered, start, members = in_line_order(pieces, narrow), 0, []
        for size in sizes:
            members += [piece[start : start + size] for piece in ordered]
            start += size
        return jnp.concatenate(members, axis=0)

    self_sizes, cross_sizes = [shard] * 4 + [8], [shard] * 4 + [mlp_down.shape[0]]
    gate_sizes = [shard] * 2
    count = jnp.sum(lengths)
    owner = wide * narrow_count + narrow
    gain_shards = jnp.stack([self_gain, cross_gain, mlp_gain, exit_gain])
    def join_self():
        return pl.pallas_call(
            join_self_kernel,
            in_specs=[SMEM] * 2 + [VMEM] * 5,
            out_specs=VMEM,
            out_shape=like((sum(self_sizes), model), BF16),
            cost_estimate=work(1),
            name="join_self",
        )(owner[None], lengths, gain_shards, self_query, self_key, self_value, self_out)

    numbers = jnp.broadcast_to(
        jnp.stack([count // 16, count % 16])[:, None], (2, shard)
    ).astype(BF16)
    own_rows = jnp.concatenate([gain_shards, numbers, jnp.zeros((2, shard), BF16)], axis=0)
    own_rows = jnp.tile(own_rows, (1, model // shard))
    own_columns = jnp.arange(model, dtype=jnp.int32)[None, :] // shard == owner
    own_rows = jnp.where(own_columns, own_rows, 0)
    self_pack = (
        join_self()
        if aligned
        else join_rows(self_query, self_key, self_value, self_out, own_rows)
    )
    members = (cross_query, cross_key, cross_value, cross_out, mlp_down)
    side = jnp.stack([targets // 256, targets % 256]).astype(BF16)
    side = jnp.pad(side, ((0, 6), (0, model - tokens)))

    self_line = gather_narrow(self_pack, narrow_count)
    self_block = line_block(self_line, self_sizes)

    vocab = embedding.shape[0]
    padded = -(-vocab // VOCAB_TILE) * VOCAB_TILE
    turned = jnp.pad(embedding.T, ((0, 0), (0, padded - vocab)))
    table = lax.all_gather(tie(turned, *self_line), "narrow", axis=0, tiled=True)

    *early, last = stage_pairs(wide_count)

    def gather_early(block, *others):
        held = block[None]
        for pairs in early:
            came = lax.ppermute(held, "wide", pairs)
            if others:
                came = tie(came, *others)
            held = jnp.concatenate([held, came], axis=0)
        return held

    cross_pack, gate_pack = join_rows(*members), join_rows(mlp_gate, mlp_up)

    def line_even(pack):
        return jnp.stack(
            [pack]
            + [
                lax.ppermute(pack, "narrow", narrow_pairs(narrow_count, step))
                for step in range(2, narrow_count, 2)
            ]
        )

    def line_odd(even):
        return lax.ppermute(even, "narrow", narrow_pairs(narrow_count, 1))

    def line_pair(even, odd, sizes):
        return pl.pallas_call(
            functools.partial(line_pair_kernel, sizes=sizes),
            in_specs=[SMEM] + [VMEM] * 2,
            out_specs=VMEM,
            out_shape=like((narrow_count * even.shape[1], even.shape[2]), BF16),
            compiler_params=PARAMS,
            cost_estimate=work(1),
            name="line_pair",
        )(narrow[None], even, odd)

    self_held = gather_early(self_block)
    if aligned:
        cross_even = line_even(tie(cross_pack, *self_line))
        cross_odd = line_odd(cross_even)
        gate_even = line_even(tie(gate_pack, cross_even))
        gate_odd = line_odd(gate_even)
        self_held = tie(self_held, cross_even)
        cross_block = line_pair(cross_even, tie(cross_odd, self_held), cross_sizes)
    else:
        cross_block = line_block(gather_narrow(cross_pack, narrow_count), cross_sizes)
        gate_block = line_block(gather_narrow(gate_pack, narrow_count), gate_sizes)
    self_came = lax.ppermute(self_held, "wide", last)
    self_parts = (
        self_held, self_came, cross_core(self_held, wide_count), cross_core(self_came, wide_count)
    )
    cross_block = tie(cross_block, self_came)
    if aligned:
        cross_block = tie(cross_block, gate_even)
    cross_held = gather_early(cross_block)
    if aligned:
        cross_held = tie(cross_held, gate_odd)
        gate_block = line_pair(gate_even, gate_odd, gate_sizes)
    cross_came = lax.ppermute(cross_held, "wide", last)

    head_rows = like((HEADS // 2, 1, 2 * tokens), F32)
    activation = like((tokens, model), BF16)
    stream_like = like((tokens, model), F32)
    matrix_sems = pltpu.SemaphoreType.DMA((kernel_count, 4))
    one_matrix_sems = pltpu.SemaphoreType.DMA((kernel_count, 1))

    self_gathered = for_kernels(self_parts, [size * narrow_count for size in self_sizes])
    (
        normed_one, query_one, key_one, value_one, attended_one, totals_one, stream_one, gain_all,
    ) = pl.pallas_call(
        self_forward_kernel,
        in_specs=[SMEM, SMEM, VMEM] + [ANY] * 4,
        out_specs=[VMEM] * 8,
        out_shape=[activation] * 5 + [head_rows, stream_like, like((8, model), F32)],
        scratch_shapes=[
            pltpu.VMEM((4, model, model), BF16),
            pltpu.VMEM((kernel_count, 8 * narrow_count * wide_count // kernel_count, model), BF16),
            pltpu.VMEM((tokens, 2 * tokens), F32),
            matrix_sems,
            pltpu.SemaphoreType.DMA((kernel_count,)),
        ],
        compiler_params=PARAMS,
        cost_estimate=work(1),
        name="self_forward",
    )(kernel_places, lengths, tie(inputs, cross_held), *self_gathered)

    numbers = (gain_all[4] * 16.0 + gain_all[5]).reshape(wide_count, narrow_count, shard)[:, :, 0]
    numbers = jnp.sum(
        jnp.where(jnp.arange(narrow_count)[None, :] == narrow, numbers, 0.0), axis=1
    ).astype(jnp.int32)
    extents = (numbers + 15) // 16 * 16
    starts = jnp.sum(jnp.where(ids[None, :] < ids[:, None], extents[None, :], 0), axis=1)
    needed = (jnp.sum(extents) + ROW_TILE - 1) // ROW_TILE
    meta = jnp.concatenate([jnp.stack([wide, needed]), starts, numbers])
    slot_of = jnp.sum(jnp.where(order, ids[None, :], 0), axis=1)

    cross_came = tie(cross_came, stream_one)
    cross_parts = (
        cross_held, cross_came, cross_core(cross_held, wide_count), cross_core(cross_came, wide_count)
    )
    cross_gathered = for_kernels(cross_parts, [size * narrow_count for size in cross_sizes])

    key_two, value_two = pl.pallas_call(
        memory_kernel,
        in_specs=[SMEM, VMEM] + [ANY] * 4,
        out_specs=[VMEM] * 2,
        out_shape=[like((slots, model), BF16)] * 2,
        scratch_shapes=[
            pltpu.VMEM((2, model, model), BF16),
            pltpu.SemaphoreType.DMA((kernel_count, 2)),
        ],
        compiler_params=PARAMS,
        cost_estimate=work(1),
        name="memory_projection",
    )(kernel_places, memory, *cross_gathered)

    gate_held = gather_early(tie(gate_block, cross_came), key_two)
    gate_came = lax.ppermute(gate_held, "wide", last)

    normed_two, query_two, attended_two, totals_two, stream_two = pl.pallas_call(
        cross_forward_kernel,
        in_specs=[SMEM, SMEM, SMEM, VMEM, VMEM, VMEM, VMEM] + [ANY] * 4,
        out_specs=[VMEM] * 5,
        out_shape=[activation] * 3 + [head_rows, stream_like],
        scratch_shapes=[
            pltpu.VMEM((2, model, model), BF16),
            pltpu.VMEM((slots, 2 * tokens), F32),
            pltpu.SemaphoreType.DMA((2, kernel_count, 1)),
        ],
        compiler_params=PARAMS,
        cost_estimate=work(1),
        name="cross_forward",
    )(
        kernel_places, lengths, sources, tie(stream_one, gate_held), gain_all, key_two, value_two,
        *cross_gathered,
    )

    gate_came = tie(gate_came, stream_two)
    gate_parts = (
        gate_held, gate_came, cross_core(gate_held, wide_count), cross_core(gate_came, wide_count)
    )
    gate_gathered = for_kernels(gate_parts, [size * narrow_count for size in gate_sizes])

    wide_f32 = like((tokens, hidden_width), F32)
    wide_low = like((tokens, hidden_width), BF16)
    normed_three, gate_pre, up_pre, hidden, stream_three, activations, normed_four = pl.pallas_call(
        mlp_forward_kernel,
        in_specs=[SMEM, VMEM, VMEM, VMEM] + [ANY] * 8,
        out_specs=[VMEM] * 7,
        out_shape=[
            activation, wide_f32, wide_f32, wide_low, stream_like, activation,
            like((tokens + 8, model), BF16),
        ],
        scratch_shapes=[
            pltpu.VMEM((2, model, hidden_width), BF16),
            pltpu.VMEM((1, hidden_width, model), BF16),
            pltpu.SemaphoreType.DMA((kernel_count, 2)),
            one_matrix_sems,
        ],
        compiler_params=PARAMS,
        cost_estimate=work(1),
        name="mlp_forward",
    )(kernel_places, stream_two, gain_all, side, *gate_gathered, *cross_gathered)

    exit_held = gather_early(normed_four)
    exit_came = tie(lax.ppermute(exit_held, "wide", last), table)
    exit_parts = (
        exit_held, exit_came, cross_core(exit_held, wide_count), cross_core(exit_came, wide_count)
    )
    group = tokens * wide_count
    tiles = -(-group // (2 * ROW_TILE)) * 2
    kept = lambda i, meta: jnp.minimum(i, meta[META_TILES] - 1)
    kept_pair = lambda i, meta: jnp.minimum(i, (meta[META_TILES] - 1) // 2)

    raised, tokens_across, stats = pl.pallas_call(
        functools.partial(exit_scores_kernel, vocab=vocab, scale=scale),
        grid_spec=pltpu.PrefetchScalarGridSpec(
            num_scalar_prefetch=2,
            grid=(tiles,),
            in_specs=[ANY] * 5,
            out_specs=[
                pl.BlockSpec((ROW_TILE, padded), lambda i, meta, slots: (kept(i, meta), 0)),
                pl.BlockSpec((model, ROW_TILE), lambda i, meta, slots: (0, kept(i, meta))),
                pl.BlockSpec((8, ROW_TILE), lambda i, meta, slots: (0, i)),
            ],
            scratch_shapes=[
                pltpu.VMEM((model, padded), BF16),
                pltpu.VMEM((tiles * ROW_TILE, model), BF16),
                pltpu.VMEM((tiles * ROW_TILE, LANES), F32),
                pltpu.VMEM((min(wide_count, 8), tokens + 8, model), BF16),
                pltpu.VMEM((ROW_TILE, padded), F32),
                pltpu.SemaphoreType.DMA,
                pltpu.SemaphoreType.DMA((min(wide_count, 8),)),
            ],
        ),
        out_shape=[
            like((tiles * ROW_TILE, padded), BF16),
            like((model, tiles * ROW_TILE), BF16),
            like((8, tiles * ROW_TILE), F32),
        ],
        compiler_params=PARAMS,
        cost_estimate=work(52),
        name="exit_scores",
    )(meta, slot_of, *exit_parts, table)

    own_peak = stats[0]
    joint = stats
    for pairs in stage_pairs(wide_count) + [flip_pairs(wide_count)]:
        came = lax.ppermute(joint, "wide", pairs)
        peak = jnp.maximum(joint[0], came[0])
        summed = joint[1] * jnp.exp(joint[0] - peak) + came[1] * jnp.exp(came[0] - peak)
        joint = jnp.concatenate([peak[None], summed[None], joint[2:3] + came[2:3], stats[3:]], axis=0)
    log_total = joint[0] + jnp.log(joint[1])
    picked, group_weight = joint[2], stats[3]
    loss_part = jnp.full((8, LANES), jnp.sum(group_weight * (log_total - picked)), F32)

    factor = jnp.exp(own_peak - log_total) * (group_weight * scale)
    at_target = (jnp.exp(picked - log_total) - 1.0) * (group_weight * scale)
    factors = jnp.concatenate([factor[None], at_target[None], stats[4:5], stats[3:]], axis=0)
    token_part = like((wide_count // 4, tokens, model), BF16)
    exit_grads = pl.pallas_call(
        functools.partial(exit_tokens_kernel, vocab=vocab),
        grid_spec=pltpu.PrefetchScalarGridSpec(
            num_scalar_prefetch=2,
            grid=(tiles,),
            in_specs=[
                ANY,
                pl.BlockSpec((ROW_TILE, padded), lambda i, meta, slots: (kept(i, meta), 0)),
                pl.BlockSpec((8, ROW_TILE), lambda i, meta, slots: (0, i)),
            ],
            out_specs=[ANY] * 4,
            scratch_shapes=[
                pltpu.VMEM((model, padded), BF16),
                pltpu.VMEM((tiles * ROW_TILE, model), BF16),
                pltpu.VMEM((2, tokens, model), BF16),
                pltpu.SemaphoreType.DMA,
                pltpu.SemaphoreType.DMA((2,)),
            ],
        ),
        out_shape=[token_part] * 4,
        compiler_params=PARAMS,
        cost_estimate=work(50),
        name="exit_tokens",
    )(meta, places, table, raised, factors)

    half = padded // 2

    def table_half(side, factors, *before):
        return pl.pallas_call(
            functools.partial(exit_table_kernel, first=side * half, vocab=vocab),
            grid_spec=pltpu.PrefetchScalarGridSpec(
                num_scalar_prefetch=1,
                grid=(tiles // 2,),
                in_specs=[
                    pl.BlockSpec((2 * ROW_TILE, half), lambda i, meta: (kept_pair(i, meta), side)),
                    pl.BlockSpec((model, 2 * ROW_TILE), lambda i, meta: (0, kept_pair(i, meta))),
                    pl.BlockSpec((8, 2 * ROW_TILE), lambda i, meta: (0, i)),
                ]
                + [ANY] * len(before),
                out_specs=pl.BlockSpec((model, half), lambda i, meta: (0, side)),
                scratch_shapes=[pltpu.VMEM((model, half), F32)],
            ),
            out_shape=like((model, padded), BF16),
            input_output_aliases={4: 0} if before else {},
            compiler_params=PARAMS,
            cost_estimate=work(15),
            name="exit_table",
        )(meta, raised, tokens_across, factors, *before)

    exit_scatter = scatter_core(exit_grads, wide_count)
    half_grad = table_half(0, tie(factors, *exit_grads))
    (own, came), exit_kept = exit_scatter
    exit_far = scatter_far((own, tie(came, half_grad)), exit_kept, wide_count)
    table_grad = table_half(1, tie(factors, exit_far[0]), half_grad)
    table_sum = lax.psum_scatter(table_grad, "narrow", scatter_dimension=0, tiled=True)
    embedding_grad = table_sum.astype(F32).T[:vocab]
    exit_near = scatter_near(tie(exit_far[1], table_grad), exit_far[2], wide_count)
    exit_grad = exit_near[2] + exit_near[1].astype(F32)

    gain_like = like((8, model), F32)
    stream_two_grad, mlp_gains, *mlp_grads = pl.pallas_call(
        mlp_backward_kernel,
        in_specs=[SMEM] + [VMEM] * 3 + [ANY] * 13,
        out_specs=[VMEM] * 2 + [ANY] * 8,
        out_shape=[stream_like, gain_like]
        + [like(part.shape, BF16) for part in gate_gathered]
        + [
            like((part.shape[0], hidden_width // kernel_count, model), BF16)
            for part in cross_gathered
        ],
        scratch_shapes=[
            pltpu.VMEM((2, model, hidden_width), BF16),
            pltpu.VMEM((1, hidden_width, model), BF16),
            pltpu.VMEM((tokens, hidden_width), BF16),
            pltpu.VMEM((tokens, hidden_width), BF16),
            pltpu.VMEM((2, model, hidden_width), BF16),
            pltpu.VMEM((hidden_width, model), BF16),
            pltpu.SemaphoreType.DMA((kernel_count, 2)),
            one_matrix_sems,
            pltpu.SemaphoreType.DMA((3, kernel_count)),
            pltpu.VMEM((tokens, hidden_width), F32),
            pltpu.VMEM((tokens, hidden_width), F32),
            pltpu.VMEM((tokens, model), BF16),
            pltpu.VMEM((tokens, hidden_width), BF16),
            pltpu.VMEM((tokens, model), F32),
            pltpu.SemaphoreType.DMA((5,)),
        ],
        compiler_params=PARAMS,
        cost_estimate=work(15),
        name="mlp_backward",
    )(
        kernel_places, exit_grad, stream_three, gain_all, gate_pre, up_pre, normed_three, hidden,
        stream_two, *gate_gathered, *cross_gathered,
    )
    gate_scatter = scatter_core(from_kernels(mlp_grads[:4], [rows, rows]), wide_count)
    down_scatter = scatter_core(from_kernels(mlp_grads[4:], [down_rows]), wide_count)

    def go_far(scatter, *others):
        (own, came), kept = scatter
        return scatter_far((own, tie(came, *others)), kept, wide_count)

    def go_near(state, *others):
        _, came, kept = state
        return scatter_near(tie(came, *others), kept, wide_count)

    low_like = like((slots, model), BF16)
    middle = 2 * (HEADS // 4) * (model // HEADS)
    low_half = like((slots, middle), BF16)
    branch_two, attended_grad, *first_lows = pl.pallas_call(
        cross_attention_first_kernel,
        in_specs=[SMEM] * 3 + [VMEM] * 5 + [ANY] * 4,
        out_specs=[VMEM] * 5,
        out_shape=[activation, activation, like((tokens, middle), BF16), low_half, low_half],
        scratch_shapes=[
            pltpu.VMEM((1, model, model), BF16),
            pltpu.VMEM((slots, 2 * tokens), F32),
            one_matrix_sems,
        ],
        compiler_params=PARAMS,
        cost_estimate=work(16),
        name="cross_attention_first",
    )(
        kernel_places, lengths, sources, stream_two_grad, query_two, key_two, value_two, totals_two,
        *cross_gathered,
    )
    gate_far = go_far(gate_scatter, first_lows[0])
    down_far = go_far(down_scatter, first_lows[0])
    query_two_low, key_two_low, value_two_low = pl.pallas_call(
        cross_attention_last_kernel,
        in_specs=[SMEM] * 2 + [VMEM] * 8,
        out_specs=[VMEM] * 3,
        out_shape=[activation, low_like, low_like],
        scratch_shapes=[pltpu.VMEM((slots, 2 * tokens), F32)],
        compiler_params=PARAMS,
        cost_estimate=work(16),
        name="cross_attention_last",
    )(
        lengths, sources, tie(attended_grad, gate_far[0], down_far[0]), query_two, key_two,
        value_two, totals_two, *first_lows,
    )

    loss_part = tie(loss_part, query_two_low)
    loss_all = loss_part
    for step in range(1, narrow_count):
        loss_all = loss_all + lax.ppermute(loss_part, "narrow", narrow_pairs(narrow_count, step))
    mean_loss = loss_all[0, 0] / slot_total
    cross_matrices = like((cross_gathered[0].shape[0], 5 * model // kernel_count, model), BF16)
    stream_one_grad, cross_gains, memory_grad, branch_one, *cross_grads = pl.pallas_call(
        cross_backward_kernel,
        in_specs=[SMEM] + [VMEM] * 3 + [ANY] * 12,
        out_specs=[VMEM] * 4 + [ANY] * 4,
        out_shape=[stream_like, gain_like, like((slots, model), F32), activation]
        + [cross_matrices] * 4,
        scratch_shapes=[
            pltpu.VMEM((3, model, model), BF16),
            pltpu.VMEM((5, model, model), BF16),
            pltpu.SemaphoreType.DMA((kernel_count, 3)),
            pltpu.SemaphoreType.DMA((5, kernel_count)),
            pltpu.VMEM((slots, model), BF16),
            pltpu.VMEM((tokens, model), BF16),
            pltpu.VMEM((tokens, model), BF16),
            pltpu.VMEM((tokens, model), BF16),
            pltpu.VMEM((tokens, model), BF16),
            pltpu.VMEM((tokens, model), F32),
            pltpu.VMEM((tokens, model), F32),
            pltpu.VMEM((tokens, model), BF16),
            pltpu.SemaphoreType.DMA((8,)),
        ],
        compiler_params=PARAMS,
        cost_estimate=work(20),
        name="cross_backward",
    )(
        kernel_places, gain_all, memory, key_two_low, value_two_low, normed_two, query_two_low,
        attended_two, branch_two, stream_one, stream_two_grad, attended_one, *cross_gathered,
    )
    cross_scatter = scatter_core(from_kernels(cross_grads, [rows] * 5), wide_count)

    gate_near = go_near(gate_far, branch_one)
    down_near = go_near(down_far, branch_one)
    query_one_low, key_one_low, value_one_low = pl.pallas_call(
        self_attention_backward_kernel,
        in_specs=[SMEM] * 2 + [VMEM] * 5 + [ANY] * 4,
        out_specs=[VMEM] * 3,
        out_shape=[activation] * 3,
        scratch_shapes=[
            pltpu.VMEM((1, model, model), BF16),
            pltpu.VMEM((tokens, 2 * tokens), F32),
            pltpu.VMEM((tokens, model), BF16),
            one_matrix_sems,
        ],
        compiler_params=PARAMS,
        cost_estimate=work(10),
        name="self_attention_backward",
    )(
        kernel_places, lengths, tie(branch_one, gate_near[0], down_near[0], loss_all), query_one, key_one, value_one, totals_one,
        *self_gathered,
    )
    def line_blocks(near, matrices, *others):
        _, came, held = near
        summed = held + tie(came, *others).astype(F32)
        width = summed.shape[-1]
        size = matrices * (summed.shape[0] // (matrices * 8 * narrow_count)) * 8 * narrow_count
        members = [
            summed[:size].reshape(matrices, narrow_count, -1, width).transpose(1, 0, 2, 3)
            .reshape(narrow_count, -1, width)
        ]
        if size < summed.shape[0]:
            members.append(summed[size:].reshape(narrow_count, -1, width))
        return jnp.concatenate(members, axis=1)

    def line_first(near, matrices, *others):
        blocks = line_blocks(near, matrices, *others)
        steps = range(0, narrow_count, 2)
        sent = jnp.stack([pick(blocks, narrow ^ (step + 1)) for step in steps]).astype(BF16)
        came = lax.ppermute(sent, "narrow", narrow_pairs(narrow_count, 1))
        return sent, came, [pick(blocks, narrow ^ step) for step in steps]

    def line_second(state, *others):
        _, came, kept = state
        came = tie(came, *others).astype(F32)
        terms = [kept[0] + came[0]]
        for place in range(1, len(kept)):
            sent = (kept[place] + came[place]).astype(BF16)
            terms.append(lax.ppermute(sent, "narrow", narrow_pairs(narrow_count, 2 * place)))
        return terms

    cross_far = go_far(cross_scatter, query_one_low)
    gate_line = line_first(gate_near, 2, query_one_low)

    extra = narrow_count * 8
    spare = extra * wide_count // kernel_count
    inputs_grad, *self_grads = pl.pallas_call(
        self_backward_kernel,
        in_specs=[SMEM] + [VMEM] * 5 + [ANY] * 8,
        out_specs=[VMEM] + [ANY] * 4,
        out_shape=[stream_like]
        + [like((part.shape[0], 3 * model // kernel_count + spare, model), BF16) for part in self_gathered],
        scratch_shapes=[
            pltpu.VMEM((3, model, model), BF16),
            pltpu.VMEM((3, model, model), BF16),
            pltpu.VMEM((spare, model), BF16),
            pltpu.SemaphoreType.DMA((kernel_count, 3)),
            pltpu.SemaphoreType.DMA((3, kernel_count)),
            pltpu.SemaphoreType.DMA((kernel_count,)),
            pltpu.VMEM((tokens, model), BF16),
            pltpu.VMEM((tokens, model), BF16),
            pltpu.VMEM((tokens, model), F32),
            pltpu.VMEM((tokens, model), BF16),
            pltpu.SemaphoreType.DMA((4,)),
        ],
        compiler_params=PARAMS,
        cost_estimate=work(12),
        name="self_backward",
    )(
        kernel_places, gain_all, normed_one, cross_gains, mlp_gains, query_one_low, key_one_low,
        value_one_low, tie(stream_one_grad, gate_line[0], cross_far[0]), inputs, *self_gathered,
    )
    self_scatter = scatter_core(from_kernels(self_grads, [rows] * 3 + [extra]), wide_count)

    cross_near = go_near(cross_far, inputs_grad)
    self_far = go_far(self_scatter, cross_near[0])
    down_line = line_first(down_near, 1, self_far[0])
    gate_terms = line_second(gate_line, self_far[0])
    cross_line = line_first(cross_near, 5, down_line[0], gate_terms[0], embedding_grad)
    self_near = go_near(self_far, cross_line[0])
    down_terms = line_second(down_line, self_near[0])
    gate_sum = add_terms(gate_terms, self_near[0]).reshape(2, shard, hidden_width)
    cross_terms = line_second(cross_line, down_terms[0], gate_sum)
    self_terms = scatter_narrow(
        line_blocks(self_near, 3, cross_terms[0]), narrow, narrow_count
    )
    down_sum = add_terms(down_terms, self_terms[0])
    cross_sum = add_terms(cross_terms, self_terms[0]).reshape(5, shard, model)
    self_sum = add_terms(self_terms)
    gains = pick(self_sum[3 * shard :].reshape(8, model // shard, shard), owner, 1)
    self_sum = self_sum[: 3 * shard].reshape(3, shard, model)

    return (
        activations,
        mean_loss,
        inputs_grad,
        memory_grad,
        gains[0],
        self_sum[0],
        self_sum[1],
        self_sum[2],
        cross_sum[4],
        gains[1],
        cross_sum[0],
        cross_sum[1],
        cross_sum[2],
        cross_sum[3],
        gains[2],
        gate_sum[0],
        gate_sum[1],
        down_sum,
        gains[3],
        embedding_grad,
    )


def solution(mesh):
    both = ("wide", "narrow")
    rows, flat = P(both, None), P(both)
    placed = (
        rows, rows, flat, rows, rows,
        flat, rows, rows, rows, rows,
        flat, rows, rows, rows, rows,
        flat, rows, rows, rows, flat,
        P("wide", "narrow"),
    )
    given = (
        rows, P(), rows, rows,
        flat, rows, rows, rows, rows,
        flat, rows, rows, rows, rows,
        flat, rows, rows, rows, flat,
        P("wide", "narrow"),
    )
    return jax.shard_map(
        per_device, mesh=mesh, in_specs=placed, out_specs=given, check_vma=False
    )
```
